32 devices in a mesh: batch: 8 (over z, core), pix: 4 (over y, x).
Axes of the slice: x: 2, y: 2, z: 4, core: 2. Of those that a mesh axis runs over, the one named last changes fastest.
Arguments:
- queries: float32 [64, 100, 256], P('batch'), may hold values from -6 to 6
- features: bfloat16 [64, 4096, 256], P('batch', 'pix'), may hold values from -6 to 6
- mask_features: bfloat16 [64, 16384, 256], P('batch', 'pix'), may hold values from -0.59765625 to 0.59765625
- attend_bits: int32 [64, 100, 256], P('batch', None, 'pix'), may hold values from 0 to 65535
- reopen_flags: int32 [64, 100], P('batch'), may hold values 0 or 1
- matched_queries: int32 [64, 50], P('batch'), may hold values from 0 to 99, as said below
- query_cotan: bfloat16 [64, 100, 256], P('batch'), may hold values from -6 to 6
- mask_cotan: bfloat16 [64, 50, 16384], P('batch', None, 'pix'), may hold values from -6 to 6
- query_weight: float32 [256, 256], replicated, may hold values from -0.5 to 0.5
- query_bias: float32 [256], replicated, may hold values from -1.8 to 1.8
- keyval_weight: float32 [256, 512], replicated, may hold values from -0.5 to 0.5
- value_bias: float32 [256], replicated, may hold values from -1.8 to 1.8
- cross_out: float32 [256, 256], replicated, may hold values from -9 to 9
- cross_out_bias: float32 [256], replicated, may hold values from -1.8 to 1.8
- norm_gain: float32 [3, 256], replicated, may hold values from 0.5 to 1.5
- norm_bias: float32 [3, 256], replicated, may hold values from -1.8 to 1.8
- self_weight: float32 [256, 768], replicated, may hold values from -0.5 to 0.5
- self_bias: float32 [2, 256], replicated, may hold values from -1.8 to 1.8
- self_out: float32 [256, 256], replicated, may hold values from -2.4 to 2.4
- self_out_bias: float32 [256], replicated, may hold values from -1.8 to 1.8
- hidden_weight: float32 [256, 2048], replicated, may hold values from -0.375 to 0.375
- hidden_bias: float32 [2048], replicated, may hold values from -1.8 to 1.8
- hidden_out: float32 [2048, 256], replicated, may hold values from -0.125 to 0.125
- hidden_out_bias: float32 [256], replicated, may hold values from -1.8 to 1.8
- embed_weight: float32 [3, 256, 256], replicated, may hold values from -0.375 to 0.375
- embed_bias: float32 [3, 256], replicated, may hold values from -1.8 to 1.8
Outputs:
- queries_out: float32 [64, 100, 256], P('batch')
- mask_logits: float32 [64, 100, 16384], P('batch', None, 'pix')
- queries_grad: float32 [64, 100, 256], P('batch')
- features_grad: float32 [64, 4096, 256], P('batch', 'pix')
- mask_features_grad: float32 [64, 16384, 256], P('batch', 'pix')
- grad_query_weight: float32 [256, 256], replicated
- grad_query_bias: float32 [256], replicated
- grad_keyval_weight: float32 [256, 512], replicated
- grad_value_bias: float32 [256], replicated
- grad_cross_out: float32 [256, 256], replicated
- grad_cross_out_bias: float32 [256], replicated
- grad_norm_gain: float32 [3, 256], replicated
- grad_norm_bias: float32 [3, 256], replicated
- grad_self_weight: float32 [256, 768], replicated
- grad_self_bias: float32 [2, 256], replicated
- grad_self_out: float32 [256, 256], replicated
- grad_self_out_bias: float32 [256], replicated
- grad_hidden_weight: float32 [256, 2048], replicated
- grad_hidden_bias: float32 [2048], replicated
- grad_hidden_out: float32 [2048, 256], replicated
- grad_hidden_out_bias: float32 [256], replicated
- grad_embed_weight: float32 [3, 256, 256], replicated
- grad_embed_bias: float32 [3, 256], replicated
The draws below stay inside these ranges and needn't reach their ends.
Inputs may be any that keep to these rules, and one draw needn't show every extreme that they name: `attend_bits`: bit b of word w of a query's row gives pixel 16 w + b of the image's row-major 1/8-scale map; 1 means the query attends to that pixel. `matched_queries`: the 50 entries of one image are distinct query indices; entry m pairs that query with row m of mask_cotan.
All inputs are finite; a program needn't handle non-finite values. No bound on the sum of `reopen_flags` on one device may be relied on, other than what follows from the above.
Results may differ from the reference program's by a relative error of at most 0.04.
The reference program's roundings to bfloat16 on the way count: a program that leaves them out, or rounds other values in their place, can miss the bound.
Values sent between devices are 32-bit elements; how exact they have to be, the bound alone decides.
No kernel may reach another device: no remote copies, remote signals or barrier semaphores. Data moves between devices by JAX's collectives and lax.ppermute only.
A program may use at most 256 MiB of HBM per device.

```python
import math
import jax
import jax.numpy as jnp
from jax import lax

D = 256
HEADS = 8
FF = 2048
OBJECT_QUERIES = 100
P8 = 4096
QUARTER_PIXELS = 16384
MATCHED = 50
HEAD_DIM = 32
IMAGES = 64


def draw_matched_queries(key, part):
    key = jax.random.fold_in(key, 7)
    keys = jax.random.split(key, IMAGES)
    picked = jax.vmap(lambda one: jax.random.permutation(one, OBJECT_QUERIES)[:MATCHED])(keys)
    return picked.astype(jnp.int32)


def plant(result, stream_key, low, top_value):
    longest = result.shape.index(max(result.shape))
    spots = []
    for shift in (0, 1):
        where = [jax.random.randint(jax.random.fold_in(stream_key, axis), (), 0, length) for axis, length in enumerate(result.shape)]
        where[longest] = (where[longest] + shift) % result.shape[longest]
        spots.append(tuple(where))
    return result.at[spots[0]].set(low).at[spots[1]].set(top_value)


def steps_of(key, dims, shards, low, high):
    def one(dim, parts):
        steps = jax.random.uniform(jax.random.fold_in(jax.random.fold_in(key, 6), dim), (parts,), jnp.float32, low / len(shards), high / len(shards))
        return jnp.repeat(jnp.exp(steps), dims[dim] // parts).reshape((-1,) + (1,) * (len(dims) - dim - 1))

    loudness = one(*shards[0])
    for cut in shards[1:]:
        loudness = loudness * one(*cut)
    return loudness


def centred(key, shape, width, most, cuts=(), held_as=jnp.bfloat16):
    array = width * jax.random.normal(key, shape, jnp.float32)
    if cuts:
        array = array * steps_of(key, shape, cuts, -0.22, 0.18)
    return jnp.clip(array, -most, most).astype(held_as)


def setup_inputs(seed: int = 0) -> dict:
    splits = jax.random.split(jax.random.key(seed), 27)
    queries = centred(splits[0], (IMAGES, OBJECT_QUERIES, D), 1.0, 6.0, ((0, 8),), jnp.float32)
    features = centred(splits[1], (IMAGES, P8, D), 1.0, 6.0, ((0, 8), (1, 4)))
    mask_features = centred(splits[2], (IMAGES, QUARTER_PIXELS, D), 0.1, 0.59765625, ((0, 8), (1, 4)))
    attend_bits = plant(jax.random.randint(splits[3], (IMAGES, OBJECT_QUERIES, P8 // 16), 0, 65536), jax.random.fold_in(splits[3], 1), 0, 65535).astype(jnp.int32)
    reopen_flags = plant((jax.random.randint(splits[4], (IMAGES, OBJECT_QUERIES), 0, 8) < 1).astype(jnp.int32), jax.random.fold_in(splits[4], 1), 0, 1)
    matched_queries = draw_matched_queries(jax.random.fold_in(splits[26], 71), 0)
    query_cotan = centred(splits[6], (IMAGES, OBJECT_QUERIES, D), 1.0, 6.0, ((0, 8),))
    mask_cotan = centred(splits[7], (IMAGES, MATCHED, QUARTER_PIXELS), 1.0, 6.0, ((0, 8), (2, 4)))
    query_weight = centred(splits[8], (D, D), (D // 2) ** -0.5, 0.5, (), jnp.float32)
    query_bias = centred(splits[9], (D,), 0.3, 1.8, (), jnp.float32)
    keyval_weight = centred(splits[10], (D, 2 * D), (D // 2) ** -0.5, 0.5, (), jnp.float32)
    value_bias = centred(splits[11], (D,), 0.3, 1.8, (), jnp.float32)
    cross_out = centred(splits[12], (D, D), 1.5, 9.0, (), jnp.float32)
    cross_out_bias = centred(splits[13], (D,), 0.3, 1.8, (), jnp.float32)
    norm_gain = jnp.clip(1.0 + 0.1 * jax.random.normal(splits[14], (3, D), jnp.float32), 0.5, 1.5)
    norm_bias = centred(splits[15], (3, D), 0.3, 1.8, (), jnp.float32)
    self_weight = centred(splits[16], (D, 3 * D), (D // 2) ** -0.5, 0.5, (), jnp.float32)
    self_bias = centred(splits[17], (2, D), 0.3, 1.8, (), jnp.float32)
    self_out = centred(splits[18], (D, D), 0.4, 2.4, (), jnp.float32)
    self_out_bias = centred(splits[19], (D,), 0.3, 1.8, (), jnp.float32)
    hidden_weight = centred(splits[20], (D, FF), D ** -0.5, 0.375, (), jnp.float32)
    hidden_bias = centred(splits[21], (FF,), 0.3, 1.8, (), jnp.float32)
    hidden_out = centred(splits[22], (FF, D), FF ** -0.5, 0.125, (), jnp.float32)
    hidden_out_bias = centred(splits[23], (D,), 0.3, 1.8, (), jnp.float32)
    embed_weight = centred(splits[24], (3, D, D), D ** -0.5, 0.375, (), jnp.float32)
    embed_bias = centred(splits[25], (3, D), 0.3, 1.8, (), jnp.float32)
    return {"queries": queries, "features": features, "mask_features": mask_features, "attend_bits": attend_bits, "reopen_flags": reopen_flags, "matched_queries": matched_queries, "query_cotan": query_cotan, "mask_cotan": mask_cotan, "query_weight": query_weight, "query_bias": query_bias, "keyval_weight": keyval_weight, "value_bias": value_bias, "cross_out": cross_out, "cross_out_bias": cross_out_bias, "norm_gain": norm_gain, "norm_bias": norm_bias, "self_weight": self_weight, "self_bias": self_bias, "self_out": self_out, "self_out_bias": self_out_bias, "hidden_weight": hidden_weight, "hidden_bias": hidden_bias, "hidden_out": hidden_out, "hidden_out_bias": hidden_out_bias, "embed_weight": embed_weight, "embed_bias": embed_bias}


EPS = 1e-05
PENALTY = 10000.0
HP = lax.Precision.HIGHEST

@jax.custom_vjp
def low(v):
    return lax.optimization_barrier(v.astype(jnp.bfloat16)).astype(jnp.float32)

@jax.custom_vjp
def low_back(v):
    return v

def low_keep(v):
    return (low(v), None)

def low_pass(kept, grad):
    return (grad,)

def back_keep(v):
    return (v, None)

def back_low(kept, grad):
    return (low(grad),)
low.defvjp(low_keep, low_pass)
low_back.defvjp(back_keep, back_low)

def both(v):
    return low(low_back(v))

def matmul(a, b):
    return jnp.matmul(a, b, precision=HP)

def layer_norm(x, gain, bias):
    centre = x - lax.optimization_barrier(jnp.mean(x, -1, keepdims=True))
    var = lax.optimization_barrier(jnp.mean(centre * centre, -1, keepdims=True))
    return centre * lax.rsqrt(var + EPS) * gain + bias

def split_heads(x):
    return x.reshape(x.shape[0], HEADS, HEAD_DIM)

def forward(params, x0, feat, mfeat, opened):
    scale = 1.0 / math.sqrt(HEAD_DIM)
    cq = low(low_back(matmul(low(x0), low(params[0])) + params[1]) * scale)
    keyval = matmul(feat, low(params[2]))
    ck = both(keyval[:, :D])
    raw = low_back(jnp.einsum('qhc,phc->hqp', split_heads(cq), split_heads(ck), precision=HP))
    scores = raw - PENALTY * (1.0 - opened)[None]
    row_max = lax.optimization_barrier(jnp.max(scores, -1))
    cv = both(keyval[:, D:] + params[3])
    expo = jnp.exp(scores - row_max[..., None])
    total = lax.optimization_barrier(jnp.sum(expo, -1))
    numer = low_back(jnp.einsum('hqp,phc->qhc', low(expo), split_heads(cv), precision=HP))
    attended = low((numer / jnp.transpose(total)[..., None]).reshape(OBJECT_QUERIES, D))
    pre1 = x0 + low_back(matmul(attended, low(params[4])) + params[5])
    x1 = layer_norm(pre1, params[6][0], params[7][0])
    mixed = matmul(low(x1), low(params[8]))
    sq = low(low_back(mixed[:, :D] + params[9][0]) * scale)
    sk = both(mixed[:, D:2 * D])
    sv = both(mixed[:, 2 * D:] + params[9][1])
    sscore = low_back(jnp.einsum('qhc,khc->hqk', split_heads(sq), split_heads(sk), precision=HP))
    probs = jax.nn.softmax(sscore, -1)
    selfout = both(jnp.einsum('hqk,khc->qhc', low(probs), split_heads(sv), precision=HP).reshape(OBJECT_QUERIES, D))
    pre2 = x1 + low_back(matmul(selfout, low(params[10])) + params[11])
    x2 = layer_norm(pre2, params[6][1], params[7][1])
    zed = low_back(matmul(low(x2), low(params[12])) + params[13])
    hidden = low(jax.nn.gelu(zed))
    pre3 = x2 + low_back(matmul(hidden, low(params[14])) + params[15])
    x3 = layer_norm(pre3, params[6][2], params[7][2])
    zed1 = low_back(matmul(low(x3), low(params[16][0])) + params[17][0])
    hid1 = low(jax.nn.gelu(zed1))
    zed2 = low_back(matmul(hid1, low(params[16][1])) + params[17][1])
    hid2 = low(jax.nn.gelu(zed2))
    embed = both(matmul(hid2, low(params[16][2])) + params[17][2])
    logits = matmul(embed, jnp.transpose(mfeat))
    return (x3, logits)

def reference(queries, features, mask_features, attend_bits, reopen_flags, matched_queries, query_cotan, mask_cotan, query_weight, query_bias, keyval_weight, value_bias, cross_out, cross_out_bias, norm_gain, norm_bias, self_weight, self_bias, self_out, self_out_bias, hidden_weight, hidden_bias, hidden_out, hidden_out_bias, embed_weight, embed_bias):
    params = (query_weight, query_bias, keyval_weight, value_bias, cross_out, cross_out_bias, norm_gain, norm_bias, self_weight, self_bias, self_out, self_out_bias, hidden_weight, hidden_bias, hidden_out, hidden_out_bias, embed_weight, embed_bias)
    shifts = jnp.arange(16, dtype=jnp.int32)
    bits = attend_bits[..., None] >> shifts & 1
    bits = bits.reshape(IMAGES, OBJECT_QUERIES, P8)
    opened = jnp.maximum(bits, reopen_flags[..., None]).astype(jnp.float32)
    zero_filled = jax.tree.map(jnp.zeros_like, params)

    def step(acc, item):
        x0, feat, mfeat, opn, query_gradient, matched_rows, mask_gradient = item

        def local(p, a, b, c):
            return forward(p, a, b, c, opn)
        outs, gather_rows = jax.vjp(local, params, x0, feat, mfeat)
        logit_gradient = jnp.zeros((OBJECT_QUERIES, QUARTER_PIXELS), mask_gradient.dtype).at[matched_rows.astype(jnp.int32)].add(mask_gradient)
        parameter_grads, input_state_grad, feature_map_grad, mask_feature_gradient = gather_rows((query_gradient, logit_gradient))
        acc = jax.tree.map(jnp.add, acc, parameter_grads)
        return (acc, (outs[0], outs[1], input_state_grad, feature_map_grad, mask_feature_gradient))
    items = (queries, features.astype(jnp.float32), mask_features.astype(jnp.float32), opened, query_cotan.astype(jnp.float32), matched_queries, mask_cotan.astype(jnp.float32))
    grads, stacked = lax.scan(step, zero_filled, items)
    return (stacked[0], stacked[1], stacked[2], stacked[3], stacked[4], grads[0], grads[1], grads[2], grads[3], grads[4], grads[5], grads[6], grads[7], grads[8], grads[9], grads[10], grads[11], grads[12], grads[13], grads[14], grads[15], grads[16], grads[17])
```

```python
import functools
import math

import jax
import jax.numpy as jnp
from jax import lax
from jax.experimental import pallas as pl
from jax.experimental.pallas import tpu as pltpu
from jax.sharding import PartitionSpec as P

HEADS = 8
EPS = 1e-05
PENALTY = 10000.0
F32 = jnp.float32
LOW = jnp.bfloat16
HIGH = lax.Precision.HIGHEST
CURVE = math.sqrt(2.0 / math.pi)
CUBE = 0.044715
MIB = 1 << 20

T_CROSS, T_SELF, T_SELFOUT, T_EMBED, T_HIDDEN = 0, 1, 4, 5, 8


def up(n, m):
    return (n + m - 1) // m * m


def nn(a, b, precision=None):
    return lax.dot_general(a, b, (((1,), (0,)), ((), ())), precision=precision, preferred_element_type=F32)


def nt(a, b, precision=None):
    return lax.dot_general(a, b, (((1,), (1,)), ((), ())), precision=precision, preferred_element_type=F32)


def tn(a, b, precision=None):
    return lax.dot_general(a, b, (((0,), (0,)), ((), ())), precision=precision, preferred_element_type=F32)


def head_mask(width):
    shape = (HEADS, 1, width)
    head = width // HEADS
    return lax.broadcasted_iota(jnp.int32, shape, 2) // head == lax.broadcasted_iota(jnp.int32, shape, 0)


def spread(x, mask):
    rows, width = x.shape
    return jnp.where(mask, x[None], 0.0).reshape(HEADS * rows, width)


def gather_heads(x, mask):
    total, width = x.shape
    return jnp.sum(jnp.where(mask, x.reshape(HEADS, total // HEADS, width), 0.0), 0)


def spread_low(x, mask):
    return spread(x, mask).astype(LOW)


def head_onehot(width, lanes, transposed=False):
    head = width // HEADS
    if transposed:
        shape, a, b = (width, lanes), 0, 1
    else:
        shape, a, b = (lanes, width), 1, 0
    hit = lax.broadcasted_iota(jnp.int32, shape, a) // head == lax.broadcasted_iota(jnp.int32, shape, b)
    return hit.astype(F32)


def cost(flops, nbytes, trans=0):
    return pl.CostEstimate(flops=int(flops), bytes_accessed=int(nbytes), transcendentals=int(trans))


def whole(x):
    shape = x.shape
    return pl.BlockSpec(shape, lambda *_: (0,) * len(shape))


def params(mib):
    return pltpu.CompilerParams(vmem_limit_bytes=mib * MIB, dimension_semantics=("arbitrary",))


def mask_part_kernel(mc_ref, mf_ref, out_ref):
    out_ref[0] = nn(mc_ref[0], mf_ref[0])


def mask_part(mask_cotan, mask_features):
    images, matched, pixels = mask_cotan.shape
    width = mask_features.shape[2]
    return pl.pallas_call(
        mask_part_kernel,
        grid=(images,),
        in_specs=[
            pl.BlockSpec((1, matched, pixels), lambda i: (i, 0, 0)),
            pl.BlockSpec((1, pixels, width), lambda i: (i, 0, 0)),
        ],
        out_specs=pl.BlockSpec((1, matched, width), lambda i: (i, 0, 0)),
        out_shape=jax.ShapeDtypeStruct((images, matched, width), F32),
        compiler_params=params(32),
        cost_estimate=cost(2 * images * 64 * pixels * width, images * pixels * (width + matched) * 2),
        name="mask_part",
    )(mask_cotan, mask_features)


def attend_kernel(groups, q_ref, f_ref, bits_ref, flag_ref, wq_ref, bq_ref, wkv_ref, vb_ref, elo_ref, ehi_ref,
                  e_ref, kv_ref, pay_ref, cq_ref, q_scr, w_scr):
    i = pl.program_id(0)
    count, width = q_ref.shape[1:]
    rows = q_scr.shape[0]
    pixels = f_ref.shape[1]
    words = bits_ref.shape[2]

    @pl.when(i == 0)
    def _():
        q_scr[...] = jnp.zeros_like(q_scr)
        w_scr[...] = jnp.zeros_like(w_scr)

    q_scr[0:count] = q_ref[0]
    row = lax.broadcasted_iota(jnp.int32, flag_ref.shape, 0)
    flags = jnp.where(row == i, flag_ref[...], 0).astype(F32).astype(LOW)
    flag_col = tn(flags, jnp.ones((flags.shape[0], words), LOW))
    w_scr[0:count] = jnp.where(flag_col > 0.5, 65535, bits_ref[0])

    hm = head_mask(width)
    scale = 1.0 / math.sqrt(width // HEADS)
    cq = ((nn(q_scr[...].astype(LOW), wq_ref[...]) + bq_ref[...]) * scale).astype(LOW).astype(F32)
    cq_ref[0] = cq
    cqx = spread_low(cq, hm)

    bits = w_scr[...]
    low = (bits & 255).astype(F32).astype(LOW)
    high = (bits >> 8).astype(F32).astype(LOW)
    byte = (nn(low, elo_ref[...]) + nn(high, ehi_ref[...])).astype(jnp.int32)
    shift = lax.broadcasted_iota(jnp.int32, (rows, pixels), 1) & 7
    pen = jnp.where(((byte >> shift) & 1) == 1, 0.0, -PENALTY)

    keyval = nn(f_ref[0], wkv_ref[...])
    ck = keyval[:, :width].astype(LOW)
    cv = (keyval[:, width:] + vb_ref[...]).astype(LOW)
    kv_ref[0, :, :width] = ck
    kv_ref[0, :, width:] = cv

    per = HEADS // groups
    numer = jnp.zeros((rows, width), F32)
    lane = lax.broadcasted_iota(jnp.int32, (rows, 128), 1)
    stats = jnp.zeros((rows, 128), F32)
    for g in range(groups):
        at = slice(g * per * rows, (g + 1) * per * rows)
        s = nt(cqx[at], ck).reshape(per, rows, pixels) + pen[None]
        m = jnp.max(s, -1, keepdims=True)
        e = jnp.exp(s - m)
        total = jnp.sum(e, -1, keepdims=True)
        e_low = e.reshape(per * rows, pixels).astype(LOW)
        e_ref[0, at] = e_low
        part = nn(e_low, cv).reshape(per, rows, width)
        numer = numer + jnp.sum(jnp.where(hm[g * per:(g + 1) * per], part, 0.0), 0)
        for h in range(per):
            stats = jnp.where(lane == g * per + h, m[h], stats)
            stats = jnp.where(lane == HEADS + g * per + h, total[h], stats)
    pay_ref[0, 0:rows] = numer
    full = jnp.concatenate([stats, jnp.ones((128 - rows, 128), F32)], 0)
    turned = jnp.transpose(full)
    pay_ref[0, rows:rows + HEADS, 0:128] = turned[0:HEADS]
    pay_ref[0, rows:rows + HEADS, 128:256] = turned[HEADS:2 * HEADS]


def attend(queries, features, attend_bits, reopen_flags, w_query, query_bias, w_keyval, value_bias):
    images, count, width = queries.shape
    pixels = features.shape[1]
    words = attend_bits.shape[2]
    rows = up(count, 8)
    pixel = jnp.arange(pixels)
    word = jnp.arange(words)
    here = pixel[None, :] // 16 == word[:, None]
    e_lo = (here & (pixel[None, :] % 16 < 8)).astype(LOW)
    e_hi = (here & (pixel[None, :] % 16 >= 8)).astype(LOW)
    per = lambda *shape: pl.BlockSpec((1,) + shape, lambda i: (i,) + (0,) * len(shape))
    args = (queries, features, attend_bits, reopen_flags, w_query, query_bias[None], w_keyval, value_bias[None], e_lo, e_hi)
    flops = 2 * images * (pixels * width * 2 * width + 2 * HEADS * rows * pixels * width)
    nbytes = images * (pixels * width * 6 + HEADS * rows * pixels * 2)
    return pl.pallas_call(
        functools.partial(attend_kernel, 2),
        grid=(images,),
        in_specs=[per(count, width), per(pixels, width), per(count, words)] + [whole(a) for a in args[3:]],
        out_specs=(per(HEADS * rows, pixels), per(pixels, 2 * width), per(rows + HEADS, width), per(rows, width)),
        out_shape=(
            jax.ShapeDtypeStruct((images, HEADS * rows, pixels), LOW),
            jax.ShapeDtypeStruct((images, pixels, 2 * width), LOW),
            jax.ShapeDtypeStruct((images, rows + HEADS, width), F32),
            jax.ShapeDtypeStruct((images, rows, width), F32),
        ),
        scratch_shapes=[pltpu.VMEM((rows, width), F32), pltpu.VMEM((rows, words), jnp.int32)],
        compiler_params=params(48),
        cost_estimate=cost(flops, nbytes, images * HEADS * rows * pixels),
        name="attend",
    )(*args)


def combine_kernel(*refs):
    out_ref = refs[-1]
    parts = refs[:-1]
    images, tall, width = out_ref.shape
    rows = tall - HEADS
    onehot = head_onehot(width, HEADS)
    for i in range(images):
        ms = [p[i, rows:tall, 0:128] for p in parts]
        ls = [p[i, rows:tall, 128:256] for p in parts]
        top = functools.reduce(jnp.maximum, ms)
        rs = [jnp.exp(m - top) for m in ms]
        total = sum(r * l for r, l in zip(rs, ls))
        acc = jnp.zeros((rows, width), F32)
        for p, r in zip(parts, rs):
            acc = acc + p[i, 0:rows] * tn(r / total, onehot, HIGH)[0:rows]
        out_ref[i, 0:rows] = acc
        out_ref[i, rows:tall, 0:128] = top
        out_ref[i, rows:tall, 128:256] = total


def combine(parts):
    shape = parts[0].shape
    return pl.pallas_call(
        combine_kernel,
        out_shape=jax.ShapeDtypeStruct(shape, F32),
        compiler_params=pltpu.CompilerParams(vmem_limit_bytes=32 * MIB),
        cost_estimate=cost(1e6, 5 * 4 * math.prod(shape)),
        name="combine",
    )(*parts)


def norm_forward(x, gain, bias):
    centre = x - jnp.mean(x, -1, keepdims=True)
    inverse = lax.rsqrt(jnp.mean(centre * centre, -1, keepdims=True) + EPS)
    normed = centre * inverse
    return normed * gain + bias, normed, inverse


def norm_backward(normed, inverse, gain, grad):
    dnormed = grad * gain
    return inverse * (
        dnormed - jnp.mean(dnormed, -1, keepdims=True) - normed * jnp.mean(dnormed * normed, -1, keepdims=True)
    )


def gelu_pair(x):
    square = x * x
    t = jnp.tanh(x * (CURVE + (CURVE * CUBE) * square))
    half = 0.5 + 0.5 * t
    slope = half + (0.5 * x) * (1.0 - t * t) * (CURVE + (3.0 * CURVE * CUBE) * square)
    return x * half, slope


def column_sum(x):
    return jnp.sum(x, 0, keepdims=True)


def chain_kernel(
    pieces, me_ref, *refs
):
    att_parts, refs = refs[:pieces], refs[pieces:]
    es_parts, refs = refs[:pieces], refs[pieces:]
    (loc_ref, q_ref, match_ref, cot_ref, wc_ref, bc_ref, gain_ref, nbias_ref, ws_ref, bs_ref, wso_ref, bso_ref,
     wh_ref, bh_ref, who_ref, bho_ref, we_ref, be_ref,
     x3_ref, emb_ref, dn_ref, dt_ref, dp1_ref, g_ref,
     att_scr, es_scr, q_scr, sq_scr, sk_scr, sv_scr, so_scr, pr_scr, h_scr, gp_scr, dso_scr, dm_scr) = refs
    step = pl.program_id(0)
    batch, count, width = q_ref.shape
    rows = dn_ref.shape[1]
    flat = batch * rows
    hidden = wh_ref.shape[1]
    scale = 1.0 / math.sqrt(width // HEADS)
    hm = head_mask(width)
    me = me_ref[0]

    @pl.when(step == 0)
    def _():
        n = att_parts[0].shape[0]
        for k in range(pieces):
            spot = pl.ds((me ^ k) * n, n)
            att_scr[spot] = att_parts[k][...]
            es_scr[spot] = es_parts[k][...]
        q_scr[...] = jnp.zeros_like(q_scr)
        g_ref[...] = jnp.zeros_like(g_ref)

    def put(tile, value):
        g_ref[tile * width:(tile + 1) * width] += value

    bias_at = (T_HIDDEN + 2 * (hidden // width)) * width

    def put_bias(index, value):
        g_ref[bias_at + index:bias_at + index + 1] += value

    first = step * batch
    q_scr[:, 0:count] = q_ref[...]
    att = att_scr[pl.ds(first, batch), 0:rows].reshape(flat, width)
    att_low = att.astype(LOW)
    queries = q_scr[...].reshape(flat, width)
    x1, n1, i1 = norm_forward(queries + nn(att_low, wc_ref[...]) + bc_ref[...], gain_ref[0:1], nbias_ref[0:1])
    x1_low = x1.astype(LOW)
    mixed = nn(x1_low, ws_ref[...])
    three = (batch, rows, width)
    sq_scr[...] = ((mixed[:, :width] + bs_ref[0:1]) * scale).reshape(three)
    sk_scr[...] = mixed[:, width:2 * width].reshape(three)
    sv_scr[...] = (mixed[:, 2 * width:] + bs_ref[1:2]).reshape(three)

    def self_forward(b, carry):
        sqx = spread_low(sq_scr[b], hm)
        ss = nt(sqx, sk_scr[b].astype(LOW))
        keys = lax.broadcasted_iota(jnp.int32, ss.shape, 1)
        ss = jnp.where(keys < count, ss, -1e30)
        p = jnp.exp(ss - jnp.max(ss, -1, keepdims=True))
        p = p / jnp.sum(p, -1, keepdims=True)
        pr_scr[b] = p
        so_scr[b] = gather_heads(nn(p.astype(LOW), sv_scr[b].astype(LOW)), hm)
        return carry

    lax.fori_loop(0, batch, self_forward, 0)
    so_low = so_scr[...].reshape(flat, width).astype(LOW)
    x2, n2, i2 = norm_forward(x1 + nn(so_low, wso_ref[...]) + bso_ref[...], gain_ref[1:2], nbias_ref[1:2])
    x2_low = x2.astype(LOW)
    block = 2 * width

    def ff_forward(j, acc):
        cols = pl.ds(pl.multiple_of(j * block, block), block)
        h, slope = gelu_pair(nn(x2_low, wh_ref[:, cols]) + bh_ref[:, cols])
        h = h.astype(LOW)
        h_scr[:, cols] = h
        gp_scr[:, cols] = slope.astype(gp_scr.dtype)
        return acc + nn(h, who_ref[cols, :])

    ff = lax.fori_loop(0, hidden // block, ff_forward, jnp.zeros((flat, width), F32))
    x3, n3, i3 = norm_forward(x2 + ff + bho_ref[...], gain_ref[2:3], nbias_ref[2:3])
    x3_ref[...] = x3.reshape(three)[:, 0:count]

    x3_low = x3.astype(LOW)
    h1, slope1 = gelu_pair(nn(x3_low, we_ref[0]) + be_ref[0:1])
    h1 = h1.astype(LOW)
    h2, slope2 = gelu_pair(nn(h1, we_ref[1]) + be_ref[1:2])
    h2 = h2.astype(LOW)
    emb_ref[...] = (nn(h2, we_ref[2]) + be_ref[2:3]).reshape(three)

    grads = []
    for b in range(batch):
        matched = match_ref.shape[1]
        spots = match_ref[pl.ds(first + b, 1), :]
        pick = (lax.broadcasted_iota(jnp.int32, (rows, matched), 0) == spots).astype(F32).astype(LOW)
        grads.append(nn(pick, es_scr[first + b].astype(LOW)))
    dz3 = jnp.concatenate(grads, 0)
    dz3_low = dz3.astype(LOW)
    put(T_EMBED + 2, tn(h2, dz3_low))
    put_bias(19, column_sum(dz3_low.astype(F32)))
    dz2 = (nt(dz3_low, we_ref[2]) * slope2).astype(LOW)
    put(T_EMBED + 1, tn(h1, dz2))
    put_bias(18, column_sum(dz2.astype(F32)))
    dz1 = (nt(dz2, we_ref[1]) * slope1).astype(LOW)
    put(T_EMBED, tn(x3_low, dz1))
    put_bias(17, column_sum(dz1.astype(F32)))
    q_scr[:, 0:count] = cot_ref[...].astype(F32)
    dx3 = q_scr[...].reshape(flat, width) + nt(dz1, we_ref[0])
    put_bias(3, column_sum(dx3 * n3))
    put_bias(6, column_sum(dx3))
    dp3 = norm_backward(n3, i3, gain_ref[2:3], dx3)
    dff = dp3.astype(LOW)
    put_bias(16, column_sum(dff.astype(F32)))

    def ff_backward(j, acc):
        cols = pl.ds(pl.multiple_of(j * block, block), block)
        base = (T_HIDDEN + hidden // width) * width
        spot = pl.ds(pl.multiple_of(base + j * block, block), block)
        g_ref[spot] += tn(h_scr[:, cols], dff)
        dz = (nt(dff, who_ref[cols, :]) * gp_scr[:, cols].astype(F32)).astype(LOW)
        gh = tn(x2_low, dz)
        sums = column_sum(dz.astype(F32))
        for t in range(block // width):
            tile = pl.ds(pl.multiple_of(T_HIDDEN * width + j * block + t * width, width), width)
            g_ref[tile] += gh[:, t * width:(t + 1) * width]
            g_ref[pl.ds(bias_at + 8 + j * (block // width) + t, 1)] += sums[:, t * width:(t + 1) * width]
        return acc + nt(dz, wh_ref[:, cols])

    dx2 = dp3 + lax.fori_loop(0, hidden // block, ff_backward, jnp.zeros((flat, width), F32))
    put_bias(2, column_sum(dx2 * n2))
    put_bias(5, column_sum(dx2))
    dp2 = norm_backward(n2, i2, gain_ref[1:2], dx2)
    dsa = dp2.astype(LOW)
    put(T_SELFOUT, tn(so_low, dsa))
    put_bias(7, column_sum(dsa.astype(F32)))
    dso_scr[...] = nt(dsa, wso_ref[...]).reshape(three)

    def self_backward(b, carry):
        sqx = spread_low(sq_scr[b], hm)
        dsox = spread_low(dso_scr[b], hm)
        p = pr_scr[b]
        dp = nt(dsox, sv_scr[b].astype(LOW))
        dss = (p * (dp - jnp.sum(p * dp, -1, keepdims=True))).astype(LOW)
        dm_scr[b, :, 0:width] = gather_heads(nn(dss, sk_scr[b].astype(LOW)), hm) * scale
        dm_scr[b, :, width:2 * width] = tn(dss, sqx)
        dm_scr[b, :, 2 * width:] = tn(p.astype(LOW), dsox)
        return carry

    lax.fori_loop(0, batch, self_backward, 0)
    dm = dm_scr[...].reshape(flat, 3 * width).astype(LOW)
    gs = tn(x1_low, dm)
    for t in range(3):
        put(T_SELF + t, gs[:, t * width:(t + 1) * width])
    put_bias(20, column_sum(dm[:, :width].astype(F32)))
    put_bias(21, column_sum(dm[:, 2 * width:].astype(F32)))
    dx1 = dp2 + nt(dm, ws_ref[...])
    put_bias(1, column_sum(dx1 * n1))
    put_bias(4, column_sum(dx1))
    dp1 = norm_backward(n1, i1, gain_ref[0:1], dx1)
    dp1_ref[...] = dp1.reshape(three)
    dca = dp1.astype(LOW)
    put(T_CROSS, tn(att_low, dca))
    put_bias(0, column_sum(dca.astype(F32)))
    d_att = nt(dca, wc_ref[...]).reshape(three)
    onehot = head_onehot(width, HEADS)
    back = head_onehot(width, 128, True)
    tall = rows + HEADS
    for b in range(batch):
        top = att_scr[first + b, rows:tall, 0:128]
        total = att_scr[first + b, rows:tall, 128:256]
        ratio = jnp.exp(loc_ref[b, rows:tall, 0:128] - top) / total
        dn = d_att[b] * tn(ratio, onehot, HIGH)[0:rows]
        dn_ref[b] = dn
        dt_ref[b] = -nn(dn * att_scr[first + b, 0:rows], back, HIGH)


def chain(me, att_parts, es_parts, pay, queries, matched, query_cotan, weights):
    images, count, width = queries.shape
    tall = pay.shape[1]
    rows = tall - HEADS
    pieces = len(att_parts)
    batch = images // 2
    hidden = weights[8].shape[1]
    tiles = T_HIDDEN + 2 * (hidden // width)
    grads = up(tiles * width + 22, 256)
    half = lambda *shape: pl.BlockSpec((batch,) + shape, lambda i, *_: (i,) + (0,) * len(shape))
    args = tuple(att_parts) + tuple(es_parts) + (pay, queries, matched, query_cotan) + weights
    in_specs = [whole(a) for a in args]
    base = 2 * pieces
    in_specs[base] = half(tall, width)
    in_specs[base + 1] = half(count, width)
    in_specs[base + 3] = half(count, width)
    out_shape = (
        jax.ShapeDtypeStruct((images, count, width), F32),
        jax.ShapeDtypeStruct((images, rows, width), F32),
        jax.ShapeDtypeStruct((images, rows, width), F32),
        jax.ShapeDtypeStruct((images, rows, 128), F32),
        jax.ShapeDtypeStruct((images, rows, width), F32),
        jax.ShapeDtypeStruct((grads, width), F32),
    )
    flat = batch * rows
    three = (batch, rows, width)
    return pl.pallas_call(
        functools.partial(chain_kernel, pieces),
        grid_spec=pltpu.PrefetchScalarGridSpec(
            num_scalar_prefetch=1,
            grid=(2,),
            in_specs=in_specs,
            out_specs=(half(count, width), half(rows, width), half(rows, width), half(rows, 128), half(rows, width),
                       pl.BlockSpec((grads, width), lambda i, *_: (0, 0))),
            scratch_shapes=[
                pltpu.VMEM((images, tall, width), F32),
                pltpu.VMEM((images,) + es_parts[0].shape[1:], F32),
                pltpu.VMEM(three, F32),
                pltpu.VMEM(three, F32),
                pltpu.VMEM(three, F32),
                pltpu.VMEM(three, F32),
                pltpu.VMEM(three, F32),
                pltpu.VMEM((batch, HEADS * rows, rows), F32),
                pltpu.VMEM((flat, hidden), LOW),
                pltpu.VMEM((flat, hidden), LOW),
                pltpu.VMEM(three, F32),
                pltpu.VMEM((batch, rows, 3 * width), F32),
            ],
        ),
        out_shape=out_shape,
        compiler_params=params(60),
        cost_estimate=cost(2 * 8e9, 20e6, 4e6),
        name="chain",
    )(me, *args)


def mask_out_kernel(emb_ref, match_ref, mc_ref, mf_ref, logit_ref, grad_ref):
    i = pl.program_id(0)
    count = logit_ref.shape[1]
    rows = emb_ref.shape[1]
    matched = match_ref.shape[1]
    emb = emb_ref[0].astype(LOW)
    spots = match_ref[pl.ds(i, 1), :]
    pick = (lax.broadcasted_iota(jnp.int32, (rows, matched), 0) == spots).astype(F32).astype(LOW)
    chosen = tn(pick, emb).astype(LOW)
    logit_ref[0] = nt(emb, mf_ref[0])[0:count]
    grad_ref[0] = tn(mc_ref[0], chosen)


def mask_out(emb, matched_queries, mask_cotan, mask_features, count):
    images, matched, pixels = mask_cotan.shape
    rows, width = emb.shape[1:]
    part = min(pixels, 2048)
    return pl.pallas_call(
        mask_out_kernel,
        grid=(images, pixels // part),
        in_specs=[
            pl.BlockSpec((1, rows, width), lambda i, j: (i, 0, 0)),
            whole(matched_queries),
            pl.BlockSpec((1, matched, part), lambda i, j: (i, 0, j)),
            pl.BlockSpec((1, part, width), lambda i, j: (i, j, 0)),
        ],
        out_specs=(
            pl.BlockSpec((1, count, part), lambda i, j: (i, 0, j)),
            pl.BlockSpec((1, part, width), lambda i, j: (i, j, 0)),
        ),
        out_shape=(
            jax.ShapeDtypeStruct((images, count, pixels), F32),
            jax.ShapeDtypeStruct((images, pixels, width), F32),
        ),
        compiler_params=pltpu.CompilerParams(vmem_limit_bytes=32 * MIB, dimension_semantics=("arbitrary", "arbitrary")),
        cost_estimate=cost(2 * images * pixels * width * 160, images * pixels * (width * 6 + count * 4 + matched * 2)),
        name="mask_out",
    )(emb, matched_queries, mask_cotan, mask_features)


def attend_back_kernel(quads, e_ref, kv_ref, f_ref, cq_ref, dn_ref, dt_ref, wkv_ref, qp_ref, fg_ref, g_ref, vb_ref, acc_scr):
    i = pl.program_id(0)
    rows, width = cq_ref.shape[1:]
    pixels = f_ref.shape[1]
    hm = head_mask(width)

    @pl.when(i == 0)
    def _():
        acc_scr[...] = jnp.zeros_like(acc_scr)
        vb_ref[...] = jnp.zeros_like(vb_ref)

    ck = kv_ref[0, :, :width]
    cv = kv_ref[0, :, width:]
    cqx = spread_low(cq_ref[0], hm)
    dnx = spread_low(dn_ref[0], hm)
    per = HEADS // quads
    lanes = width // quads
    part = jnp.zeros((rows, width), F32)
    keys, values = [], []
    for g in range(quads):
        at = slice(g * per * rows, (g + 1) * per * rows)
        cols = slice(g * lanes, (g + 1) * lanes)
        e_low = e_ref[0, at]
        dw = nt(dnx[at], cv).reshape(per, rows, pixels)
        dt = jnp.stack([dt_ref[0, :, g * per + h:g * per + h + 1] for h in range(per)], 0)
        ds = (e_low.astype(F32).reshape(per, rows, pixels) * (dw + dt)).reshape(per * rows, pixels).astype(LOW)
        back = nn(ds, ck).reshape(per, rows, width)
        part = part + jnp.sum(jnp.where(hm[g * per:(g + 1) * per], back, 0.0), 0)
        keys.append(tn(cqx[at, cols], ds))
        values.append(tn(dnx[at, cols], e_low))
    qp_ref[0] = part
    turned = jnp.concatenate(keys + values, 0).astype(LOW)
    acc_scr[...] += nn(turned, f_ref[0])
    summed = turned[width:].astype(F32)
    lanes_sum = summed[:, 0:128]
    for t in range(1, pixels // 128):
        lanes_sum = lanes_sum + summed[:, t * 128:(t + 1) * 128]
    vb_ref[...] += lanes_sum
    fg_ref[0] = tn(turned, wkv_ref[...])

    @pl.when(i == pl.num_programs(0) - 1)
    def _():
        g_ref[0:width] = jnp.transpose(acc_scr[0:width])
        g_ref[width:] = jnp.transpose(acc_scr[width:])


def attend_back(e, kv, features, cq, dn, dt, wkv_turned):
    images, pixels, width = features.shape
    rows = cq.shape[1]
    per = lambda *shape: pl.BlockSpec((1,) + shape, lambda i: (i,) + (0,) * len(shape))
    tall = HEADS * rows
    flops = 2 * images * (4 * tall * pixels * width + 4 * pixels * width * width)
    nbytes = images * (tall * pixels * 2 + pixels * width * 10)
    return pl.pallas_call(
        functools.partial(attend_back_kernel, 2),
        grid=(images,),
        in_specs=[per(tall, pixels), per(pixels, 2 * width), per(pixels, width), per(rows, width), per(rows, width),
                  per(rows, 128), whole(wkv_turned)],
        out_specs=(per(rows, width), per(pixels, width), pl.BlockSpec((2 * width, width), lambda i: (0, 0)),
                   pl.BlockSpec((width, 128), lambda i: (0, 0))),
        out_shape=(
            jax.ShapeDtypeStruct((images, rows, width), F32),
            jax.ShapeDtypeStruct((images, pixels, width), F32),
            jax.ShapeDtypeStruct((2 * width, width), F32),
            jax.ShapeDtypeStruct((width, 128), F32),
        ),
        scratch_shapes=[pltpu.VMEM((2 * width, width), F32)],
        compiler_params=params(48),
        cost_estimate=cost(flops, nbytes),
        name="attend_back",
    )(e, kv, features, cq, dn, dt, wkv_turned)


def query_back_kernel(pieces, me_ref, *refs):
    parts = refs[:pieces]
    q_ref, dp_ref, wq_ref, qg_ref, g_ref, scr = refs[pieces:]
    n, count, width = q_ref.shape
    rows = dp_ref.shape[1]
    scale = 1.0 / math.sqrt(width // HEADS)
    total = parts[0][...]
    for p in parts[1:]:
        total = total + p[...]
    scr[...] = jnp.zeros_like(scr)
    scr[:, 0:count] = q_ref[...]
    d_cq = (total * scale).reshape(n * rows, width).astype(LOW)
    out = dp_ref[...] + nt(d_cq, wq_ref[...]).reshape(n, rows, width)
    qg_ref[...] = out[:, 0:count]
    g_ref[0:width] = tn(scr[...].reshape(n * rows, width).astype(LOW), d_cq)
    g_ref[width:] = jnp.zeros((g_ref.shape[0] - width, width), F32)
    g_ref[width:width + 1] = column_sum(d_cq.astype(F32))


def query_back(me, parts, queries, dp1, w_query):
    n, rows, width = parts[0].shape
    count = queries.shape[1]
    pieces = len(parts)
    args = tuple(parts) + (queries, dp1, w_query)
    mine = lambda *shape: pl.BlockSpec((n,) + shape, lambda i, at: (at[0],) + (0,) * len(shape))
    in_specs = [whole(a) for a in parts] + [mine(count, width), mine(rows, width), whole(w_query)]
    out_shape = (jax.ShapeDtypeStruct((n, count, width), F32), jax.ShapeDtypeStruct((width + 8, width), F32))
    return pl.pallas_call(
        functools.partial(query_back_kernel, pieces),
        grid_spec=pltpu.PrefetchScalarGridSpec(
            num_scalar_prefetch=1,
            grid=(1,),
            in_specs=in_specs,
            out_specs=tuple(whole(o) for o in out_shape),
            scratch_shapes=[pltpu.VMEM((n, rows, width), F32)],
        ),
        out_shape=out_shape,
        compiler_params=params(32),
        cost_estimate=cost(2e8, 4e6),
        name="query_back",
    )(me, *args)


def swap(x, axis, n, k):
    return lax.ppermute(x, axis, [(i, i ^ k) for i in range(n)])


def scatter_parts(x, axis, n, keys):
    me = lax.axis_index(axis)
    step = keys[1] if len(keys) > 1 else 1
    got = []
    for k in keys:
        chunk = lax.dynamic_index_in_dim(x, ((me ^ k) // step) % len(keys), 0, keepdims=False)
        got.append(chunk if k == 0 else swap(chunk, axis, n, k))
    return got


def gather_parts(x, axis, n, keys):
    return [x if k == 0 else swap(x, axis, n, k) for k in keys]


def in_order(parts, axis, keys):
    me = lax.axis_index(axis)
    step = keys[1] if len(keys) > 1 else 1
    out = jnp.zeros((len(keys),) + parts[0].shape, parts[0].dtype)
    for k, part in zip(keys, parts):
        out = lax.dynamic_update_index_in_dim(out, part, ((me ^ k) // step) % len(keys), 0)
    return out


def reduce_parts(x, axis, n, keys):
    parts = scatter_parts(x.reshape((len(keys), -1) + x.shape[1:]), axis, n, keys)
    return functools.reduce(jnp.add, parts)


def gather_all(x, axis, n, keys):
    out = in_order(gather_parts(x, axis, n, keys), axis, keys)
    return out.reshape((-1,) + x.shape[1:])


def local(
    queries, features, mask_features, attend_bits, reopen_flags, matched_queries, query_cotan, mask_cotan,
    query_weight, query_bias, keyval_weight, value_bias, cross_out, cross_out_bias, norm_gain, norm_bias,
    self_weight, self_bias, self_out, self_out_bias, hidden_weight, hidden_bias, hidden_out, hidden_out_bias,
    embed_weight, embed_bias, *, n_pix, n_batch,
):
    images, count, width = queries.shape
    hidden = hidden_weight.shape[1]
    rows = up(count, 8)
    tall = rows + HEADS
    pix_keys = list(range(n_pix))
    core_keys, z_keys = [0, 1], list(range(0, n_batch, 2))
    split = images % n_pix == 0
    pix = lax.axis_index("pix")
    w_query = query_weight.astype(LOW)
    w_keyval = keyval_weight.astype(LOW)

    es_local = mask_part(mask_cotan, mask_features)
    e, kv, pay, cq = attend(
        queries, features, attend_bits, reopen_flags, w_query, query_bias, w_keyval, value_bias)
    if split:
        me = pix.astype(jnp.int32).reshape(1)
        es_sum = reduce_parts(es_local, "pix", n_pix, pix_keys)
        es_parts = gather_parts(es_sum, "pix", n_pix, pix_keys)
        chunks = pay.reshape((n_pix, images // n_pix, tall, width))
        mine = combine(scatter_parts(chunks, "pix", n_pix, pix_keys))
        att_parts = gather_parts(mine, "pix", n_pix, pix_keys)
    else:
        me = jnp.zeros((1,), jnp.int32)
        es_parts = [lax.psum(es_local, "pix")]
        top = lax.pmax(pay[:, rows:, :128], "pix")
        ratio = jnp.exp(pay[:, rows:, :128] - top)

        def widen(x):
            return jnp.repeat(jnp.transpose(x, (0, 2, 1))[:, :rows], width // HEADS, axis=2)

        numer, total = lax.psum((pay[:, :rows] * widen(ratio), pay[:, rows:, 128:] * ratio), "pix")
        att_parts = [jnp.concatenate([numer / widen(total), jnp.concatenate([top, total], 2)], 1)]

    weights = (
        cross_out.astype(LOW), cross_out_bias[None], norm_gain, norm_bias, self_weight.astype(LOW), self_bias,
        self_out.astype(LOW), self_out_bias[None], hidden_weight.astype(LOW), hidden_bias[None],
        hidden_out.astype(LOW), hidden_out_bias[None], embed_weight.astype(LOW), embed_bias,
    )
    x3, emb, dn, dt, dp1, grads = chain(
        me, att_parts, es_parts, pay, queries, matched_queries, query_cotan, weights)

    part = lax.dynamic_index_in_dim(grads.reshape(n_pix, -1, width), pix, 0, keepdims=False)
    part = reduce_parts(part, "batch", n_batch, core_keys)
    part = reduce_parts(part, "batch", n_batch, z_keys)
    part = gather_all(part, "batch", n_batch, z_keys)
    part = gather_all(part, "pix", n_pix, pix_keys)
    pair = gather_all(part, "batch", n_batch, core_keys)
    all_grads = jnp.swapaxes(pair.reshape(2, n_pix, -1, width), 0, 1).reshape(-1, width)

    qp, feat_grad, g_kv, g_vb = attend_back(e, kv, features, cq, dn, dt, jnp.transpose(w_keyval))
    logits, mask_grad = mask_out(emb, matched_queries, mask_cotan, mask_features, count)
    if split:
        parts = scatter_parts(qp.reshape((n_pix, images // n_pix, rows, width)), "pix", n_pix, pix_keys)
        my_grad, g_q = query_back(me, parts, queries, dp1, w_query)
        queries_grad = gather_all(my_grad, "pix", n_pix, pix_keys)
    else:
        queries_grad, g_q = query_back(me, [lax.psum(qp, "pix")], queries, dp1, w_query)
        g_q = g_q / n_pix
    tail = jnp.concatenate([g_kv, g_q, jnp.zeros((256 - 8, width), F32)], 0)
    tail = lax.dynamic_update_slice(tail, jnp.sum(g_vb, 1)[None], (3 * width + 1, 0))
    tail = reduce_parts(tail, "pix", n_pix, pix_keys)
    tail = reduce_parts(tail, "batch", n_batch, core_keys)
    tail = reduce_parts(tail, "batch", n_batch, z_keys)
    tail = gather_all(tail, "batch", n_batch, z_keys)
    tail = gather_all(tail, "batch", n_batch, core_keys)
    tail = gather_all(tail, "pix", n_pix, pix_keys)

    def tile(t, k=1):
        return all_grads[t * width:(t + k) * width]

    def wide(t, k):
        return jnp.concatenate([tile(t + j) for j in range(k)], 1)

    many = hidden // width
    bias = all_grads[(T_HIDDEN + 2 * many) * width:]
    return (
        x3,
        logits,
        queries_grad,
        feat_grad,
        mask_grad,
        tail[2 * width:3 * width],
        tail[3 * width],
        jnp.concatenate([tail[:width], tail[width:2 * width]], 1),
        tail[3 * width + 1],
        tile(T_CROSS),
        bias[0],
        bias[1:4],
        bias[4:7],
        wide(T_SELF, 3),
        bias[20:22],
        tile(T_SELFOUT),
        bias[7],
        wide(T_HIDDEN, many),
        bias[8:8 + many].reshape(-1),
        tile(T_HIDDEN + many, many),
        bias[16],
        tile(T_EMBED, 3).reshape(3, width, width),
        bias[17:20],
    )


def solution(mesh):
    n_pix, n_batch = mesh.shape["pix"], mesh.shape["batch"]
    rep = P()
    row, pixel, column = P("batch", None, None), P("batch", "pix", None), P("batch", None, "pix")
    in_specs = (row, pixel, pixel, column, P("batch", None), P("batch", None), row, column) + (rep,) * 18
    out_specs = (row, column, row, pixel, pixel) + (rep,) * 18
    body = functools.partial(local, n_pix=n_pix, n_batch=n_batch)
    return jax.shard_map(body, mesh=mesh, in_specs=in_specs, out_specs=out_specs, check_vma=False)
```

```python
import functools
import math

import jax
import jax.numpy as jnp
from jax import lax
from jax.experimental import pallas as pl
from jax.experimental.pallas import tpu as pltpu
from jax.sharding import PartitionSpec as P

HEADS = 8
EPS = 1e-05
PENALTY = 10000.0
F32 = jnp.float32
LOW = jnp.bfloat16
HIGH = lax.Precision.HIGHEST
CURVE = math.sqrt(2.0 / math.pi)
CUBE = 0.044715
MIB = 1 << 20

T_CROSS, T_SELF, T_SELFOUT, T_EMBED, T_HIDDEN = 0, 1, 4, 5, 8


def up(n, m):
    return (n + m - 1) // m * m


def nn(a, b, precision=None):
    return lax.dot_general(a, b, (((1,), (0,)), ((), ())), precision=precision, preferred_element_type=F32)


def nt(a, b, precision=None):
    return lax.dot_general(a, b, (((1,), (1,)), ((), ())), precision=precision, preferred_element_type=F32)


def tn(a, b, precision=None):
    return lax.dot_general(a, b, (((0,), (0,)), ((), ())), precision=precision, preferred_element_type=F32)


def head_mask(width):
    shape = (HEADS, 1, width)
    head = width // HEADS
    return lax.broadcasted_iota(jnp.int32, shape, 2) // head == lax.broadcasted_iota(jnp.int32, shape, 0)


def spread(x, mask):
    rows, width = x.shape
    return jnp.where(mask, x[None], 0.0).reshape(HEADS * rows, width)


def gather_heads(x, mask):
    total, width = x.shape
    return jnp.sum(jnp.where(mask, x.reshape(HEADS, total // HEADS, width), 0.0), 0)


def spread_low(x, mask):
    return spread(x, mask).astype(LOW)


def head_onehot(width, lanes, transposed=False):
    head = width // HEADS
    if transposed:
        shape, a, b = (width, lanes), 0, 1
    else:
        shape, a, b = (lanes, width), 1, 0
    hit = lax.broadcasted_iota(jnp.int32, shape, a) // head == lax.broadcasted_iota(jnp.int32, shape, b)
    return hit.astype(F32)


def slabs_in(scr, value):
    for t in range(scr.shape[0]):
        scr[t] = value[:, t * 128:(t + 1) * 128]


def take_image(scr, image, count, images):
    rows = pl.ds(image, count, images)
    return jnp.concatenate([scr[t, rows, :] for t in range(scr.shape[0])], 1)


def put_image(scr, image, count, images, value):
    for t in range(scr.shape[0]):
        scr[t, pl.ds(image, count, images), :] = value[:, t * 128:(t + 1) * 128]


def slabs(rows, columns):
    return pltpu.VMEM((columns // 128, rows, 128), F32)


def cost(flops, nbytes, trans=0):
    return pl.CostEstimate(flops=int(flops), bytes_accessed=int(nbytes), transcendentals=int(trans))


def whole(x):
    shape = x.shape
    return pl.BlockSpec(shape, lambda *_: (0,) * len(shape))


def params(mib):
    return pltpu.CompilerParams(vmem_limit_bytes=mib * MIB, dimension_semantics=("arbitrary",))


def attend_kernel(groups, q_ref, f_ref, bits_ref, flag_ref, mc_ref, mf_ref, wq_ref, bq_ref, wkv_ref, vb_ref, elo_ref,
                  ehi_ref, e_ref, kv_ref, pay_ref, cq_ref, q_scr, w_scr, all_scr, mc_scr, wq_scr, wkv_scr):
    i = pl.program_id(0)
    matched, images, wide = mc_ref.shape
    width = q_ref.shape[1]
    count = q_ref.shape[0] // images
    rows = q_scr.shape[0]
    pixels = f_ref.shape[1]
    tall = rows + HEADS

    @pl.when(i == 0)
    def _():
        q_scr[...] = jnp.zeros_like(q_scr)
        w_scr[...] = jnp.zeros_like(w_scr)
        slabs_in(all_scr, q_ref[...])
        slabs_in(mc_scr, mc_ref[...].astype(F32).reshape(matched * images, wide))
        wq_scr[...] = wq_ref[...].astype(LOW)
        wkv_scr[...] = wkv_ref[...].astype(LOW)

    pay_ref[0, tall:] = jnp.zeros((pay_ref.shape[1] - tall, width), F32)
    pay_ref[0, tall:tall + matched] = nn(take_image(mc_scr, i, matched, images).astype(LOW), mf_ref[0])

    q_scr[0:count] = take_image(all_scr, i, count, images)
    w_scr[:, 0:count] = jnp.where(flag_ref[pl.ds(i, 1), :] > 0, 65535, bits_ref[0])

    hm = head_mask(width)
    scale = 1.0 / math.sqrt(width // HEADS)
    cq = ((nn(q_scr[...].astype(LOW), wq_scr[...]) + bq_ref[...]) * scale).astype(LOW).astype(F32)
    cq_ref[0] = cq
    cqx = spread_low(cq, hm)

    bits = w_scr[...]
    low = (bits & 255).astype(F32).astype(LOW)
    high = (bits >> 8).astype(F32).astype(LOW)
    byte = (tn(low, elo_ref[...]) + tn(high, ehi_ref[...])).astype(jnp.int32)
    shift = lax.broadcasted_iota(jnp.int32, (rows, pixels), 1) & 7
    pen = jnp.where(((byte >> shift) & 1) == 1, 0.0, -PENALTY)

    keyval = nn(f_ref[0], wkv_scr[...])
    ck = keyval[:, :width].astype(LOW)
    cv = (keyval[:, width:] + vb_ref[...]).astype(LOW)
    kv_ref[0, :, :width] = ck
    kv_ref[0, :, width:] = cv

    per = HEADS // groups
    numer = jnp.zeros((rows, width), F32)
    lane = lax.broadcasted_iota(jnp.int32, (rows, 128), 1)
    stats = jnp.zeros((rows, 128), F32)
    for g in range(groups):
        at = slice(g * per * rows, (g + 1) * per * rows)
        s = nt(cqx[at], ck).reshape(per, rows, pixels) + pen[None]
        m = jnp.max(s, -1, keepdims=True)
        e = jnp.exp(s - m)
        total = jnp.sum(e, -1, keepdims=True)
        e_low = e.reshape(per * rows, pixels).astype(LOW)
        e_ref[0, at] = e_low
        part = nn(e_low, cv).reshape(per, rows, width)
        numer = numer + jnp.sum(jnp.where(hm[g * per:(g + 1) * per], part, 0.0), 0)
        for h in range(per):
            stats = jnp.where(lane == g * per + h, m[h], stats)
            stats = jnp.where(lane == HEADS + g * per + h, total[h], stats)
    pay_ref[0, 0:rows] = numer
    full = jnp.concatenate([stats, jnp.ones((128 - rows, 128), F32)], 0)
    turned = jnp.transpose(full)
    pay_ref[0, rows:tall, 0:128] = turned[0:HEADS]
    pay_ref[0, rows:tall, 128:256] = turned[HEADS:2 * HEADS]


def attend(queries, features, bits, reopen_flags, mask_cotan, mask_features, query_weight, query_bias, keyval_weight,
           value_bias):
    images, pixels, width = features.shape
    words, count = bits.shape[1:]
    rows = up(count, 8)
    matched, _, wide = mask_cotan.shape
    tall = rows + HEADS + up(matched, 8)
    pixel = jnp.arange(pixels)
    word = jnp.arange(words)
    here = pixel[None, :] // 16 == word[:, None]
    e_lo = (here & (pixel[None, :] % 16 < 8)).astype(LOW)
    e_hi = (here & (pixel[None, :] % 16 >= 8)).astype(LOW)
    per = lambda *shape: pl.BlockSpec((1,) + shape, lambda i: (i,) + (0,) * len(shape))
    args = (queries, features, bits, reopen_flags, mask_cotan, mask_features, query_weight, query_bias[None],
            keyval_weight, value_bias[None], e_lo, e_hi)
    in_specs = [whole(a) for a in args]
    in_specs[1] = per(pixels, width)
    in_specs[2] = per(words, count)
    in_specs[5] = per(wide, width)
    flops = 2 * images * (pixels * width * 2 * width + 2 * HEADS * rows * pixels * width + 64 * wide * width)
    nbytes = images * (pixels * width * 6 + HEADS * rows * pixels * 2 + wide * (width + matched) * 2)
    return pl.pallas_call(
        functools.partial(attend_kernel, 2),
        grid=(images,),
        in_specs=in_specs,
        out_specs=(per(HEADS * rows, pixels), per(pixels, 2 * width), per(tall, width), per(rows, width)),
        out_shape=(
            jax.ShapeDtypeStruct((images, HEADS * rows, pixels), LOW),
            jax.ShapeDtypeStruct((images, pixels, 2 * width), LOW),
            jax.ShapeDtypeStruct((images, tall, width), F32),
            jax.ShapeDtypeStruct((images, rows, width), F32),
        ),
        scratch_shapes=[
            pltpu.VMEM((rows, width), F32),
            pltpu.VMEM((words, rows), jnp.int32),
            slabs(count * images, width),
            slabs(matched * images, wide),
            pltpu.VMEM((width, width), LOW),
            pltpu.VMEM((width, 2 * width), LOW),
        ],
        compiler_params=params(56),
        cost_estimate=cost(flops, nbytes, images * HEADS * rows * pixels),
        name="attend",
    )(*args)


def combine_kernel(matched, parts_ref, out_ref):
    pieces, images, tall, width = parts_ref.shape
    copies = out_ref.shape[0]
    top_at = tall - up(matched, 8) - HEADS
    rows = top_at
    es_at = rows + HEADS
    onehot = head_onehot(width, HEADS)
    for i in range(images):
        ms = [parts_ref[p, i, rows:es_at, 0:128] for p in range(pieces)]
        ls = [parts_ref[p, i, rows:es_at, 128:256] for p in range(pieces)]
        top = functools.reduce(jnp.maximum, ms)
        rs = [jnp.exp(m - top) for m in ms]
        total = sum(r * l for r, l in zip(rs, ls))
        acc = jnp.zeros((rows, width), F32)
        es = jnp.zeros((tall - es_at, width), F32)
        for p, r in enumerate(rs):
            acc = acc + parts_ref[p, i, 0:rows] * tn(r / total, onehot, HIGH)[0:rows]
            es = es + parts_ref[p, i, es_at:]
        for c in range(copies):
            out_ref[c, i, 0:rows] = acc
            out_ref[c, i, rows:es_at, 0:128] = top
            out_ref[c, i, rows:es_at, 128:256] = total
            out_ref[c, i, es_at:] = es


def combine(parts, matched):
    return pl.pallas_call(
        functools.partial(combine_kernel, matched),
        out_shape=jax.ShapeDtypeStruct(parts.shape, F32),
        compiler_params=pltpu.CompilerParams(vmem_limit_bytes=32 * MIB),
        cost_estimate=cost(1e6, 2 * 4 * math.prod(parts.shape)),
        name="combine",
    )(parts)


def norm_forward(x, gain, bias):
    centre = x - jnp.mean(x, -1, keepdims=True)
    inverse = lax.rsqrt(jnp.mean(centre * centre, -1, keepdims=True) + EPS)
    normed = centre * inverse
    return normed * gain + bias, normed, inverse


def norm_backward(normed, inverse, gain, grad):
    dnormed = grad * gain
    return inverse * (
        dnormed - jnp.mean(dnormed, -1, keepdims=True) - normed * jnp.mean(dnormed * normed, -1, keepdims=True)
    )


def gelu_pair(x):
    square = x * x
    t = jnp.tanh(x * (CURVE + (CURVE * CUBE) * square))
    half = 0.5 + 0.5 * t
    slope = half + (0.5 * x) * (1.0 - t * t) * (CURVE + (3.0 * CURVE * CUBE) * square)
    return x * half, slope


def column_sum(x):
    return jnp.sum(x, 0, keepdims=True)


def chain_kernel(
    att_ref, loc_ref, q_ref, match_ref, cot_ref, wc_raw, bc_ref, gain_ref, nbias_ref, ws_raw, bs_ref, wso_raw, bso_ref,
    wh_raw, bh_ref, who_raw, bho_ref, we_raw, be_ref,
    x3_ref, emb_ref, dn_ref, dt_ref, dp1_ref, g_ref,
    wc_ref, ws_ref, wso_ref, wh_ref, who_ref, we_ref, all_scr, cot_scr, out_scr,
    q_scr, sq_scr, sk_scr, sv_scr, so_scr, pr_scr, h_scr, gp_scr, dso_scr, dm_scr
):
    step = pl.program_id(0)
    batch, rows, width = dn_ref.shape
    matched = match_ref.shape[1]
    count, images = cot_ref.shape[:2]
    tall = rows + HEADS
    flat = batch * rows
    hidden = wh_ref.shape[1]
    scale = 1.0 / math.sqrt(width // HEADS)
    hm = head_mask(width)

    @pl.when(step == 0)
    def _():
        q_scr[...] = jnp.zeros_like(q_scr)
        g_ref[...] = jnp.zeros_like(g_ref)
        slabs_in(all_scr, q_ref[...])
        slabs_in(cot_scr, cot_ref[...].astype(F32).reshape(count * images, width))
        for raw, ref in ((wc_raw, wc_ref), (ws_raw, ws_ref), (wso_raw, wso_ref), (wh_raw, wh_ref), (who_raw, who_ref),
                         (we_raw, we_ref)):
            ref[...] = raw[...].astype(LOW)

    def put(tile, value):
        g_ref[tile * width:(tile + 1) * width] += value

    bias_at = (T_HIDDEN + 2 * (hidden // width)) * width

    def put_bias(index, value):
        g_ref[bias_at + index:bias_at + index + 1] += value

    first = step * batch
    for b in range(batch):
        q_scr[b, 0:count] = take_image(all_scr, first + b, count, images)
    att = att_ref[:, 0:rows].reshape(flat, width)
    att_low = att.astype(LOW)
    queries = q_scr[...].reshape(flat, width)
    x1, n1, i1 = norm_forward(queries + nn(att_low, wc_ref[...]) + bc_ref[...], gain_ref[0:1], nbias_ref[0:1])
    x1_low = x1.astype(LOW)
    mixed = nn(x1_low, ws_ref[...])
    three = (batch, rows, width)
    sq_scr[...] = ((mixed[:, :width] + bs_ref[0:1]) * scale).reshape(three)
    sk_scr[...] = mixed[:, width:2 * width].reshape(three)
    sv_scr[...] = (mixed[:, 2 * width:] + bs_ref[1:2]).reshape(three)

    def self_forward(b, carry):
        sqx = spread_low(sq_scr[b], hm)
        ss = nt(sqx, sk_scr[b].astype(LOW))
        keys = lax.broadcasted_iota(jnp.int32, ss.shape, 1)
        ss = jnp.where(keys < count, ss, -1e30)
        p = jnp.exp(ss - jnp.max(ss, -1, keepdims=True))
        p = p / jnp.sum(p, -1, keepdims=True)
        pr_scr[b] = p
        so_scr[b] = gather_heads(nn(p.astype(LOW), sv_scr[b].astype(LOW)), hm)
        return carry

    lax.fori_loop(0, batch, self_forward, 0)
    so_low = so_scr[...].reshape(flat, width).astype(LOW)
    x2, n2, i2 = norm_forward(x1 + nn(so_low, wso_ref[...]) + bso_ref[...], gain_ref[1:2], nbias_ref[1:2])
    x2_low = x2.astype(LOW)
    block = 2 * width

    def ff_forward(j, acc):
        cols = pl.ds(pl.multiple_of(j * block, block), block)
        h, slope = gelu_pair(nn(x2_low, wh_ref[:, cols]) + bh_ref[:, cols])
        h = h.astype(LOW)
        h_scr[:, cols] = h
        gp_scr[:, cols] = slope.astype(gp_scr.dtype)
        return acc + nn(h, who_ref[cols, :])

    ff = lax.fori_loop(0, hidden // block, ff_forward, jnp.zeros((flat, width), F32))
    x3, n3, i3 = norm_forward(x2 + ff + bho_ref[...], gain_ref[2:3], nbias_ref[2:3])
    for b in range(batch):
        put_image(out_scr, first + b, count, images, x3[b * rows:b * rows + count])

    x3_low = x3.astype(LOW)
    h1, slope1 = gelu_pair(nn(x3_low, we_ref[0]) + be_ref[0:1])
    h1 = h1.astype(LOW)
    h2, slope2 = gelu_pair(nn(h1, we_ref[1]) + be_ref[1:2])
    h2 = h2.astype(LOW)
    emb_ref[...] = (nn(h2, we_ref[2]) + be_ref[2:3]).reshape(three)

    grads = []
    for b in range(batch):
        spots = match_ref[pl.ds(first + b, 1), :]
        pick = (lax.broadcasted_iota(jnp.int32, (rows, matched), 0) == spots).astype(F32).astype(LOW)
        grads.append(nn(pick, att_ref[b, tall:tall + matched].astype(LOW)))
    dz3 = jnp.concatenate(grads, 0)
    dz3_low = dz3.astype(LOW)
    put(T_EMBED + 2, tn(h2, dz3_low))
    put_bias(19, column_sum(dz3_low.astype(F32)))
    dz2 = (nt(dz3_low, we_ref[2]) * slope2).astype(LOW)
    put(T_EMBED + 1, tn(h1, dz2))
    put_bias(18, column_sum(dz2.astype(F32)))
    dz1 = (nt(dz2, we_ref[1]) * slope1).astype(LOW)
    put(T_EMBED, tn(x3_low, dz1))
    put_bias(17, column_sum(dz1.astype(F32)))
    for b in range(batch):
        q_scr[b, 0:count] = take_image(cot_scr, first + b, count, images)
    dx3 = q_scr[...].reshape(flat, width) + nt(dz1, we_ref[0])
    put_bias(3, column_sum(dx3 * n3))
    put_bias(6, column_sum(dx3))
    dp3 = norm_backward(n3, i3, gain_ref[2:3], dx3)
    dff = dp3.astype(LOW)
    put_bias(16, column_sum(dff.astype(F32)))

    def ff_backward(j, acc):
        cols = pl.ds(pl.multiple_of(j * block, block), block)
        base = (T_HIDDEN + hidden // width) * width
        spot = pl.ds(pl.multiple_of(base + j * block, block), block)
        g_ref[spot] += tn(h_scr[:, cols], dff)
        dz = (nt(dff, who_ref[cols, :]) * gp_scr[:, cols].astype(F32)).astype(LOW)
        gh = tn(x2_low, dz)
        sums = column_sum(dz.astype(F32))
        for t in range(block // width):
            tile = pl.ds(pl.multiple_of(T_HIDDEN * width + j * block + t * width, width), width)
            g_ref[tile] += gh[:, t * width:(t + 1) * width]
            g_ref[pl.ds(bias_at + 8 + j * (block // width) + t, 1)] += sums[:, t * width:(t + 1) * width]
        return acc + nt(dz, wh_ref[:, cols])

    dx2 = dp3 + lax.fori_loop(0, hidden // block, ff_backward, jnp.zeros((flat, width), F32))
    put_bias(2, column_sum(dx2 * n2))
    put_bias(5, column_sum(dx2))
    dp2 = norm_backward(n2, i2, gain_ref[1:2], dx2)
    dsa = dp2.astype(LOW)
    put(T_SELFOUT, tn(so_low, dsa))
    put_bias(7, column_sum(dsa.astype(F32)))
    dso_scr[...] = nt(dsa, wso_ref[...]).reshape(three)

    def self_backward(b, carry):
        sqx = spread_low(sq_scr[b], hm)
        dsox = spread_low(dso_scr[b], hm)
        p = pr_scr[b]
        dp = nt(dsox, sv_scr[b].astype(LOW))
        dss = (p * (dp - jnp.sum(p * dp, -1, keepdims=True))).astype(LOW)
        dm_scr[b, :, 0:width] = gather_heads(nn(dss, sk_scr[b].astype(LOW)), hm) * scale
        dm_scr[b, :, width:2 * width] = tn(dss, sqx)
        dm_scr[b, :, 2 * width:] = tn(p.astype(LOW), dsox)
        return carry

    lax.fori_loop(0, batch, self_backward, 0)
    dm = dm_scr[...].reshape(flat, 3 * width).astype(LOW)
    gs = tn(x1_low, dm)
    for t in range(3):
        put(T_SELF + t, gs[:, t * width:(t + 1) * width])
    put_bias(20, column_sum(dm[:, :width].astype(F32)))
    put_bias(21, column_sum(dm[:, 2 * width:].astype(F32)))
    dx1 = dp2 + nt(dm, ws_ref[...])
    put_bias(1, column_sum(dx1 * n1))
    put_bias(4, column_sum(dx1))
    dp1 = norm_backward(n1, i1, gain_ref[0:1], dx1)
    dp1_ref[...] = dp1.reshape(three)
    dca = dp1.astype(LOW)
    put(T_CROSS, tn(att_low, dca))
    put_bias(0, column_sum(dca.astype(F32)))
    d_att = nt(dca, wc_ref[...]).reshape(three)
    onehot = head_onehot(width, HEADS)
    back = head_onehot(width, 128, True)
    for b in range(batch):
        top = att_ref[b, rows:tall, 0:128]
        total = att_ref[b, rows:tall, 128:256]
        ratio = jnp.exp(loc_ref[b, rows:tall, 0:128] - top) / total
        dn = d_att[b] * tn(ratio, onehot, HIGH)[0:rows]
        dn_ref[b] = dn
        dt_ref[b] = -nn(dn * att_ref[b, 0:rows], back, HIGH)

    @pl.when(step == 1)
    def _():
        x3_ref[...] = jnp.concatenate([out_scr[t] for t in range(out_scr.shape[0])], 1)


def chain(att, pay, queries, matched, query_cotan, weights):
    images, tall, width = att.shape
    count = query_cotan.shape[0]
    rows = up(count, 8)
    batch = images // 2
    hidden = weights[8].shape[1]
    tiles = T_HIDDEN + 2 * (hidden // width)
    grads = up(tiles * width + 22, 256)
    half = lambda *shape: pl.BlockSpec((batch,) + shape, lambda i: (i,) + (0,) * len(shape))
    args = (att, pay, queries, matched, query_cotan) + weights
    in_specs = [whole(a) for a in args]
    in_specs[0] = half(tall, width)
    in_specs[1] = half(tall, width)
    out_shape = (
        jax.ShapeDtypeStruct((count * images, width), F32),
        jax.ShapeDtypeStruct((images, rows, width), F32),
        jax.ShapeDtypeStruct((images, rows, width), F32),
        jax.ShapeDtypeStruct((images, rows, 128), F32),
        jax.ShapeDtypeStruct((images, rows, width), F32),
        jax.ShapeDtypeStruct((grads, width), F32),
    )
    flat = batch * rows
    three = (batch, rows, width)
    return pl.pallas_call(
        chain_kernel,
        grid=(2,),
        in_specs=in_specs,
        out_specs=(whole(out_shape[0]), half(rows, width), half(rows, width), half(rows, 128), half(rows, width),
                   whole(out_shape[5])),
        scratch_shapes=[pltpu.VMEM(weights[k].shape, LOW) for k in (0, 4, 6, 8, 10, 12)] + [
            slabs(count * images, width),
            slabs(count * images, width),
            slabs(count * images, width),
            pltpu.VMEM(three, F32),
            pltpu.VMEM(three, F32),
            pltpu.VMEM(three, F32),
            pltpu.VMEM(three, F32),
            pltpu.VMEM(three, F32),
            pltpu.VMEM((batch, HEADS * rows, rows), F32),
            pltpu.VMEM((flat, hidden), LOW),
            pltpu.VMEM((flat, hidden), LOW),
            pltpu.VMEM(three, F32),
            pltpu.VMEM((batch, rows, 3 * width), F32),
        ],
        out_shape=out_shape,
        compiler_params=params(60),
        cost_estimate=cost(2 * 8e9, 20e6, 4e6),
        name="chain",
    )(*args)


def mask_out_kernel(emb_ref, match_ref, mc_ref, mf_ref, logit_old, grad_old, logit_ref, grad_ref, chosen_scr, mc_scr, logit_scr):
    images, rows, width = emb_ref.shape
    count = logit_ref.shape[0] // images
    matched, _, part = mc_ref.shape

    @pl.when(pl.program_id(0) == 0)
    def _():
        for b in range(images):
            pick = (lax.broadcasted_iota(jnp.int32, (rows, matched), 0) == match_ref[b:b + 1, :]).astype(F32).astype(LOW)
            chosen_scr[b] = tn(pick, emb_ref[b].astype(LOW))

    slabs_in(mc_scr, mc_ref[...].astype(F32).reshape(matched * images, part))
    for b in range(images):
        put_image(logit_scr, b, count, images, nt(emb_ref[b].astype(LOW), mf_ref[b])[0:count])
        grad_ref[b] = tn(take_image(mc_scr, b, matched, images).astype(LOW), chosen_scr[b].astype(LOW))
    for t in range(part // 128):
        logit_ref[:, t * 128:(t + 1) * 128] = logit_scr[t]


def mask_out(emb, matched_queries, mask_cotan, mask_features, count, pieces, steps, old=None):
    matched, images, pixels = mask_cotan.shape
    rows, width = emb.shape[1:]
    part = pixels // pieces
    first, last = steps
    out_shape = (
        jax.ShapeDtypeStruct((count * images, pixels), F32),
        jax.ShapeDtypeStruct((images, pixels, width), F32),
    )
    args = (emb, matched_queries, mask_cotan, mask_features)
    here = pl.BlockSpec(memory_space=pl.ANY)
    kernel = mask_out_kernel
    aliases = {}
    specs = []
    if old is None:
        def kernel(a, b, c, d, *rest):
            mask_out_kernel(a, b, c, d, None, None, *rest)
    else:
        args += old
        aliases = {4: 0, 5: 1}
        specs = [here, here]
    return pl.pallas_call(
        kernel,
        grid=(last - first,),
        in_specs=[
            whole(emb),
            whole(matched_queries),
            pl.BlockSpec((matched, images, part), lambda j: (0, 0, j + first)),
            pl.BlockSpec((images, part, width), lambda j: (0, j + first, 0)),
        ] + specs,
        out_specs=(
            pl.BlockSpec((count * images, part), lambda j: (0, j + first)),
            pl.BlockSpec((images, part, width), lambda j: (0, j + first, 0)),
        ),
        out_shape=out_shape,
        input_output_aliases=aliases,
        scratch_shapes=[pltpu.VMEM((images, matched, width), F32), slabs(matched * images, part), slabs(count * images, part)],
        compiler_params=params(48),
        cost_estimate=cost(
            2 * images * pixels * width * 160 * (last - first) / pieces,
            images * pixels * (width * 6 + count * 4 + matched * 2) * (last - first) / pieces),
        name="mask_out",
    )(*args)


def attend_back_kernel(quads, e_ref, kv_ref, f_ref, cq_ref, dn_ref, dt_ref, wkv_ref, fg_old, qp_old, g_old, vb_old,
                       fg_ref, qp_ref, g_ref, vb_ref, acc_scr, w_scr):
    i = pl.program_id(0)
    rows, width = cq_ref.shape[1:]
    pixels = f_ref.shape[1]
    hm = head_mask(width)

    @pl.when(i == 0)
    def _():
        acc_scr[...] = jnp.zeros_like(acc_scr)
        vb_ref[...] = jnp.zeros_like(vb_ref) if vb_old is None else vb_old[...]
        w_scr[0:width] = jnp.transpose(wkv_ref[:, :width]).astype(LOW)
        w_scr[width:] = jnp.transpose(wkv_ref[:, width:]).astype(LOW)

    ck = kv_ref[0, :, :width]
    cv = kv_ref[0, :, width:]
    cqx = spread_low(cq_ref[0], hm)
    dnx = spread_low(dn_ref[0], hm)
    per = HEADS // quads
    lanes = width // quads
    part = jnp.zeros((rows, width), F32)
    keys, values = [], []
    for g in range(quads):
        at = slice(g * per * rows, (g + 1) * per * rows)
        cols = slice(g * lanes, (g + 1) * lanes)
        e_low = e_ref[0, at]
        dw = nt(dnx[at], cv).reshape(per, rows, pixels)
        dt = jnp.stack([dt_ref[0, :, g * per + h:g * per + h + 1] for h in range(per)], 0)
        ds = (e_low.astype(F32).reshape(per, rows, pixels) * (dw + dt)).reshape(per * rows, pixels).astype(LOW)
        back = nn(ds, ck).reshape(per, rows, width)
        part = part + jnp.sum(jnp.where(hm[g * per:(g + 1) * per], back, 0.0), 0)
        keys.append(tn(cqx[at, cols], ds))
        values.append(tn(dnx[at, cols], e_low))
    qp_ref[0] = part
    turned = jnp.concatenate(keys + values, 0).astype(LOW)
    acc_scr[...] += nn(turned, f_ref[0])
    summed = turned[width:].astype(F32)
    lanes_sum = summed[:, 0:128]
    for t in range(1, pixels // 128):
        lanes_sum = lanes_sum + summed[:, t * 128:(t + 1) * 128]
    vb_ref[...] += lanes_sum
    fg_ref[0] = tn(turned, w_scr[...])

    @pl.when(i == pl.num_programs(0) - 1)
    def _():
        old = 0.0 if g_old is None else g_old[...]
        g_ref[...] = old + jnp.concatenate([jnp.transpose(acc_scr[0:width]), jnp.transpose(acc_scr[width:])], 0)


def attend_back(e, kv, features, cq, dn, dt, keyval_weight, steps, old=None):
    images, pixels, width = features.shape
    rows = cq.shape[1]
    first, last = steps
    per = lambda *shape: pl.BlockSpec((1,) + shape, lambda i: (i + first,) + (0,) * len(shape))
    tall = HEADS * rows
    share = last - first
    flops = 2 * share * (4 * tall * pixels * width + 4 * pixels * width * width)
    nbytes = share * (tall * pixels * 2 + pixels * width * 10)
    out_shape = (
        jax.ShapeDtypeStruct((images, pixels, width), F32),
        jax.ShapeDtypeStruct((images, rows, width), F32),
        jax.ShapeDtypeStruct((2 * width, width), F32),
        jax.ShapeDtypeStruct((width, 128), F32),
    )
    args = (e, kv, features, cq, dn, dt, keyval_weight)
    in_specs = [per(tall, pixels), per(pixels, 2 * width), per(pixels, width), per(rows, width), per(rows, width),
                per(rows, 128), whole(keyval_weight)]
    aliases = {}
    if old is None:
        def kernel(*refs):
            attend_back_kernel(2, *refs[:7], None, None, None, None, *refs[7:])
    else:
        kernel = functools.partial(attend_back_kernel, 2)
        here = pl.BlockSpec(memory_space=pl.ANY)
        args += old
        in_specs += [here, here, whole(out_shape[2]), whole(out_shape[3])]
        aliases = {7: 0, 8: 1}
    return pl.pallas_call(
        kernel,
        grid=(share,),
        in_specs=in_specs,
        out_specs=(per(pixels, width), per(rows, width), whole(out_shape[2]), whole(out_shape[3])),
        out_shape=out_shape,
        input_output_aliases=aliases,
        scratch_shapes=[pltpu.VMEM((2 * width, width), F32), pltpu.VMEM((2 * width, width), LOW)],
        compiler_params=params(48),
        cost_estimate=cost(flops, nbytes),
        name="attend_back",
    )(*args)


def query_back_kernel(me_ref, parts_ref, q_ref, dp_ref, wq_ref, qg_ref, g_ref, scr, all_scr):
    pieces, n, rows, width = parts_ref.shape
    images = dp_ref.shape[0]
    count = q_ref.shape[0] // images
    copies = qg_ref.shape[0]
    scale = 1.0 / math.sqrt(width // HEADS)
    total = parts_ref[0]
    for p in range(1, pieces):
        total = total + parts_ref[p]
    first = me_ref[0] * n
    scr[...] = jnp.zeros_like(scr)
    slabs_in(all_scr, q_ref[...])
    for b in range(n):
        scr[b, 0:count] = take_image(all_scr, first + b, count, images)
    d_cq = (total * scale).reshape(n * rows, width).astype(LOW)
    out = dp_ref[pl.ds(first, n)] + nt(d_cq, wq_ref[...].astype(LOW)).reshape(n, rows, width)
    for c in range(copies):
        qg_ref[c] = out
    g_ref[0:width] = tn(scr[...].reshape(n * rows, width).astype(LOW), d_cq)
    g_ref[width:] = jnp.zeros((g_ref.shape[0] - width, width), F32)
    g_ref[width:width + 1] = column_sum(d_cq.astype(F32))


def query_back(me, parts, queries, dp1, query_weight):
    pieces, n, rows, width = parts.shape
    args = (parts, queries, dp1, query_weight)
    out_shape = (jax.ShapeDtypeStruct((pieces, n, rows, width), F32), jax.ShapeDtypeStruct((width + 8, width), F32))
    return pl.pallas_call(
        query_back_kernel,
        grid_spec=pltpu.PrefetchScalarGridSpec(
            num_scalar_prefetch=1,
            grid=(1,),
            in_specs=[whole(a) for a in args],
            out_specs=tuple(whole(o) for o in out_shape),
            scratch_shapes=[pltpu.VMEM((n, rows, width), F32), slabs(*queries.shape)],
        ),
        out_shape=out_shape,
        compiler_params=params(32),
        cost_estimate=cost(2e8, 8e6),
        name="query_back",
    )(me, *args)


def beside(*values):
    return lax.optimization_barrier(values)


def trade(x, axis, groups=None):
    return lax.all_to_all(x, axis, 0, 0, axis_index_groups=groups, tiled=True)


def spread_out(x, axis, n, groups=None):
    out = trade(jnp.broadcast_to(x[None], (n,) + x.shape), axis, groups)
    return out.reshape((-1,) + x.shape[1:])


def sum_out(x, axis, n, groups=None):
    return trade(x.reshape((n, -1) + x.shape[1:]), axis, groups)


def swap_half(x, n):
    core = lax.axis_index("batch") % 2
    halves = x.reshape((2, -1) + x.shape[1:])
    mine = lax.dynamic_index_in_dim(halves, core, 0, keepdims=False)
    away = lax.dynamic_index_in_dim(halves, 1 - core, 0, keepdims=False)
    return mine, lax.ppermute(away, "batch", [(d, d ^ 1) for d in range(n)])


def swap_all(x, n):
    return lax.ppermute(x, "batch", [(d, d ^ 1) for d in range(n)])


def by_core(mine, other):
    first = lax.axis_index("batch") % 2 == 0
    return jnp.concatenate([jnp.where(first, mine, other), jnp.where(first, other, mine)], 0)


def local(
    queries, features, mask_features, attend_bits, reopen_flags, matched_queries, query_cotan, mask_cotan,
    query_weight, query_bias, keyval_weight, value_bias, cross_out, cross_out_bias, norm_gain, norm_bias,
    self_weight, self_bias, self_out, self_out_bias, hidden_weight, hidden_bias, hidden_out, hidden_out_bias,
    embed_weight, embed_bias, *, n_pix, n_batch,
):
    images, count, width = queries.shape
    hidden = hidden_weight.shape[1]
    rows = up(count, 8)
    matched = matched_queries.shape[1]
    split = images % n_pix == 0
    pix = lax.axis_index("pix")
    n_z = n_batch // 2
    z_groups = [[2 * z + c for z in range(n_z)] for c in range(2)]
    core_groups = [[2 * z, 2 * z + 1] for z in range(n_z)]

    queries = jnp.transpose(queries, (1, 0, 2)).reshape(count * images, width)
    query_cotan = jnp.transpose(query_cotan, (1, 0, 2))
    mask_cotan = jnp.transpose(mask_cotan, (1, 0, 2))
    bits = jnp.transpose(attend_bits, (0, 2, 1))

    e, kv, pay, cq = attend(
        queries, features, bits, reopen_flags, mask_cotan, mask_features, query_weight, query_bias, keyval_weight,
        value_bias)
    tall = pay.shape[1]
    if split:
        me = pix.astype(jnp.int32).reshape(1)
        shares = pay.reshape((n_pix, images // n_pix, tall, width))
        att = trade(combine(trade(shares, "pix"), matched), "pix").reshape(pay.shape)
    else:
        me = jnp.zeros((1,), jnp.int32)
        top = lax.pmax(pay[:, rows:rows + HEADS, :128], "pix")
        ratio = jnp.exp(pay[:, rows:rows + HEADS, :128] - top)

        def widen(x):
            return jnp.repeat(jnp.transpose(x, (0, 2, 1))[:, :rows], width // HEADS, axis=2)

        numer, total, es = lax.psum(
            (pay[:, :rows] * widen(ratio), pay[:, rows:rows + HEADS, 128:] * ratio, pay[:, rows + HEADS:]), "pix")
        att = jnp.concatenate([numer / widen(total), jnp.concatenate([top, total], 2), es], 1)

    weights = (
        cross_out, cross_out_bias[None], norm_gain, norm_bias, self_weight, self_bias, self_out, self_out_bias[None],
        hidden_weight, hidden_bias[None], hidden_out, hidden_out_bias[None], embed_weight, embed_bias,
    )
    x3, emb, dn, dt, dp1, grads = chain(att, pay, queries, matched_queries, query_cotan, weights)

    half = images // 2
    mask = functools.partial(mask_out, emb, matched_queries, mask_cotan, mask_features, count, 8)
    part = lax.dynamic_index_in_dim(grads.reshape(n_pix, -1, width), pix, 0, keepdims=False)
    part, other = swap_half(part, n_batch)
    back = attend_back(e, kv, features, cq, dn, dt, keyval_weight, (0, half))
    other, back = beside(other, back)
    part = sum_out(part + other, "batch", n_z, z_groups)
    back = attend_back(e, kv, features, cq, dn, dt, keyval_weight, (half, images), back)
    part, back = beside(part, back)
    feat_grad, qp, g_kv, g_vb = back
    part = spread_out(jnp.sum(part, 0), "batch", n_z, z_groups)
    if split:
        parts = trade(qp.reshape((n_pix, images // n_pix, rows, width)), "pix")
    else:
        parts = lax.psum(qp, "pix")[None]
    outs = mask((0, 2))
    part, parts, outs = beside(part, parts, outs)
    part = spread_out(part, "pix", n_pix)
    my_grad, g_q = query_back(me, parts, queries, dp1, query_weight)
    if split:
        queries_grad = trade(my_grad, "pix").reshape(images, rows, width)
    else:
        queries_grad = my_grad[0]
        g_q = g_q / n_pix
    tail = jnp.concatenate([g_kv, g_q, jnp.zeros((256 - 8, width), F32)], 0)
    tail = lax.dynamic_update_slice(tail, jnp.sum(g_vb, 1)[None], (3 * width + 1, 0))
    tail = sum_out(tail, "pix", n_pix)
    outs = mask((2, 4), outs)
    tail, outs = beside(tail, outs)
    tail, other = swap_half(jnp.sum(tail, 0), n_batch)
    outs = mask((4, 6), outs)
    part, other, outs = beside(part, other, outs)
    tail = sum_out(tail + other, "batch", n_z, z_groups)
    other = swap_all(part, n_batch)
    outs = mask((6, 8), outs)
    tail, outs = beside(tail, outs)
    logits, mask_grad = outs
    tail = spread_out(jnp.sum(tail, 0), "batch", n_z, z_groups)
    tail = by_core(tail, swap_all(tail, n_batch))
    tail = spread_out(tail, "pix", n_pix)
    pair = by_core(part, other)
    all_grads = jnp.swapaxes(pair.reshape(2, n_pix, -1, width), 0, 1).reshape(-1, width)

    def tile(t, k=1):
        return all_grads[t * width:(t + k) * width]

    def wide(t, k):
        return jnp.concatenate([tile(t + j) for j in range(k)], 1)

    many = hidden // width
    bias = all_grads[(T_HIDDEN + 2 * many) * width:]
    return (
        jnp.transpose(x3.reshape(count, images, width), (1, 0, 2)),
        jnp.transpose(logits.reshape(count, images, -1), (1, 0, 2)),
        queries_grad[:, :count],
        feat_grad,
        mask_grad,
        tail[2 * width:3 * width],
        tail[3 * width],
        jnp.concatenate([tail[:width], tail[width:2 * width]], 1),
        tail[3 * width + 1],
        tile(T_CROSS),
        bias[0],
        bias[1:4],
        bias[4:7],
        wide(T_SELF, 3),
        bias[20:22],
        tile(T_SELFOUT),
        bias[7],
        wide(T_HIDDEN, many),
        bias[8:8 + many].reshape(-1),
        tile(T_HIDDEN + many, many),
        bias[16],
        tile(T_EMBED, 3).reshape(3, width, width),
        bias[17:20],
    )


def solution(mesh):
    n_pix, n_batch = mesh.shape["pix"], mesh.shape["batch"]
    rep = P()
    row, pixel, column = P("batch", None, None), P("batch", "pix", None), P("batch", None, "pix")
    in_specs = (row, pixel, pixel, column, P("batch", None), P("batch", None), row, column) + (rep,) * 18
    out_specs = (row, column, row, pixel, pixel) + (rep,) * 18
    body = functools.partial(local, n_pix=n_pix, n_batch=n_batch)
    return jax.shard_map(body, mesh=mesh, in_specs=in_specs, out_specs=out_specs, check_vma=False)
```

```python
import functools
import math

import jax
import jax.numpy as jnp
from jax import lax
from jax.experimental import pallas as pl
from jax.experimental.pallas import tpu as pltpu
from jax.sharding import PartitionSpec as P

HEADS = 8
EPS = 1e-05
PENALTY = 10000.0
F32 = jnp.float32
LOW = jnp.bfloat16
HIGH = lax.Precision.HIGHEST
CURVE = math.sqrt(2.0 / math.pi)
CUBE = 0.044715
MIB = 1 << 20

T_CROSS, T_SELF, T_SELFOUT, T_EMBED, T_HIDDEN = 0, 1, 4, 5, 8


def up(n, m):
    return (n + m - 1) // m * m


def nn(a, b, precision=None):
    return lax.dot_general(a, b, (((1,), (0,)), ((), ())), precision=precision, preferred_element_type=F32)


def nt(a, b, precision=None):
    return lax.dot_general(a, b, (((1,), (1,)), ((), ())), precision=precision, preferred_element_type=F32)


def tn(a, b, precision=None):
    return lax.dot_general(a, b, (((0,), (0,)), ((), ())), precision=precision, preferred_element_type=F32)


def head_mask(width):
    shape = (HEADS, 1, width)
    head = width // HEADS
    return lax.broadcasted_iota(jnp.int32, shape, 2) // head == lax.broadcasted_iota(jnp.int32, shape, 0)


def spread(x, mask):
    rows, width = x.shape
    return jnp.where(mask, x[None], 0.0).reshape(HEADS * rows, width)


def gather_heads(x, mask):
    total, width = x.shape
    return jnp.sum(jnp.where(mask, x.reshape(HEADS, total // HEADS, width), 0.0), 0)


def spread_low(x, mask):
    return spread(x, mask).astype(LOW)


def head_onehot(width, lanes, transposed=False):
    head = width // HEADS
    if transposed:
        shape, a, b = (width, lanes), 0, 1
    else:
        shape, a, b = (lanes, width), 1, 0
    hit = lax.broadcasted_iota(jnp.int32, shape, a) // head == lax.broadcasted_iota(jnp.int32, shape, b)
    return hit.astype(F32)


def slabs_in(scr, value):
    for t in range(scr.shape[0]):
        scr[t] = value[:, t * 128:(t + 1) * 128]


def take_image(scr, image, count, images):
    rows = pl.ds(image, count, images)
    return jnp.concatenate([scr[t, rows, :] for t in range(scr.shape[0])], 1)


def put_image(scr, image, count, images, value):
    for t in range(scr.shape[0]):
        scr[t, pl.ds(image, count, images), :] = value[:, t * 128:(t + 1) * 128]


def slabs(rows, columns):
    return pltpu.VMEM((columns // 128, rows, 128), F32)


def cost(flops, nbytes, trans=0):
    return pl.CostEstimate(flops=int(flops), bytes_accessed=int(nbytes), transcendentals=int(trans))


def whole(x):
    shape = x.shape
    return pl.BlockSpec(shape, lambda *_: (0,) * len(shape))


def params(mib):
    return pltpu.CompilerParams(vmem_limit_bytes=mib * MIB, dimension_semantics=("arbitrary",))


def mask_part_kernel(mc_ref, mf_ref, out_ref, mc_scr):
    matched, images, part = mc_ref.shape
    slabs_in(mc_scr, mc_ref[...].astype(F32).reshape(matched * images, part))

    @pl.when(pl.program_id(0) == 0)
    def _():
        out_ref[...] = jnp.zeros_like(out_ref)

    for b in range(images):
        out_ref[b] += nn(take_image(mc_scr, b, matched, images).astype(LOW), mf_ref[b])


def mask_part(mask_cotan, mask_features, pieces):
    matched, images, pixels = mask_cotan.shape
    width = mask_features.shape[2]
    part = pixels // pieces
    return pl.pallas_call(
        mask_part_kernel,
        grid=(pieces,),
        in_specs=[
            pl.BlockSpec((matched, images, part), lambda j: (0, 0, j)),
            pl.BlockSpec((images, part, width), lambda j: (0, j, 0)),
        ],
        out_specs=pl.BlockSpec((images, matched, width), lambda j: (0, 0, 0)),
        out_shape=jax.ShapeDtypeStruct((images, matched, width), F32),
        scratch_shapes=[slabs(matched * images, part)],
        compiler_params=params(48),
        cost_estimate=cost(2 * images * 64 * pixels * width, images * pixels * (width + matched) * 2),
        name="mask_part",
    )(mask_cotan, mask_features)


def attend_kernel(groups, q_ref, f_ref, bits_ref, flag_ref, wq_ref, bq_ref, wkv_ref, vb_ref, elo_ref,
                  ehi_ref, e_ref, kv_ref, pay_ref, cq_ref, q_scr, w_scr, all_scr, wq_scr, wkv_scr):
    i = pl.program_id(0)
    images = flag_ref.shape[0]
    width = q_ref.shape[1]
    count = q_ref.shape[0] // images
    rows = q_scr.shape[0]
    pixels = f_ref.shape[1]
    tall = rows + HEADS

    @pl.when(i == 0)
    def _():
        q_scr[...] = jnp.zeros_like(q_scr)
        w_scr[...] = jnp.zeros_like(w_scr)
        slabs_in(all_scr, q_ref[...])
        wq_scr[...] = wq_ref[...].astype(LOW)
        wkv_scr[...] = wkv_ref[...].astype(LOW)

    q_scr[0:count] = take_image(all_scr, i, count, images)
    w_scr[:, 0:count] = jnp.where(flag_ref[pl.ds(i, 1), :] > 0, 65535, bits_ref[0])

    hm = head_mask(width)
    scale = 1.0 / math.sqrt(width // HEADS)
    cq = ((nn(q_scr[...].astype(LOW), wq_scr[...]) + bq_ref[...]) * scale).astype(LOW).astype(F32)
    cq_ref[0] = cq
    cqx = spread_low(cq, hm)

    bits = w_scr[...]
    low = (bits & 255).astype(F32).astype(LOW)
    high = (bits >> 8).astype(F32).astype(LOW)
    byte = (tn(low, elo_ref[...]) + tn(high, ehi_ref[...])).astype(jnp.int32)
    shift = lax.broadcasted_iota(jnp.int32, (rows, pixels), 1) & 7
    pen = jnp.where(((byte >> shift) & 1) == 1, 0.0, -PENALTY)

    keyval = nn(f_ref[0], wkv_scr[...])
    ck = keyval[:, :width].astype(LOW)
    cv = (keyval[:, width:] + vb_ref[...]).astype(LOW)
    kv_ref[0, :, :width] = ck
    kv_ref[0, :, width:] = cv

    per = HEADS // groups
    numer = jnp.zeros((rows, width), F32)
    lane = lax.broadcasted_iota(jnp.int32, (rows, 128), 1)
    stats = jnp.zeros((rows, 128), F32)


    def scores(g):
        return nt(cqx[g * per * rows:(g + 1) * per * rows], ck).reshape(per, rows, pixels) + pen[None]

    following = scores(0)
    for g in range(groups):
        at = slice(g * per * rows, (g + 1) * per * rows)
        s = following
        if g + 1 < groups:
            following = scores(g + 1)
        m = jnp.max(s, -1, keepdims=True)
        e = jnp.exp(s - m)
        total = jnp.sum(e, -1, keepdims=True)
        e_low = e.reshape(per * rows, pixels).astype(LOW)
        e_ref[0, at] = e_low
        part = nn(e_low, cv).reshape(per, rows, width)
        numer = numer + jnp.sum(jnp.where(hm[g * per:(g + 1) * per], part, 0.0), 0)
        for h in range(per):
            stats = jnp.where(lane == g * per + h, m[h], stats)
            stats = jnp.where(lane == HEADS + g * per + h, total[h], stats)
    pay_ref[0, 0:rows] = numer
    full = jnp.concatenate([stats, jnp.ones((128 - rows, 128), F32)], 0)
    turned = jnp.transpose(full)
    pay_ref[0, rows:tall, 0:128] = turned[0:HEADS]
    pay_ref[0, rows:tall, 128:256] = turned[HEADS:2 * HEADS]


def attend(queries, features, bits, reopen_flags, query_weight, query_bias, keyval_weight, value_bias):
    images, pixels, width = features.shape
    words, count = bits.shape[1:]
    rows = up(count, 8)
    tall = rows + HEADS
    pixel = jnp.arange(pixels)
    word = jnp.arange(words)
    here = pixel[None, :] // 16 == word[:, None]
    e_lo = (here & (pixel[None, :] % 16 < 8)).astype(LOW)
    e_hi = (here & (pixel[None, :] % 16 >= 8)).astype(LOW)
    per = lambda *shape: pl.BlockSpec((1,) + shape, lambda i: (i,) + (0,) * len(shape))
    args = (queries, features, bits, reopen_flags, query_weight, query_bias[None], keyval_weight, value_bias[None],
            e_lo, e_hi)
    in_specs = [whole(a) for a in args]
    in_specs[1] = per(pixels, width)
    in_specs[2] = per(words, count)
    flops = 2 * images * (pixels * width * 2 * width + 2 * HEADS * rows * pixels * width)
    nbytes = images * (pixels * width * 6 + HEADS * rows * pixels * 2)
    return pl.pallas_call(
        functools.partial(attend_kernel, 4),
        grid=(images,),
        in_specs=in_specs,
        out_specs=(per(HEADS * rows, pixels), per(pixels, 2 * width), per(tall, width), per(rows, width)),
        out_shape=(
            jax.ShapeDtypeStruct((images, HEADS * rows, pixels), LOW),
            jax.ShapeDtypeStruct((images, pixels, 2 * width), LOW),
            jax.ShapeDtypeStruct((images, tall, width), F32),
            jax.ShapeDtypeStruct((images, rows, width), F32),
        ),
        scratch_shapes=[
            pltpu.VMEM((rows, width), F32),
            pltpu.VMEM((words, rows), jnp.int32),
            slabs(count * images, width),
            pltpu.VMEM((width, width), LOW),
            pltpu.VMEM((width, 2 * width), LOW),
        ],
        compiler_params=params(56),
        cost_estimate=cost(flops, nbytes, images * HEADS * rows * pixels),
        name="attend",
    )(*args)


def combine_kernel(*refs):
    parts, out_ref = refs[:-1], refs[-1]
    images, tall, width = out_ref.shape
    rows = tall - HEADS
    onehot = head_onehot(width, HEADS)
    for i in range(images):
        ms = [p[i, rows:tall, 0:128] for p in parts]
        ls = [p[i, rows:tall, 128:256] for p in parts]
        top = functools.reduce(jnp.maximum, ms)
        rs = [jnp.exp(m - top) for m in ms]
        total = sum(r * l for r, l in zip(rs, ls))
        acc = jnp.zeros((rows, width), F32)
        for p, r in zip(parts, rs):
            acc = acc + p[i, 0:rows] * tn(r / total, onehot, HIGH)[0:rows]
        out_ref[i, 0:rows] = acc
        out_ref[i, rows:tall, 0:128] = top
        out_ref[i, rows:tall, 128:256] = total


def combine(parts):
    shape = parts[0].shape
    return pl.pallas_call(
        combine_kernel,
        out_shape=jax.ShapeDtypeStruct(shape, F32),
        compiler_params=pltpu.CompilerParams(vmem_limit_bytes=32 * MIB),
        cost_estimate=cost(1e6, 5 * 4 * math.prod(shape)),
        name="combine",
    )(*parts)


def norm_forward(x, gain, bias):
    centre = x - jnp.mean(x, -1, keepdims=True)
    inverse = lax.rsqrt(jnp.mean(centre * centre, -1, keepdims=True) + EPS)
    normed = centre * inverse
    return normed * gain + bias, normed, inverse


def norm_backward(normed, inverse, gain, grad):
    dnormed = grad * gain
    return inverse * (
        dnormed - jnp.mean(dnormed, -1, keepdims=True) - normed * jnp.mean(dnormed * normed, -1, keepdims=True)
    )


def gelu_pair(x):
    square = x * x
    t = jnp.tanh(x * (CURVE + (CURVE * CUBE) * square))
    half = 0.5 + 0.5 * t
    slope = half + (0.5 * x) * (1.0 - t * t) * (CURVE + (3.0 * CURVE * CUBE) * square)
    return x * half, slope


def column_sum(x):
    return jnp.sum(x, 0, keepdims=True)


def chain_kernel(
    pieces, me_ref, *refs
):
    att_parts, refs = refs[:pieces], refs[pieces:]
    chain_body(me_ref, att_parts, *refs)


def chain_body(
    me_ref, att_parts, es_ref, loc_ref, q_ref, match_ref, cot_ref, wc_raw, bc_ref, gain_ref, nbias_ref, ws_raw, bs_ref, wso_raw, bso_ref,
    wh_raw, bh_ref, who_raw, bho_ref, we_raw, be_ref,
    x3_ref, emb_ref, dn_ref, dt_ref, dp1_ref, g_ref,
    wc_ref, ws_ref, wso_ref, wh_ref, who_ref, we_ref, all_scr, cot_scr, out_scr, att_scr, emb_scr,
    q_scr, sq_scr, sk_scr, sv_scr, so_scr, pr_scr, h_scr, gp_scr, dso_scr, dm_scr
):
    step = pl.program_id(0)
    batch, rows, width = dn_ref.shape
    matched = match_ref.shape[1]
    count, images = cot_ref.shape[:2]
    tall = rows + HEADS
    flat = batch * rows
    hidden = wh_ref.shape[1]
    scale = 1.0 / math.sqrt(width // HEADS)
    hm = head_mask(width)

    @pl.when(step == 0)
    def _():
        q_scr[...] = jnp.zeros_like(q_scr)
        g_ref[...] = jnp.zeros_like(g_ref)
        n = att_parts[0].shape[0]
        for k, part in enumerate(att_parts):
            att_scr[pl.ds((me_ref[0] ^ k) * n, n)] = part[...]
        slabs_in(all_scr, q_ref[...])
        slabs_in(cot_scr, cot_ref[...].astype(F32).reshape(count * images, width))
        for raw, ref in ((wc_raw, wc_ref), (ws_raw, ws_ref), (wso_raw, wso_ref), (wh_raw, wh_ref), (who_raw, who_ref),
                         (we_raw, we_ref)):
            ref[...] = raw[...].astype(LOW)

    def put(tile, value):
        g_ref[tile * width:(tile + 1) * width] += value

    bias_at = (T_HIDDEN + 2 * (hidden // width)) * width

    def put_bias(index, value):
        g_ref[bias_at + index:bias_at + index + 1] += value

    first = step * batch
    for b in range(batch):
        q_scr[b, 0:count] = take_image(all_scr, first + b, count, images)
    att = att_scr[pl.ds(first, batch), 0:rows].reshape(flat, width)
    att_low = att.astype(LOW)
    queries = q_scr[...].reshape(flat, width)
    x1, n1, i1 = norm_forward(queries + nn(att_low, wc_ref[...]) + bc_ref[...], gain_ref[0:1], nbias_ref[0:1])
    x1_low = x1.astype(LOW)
    mixed = nn(x1_low, ws_ref[...])
    three = (batch, rows, width)
    sq_scr[...] = ((mixed[:, :width] + bs_ref[0:1]) * scale).reshape(three)
    sk_scr[...] = mixed[:, width:2 * width].reshape(three)
    sv_scr[...] = (mixed[:, 2 * width:] + bs_ref[1:2]).reshape(three)

    head = width // HEADS
    lanes = lambda h: slice(h * 128, (h + 1) * 128)
    fill = jnp.zeros((128 - rows, width), F32)

    def tall_heads(x):
        return spread_low(jnp.concatenate([x, fill], 0), hm)

    def turn(x):
        return jnp.transpose(jnp.concatenate([x, fill], 0))[:, 0:rows].astype(LOW)

    def by_head(turned, x):
        return jnp.transpose(jnp.concatenate(
            [nn(turned[h * head:(h + 1) * head], x[:, lanes(h)]) for h in range(HEADS)], 0))[0:rows]

    for b in range(batch):
        ss = nt(sk_scr[b].astype(LOW), tall_heads(sq_scr[b]))
        keys = lax.broadcasted_iota(jnp.int32, ss.shape, 0)
        ss = jnp.where(keys < count, ss, -1e30)
        p = jnp.exp(ss - jnp.max(ss, 0, keepdims=True))
        p = p * (1.0 / jnp.sum(p, 0, keepdims=True))
        pr_scr[b] = p
        so_scr[b] = by_head(turn(sv_scr[b]), p.astype(LOW))
    so_low = so_scr[...].reshape(flat, width).astype(LOW)
    x2, n2, i2 = norm_forward(x1 + nn(so_low, wso_ref[...]) + bso_ref[...], gain_ref[1:2], nbias_ref[1:2])
    x2_low = x2.astype(LOW)
    block = 2 * width

    def ff_forward(j, acc):
        cols = pl.ds(pl.multiple_of(j * block, block), block)
        h, slope = gelu_pair(nn(x2_low, wh_ref[:, cols]) + bh_ref[:, cols])
        h = h.astype(LOW)
        h_scr[:, cols] = h
        gp_scr[:, cols] = slope.astype(gp_scr.dtype)
        return acc + nn(h, who_ref[cols, :])

    ff = lax.fori_loop(0, hidden // block, ff_forward, jnp.zeros((flat, width), F32))
    x3, n3, i3 = norm_forward(x2 + ff + bho_ref[...], gain_ref[2:3], nbias_ref[2:3])
    for b in range(batch):
        put_image(out_scr, first + b, count, images, x3[b * rows:b * rows + count])

    x3_low = x3.astype(LOW)
    h1, slope1 = gelu_pair(nn(x3_low, we_ref[0]) + be_ref[0:1])
    h1 = h1.astype(LOW)
    h2, slope2 = gelu_pair(nn(h1, we_ref[1]) + be_ref[1:2])
    h2 = h2.astype(LOW)
    emb = nn(h2, we_ref[2]) + be_ref[2:3]
    for b in range(batch):
        put_image(emb_scr, first + b, count, images, emb[b * rows:b * rows + count])

    grads = []
    for b in range(batch):
        spots = match_ref[pl.ds(first + b, 1), :]
        pick = (lax.broadcasted_iota(jnp.int32, (rows, matched), 0) == spots).astype(F32).astype(LOW)
        grads.append(nn(pick, es_ref[b].astype(LOW)))
    dz3 = jnp.concatenate(grads, 0)
    dz3_low = dz3.astype(LOW)
    put(T_EMBED + 2, tn(h2, dz3_low))
    put_bias(19, column_sum(dz3_low.astype(F32)))
    dz2 = (nt(dz3_low, we_ref[2]) * slope2).astype(LOW)
    put(T_EMBED + 1, tn(h1, dz2))
    put_bias(18, column_sum(dz2.astype(F32)))
    dz1 = (nt(dz2, we_ref[1]) * slope1).astype(LOW)
    put(T_EMBED, tn(x3_low, dz1))
    put_bias(17, column_sum(dz1.astype(F32)))
    for b in range(batch):
        q_scr[b, 0:count] = take_image(cot_scr, first + b, count, images)
    dx3 = q_scr[...].reshape(flat, width) + nt(dz1, we_ref[0])
    put_bias(3, column_sum(dx3 * n3))
    put_bias(6, column_sum(dx3))
    dp3 = norm_backward(n3, i3, gain_ref[2:3], dx3)
    dff = dp3.astype(LOW)
    put_bias(16, column_sum(dff.astype(F32)))

    def ff_backward(j, acc):
        cols = pl.ds(pl.multiple_of(j * block, block), block)
        base = (T_HIDDEN + hidden // width) * width
        spot = pl.ds(pl.multiple_of(base + j * block, block), block)
        g_ref[spot] += tn(h_scr[:, cols], dff)
        dz = (nt(dff, who_ref[cols, :]) * gp_scr[:, cols].astype(F32)).astype(LOW)
        gh = tn(x2_low, dz)
        sums = column_sum(dz.astype(F32))
        for t in range(block // width):
            tile = pl.ds(pl.multiple_of(T_HIDDEN * width + j * block + t * width, width), width)
            g_ref[tile] += gh[:, t * width:(t + 1) * width]
            g_ref[pl.ds(bias_at + 8 + j * (block // width) + t, 1)] += sums[:, t * width:(t + 1) * width]
        return acc + nt(dz, wh_ref[:, cols])

    dx2 = dp3 + lax.fori_loop(0, hidden // block, ff_backward, jnp.zeros((flat, width), F32))
    put_bias(2, column_sum(dx2 * n2))
    put_bias(5, column_sum(dx2))
    dp2 = norm_backward(n2, i2, gain_ref[1:2], dx2)
    dsa = dp2.astype(LOW)
    put(T_SELFOUT, tn(so_low, dsa))
    put_bias(7, column_sum(dsa.astype(F32)))
    dso_scr[...] = nt(dsa, wso_ref[...]).reshape(three)

    for b in range(batch):
        dsox = tall_heads(dso_scr[b])
        p = pr_scr[b]
        dp = nt(sv_scr[b].astype(LOW), dsox)
        dss = (p * (dp - jnp.sum(p * dp, 0, keepdims=True))).astype(LOW)
        dm_scr[b, :, 0:width] = by_head(turn(sk_scr[b]), dss) * scale
        dm_scr[b, :, width:2 * width] = nn(dss, tall_heads(sq_scr[b]))
        dm_scr[b, :, 2 * width:] = nn(p.astype(LOW), dsox)

    dm = dm_scr[...].reshape(flat, 3 * width).astype(LOW)
    gs = tn(x1_low, dm)
    for t in range(3):
        put(T_SELF + t, gs[:, t * width:(t + 1) * width])
    put_bias(20, column_sum(dm[:, :width].astype(F32)))
    put_bias(21, column_sum(dm[:, 2 * width:].astype(F32)))
    dx1 = dp2 + nt(dm, ws_ref[...])
    put_bias(1, column_sum(dx1 * n1))
    put_bias(4, column_sum(dx1))
    dp1 = norm_backward(n1, i1, gain_ref[0:1], dx1)
    dp1_ref[...] = dp1.reshape(three)
    dca = dp1.astype(LOW)
    put(T_CROSS, tn(att_low, dca))
    put_bias(0, column_sum(dca.astype(F32)))
    d_att = nt(dca, wc_ref[...]).reshape(three)
    onehot = head_onehot(width, HEADS)
    back = head_onehot(width, 128, True)
    for b in range(batch):
        top = att_scr[first + b, rows:tall, 0:128]
        total = att_scr[first + b, rows:tall, 128:256]
        ratio = jnp.exp(loc_ref[b, rows:tall, 0:128] - top) / total
        dn = d_att[b] * tn(ratio, onehot, HIGH)[0:rows]
        dn_ref[b] = dn
        dt_ref[b] = -nn(dn * att_scr[first + b, 0:rows], back, HIGH)

    @pl.when(step == 1)
    def _():
        x3_ref[...] = jnp.concatenate([out_scr[t] for t in range(out_scr.shape[0])], 1)
        emb_ref[...] = jnp.concatenate([emb_scr[t] for t in range(emb_scr.shape[0])], 1)


def chain(me, parts, es, pay, queries, matched, query_cotan, weights):
    images, tall, width = pay.shape
    count = query_cotan.shape[0]
    rows = up(count, 8)
    batch = images // 2
    hidden = weights[8].shape[1]
    tiles = T_HIDDEN + 2 * (hidden // width)
    grads = up(tiles * width + 22, 256)
    half = lambda *shape: pl.BlockSpec((batch,) + shape, lambda i, *_: (i,) + (0,) * len(shape))
    pieces = len(parts)
    args = tuple(parts) + (es, pay, queries, matched, query_cotan) + weights
    in_specs = [whole(a) for a in args]
    in_specs[pieces] = half(es.shape[1], width)
    in_specs[pieces + 1] = half(tall, width)
    out_shape = (
        jax.ShapeDtypeStruct((count * images, width), F32),
        jax.ShapeDtypeStruct((count * images, width), F32),
        jax.ShapeDtypeStruct((images, rows, width), F32),
        jax.ShapeDtypeStruct((images, rows, 128), F32),
        jax.ShapeDtypeStruct((images, rows, width), F32),
        jax.ShapeDtypeStruct((grads, width), F32),
    )
    flat = batch * rows
    three = (batch, rows, width)
    many = slabs(count * images, width)
    return pl.pallas_call(
        functools.partial(chain_kernel, pieces),
        grid_spec=pltpu.PrefetchScalarGridSpec(
            num_scalar_prefetch=1,
            grid=(2,),
            in_specs=in_specs,
            out_specs=(whole(out_shape[0]), whole(out_shape[1]), half(rows, width), half(rows, 128), half(rows, width),
                       whole(out_shape[5])),
            scratch_shapes=[pltpu.VMEM(weights[k].shape, LOW) for k in (0, 4, 6, 8, 10, 12)] + [
                many,
                many,
                many,
                pltpu.VMEM((images, tall, width), F32),
                many,
                pltpu.VMEM(three, F32),
                pltpu.VMEM(three, F32),
                pltpu.VMEM(three, F32),
                pltpu.VMEM(three, F32),
                pltpu.VMEM(three, F32),
                pltpu.VMEM((batch, rows, HEADS * 128), F32),
                pltpu.VMEM((flat, hidden), LOW),
                pltpu.VMEM((flat, hidden), LOW),
                pltpu.VMEM(three, F32),
                pltpu.VMEM((batch, rows, 3 * width), F32),
            ],
        ),
        out_shape=out_shape,
        compiler_params=params(62),
        cost_estimate=cost(2 * 8e9, 20e6, 4e6),
        name="chain",
    )(me, *args)


def mask_out_kernel(emb_ref, match_ref, mc_ref, mf_ref, logit_old, grad_old, logit_ref, grad_ref, chosen_scr, mc_scr,
                    wide_scr, emb_scr):
    images, matched, width = chosen_scr.shape
    count = logit_ref.shape[0] // images
    rows = count * images
    part = mc_ref.shape[2]

    @pl.when(pl.program_id(0) == 0)
    def _():
        image = lax.broadcasted_iota(jnp.int32, (rows, width), 0) % images
        emb = emb_ref[...]
        slabs_in(emb_scr, emb)
        for b in range(images):
            wide_scr[:, b * width:(b + 1) * width] = jnp.where(image == b, emb, 0.0).astype(LOW)
            pick = (lax.broadcasted_iota(jnp.int32, (count, matched), 0) == match_ref[b:b + 1, :]).astype(F32).astype(LOW)
            chosen_scr[b] = tn(pick, take_image(emb_scr, b, count, images).astype(LOW))

    slabs_in(mc_scr, mc_ref[...].astype(F32).reshape(matched * images, part))
    logits = nt(wide_scr[:, 0:width], mf_ref[0])
    for b in range(1, images):
        logits = logits + nt(wide_scr[:, b * width:(b + 1) * width], mf_ref[b])
    logit_ref[...] = logits
    for b in range(images):
        grad_ref[b] = tn(take_image(mc_scr, b, matched, images).astype(LOW), chosen_scr[b].astype(LOW))


def mask_out(emb, matched_queries, mask_cotan, mask_features, count, pieces, steps, old=None):
    matched, images, pixels = mask_cotan.shape
    width = emb.shape[1]
    part = pixels // pieces
    first, last = steps
    out_shape = (
        jax.ShapeDtypeStruct((count * images, pixels), F32),
        jax.ShapeDtypeStruct((images, pixels, width), F32),
    )
    args = (emb, matched_queries, mask_cotan, mask_features)
    here = pl.BlockSpec(memory_space=pl.ANY)
    kernel = mask_out_kernel
    aliases = {}
    specs = []
    if old is None:
        def kernel(a, b, c, d, *rest):
            mask_out_kernel(a, b, c, d, None, None, *rest)
    else:
        args += old
        aliases = {4: 0, 5: 1}
        specs = [here, here]
    return pl.pallas_call(
        kernel,
        grid=(last - first,),
        in_specs=[
            whole(emb),
            whole(matched_queries),
            pl.BlockSpec((matched, images, part), lambda j: (0, 0, j + first)),
            pl.BlockSpec((images, part, width), lambda j: (0, j + first, 0)),
        ] + specs,
        out_specs=(
            pl.BlockSpec((count * images, part), lambda j: (0, j + first)),
            pl.BlockSpec((images, part, width), lambda j: (0, j + first, 0)),
        ),
        out_shape=out_shape,
        input_output_aliases=aliases,
        scratch_shapes=[pltpu.VMEM((images, matched, width), F32), slabs(matched * images, part),
                        pltpu.VMEM((count * images, images * width), LOW), slabs(count * images, width)],
        compiler_params=params(48),
        cost_estimate=cost(
            2 * images * pixels * width * 900 * (last - first) / pieces,
            images * pixels * (width * 6 + count * 4 + matched * 2) * (last - first) / pieces),
        name="mask_out",
    )(*args)


def attend_back_kernel(groups, e_ref, kv_ref, f_ref, cq_ref, dn_ref, dt_ref, wkv_ref, fg_old, qp_old, g_old,
                       fg_ref, qp_ref, g_ref, acc_scr, w_scr, vb_scr):
    i = pl.program_id(0)
    rows, width = cq_ref.shape[1:]
    pixels = f_ref.shape[1]
    hm = head_mask(width)

    @pl.when(i == 0)
    def _():
        acc_scr[...] = jnp.zeros_like(acc_scr)
        vb_scr[...] = jnp.zeros_like(vb_scr)
        w_scr[0:width] = jnp.transpose(wkv_ref[:, :width]).astype(LOW)
        w_scr[width:] = jnp.transpose(wkv_ref[:, width:]).astype(LOW)

    ck = kv_ref[0, :, :width]
    cv = kv_ref[0, :, width:]
    cqx = spread_low(cq_ref[0], hm)
    dnx = spread_low(dn_ref[0], hm)
    per = HEADS // groups
    wide = min(width, 128)
    part = jnp.zeros((rows, width), F32)
    keys = [None] * (width // wide)
    values = [None] * (width // wide)

    def plus(old, new):
        return new if old is None else old + new

    def weigh(g):
        return nt(dnx[g * per * rows:(g + 1) * per * rows], cv).reshape(per, rows, pixels)

    following = weigh(0)
    for g in range(groups):
        at = slice(g * per * rows, (g + 1) * per * rows)
        slot = g * per * (width // HEADS) // wide
        cols = slice(slot * wide, (slot + 1) * wide)
        e_low = e_ref[0, at]
        dw = following
        if g + 1 < groups:
            following = weigh(g + 1)
        dt = jnp.stack([dt_ref[0, :, g * per + h:g * per + h + 1] for h in range(per)], 0)
        ds = (e_low.astype(F32).reshape(per, rows, pixels) * (dw + dt)).reshape(per * rows, pixels).astype(LOW)
        values[slot] = plus(values[slot], tn(dnx[at, cols], e_low))
        back = nn(ds, ck).reshape(per, rows, width)
        part = part + jnp.sum(jnp.where(hm[g * per:(g + 1) * per], back, 0.0), 0)
        keys[slot] = plus(keys[slot], tn(cqx[at, cols], ds))
    qp_ref[0] = part
    turned = jnp.concatenate(keys + values, 0).astype(LOW)
    acc_scr[...] += nn(turned, f_ref[0])
    summed = turned[width:].astype(F32)
    lanes_sum = summed[:, 0:128]
    for t in range(1, pixels // 128):
        lanes_sum = lanes_sum + summed[:, t * 128:(t + 1) * 128]
    vb_scr[...] += lanes_sum
    fg_ref[0] = tn(turned, w_scr[...])

    @pl.when(i == pl.num_programs(0) - 1)
    def _():
        old = 0.0 if g_old is None else g_old[...]
        sums = jnp.sum(jnp.transpose(vb_scr[...]), 0, keepdims=True)
        fill = jnp.zeros((g_ref.shape[0] - 2 * width - 1, width), F32)
        turned = [jnp.transpose(acc_scr[0:width]), jnp.transpose(acc_scr[width:]), sums, fill]
        g_ref[...] = old + jnp.concatenate(turned, 0)


def attend_back(e, kv, features, cq, dn, dt, keyval_weight, steps, old=None):
    images, pixels, width = features.shape
    rows = cq.shape[1]
    first, last = steps
    per = lambda *shape: pl.BlockSpec((1,) + shape, lambda i: (i + first,) + (0,) * len(shape))
    tall = HEADS * rows
    share = last - first
    flops = 2 * share * (4 * tall * pixels * width + 4 * pixels * width * width)
    nbytes = share * (tall * pixels * 2 + pixels * width * 10)
    out_shape = (
        jax.ShapeDtypeStruct((images, pixels, width), F32),
        jax.ShapeDtypeStruct((images, rows, width), F32),
        jax.ShapeDtypeStruct((2 * width + 32, width), F32),
    )
    args = (e, kv, features, cq, dn, dt, keyval_weight)
    in_specs = [per(tall, pixels), per(pixels, 2 * width), per(pixels, width), per(rows, width), per(rows, width),
                per(rows, 128), whole(keyval_weight)]
    aliases = {}
    if old is None:
        def kernel(*refs):
            attend_back_kernel(4, *refs[:7], None, None, None, *refs[7:])
    else:
        kernel = functools.partial(attend_back_kernel, 4)
        here = pl.BlockSpec(memory_space=pl.ANY)
        args += old
        in_specs += [here, here, whole(out_shape[2])]
        aliases = {7: 0, 8: 1}
    return pl.pallas_call(
        kernel,
        grid=(share,),
        in_specs=in_specs,
        out_specs=(per(pixels, width), per(rows, width), whole(out_shape[2])),
        out_shape=out_shape,
        input_output_aliases=aliases,
        scratch_shapes=[pltpu.VMEM((2 * width, width), F32), pltpu.VMEM((2 * width, width), LOW), pltpu.VMEM((width, 128), F32)],
        compiler_params=params(48),
        cost_estimate=cost(flops, nbytes),
        name="attend_back",
    )(*args)


def query_sum_kernel(*refs):
    parts, out_ref = refs[:-1], refs[-1]
    total = parts[0][...]
    for p in parts[1:]:
        total = total + p[...]
    out_ref[...] = total


def query_sum(parts):
    return pl.pallas_call(
        query_sum_kernel,
        out_shape=jax.ShapeDtypeStruct(parts[0].shape, F32),
        compiler_params=pltpu.CompilerParams(vmem_limit_bytes=32 * MIB),
        cost_estimate=cost(1e6, 5 * 4 * math.prod(parts[0].shape)),
        name="query_sum",
    )(*parts)


def query_back_kernel(pieces, me_ref, *refs):
    parts = refs[:pieces]
    q_ref, dp_ref, wq_ref, qg_ref, g_ref, scr, sum_scr, all_scr, out_scr = refs[pieces:]
    images, rows, width = dp_ref.shape
    count = q_ref.shape[0] // images
    scale = 1.0 / math.sqrt(width // HEADS)
    n = parts[0].shape[0]
    for k, part in enumerate(parts):
        sum_scr[pl.ds((me_ref[0] ^ k) * n, n)] = part[...]
    scr[...] = jnp.zeros_like(scr)
    slabs_in(all_scr, q_ref[...])
    for b in range(images):
        scr[b, 0:count] = take_image(all_scr, b, count, images)
    d_cq = (sum_scr[...].reshape(images * rows, width) * scale).astype(LOW)
    out = dp_ref[...] + nt(d_cq, wq_ref[...].astype(LOW)).reshape(images, rows, width)
    for b in range(images):
        put_image(out_scr, b, count, images, out[b, 0:count])
    qg_ref[...] = jnp.concatenate([out_scr[t] for t in range(out_scr.shape[0])], 1)
    g_ref[0:width] = tn(scr[...].reshape(images * rows, width).astype(LOW), d_cq)
    g_ref[width:] = jnp.zeros((g_ref.shape[0] - width, width), F32)
    g_ref[width:width + 1] = column_sum(d_cq.astype(F32))


def query_back(me, parts, queries, dp1, query_weight):
    images, rows, width = dp1.shape
    args = tuple(parts) + (queries, dp1, query_weight)
    out_shape = (jax.ShapeDtypeStruct(queries.shape, F32), jax.ShapeDtypeStruct((width + 32, width), F32))
    return pl.pallas_call(
        functools.partial(query_back_kernel, len(parts)),
        grid_spec=pltpu.PrefetchScalarGridSpec(
            num_scalar_prefetch=1,
            grid=(1,),
            in_specs=[whole(a) for a in args],
            out_specs=tuple(whole(o) for o in out_shape),
            scratch_shapes=[pltpu.VMEM((images, rows, width), F32), pltpu.VMEM((images, rows, width), F32),
                            slabs(*queries.shape), slabs(*queries.shape)],
        ),
        out_shape=out_shape,
        compiler_params=params(32),
        cost_estimate=cost(5e8, 8e6),
        name="query_back",
    )(me, *args)


def beside(*values):
    return lax.optimization_barrier(values)


def swap(x, axis, n, key):
    return lax.ppermute(x, axis, [(d, d ^ key) for d in range(n)])


def scatter_out(x, axis, n):
    me = lax.axis_index(axis)
    chunks = [lax.dynamic_index_in_dim(x, me ^ k, 0, keepdims=False) for k in range(n)]
    return tuple(c if k == 0 else swap(c, axis, n, k) for k, c in enumerate(chunks))


def gather_in(x, axis, n):
    return tuple(x if k == 0 else swap(x, axis, n, k) for k in range(n))


def side(axis, key):
    return (lax.axis_index(axis) // key) % 2


def halve(x, axis, n, key):
    halves = x.reshape((2, -1) + x.shape[1:])
    mine = lax.dynamic_index_in_dim(halves, side(axis, key), 0, keepdims=False)
    away = lax.dynamic_index_in_dim(halves, 1 - side(axis, key), 0, keepdims=False)
    return mine, swap(away, axis, n, key)


def join(mine, other, axis, key):
    first = side(axis, key) == 0
    return jnp.concatenate([jnp.where(first, mine, other), jnp.where(first, other, mine)], 0)


def local(
    queries, features, mask_features, attend_bits, reopen_flags, matched_queries, query_cotan, mask_cotan,
    query_weight, query_bias, keyval_weight, value_bias, cross_out, cross_out_bias, norm_gain, norm_bias,
    self_weight, self_bias, self_out, self_out_bias, hidden_weight, hidden_bias, hidden_out, hidden_out_bias,
    embed_weight, embed_bias, *, n_pix, n_batch,
):
    images, count, width = queries.shape
    hidden = hidden_weight.shape[1]
    rows = up(count, 8)
    tall = rows + HEADS
    pix = lax.axis_index("pix")
    direct = n_pix == 4 and n_batch == 8

    queries = jnp.transpose(queries, (1, 0, 2)).reshape(count * images, width)
    query_cotan = jnp.transpose(query_cotan, (1, 0, 2))
    mask_cotan = jnp.transpose(mask_cotan, (1, 0, 2))
    bits = jnp.transpose(attend_bits, (0, 2, 1))

    es, reopen_flags = beside(mask_part(mask_cotan, mask_features, mask_features.shape[1] // 512), reopen_flags)
    es = lax.psum(es, "pix")
    e, kv, pay, cq = attend(
        queries, features, bits, reopen_flags, query_weight, query_bias, keyval_weight, value_bias)
    es, pay = beside(es, pay)
    if direct:
        me = pix.astype(jnp.int32).reshape(1)
        shares = pay.reshape((n_pix, images // n_pix, tall, width))
        att = gather_in(combine(scatter_out(shares, "pix", n_pix)), "pix", n_pix)
    else:
        me = jnp.zeros((1,), jnp.int32)
        top = lax.pmax(pay[:, rows:, :128], "pix")
        ratio = jnp.exp(pay[:, rows:, :128] - top)

        def widen(x):
            return jnp.repeat(jnp.transpose(x, (0, 2, 1))[:, :rows], width // HEADS, axis=2)

        numer, total = lax.psum((pay[:, :rows] * widen(ratio), pay[:, rows:, 128:] * ratio), "pix")
        att = (jnp.concatenate([numer / widen(total), jnp.concatenate([top, total], 2)], 1),)

    weights = (
        cross_out, cross_out_bias[None], norm_gain, norm_bias, self_weight, self_bias, self_out, self_out_bias[None],
        hidden_weight, hidden_bias[None], hidden_out, hidden_out_bias[None], embed_weight, embed_bias,
    )
    x3, emb, dn, dt, dp1, grads = chain(me, att, es, pay, queries, matched_queries, query_cotan, weights)

    part = lax.dynamic_index_in_dim(grads.reshape(n_pix, -1, width), pix, 0, keepdims=False)
    part = lax.psum_scatter(part, "batch", scatter_dimension=0, tiled=True)
    blocks = mask_features.shape[1] // 256
    mask = functools.partial(mask_out, emb, matched_queries, mask_cotan, mask_features, count, blocks)
    cut, cut2 = blocks * 6 // 16, blocks * 11 // 16
    back = attend_back(e, kv, features, cq, dn, dt, keyval_weight, (0, images))
    part, feat_grad, qp, g_kv = beside(part, *back)
    all_grads = lax.all_gather(part, ("pix", "batch"), axis=0, tiled=True)
    if direct:
        parts = scatter_out(qp.reshape((n_pix, images // n_pix, rows, width)), "pix", n_pix)
        kv_parts = scatter_out(g_kv.reshape((n_pix, -1, width)), "pix", n_pix)
        outs = mask((0, cut))
        parts, kv_parts, outs = beside(parts, kv_parts, outs)
        parts = gather_in(query_sum(parts), "pix", n_pix)
        kv_sum = functools.reduce(jnp.add, kv_parts)
        outs = mask((cut, cut2), outs)
        parts, outs = beside(parts, outs)
        queries_grad, g_q = query_back(me, parts, queries, dp1, query_weight)
        g_q = lax.dynamic_index_in_dim(g_q.reshape(n_pix, -1, width), pix, 0, keepdims=False)
        tail = jnp.concatenate([kv_sum, g_q], 0)
        tail, other = halve(tail, "batch", n_batch, 1)
        tail, other = halve(tail + other, "batch", n_batch, 2)
        outs = mask((cut2, blocks), outs)
        other, outs = beside(other, outs)
        tail, other = halve(tail + other, "batch", n_batch, 4)
        tail = tail + other
        for key in (4, 2, 1):
            tail = join(tail, swap(tail, "batch", n_batch, key), "batch", key)
        split = kv_sum.shape[0]
        tails = gather_in(tail, "pix", n_pix)
        ordered = jnp.zeros((n_pix,) + tail.shape, F32)
        for k, t in enumerate(tails):
            ordered = lax.dynamic_update_index_in_dim(ordered, t, pix ^ k, 0)
        g_kv = ordered[:, :split].reshape(-1, width)
        g_q = ordered[:, split:].reshape(-1, width)
    else:
        outs = mask((0, blocks))
        queries_grad, g_q = query_back(me, (lax.psum(qp, "pix"),), queries, dp1, query_weight)
        g_q = lax.psum(g_q, "batch")
        g_kv = lax.psum(g_kv, ("batch", "pix"))
    logits, mask_grad = outs

    def tile(t, k=1):
        return all_grads[t * width:(t + k) * width]

    def wide(t, k):
        return jnp.concatenate([tile(t + j) for j in range(k)], 1)

    def unflat(x):
        return jnp.transpose(x.reshape(count, images, -1), (1, 0, 2))

    many = hidden // width
    bias = all_grads[(T_HIDDEN + 2 * many) * width:]
    return (
        unflat(x3),
        unflat(logits),
        unflat(queries_grad),
        feat_grad,
        mask_grad,
        g_q[:width],
        g_q[width],
        jnp.concatenate([g_kv[:width], g_kv[width:2 * width]], 1),
        g_kv[2 * width],
        tile(T_CROSS),
        bias[0],
        bias[1:4],
        bias[4:7],
        wide(T_SELF, 3),
        bias[20:22],
        tile(T_SELFOUT),
        bias[7],
        wide(T_HIDDEN, many),
        bias[8:8 + many].reshape(-1),
        tile(T_HIDDEN + many, many),
        bias[16],
        tile(T_EMBED, 3).reshape(3, width, width),
        bias[17:20],
    )


def solution(mesh):
    n_pix, n_batch = mesh.shape["pix"], mesh.shape["batch"]
    rep = P()
    row, pixel, column = P("batch", None, None), P("batch", "pix", None), P("batch", None, "pix")
    in_specs = (row, pixel, pixel, column, P("batch", None), P("batch", None), row, column) + (rep,) * 18
    out_specs = (row, column, row, pixel, pixel) + (rep,) * 18
    body = functools.partial(local, n_pix=n_pix, n_batch=n_batch)
    return jax.shard_map(body, mesh=mesh, in_specs=in_specs, out_specs=out_specs, check_vma=False)
```

```python
import functools
import math

import jax
import jax.numpy as jnp
from jax import lax
from jax.experimental import pallas as pl
from jax.experimental.pallas import tpu as pltpu
from jax.sharding import PartitionSpec as P

HEADS = 8
EPS = 1e-05
PENALTY = 10000.0
F32 = jnp.float32
LOW = jnp.bfloat16
HIGH = lax.Precision.HIGHEST
CURVE = math.sqrt(2.0 / math.pi)
CUBE = 0.044715
MIB = 1 << 20

T_CROSS, T_SELF, T_SELFOUT, T_EMBED, T_HIDDEN = 0, 1, 4, 5, 8


def up(n, m):
    return (n + m - 1) // m * m


def nn(a, b, precision=None):
    return lax.dot_general(a, b, (((1,), (0,)), ((), ())), precision=precision, preferred_element_type=F32)


def nt(a, b, precision=None):
    return lax.dot_general(a, b, (((1,), (1,)), ((), ())), precision=precision, preferred_element_type=F32)


def tn(a, b, precision=None):
    return lax.dot_general(a, b, (((0,), (0,)), ((), ())), precision=precision, preferred_element_type=F32)


def head_mask(width):
    shape = (HEADS, 1, width)
    head = width // HEADS
    return lax.broadcasted_iota(jnp.int32, shape, 2) // head == lax.broadcasted_iota(jnp.int32, shape, 0)


def spread(x, mask):
    rows, width = x.shape
    return jnp.where(mask, x[None], 0.0).reshape(HEADS * rows, width)


def gather_heads(x, mask):
    total, width = x.shape
    return jnp.sum(jnp.where(mask, x.reshape(HEADS, total // HEADS, width), 0.0), 0)


def spread_low(x, mask):
    return spread(x, mask).astype(LOW)


def head_onehot(width, lanes, transposed=False):
    head = width // HEADS
    if transposed:
        shape, a, b = (width, lanes), 0, 1
    else:
        shape, a, b = (lanes, width), 1, 0
    hit = lax.broadcasted_iota(jnp.int32, shape, a) // head == lax.broadcasted_iota(jnp.int32, shape, b)
    return hit.astype(F32)


def slabs_in(scr, value):
    for t in range(scr.shape[0]):
        scr[t] = value[:, t * 128:(t + 1) * 128]


def take_image(scr, image, count, images):
    rows = pl.ds(image, count, images)
    return jnp.concatenate([scr[t, rows, :] for t in range(scr.shape[0])], 1)


def put_image(scr, image, count, images, value):
    for t in range(scr.shape[0]):
        scr[t, pl.ds(image, count, images), :] = value[:, t * 128:(t + 1) * 128]


def slabs(rows, columns):
    return pltpu.VMEM((columns // 128, rows, 128), F32)


def cost(flops, nbytes, trans=0):
    return pl.CostEstimate(flops=int(flops), bytes_accessed=int(nbytes), transcendentals=int(trans))


def whole(x):
    shape = x.shape
    return pl.BlockSpec(shape, lambda *_: (0,) * len(shape))


def params(mib):
    return pltpu.CompilerParams(vmem_limit_bytes=mib * MIB, dimension_semantics=("arbitrary",))


def turned_heads(x, fill):
    return jnp.transpose(jnp.concatenate([x, fill], 0))[:, 0:x.shape[0]].astype(LOW)


def attend_kernel(q_ref, f_ref, bits_ref, flag_ref, mc_ref, mf_ref, wq_ref, bq_ref, wkv_ref, vb_ref, elo_ref,
                  ehi_ref, e_ref, kv_ref, pay_ref, cq_ref, q_scr, w_scr, all_scr, mc_scr, wq_scr, wkv_scr, vb_scr):
    i = pl.program_id(0)
    matched, images, wide = mc_ref.shape
    width = q_ref.shape[1]
    count = q_ref.shape[0] // images
    rows = q_scr.shape[0]
    pixels = f_ref.shape[1]
    tall = rows + HEADS
    head = width // HEADS

    @pl.when(i == 0)
    def _():
        q_scr[...] = jnp.zeros_like(q_scr)
        w_scr[...] = jnp.zeros_like(w_scr)
        slabs_in(all_scr, q_ref[...])
        slabs_in(mc_scr, mc_ref[...].astype(F32).reshape(matched * images, wide))
        wq_scr[...] = wq_ref[...].astype(LOW)
        wkv_scr[0:width] = jnp.transpose(wkv_ref[:, :width]).astype(LOW)
        wkv_scr[width:] = jnp.transpose(wkv_ref[:, width:]).astype(LOW)
        vb_scr[...] = jnp.transpose(jnp.broadcast_to(vb_ref[...], (128, width)))

    pay_ref[0, tall:] = jnp.zeros((pay_ref.shape[1] - tall, width), F32)
    pay_ref[0, tall:tall + matched] = nn(take_image(mc_scr, i, matched, images).astype(LOW), mf_ref[0])

    q_scr[0:count] = take_image(all_scr, i, count, images)
    w_scr[:, 0:count] = jnp.where(flag_ref[pl.ds(i, 1), :] > 0, 65535, bits_ref[0])

    scale = 1.0 / math.sqrt(head)
    cq = ((nn(q_scr[...].astype(LOW), wq_scr[...]) + bq_ref[...]) * scale).astype(LOW).astype(F32)
    cq_ref[0] = cq

    bits = w_scr[...]
    low = (bits & 255).astype(F32).astype(LOW)
    high = (bits >> 8).astype(F32).astype(LOW)
    byte = (tn(low, elo_ref[...]) + tn(high, ehi_ref[...])).astype(jnp.int32)
    shift = lax.broadcasted_iota(jnp.int32, (rows, pixels), 1) & 7
    pen = jnp.where(((byte >> shift) & 1) == 1, 0.0, -PENALTY)

    keyval = nt(wkv_scr[...], f_ref[0])
    ck = keyval[:width].astype(LOW)
    cv = (keyval[width:] + jnp.concatenate([vb_scr[...]] * (pixels // 128), 1)).astype(LOW)
    kv_ref[0, :width] = ck
    kv_ref[0, width:] = cv

    def scores(h):
        at = slice(h * head, (h + 1) * head)
        return nn(cq[:, at].astype(LOW), ck[at]) + pen

    lane = lax.broadcasted_iota(jnp.int32, (rows, 128), 1)
    stats = jnp.zeros((rows, 128), F32)
    parts = []
    following = scores(0)
    for h in range(HEADS):
        s = following
        if h + 1 < HEADS:
            following = scores(h + 1)
        m = jnp.max(s, -1, keepdims=True)
        e = jnp.exp(s - m)
        total = jnp.sum(e, -1, keepdims=True)
        e_low = e.astype(LOW)
        e_ref[0, h] = e_low
        parts.append(nt(cv[h * head:(h + 1) * head], e_low))
        stats = jnp.where(lane == h, m, stats)
        stats = jnp.where(lane == HEADS + h, total, stats)
    pay_ref[0, 0:rows] = jnp.transpose(jnp.concatenate(parts, 0))
    full = jnp.concatenate([stats, jnp.ones((128 - rows, 128), F32)], 0)
    turned = jnp.transpose(full)
    pay_ref[0, rows:tall, 0:128] = turned[0:HEADS]
    pay_ref[0, rows:tall, 128:256] = turned[HEADS:2 * HEADS]


def attend(queries, features, bits, reopen_flags, mask_cotan, mask_features, query_weight, query_bias, keyval_weight,
           value_bias):
    images, pixels, width = features.shape
    words, count = bits.shape[1:]
    rows = up(count, 8)
    matched, _, wide = mask_cotan.shape
    tall = rows + HEADS + up(matched, 8)
    pixel = jnp.arange(pixels)
    word = jnp.arange(words)
    here = pixel[None, :] // 16 == word[:, None]
    e_lo = (here & (pixel[None, :] % 16 < 8)).astype(LOW)
    e_hi = (here & (pixel[None, :] % 16 >= 8)).astype(LOW)
    per = lambda *shape: pl.BlockSpec((1,) + shape, lambda i: (i,) + (0,) * len(shape))
    args = (queries, features, bits, reopen_flags, mask_cotan, mask_features, query_weight, query_bias[None],
            keyval_weight, value_bias[None], e_lo, e_hi)
    in_specs = [whole(a) for a in args]
    in_specs[1] = per(pixels, width)
    in_specs[2] = per(words, count)
    in_specs[5] = per(wide, width)
    flops = 2 * images * (pixels * width * 2 * width + 2 * HEADS * rows * pixels * width + 64 * wide * width)
    nbytes = images * (pixels * width * 6 + HEADS * rows * pixels * 2 + wide * (width + matched) * 2)
    return pl.pallas_call(
        attend_kernel,
        grid=(images,),
        in_specs=in_specs,
        out_specs=(per(HEADS, rows, pixels), per(2 * width, pixels), per(tall, width), per(rows, width)),
        out_shape=(
            jax.ShapeDtypeStruct((images, HEADS, rows, pixels), LOW),
            jax.ShapeDtypeStruct((images, 2 * width, pixels), LOW),
            jax.ShapeDtypeStruct((images, tall, width), F32),
            jax.ShapeDtypeStruct((images, rows, width), F32),
        ),
        scratch_shapes=[
            pltpu.VMEM((rows, width), F32),
            pltpu.VMEM((words, rows), jnp.int32),
            slabs(count * images, width),
            slabs(matched * images, wide),
            pltpu.VMEM((width, width), LOW),
            pltpu.VMEM((2 * width, width), LOW),
            pltpu.VMEM((width, 128), F32),
        ],
        compiler_params=params(60),
        cost_estimate=cost(flops, nbytes, images * HEADS * rows * pixels),
        name="attend",
    )(*args)


def combine_kernel(rows, *refs):
    parts, out_ref = refs[:-1], refs[-1]
    images, full, width = out_ref.shape
    tall = rows + HEADS
    onehot = head_onehot(width, HEADS)
    for i in range(images):
        ms = [p[i, rows:tall, 0:128] for p in parts]
        ls = [p[i, rows:tall, 128:256] for p in parts]
        top = functools.reduce(jnp.maximum, ms)
        rs = [jnp.exp(m - top) for m in ms]
        total = sum(r * l for r, l in zip(rs, ls))
        acc = jnp.zeros((rows, width), F32)
        es = jnp.zeros((full - tall, width), F32)
        for p, r in zip(parts, rs):
            acc = acc + p[i, 0:rows] * tn(r / total, onehot, HIGH)[0:rows]
            es = es + p[i, tall:]
        out_ref[i, 0:rows] = acc
        out_ref[i, rows:tall, 0:128] = top
        out_ref[i, rows:tall, 128:256] = total
        out_ref[i, tall:] = es


def combine(parts, rows):
    shape = parts[0].shape
    return pl.pallas_call(
        functools.partial(combine_kernel, rows),
        out_shape=jax.ShapeDtypeStruct(shape, F32),
        compiler_params=pltpu.CompilerParams(vmem_limit_bytes=32 * MIB),
        cost_estimate=cost(1e6, 5 * 4 * math.prod(shape)),
        name="combine",
    )(*parts)


def norm_forward(x, gain, bias):
    centre = x - jnp.mean(x, -1, keepdims=True)
    inverse = lax.rsqrt(jnp.mean(centre * centre, -1, keepdims=True) + EPS)
    normed = centre * inverse
    return normed * gain + bias, normed, inverse


def norm_backward(normed, inverse, gain, grad):
    dnormed = grad * gain
    return inverse * (
        dnormed - jnp.mean(dnormed, -1, keepdims=True) - normed * jnp.mean(dnormed * normed, -1, keepdims=True)
    )


def gelu_pair(x):
    square = x * x
    t = jnp.tanh(x * (CURVE + (CURVE * CUBE) * square))
    half = 0.5 + 0.5 * t
    slope = half + (0.5 * x) * (1.0 - t * t) * (CURVE + (3.0 * CURVE * CUBE) * square)
    return x * half, slope


def column_sum(x):
    return jnp.sum(x, 0, keepdims=True)


def chain_kernel(
    pieces, me_ref, *refs
):
    att_parts, refs = refs[:pieces], refs[pieces:]
    chain_body(me_ref, att_parts, *refs)


def chain_body(
    me_ref, att_parts, loc_ref, q_ref, match_ref, cot_ref, wc_raw, bc_ref, gain_ref, nbias_ref, ws_raw, bs_ref, wso_raw, bso_ref,
    wh_raw, bh_ref, who_raw, bho_ref, we_raw, be_ref,
    x3_ref, emb_ref, dn_ref, dt_ref, dp1_ref, mine_ref, away_ref,
    g_ref, wc_ref, ws_ref, wso_ref, wh_ref, who_ref, we_ref, all_scr, cot_scr, out_scr, att_scr, emb_scr,
    q_scr, sq_scr, sk_scr, sv_scr, so_scr, pr_scr, h_scr, gp_scr, dso_scr, dm_scr
):
    step = pl.program_id(0)
    batch, rows, width = dn_ref.shape
    matched = match_ref.shape[1]
    count, images = cot_ref.shape[:2]
    tall = rows + HEADS
    flat = batch * rows
    hidden = wh_ref.shape[1]
    scale = 1.0 / math.sqrt(width // HEADS)
    hm = head_mask(width)

    @pl.when(step == 0)
    def _():
        q_scr[...] = jnp.zeros_like(q_scr)
        g_ref[...] = jnp.zeros_like(g_ref)
        n = att_parts[0].shape[0]
        for k, part in enumerate(att_parts):
            att_scr[pl.ds((me_ref[0] ^ k) * n, n)] = part[...]
        slabs_in(all_scr, q_ref[...])
        slabs_in(cot_scr, cot_ref[...].astype(F32).reshape(count * images, width))
        for raw, ref in ((wc_raw, wc_ref), (ws_raw, ws_ref), (wso_raw, wso_ref), (wh_raw, wh_ref), (who_raw, who_ref),
                         (we_raw, we_ref)):
            ref[...] = raw[...].astype(LOW)

    def put(tile, value):
        g_ref[tile * width:(tile + 1) * width] += value

    bias_at = (T_HIDDEN + 2 * (hidden // width)) * width

    def put_bias(index, value):
        g_ref[bias_at + index:bias_at + index + 1] += value

    first = step * batch
    for b in range(batch):
        q_scr[b, 0:count] = take_image(all_scr, first + b, count, images)
    att = att_scr[pl.ds(first, batch), 0:rows].reshape(flat, width)
    att_low = att.astype(LOW)
    queries = q_scr[...].reshape(flat, width)
    x1, n1, i1 = norm_forward(queries + nn(att_low, wc_ref[...]) + bc_ref[...], gain_ref[0:1], nbias_ref[0:1])
    x1_low = x1.astype(LOW)
    mixed = nn(x1_low, ws_ref[...])
    three = (batch, rows, width)
    sq_scr[...] = ((mixed[:, :width] + bs_ref[0:1]) * scale).reshape(three)
    sk_scr[...] = mixed[:, width:2 * width].reshape(three)
    sv_scr[...] = (mixed[:, 2 * width:] + bs_ref[1:2]).reshape(three)

    head = width // HEADS
    lanes = lambda h: slice(h * 128, (h + 1) * 128)
    fill = jnp.zeros((128 - rows, width), F32)

    def tall_heads(x):
        return spread_low(jnp.concatenate([x, fill], 0), hm)

    def turn(x):
        return jnp.transpose(jnp.concatenate([x, fill], 0))[:, 0:rows].astype(LOW)

    def by_head(turned, x):
        return jnp.transpose(jnp.concatenate(
            [nn(turned[h * head:(h + 1) * head], x[:, lanes(h)]) for h in range(HEADS)], 0))[0:rows]

    for b in range(batch):
        ss = nt(sk_scr[b].astype(LOW), tall_heads(sq_scr[b]))
        keys = lax.broadcasted_iota(jnp.int32, ss.shape, 0)
        ss = jnp.where(keys < count, ss, -1e30)
        p = jnp.exp(ss - jnp.max(ss, 0, keepdims=True))
        p = p * (1.0 / jnp.sum(p, 0, keepdims=True))
        pr_scr[b] = p
        so_scr[b] = by_head(turn(sv_scr[b]), p.astype(LOW))
    so_low = so_scr[...].reshape(flat, width).astype(LOW)
    x2, n2, i2 = norm_forward(x1 + nn(so_low, wso_ref[...]) + bso_ref[...], gain_ref[1:2], nbias_ref[1:2])
    x2_low = x2.astype(LOW)
    block = 2 * width

    def ff_forward(j, acc):
        cols = pl.ds(pl.multiple_of(j * block, block), block)
        h, slope = gelu_pair(nn(x2_low, wh_ref[:, cols]) + bh_ref[:, cols])
        h = h.astype(LOW)
        h_scr[:, cols] = h
        gp_scr[:, cols] = slope.astype(gp_scr.dtype)
        return acc + nn(h, who_ref[cols, :])

    ff = lax.fori_loop(0, hidden // block, ff_forward, jnp.zeros((flat, width), F32))
    x3, n3, i3 = norm_forward(x2 + ff + bho_ref[...], gain_ref[2:3], nbias_ref[2:3])
    for b in range(batch):
        put_image(out_scr, first + b, count, images, x3[b * rows:b * rows + count])

    x3_low = x3.astype(LOW)
    h1, slope1 = gelu_pair(nn(x3_low, we_ref[0]) + be_ref[0:1])
    h1 = h1.astype(LOW)
    h2, slope2 = gelu_pair(nn(h1, we_ref[1]) + be_ref[1:2])
    h2 = h2.astype(LOW)
    emb = nn(h2, we_ref[2]) + be_ref[2:3]
    for b in range(batch):
        put_image(emb_scr, first + b, count, images, emb[b * rows:b * rows + count])

    grads = []
    for b in range(batch):
        spots = match_ref[pl.ds(first + b, 1), :]
        pick = (lax.broadcasted_iota(jnp.int32, (rows, matched), 0) == spots).astype(F32).astype(LOW)
        grads.append(nn(pick, att_scr[first + b, tall:tall + matched].astype(LOW)))
    dz3 = jnp.concatenate(grads, 0)
    dz3_low = dz3.astype(LOW)
    put(T_EMBED + 2, tn(h2, dz3_low))
    put_bias(19, column_sum(dz3_low.astype(F32)))
    dz2 = (nt(dz3_low, we_ref[2]) * slope2).astype(LOW)
    put(T_EMBED + 1, tn(h1, dz2))
    put_bias(18, column_sum(dz2.astype(F32)))
    dz1 = (nt(dz2, we_ref[1]) * slope1).astype(LOW)
    put(T_EMBED, tn(x3_low, dz1))
    put_bias(17, column_sum(dz1.astype(F32)))
    for b in range(batch):
        q_scr[b, 0:count] = take_image(cot_scr, first + b, count, images)
    dx3 = q_scr[...].reshape(flat, width) + nt(dz1, we_ref[0])
    put_bias(3, column_sum(dx3 * n3))
    put_bias(6, column_sum(dx3))
    dp3 = norm_backward(n3, i3, gain_ref[2:3], dx3)
    dff = dp3.astype(LOW)
    put_bias(16, column_sum(dff.astype(F32)))

    def ff_backward(j, acc):
        cols = pl.ds(pl.multiple_of(j * block, block), block)
        base = (T_HIDDEN + hidden // width) * width
        spot = pl.ds(pl.multiple_of(base + j * block, block), block)
        g_ref[spot] += tn(h_scr[:, cols], dff)
        dz = (nt(dff, who_ref[cols, :]) * gp_scr[:, cols].astype(F32)).astype(LOW)
        gh = tn(x2_low, dz)
        sums = column_sum(dz.astype(F32))
        for t in range(block // width):
            tile = pl.ds(pl.multiple_of(T_HIDDEN * width + j * block + t * width, width), width)
            g_ref[tile] += gh[:, t * width:(t + 1) * width]
            g_ref[pl.ds(bias_at + 8 + j * (block // width) + t, 1)] += sums[:, t * width:(t + 1) * width]
        return acc + nt(dz, wh_ref[:, cols])

    dx2 = dp3 + lax.fori_loop(0, hidden // block, ff_backward, jnp.zeros((flat, width), F32))
    put_bias(2, column_sum(dx2 * n2))
    put_bias(5, column_sum(dx2))
    dp2 = norm_backward(n2, i2, gain_ref[1:2], dx2)
    dsa = dp2.astype(LOW)
    put(T_SELFOUT, tn(so_low, dsa))
    put_bias(7, column_sum(dsa.astype(F32)))
    dso_scr[...] = nt(dsa, wso_ref[...]).reshape(three)

    for b in range(batch):
        dsox = tall_heads(dso_scr[b])
        p = pr_scr[b]
        dp = nt(sv_scr[b].astype(LOW), dsox)
        dss = (p * (dp - jnp.sum(p * dp, 0, keepdims=True))).astype(LOW)
        dm_scr[b, :, 0:width] = by_head(turn(sk_scr[b]), dss) * scale
        dm_scr[b, :, width:2 * width] = nn(dss, tall_heads(sq_scr[b]))
        dm_scr[b, :, 2 * width:] = nn(p.astype(LOW), dsox)

    dm = dm_scr[...].reshape(flat, 3 * width).astype(LOW)
    gs = tn(x1_low, dm)
    for t in range(3):
        put(T_SELF + t, gs[:, t * width:(t + 1) * width])
    put_bias(20, column_sum(dm[:, :width].astype(F32)))
    put_bias(21, column_sum(dm[:, 2 * width:].astype(F32)))
    dx1 = dp2 + nt(dm, ws_ref[...])
    put_bias(1, column_sum(dx1 * n1))
    put_bias(4, column_sum(dx1))
    dp1 = norm_backward(n1, i1, gain_ref[0:1], dx1)
    dp1_ref[...] = dp1.reshape(three)
    dca = dp1.astype(LOW)
    put(T_CROSS, tn(att_low, dca))
    put_bias(0, column_sum(dca.astype(F32)))
    d_att = nt(dca, wc_ref[...]).reshape(three)
    onehot = head_onehot(width, HEADS)
    back = head_onehot(width, 128, True)
    for b in range(batch):
        top = att_scr[first + b, rows:tall, 0:128]
        total = att_scr[first + b, rows:tall, 128:256]
        ratio = jnp.exp(loc_ref[b, rows:tall, 0:128] - top) / total
        dn = d_att[b] * tn(ratio, onehot, HIGH)[0:rows]
        dn_ref[b] = dn
        dt_ref[b] = -nn(dn * att_scr[first + b, 0:rows], back, HIGH)

    @pl.when(step == 1)
    def _():
        x3_ref[...] = jnp.concatenate([out_scr[t] for t in range(out_scr.shape[0])], 1)
        emb_ref[...] = jnp.concatenate([emb_scr[t] for t in range(emb_scr.shape[0])], 1)
        share = mine_ref.shape[0]
        at = me_ref[1] * 2 + me_ref[2]
        mine_ref[...] = g_ref[pl.ds(pl.multiple_of(at * share, 8), share)]
        away_ref[...] = g_ref[pl.ds(pl.multiple_of((at + 1 - 2 * me_ref[2]) * share, 8), share)]


def chain(me, parts, pay, queries, matched, query_cotan, weights, n_pix):
    images, full, width = pay.shape
    count = query_cotan.shape[0]
    rows = up(count, 8)
    batch = images // 2
    hidden = weights[8].shape[1]
    tiles = T_HIDDEN + 2 * (hidden // width)
    grads = up(tiles * width + 22, 256)
    half = lambda *shape: pl.BlockSpec((batch,) + shape, lambda i, *_: (i,) + (0,) * len(shape))
    pieces = len(parts)
    args = tuple(parts) + (pay, queries, matched, query_cotan) + weights
    in_specs = [whole(a) for a in args]
    in_specs[pieces] = half(full, width)
    out_shape = (
        jax.ShapeDtypeStruct((count * images, width), F32),
        jax.ShapeDtypeStruct((count * images, width), F32),
        jax.ShapeDtypeStruct((images, rows, width), F32),
        jax.ShapeDtypeStruct((images, rows, 128), F32),
        jax.ShapeDtypeStruct((images, rows, width), F32),
        jax.ShapeDtypeStruct((grads // n_pix // 2, width), F32),
        jax.ShapeDtypeStruct((grads // n_pix // 2, width), F32),
    )
    flat = batch * rows
    three = (batch, rows, width)
    many = slabs(count * images, width)
    return pl.pallas_call(
        functools.partial(chain_kernel, pieces),
        grid_spec=pltpu.PrefetchScalarGridSpec(
            num_scalar_prefetch=1,
            grid=(2,),
            in_specs=in_specs,
            out_specs=(whole(out_shape[0]), whole(out_shape[1]), half(rows, width), half(rows, 128), half(rows, width),
                       whole(out_shape[5]), whole(out_shape[6])),
            scratch_shapes=[pltpu.VMEM((grads, width), F32)] + [pltpu.VMEM(weights[k].shape, LOW) for k in (0, 4, 6, 8, 10, 12)] + [
                many,
                many,
                many,
                pltpu.VMEM((images, full, width), F32),
                many,
                pltpu.VMEM(three, F32),
                pltpu.VMEM(three, F32),
                pltpu.VMEM(three, F32),
                pltpu.VMEM(three, F32),
                pltpu.VMEM(three, F32),
                pltpu.VMEM((batch, rows, HEADS * 128), F32),
                pltpu.VMEM((flat, hidden), LOW),
                pltpu.VMEM((flat, hidden), LOW),
                pltpu.VMEM(three, F32),
                pltpu.VMEM((batch, rows, 3 * width), F32),
            ],
        ),
        out_shape=out_shape,
        compiler_params=params(62),
        cost_estimate=cost(2 * 8e9, 20e6, 4e6),
        name="chain",
    )(me, *args)


def mask_out_kernel(emb_ref, match_ref, mc_ref, mf_ref, logit_old, grad_old, logit_ref, grad_ref, chosen_scr, mc_scr,
                    emb_scr, low_scr, logit_scr):
    images, matched, width = chosen_scr.shape
    count = logit_ref.shape[0] // images
    rows = low_scr.shape[1]
    part = mc_ref.shape[2]

    @pl.when(pl.program_id(0) == 0)
    def _():
        slabs_in(emb_scr, emb_ref[...])
        low_scr[...] = jnp.zeros_like(low_scr)
        for b in range(images):
            pick = (lax.broadcasted_iota(jnp.int32, (count, matched), 0) == match_ref[b:b + 1, :]).astype(F32).astype(LOW)
            emb = take_image(emb_scr, b, count, images).astype(LOW)
            low_scr[b, 0:count] = emb.astype(F32)
            chosen_scr[b] = tn(pick, emb)

    slabs_in(mc_scr, mc_ref[...].astype(F32).reshape(matched * images, part))
    for b in range(images):
        put_image(logit_scr, b, count, images, nt(low_scr[b].astype(LOW), mf_ref[b])[0:count])
        grad_ref[b] = tn(take_image(mc_scr, b, matched, images).astype(LOW), chosen_scr[b].astype(LOW))
    for t in range(part // 128):
        logit_ref[:, t * 128:(t + 1) * 128] = logit_scr[t]


def mask_out(emb, matched_queries, mask_cotan, mask_features, count, pieces, steps, old=None):
    matched, images, pixels = mask_cotan.shape
    width = emb.shape[1]
    part = pixels // pieces
    first, last = steps
    out_shape = (
        jax.ShapeDtypeStruct((count * images, pixels), F32),
        jax.ShapeDtypeStruct((images, pixels, width), F32),
    )
    args = (emb, matched_queries, mask_cotan, mask_features)
    here = pl.BlockSpec(memory_space=pl.ANY)
    kernel = mask_out_kernel
    aliases = {}
    specs = []
    if old is None:
        def kernel(a, b, c, d, *rest):
            mask_out_kernel(a, b, c, d, None, None, *rest)
    else:
        args += old
        aliases = {4: 0, 5: 1}
        specs = [here, here]
    return pl.pallas_call(
        kernel,
        grid=(last - first,),
        in_specs=[
            whole(emb),
            whole(matched_queries),
            pl.BlockSpec((matched, images, part), lambda j: (0, 0, j + first)),
            pl.BlockSpec((images, part, width), lambda j: (0, j + first, 0)),
        ] + specs,
        out_specs=(
            pl.BlockSpec((count * images, part), lambda j: (0, j + first)),
            pl.BlockSpec((images, part, width), lambda j: (0, j + first, 0)),
        ),
        out_shape=out_shape,
        input_output_aliases=aliases,
        scratch_shapes=[pltpu.VMEM((images, matched, width), F32), slabs(matched * images, part),
                        slabs(count * images, width), pltpu.VMEM((images, up(count, 8), width), F32),
                        slabs(count * images, part)],
        compiler_params=params(60),
        cost_estimate=cost(
            2 * images * pixels * width * 160 * (last - first) / pieces,
            images * pixels * (width * 6 + count * 4 + matched * 2) * (last - first) / pieces),
        name="mask_out",
    )(*args)


def attend_back_kernel(e_ref, kv_ref, f_ref, cq_ref, dn_ref, dt_ref, wkv_ref, fg_old, qp_old, g_old,
                       fg_ref, qp_ref, g_ref, acc_scr, w_scr, vb_scr):
    i = pl.program_id(0)
    rows, width = cq_ref.shape[1:]
    pixels = f_ref.shape[1]
    head = width // HEADS

    @pl.when(i == 0)
    def _():
        acc_scr[...] = jnp.zeros_like(acc_scr)
        vb_scr[...] = jnp.zeros_like(vb_scr)
        w_scr[0:width] = jnp.transpose(wkv_ref[:, :width]).astype(LOW)
        w_scr[width:] = jnp.transpose(wkv_ref[:, width:]).astype(LOW)

    dn = dn_ref[0]
    fill = jnp.zeros((128 - rows, width), F32)
    cq_turned = turned_heads(cq_ref[0], fill)
    dn_turned = turned_heads(dn, fill)

    def weigh(h):
        at = slice(h * head, (h + 1) * head)
        return nn(dn[:, at].astype(LOW), kv_ref[0, width + h * head:width + (h + 1) * head]) + dt_ref[0, :, h:h + 1]

    parts, keys, values = [], [], []
    following = weigh(0)
    for h in range(HEADS):
        at = slice(h * head, (h + 1) * head)
        dw = following
        if h + 1 < HEADS:
            following = weigh(h + 1)
        e_low = e_ref[0, h]
        ds = (e_low.astype(F32) * dw).astype(LOW)
        values.append(nn(dn_turned[at], e_low).astype(LOW))
        keys.append(nn(cq_turned[at], ds).astype(LOW))
        parts.append(nt(kv_ref[0, at], ds))
    qp_ref[0] = jnp.transpose(jnp.concatenate(parts, 0))
    turned = jnp.concatenate(keys + values, 0)
    acc_scr[...] += nn(turned, f_ref[0])
    summed = turned[width:].astype(F32)
    lanes_sum = summed[:, 0:128]
    for t in range(1, pixels // 128):
        lanes_sum = lanes_sum + summed[:, t * 128:(t + 1) * 128]
    vb_scr[...] += lanes_sum
    fg_ref[0] = tn(turned, w_scr[...])

    @pl.when(i == pl.num_programs(0) - 1)
    def _():
        old = 0.0 if g_old is None else g_old[...]
        sums = jnp.sum(jnp.transpose(vb_scr[...]), 0, keepdims=True)
        fill = jnp.zeros((g_ref.shape[0] - 2 * width - 1, width), F32)
        turned = [jnp.transpose(acc_scr[0:width]), jnp.transpose(acc_scr[width:]), sums, fill]
        g_ref[...] = old + jnp.concatenate(turned, 0)


def attend_back(e, kv, features, cq, dn, dt, keyval_weight, steps, old=None):
    images, pixels, width = features.shape
    rows = cq.shape[1]
    first, last = steps
    per = lambda *shape: pl.BlockSpec((1,) + shape, lambda i: (i + first,) + (0,) * len(shape))
    tall = HEADS * rows
    share = last - first
    flops = 2 * share * (4 * tall * pixels * width + 4 * pixels * width * width)
    nbytes = share * (tall * pixels * 2 + pixels * width * 10)
    out_shape = (
        jax.ShapeDtypeStruct((images, pixels, width), F32),
        jax.ShapeDtypeStruct((images, rows, width), F32),
        jax.ShapeDtypeStruct((2 * width + 32, width), F32),
    )
    args = (e, kv, features, cq, dn, dt, keyval_weight)
    in_specs = [per(HEADS, rows, pixels), per(2 * width, pixels), per(pixels, width), per(rows, width), per(rows, width),
                per(rows, 128), whole(keyval_weight)]
    aliases = {}
    if old is None:
        def kernel(*refs):
            attend_back_kernel(*refs[:7], None, None, None, *refs[7:])
    else:
        kernel = attend_back_kernel
        here = pl.BlockSpec(memory_space=pl.ANY)
        args += old
        in_specs += [here, here, whole(out_shape[2])]
        aliases = {7: 0, 8: 1}
    return pl.pallas_call(
        kernel,
        grid=(share,),
        in_specs=in_specs,
        out_specs=(per(pixels, width), per(rows, width), whole(out_shape[2])),
        out_shape=out_shape,
        input_output_aliases=aliases,
        scratch_shapes=[pltpu.VMEM((2 * width, width), F32), pltpu.VMEM((2 * width, width), LOW), pltpu.VMEM((width, 128), F32)],
        compiler_params=params(60),
        cost_estimate=cost(flops, nbytes),
        name="attend_back",
    )(*args)


def query_sum_kernel(*refs):
    parts, out_ref = refs[:-1], refs[-1]
    total = parts[0][...]
    for p in parts[1:]:
        total = total + p[...]
    out_ref[...] = total


def query_sum(parts):
    return pl.pallas_call(
        query_sum_kernel,
        out_shape=jax.ShapeDtypeStruct(parts[0].shape, F32),
        compiler_params=pltpu.CompilerParams(vmem_limit_bytes=32 * MIB),
        cost_estimate=cost(1e6, 5 * 4 * math.prod(parts[0].shape)),
        name="query_sum",
    )(*parts)


def query_back_kernel(pieces, me_ref, *refs):
    parts = refs[:pieces]
    q_ref, dp_ref, wq_ref, qg_ref, g_ref, scr, sum_scr, all_scr, out_scr = refs[pieces:]
    images, rows, width = dp_ref.shape
    count = q_ref.shape[0] // images
    scale = 1.0 / math.sqrt(width // HEADS)
    n = parts[0].shape[0]
    for k, part in enumerate(parts):
        sum_scr[pl.ds((me_ref[0] ^ k) * n, n)] = part[...]
    scr[...] = jnp.zeros_like(scr)
    slabs_in(all_scr, q_ref[...])
    for b in range(images):
        scr[b, 0:count] = take_image(all_scr, b, count, images)
    d_cq = (sum_scr[...].reshape(images * rows, width) * scale).astype(LOW)
    out = dp_ref[...] + nt(d_cq, wq_ref[...].astype(LOW)).reshape(images, rows, width)
    for b in range(images):
        put_image(out_scr, b, count, images, out[b, 0:count])
    qg_ref[...] = jnp.concatenate([out_scr[t] for t in range(out_scr.shape[0])], 1)
    g_ref[0:width] = tn(scr[...].reshape(images * rows, width).astype(LOW), d_cq)
    g_ref[width:] = jnp.zeros((g_ref.shape[0] - width, width), F32)
    g_ref[width:width + 1] = column_sum(d_cq.astype(F32))


def query_back(me, parts, queries, dp1, query_weight):
    images, rows, width = dp1.shape
    args = tuple(parts) + (queries, dp1, query_weight)
    out_shape = (jax.ShapeDtypeStruct(queries.shape, F32), jax.ShapeDtypeStruct((width + 32, width), F32))
    return pl.pallas_call(
        functools.partial(query_back_kernel, len(parts)),
        grid_spec=pltpu.PrefetchScalarGridSpec(
            num_scalar_prefetch=1,
            grid=(1,),
            in_specs=[whole(a) for a in args],
            out_specs=tuple(whole(o) for o in out_shape),
            scratch_shapes=[pltpu.VMEM((images, rows, width), F32), pltpu.VMEM((images, rows, width), F32),
                            slabs(*queries.shape), slabs(*queries.shape)],
        ),
        out_shape=out_shape,
        compiler_params=params(32),
        cost_estimate=cost(5e8, 8e6),
        name="query_back",
    )(me, *args)


def unpack_kernel(split, me_ref, *refs):
    (sa, sb, ra, rb, sa2, sb2, ra2, rb2, tail, tail2,
     query_ref, query_bias_ref, keyval_ref, value_bias_ref, cross_ref, cross_bias_ref, gain_ref, nbias_ref,
     self_ref, self_bias_ref, selfout_ref, selfout_bias_ref, hidden_ref, hidden_bias_ref, hidout_ref, hidout_bias_ref,
     embed_ref, embed_bias_ref, g, t) = refs
    pix, core = me_ref[1], me_ref[2]
    width = query_ref.shape[0]
    short = sa.shape[0] // 2

    def place(ref, row, block, half, second):
        at = ((pix ^ block) * 2 + half) * 2 + second
        g[pl.ds(pl.multiple_of(at * short, 8), short)] = ref[row * short:(row + 1) * short]

    for half, four in ((core, (sa, sb, ra, rb)), (1 - core, (sa2, sb2, ra2, rb2))):
        for row in range(2):
            place(four[0], row, (0, 1)[row], half, 0)
            place(four[1], row, (0, 2)[row], half, 1)
            place(four[2], row, (2, 3)[row], half, 0)
            place(four[3], row, (1, 3)[row], half, 1)
    small = tail.shape[0] // 4
    for half, ref in ((core, tail), (1 - core, tail2)):
        for k in range(4):
            at = (pix ^ k) * 2 + half
            t[pl.ds(pl.multiple_of(at * small, 8), small)] = ref[k * small:(k + 1) * small]

    def tile(n, k=1):
        return g[n * width:(n + k) * width]

    many = hidden_ref.shape[1] // width
    bias = (T_HIDDEN + 2 * many) * width
    cross_ref[...] = tile(T_CROSS)
    selfout_ref[...] = tile(T_SELFOUT)
    embed_ref[...] = tile(T_EMBED, 3)
    hidout_ref[...] = tile(T_HIDDEN + many, many)
    for n in range(3):
        self_ref[:, n * width:(n + 1) * width] = tile(T_SELF + n)
    for n in range(many):
        hidden_ref[:, n * width:(n + 1) * width] = tile(T_HIDDEN + n)
        hidden_bias_ref[:, n * width:(n + 1) * width] = g[bias + 8 + n:bias + 9 + n]
    cross_bias_ref[...] = g[bias:bias + 1]
    gain_ref[...] = g[bias + 1:bias + 4]
    nbias_ref[...] = g[bias + 4:bias + 7]
    selfout_bias_ref[...] = g[bias + 7:bias + 8]
    hidout_bias_ref[...] = g[bias + 16:bias + 17]
    embed_bias_ref[...] = g[bias + 17:bias + 20]
    self_bias_ref[...] = g[bias + 20:bias + 22]
    block = 2 * small
    low, high = [], []
    for k in range(4):
        low.append(t[k * block:k * block + split])
        high.append(t[k * block + split:(k + 1) * block])
    low, high = jnp.concatenate(low, 0), jnp.concatenate(high, 0)
    keyval_ref[:, 0:width] = low[0:width]
    keyval_ref[:, width:] = low[width:2 * width]
    value_bias_ref[...] = low[2 * width:2 * width + 1]
    query_ref[...] = high[0:width]
    query_bias_ref[...] = high[width:width + 1]


def unpack(me, pieces, tails, split, width, hidden):
    args = tuple(pieces) + tuple(tails)
    shapes = ((width, width), (1, width), (width, 2 * width), (1, width), (width, width), (1, width), (3, width), (3, width),
              (width, 3 * width), (2, width), (width, width), (1, width), (width, hidden), (1, hidden), (hidden, width),
              (1, width), (3 * width, width), (3, width))
    out_shape = tuple(jax.ShapeDtypeStruct(shape, F32) for shape in shapes)
    rows = sum(p.shape[0] for p in pieces)
    return pl.pallas_call(
        functools.partial(unpack_kernel, split),
        grid_spec=pltpu.PrefetchScalarGridSpec(
            num_scalar_prefetch=1,
            grid=(1,),
            in_specs=[whole(a) for a in args],
            out_specs=tuple(whole(o) for o in out_shape),
            scratch_shapes=[pltpu.VMEM((rows, width), F32), pltpu.VMEM((2 * tails[0].shape[0], width), F32)],
        ),
        out_shape=out_shape,
        compiler_params=params(60),
        cost_estimate=cost(1e6, 16e6),
        name="unpack",
    )(me, *args)


def beside(*values):
    return lax.optimization_barrier(values)


def swap(x, axis, n, key):
    return lax.ppermute(x, axis, [(d, d ^ key) for d in range(n)])


def scatter_out(x, axis, n):
    me = lax.axis_index(axis)
    chunks = [lax.dynamic_index_in_dim(x, me ^ k, 0, keepdims=False) for k in range(n)]
    return tuple(c if k == 0 else swap(c, axis, n, k) for k, c in enumerate(chunks))


def gather_in(x, axis, n):
    return tuple(x if k == 0 else swap(x, axis, n, k) for k in range(n))


def side(axis, key):
    return (lax.axis_index(axis) // key) % 2


def halve(x, axis, n, key):
    halves = x.reshape((2, -1) + x.shape[1:])
    mine = lax.dynamic_index_in_dim(halves, side(axis, key), 0, keepdims=False)
    away = lax.dynamic_index_in_dim(halves, 1 - side(axis, key), 0, keepdims=False)
    return mine, swap(away, axis, n, key)


def join(mine, other, axis, key):
    first = side(axis, key) == 0
    return jnp.concatenate([jnp.where(first, mine, other), jnp.where(first, other, mine)], 0)


def local(
    queries, features, mask_features, attend_bits, reopen_flags, matched_queries, query_cotan, mask_cotan,
    query_weight, query_bias, keyval_weight, value_bias, cross_out, cross_out_bias, norm_gain, norm_bias,
    self_weight, self_bias, self_out, self_out_bias, hidden_weight, hidden_bias, hidden_out, hidden_out_bias,
    embed_weight, embed_bias, *, n_pix, n_batch,
):
    images, count, width = queries.shape
    hidden = hidden_weight.shape[1]
    rows = up(count, 8)
    tall = rows + HEADS
    pix = lax.axis_index("pix")
    direct = n_pix == 4 and n_batch == 8

    queries = jnp.transpose(queries, (1, 0, 2)).reshape(count * images, width)
    query_cotan = jnp.transpose(query_cotan, (1, 0, 2))
    mask_cotan = jnp.transpose(mask_cotan, (1, 0, 2))
    bits = jnp.transpose(attend_bits, (0, 2, 1))

    e, kv, pay, cq = attend(
        queries, features, bits, reopen_flags, mask_cotan, mask_features, query_weight, query_bias, keyval_weight,
        value_bias)
    full = pay.shape[1]
    core = lax.axis_index("batch") % 2
    if direct:
        me = jnp.stack([pix, pix, core]).astype(jnp.int32)
        shares = pay.reshape((n_pix, images // n_pix, full, width))
        att = gather_in(combine(scatter_out(shares, "pix", n_pix), rows), "pix", n_pix)
    else:
        me = jnp.stack([0 * pix, pix, core]).astype(jnp.int32)
        top = lax.pmax(pay[:, rows:tall, :128], "pix")
        ratio = jnp.exp(pay[:, rows:tall, :128] - top)

        def widen(x):
            return jnp.repeat(jnp.transpose(x, (0, 2, 1))[:, :rows], width // HEADS, axis=2)

        numer, total, es = lax.psum(
            (pay[:, :rows] * widen(ratio), pay[:, rows:tall, 128:] * ratio, pay[:, tall:]), "pix")
        att = (jnp.concatenate([numer / widen(total), jnp.concatenate([top, total], 2), es], 1),)

    weights = (
        cross_out, cross_out_bias[None], norm_gain, norm_bias, self_weight, self_bias, self_out, self_out_bias[None],
        hidden_weight, hidden_bias[None], hidden_out, hidden_out_bias[None], embed_weight, embed_bias,
    )
    x3, emb, dn, dt, dp1, mine, away = chain(
        me, att, pay, queries, matched_queries, query_cotan, weights, n_pix)

    def unflat(x):
        return jnp.transpose(x.reshape(count, images, -1), (1, 0, 2))

    blocks = mask_features.shape[1] // 256
    mask = functools.partial(mask_out, emb, matched_queries, mask_cotan, mask_features, count, blocks)
    backward = functools.partial(attend_back, e, kv, features, cq, dn, dt, keyval_weight)
    half = images // 2
    other = swap(away, "batch", n_batch, 1)
    if direct:
        back = backward((0, half))
        other, back = beside(other, back)
        own, other = halve(mine + other, "batch", n_batch, 2)
        back = backward((half, images), back)
        other, back = beside(other, back)
        feat_grad, qp, g_kv = back
        own, other = halve(own + other, "batch", n_batch, 4)
        parts = scatter_out(qp.reshape((n_pix, images // n_pix, rows, width)), "pix", n_pix)
        kv_parts = scatter_out(g_kv.reshape((n_pix, -1, width)), "pix", n_pix)
        outs = mask((0, 5))
        other, parts, kv_parts, outs = beside(other, parts, kv_parts, outs)
        own = own + other
        other = swap(own, "batch", n_batch, 4)
        parts = gather_in(query_sum(parts), "pix", n_pix)
        outs = mask((5, 9), outs)
        other, parts, outs = beside(other, parts, outs)
        own = join(own, other, "batch", 4)
        other = swap(own, "batch", n_batch, 2)
        queries_grad, g_q = query_back(me, parts, queries, dp1, query_weight)
        g_q = lax.dynamic_index_in_dim(g_q.reshape(n_pix, -1, width), pix, 0, keepdims=False)
        tail = jnp.concatenate([functools.reduce(jnp.add, kv_parts), g_q], 0)
        tail, tail2 = halve(tail, "batch", n_batch, 1)
        outs = mask((9, 12), outs)
        other, tail2, outs = beside(other, tail2, outs)
        own = join(own, other, "batch", 2)
        low, high = own[:own.shape[0] // 2], own[own.shape[0] // 2:]
        low2, high2 = swap(low, "pix", n_pix, 1), swap(high, "pix", n_pix, 2)
        tail = tail + tail2
        tail2 = swap(tail, "batch", n_batch, 2)
        outs = mask((12, 16), outs)
        low2, high2, tail2, outs = beside(low2, high2, tail2, outs)
        low, high = jnp.concatenate([low, low2], 0), jnp.concatenate([high, high2], 0)
        pieces = (low, high, swap(low, "pix", n_pix, 2), swap(high, "pix", n_pix, 1))
        tail = tail + tail2
        tail = tail + swap(tail, "batch", n_batch, 4)
        tail = jnp.concatenate([tail] + [swap(tail, "pix", n_pix, k) for k in (1, 2, 3)], 0)
        pieces += tuple(swap(p, "batch", n_batch, 1) for p in pieces)
        tails = (tail, swap(tail, "batch", n_batch, 1))
        grads = unpack(me, pieces, tails, g_kv.shape[0] // n_pix, width, hidden)
        (d_query, d_query_bias, d_keyval, d_value_bias, d_cross, d_cross_bias, d_gain, d_nbias, d_self, d_self_bias,
         d_selfout, d_selfout_bias, d_hidden, d_hidden_bias, d_hidout, d_hidout_bias, d_embed, d_embed_bias) = grads
    else:
        feat_grad, qp, g_kv = backward((0, images))
        outs = mask((0, blocks))
        queries_grad, g_q = query_back(me, (lax.psum(qp, "pix"),), queries, dp1, query_weight)
        g_q = lax.psum(g_q, "batch")
        g_kv = lax.psum(g_kv, ("batch", "pix"))
        every = [(2 * z, 2 * z + 1) for z in range(n_batch // 2)]
        groups = [[z[c] for z in every] for c in range(2)]
        part = lax.psum(mine + other, "batch", axis_index_groups=groups)
        both = lax.all_gather(part, "batch", axis_index_groups=[list(z) for z in every])
        packed = lax.all_gather(both, "pix").reshape(-1, width)

        def tile(t, k=1):
            return packed[t * width:(t + k) * width]

        def wide(t, k):
            return jnp.concatenate([tile(t + j) for j in range(k)], 1)

        many = hidden // width
        bias = packed[(T_HIDDEN + 2 * many) * width:]
        d_query, d_query_bias = g_q[:width], g_q[width]
        d_keyval, d_value_bias = jnp.concatenate([g_kv[:width], g_kv[width:2 * width]], 1), g_kv[2 * width]
        d_cross, d_cross_bias, d_gain, d_nbias = tile(T_CROSS), bias[0], bias[1:4], bias[4:7]
        d_self, d_self_bias, d_selfout, d_selfout_bias = wide(T_SELF, 3), bias[20:22], tile(T_SELFOUT), bias[7]
        d_hidden, d_hidden_bias = wide(T_HIDDEN, many), bias[8:8 + many]
        d_hidout, d_hidout_bias = tile(T_HIDDEN + many, many), bias[16]
        d_embed, d_embed_bias = tile(T_EMBED, 3), bias[17:20]
    logits, mask_grad = outs
    return (
        unflat(x3),
        unflat(logits),
        unflat(queries_grad),
        feat_grad,
        mask_grad,
        d_query,
        d_query_bias.reshape(-1),
        d_keyval,
        d_value_bias.reshape(-1),
        d_cross,
        d_cross_bias.reshape(-1),
        d_gain,
        d_nbias,
        d_self,
        d_self_bias,
        d_selfout,
        d_selfout_bias.reshape(-1),
        d_hidden,
        d_hidden_bias.reshape(-1),
        d_hidout,
        d_hidout_bias.reshape(-1),
        d_embed.reshape(3, width, width),
        d_embed_bias,
    )


def solution(mesh):
    n_pix, n_batch = mesh.shape["pix"], mesh.shape["batch"]
    rep = P()
    row, pixel, column = P("batch", None, None), P("batch", "pix", None), P("batch", None, "pix")
    in_specs = (row, pixel, pixel, column, P("batch", None), P("batch", None), row, column) + (rep,) * 18
    out_specs = (row, column, row, pixel, pixel) + (rep,) * 18
    body = functools.partial(local, n_pix=n_pix, n_batch=n_batch)
    return jax.shard_map(body, mesh=mesh, in_specs=in_specs, out_specs=out_specs, check_vma=False)
```

```python
import functools
import math

import jax
import jax.numpy as jnp
from jax import lax
from jax.experimental import pallas as pl
from jax.experimental.pallas import tpu as pltpu
from jax.sharding import PartitionSpec as P

HEADS = 8
EPS = 1e-05
PENALTY = 10000.0
F32 = jnp.float32
LOW = jnp.bfloat16
HIGH = lax.Precision.HIGHEST
CURVE = math.sqrt(2.0 / math.pi)
CUBE = 0.044715
MIB = 1 << 20
PARTS = 4

T_CROSS, T_SELF, T_SELFOUT, T_EMBED, T_HIDDEN = 0, 1, 4, 5, 8


def up(n, m):
    return (n + m - 1) // m * m


def nn(a, b, precision=None):
    return lax.dot_general(a, b, (((1,), (0,)), ((), ())), precision=precision, preferred_element_type=F32)


def nt(a, b, precision=None):
    return lax.dot_general(a, b, (((1,), (1,)), ((), ())), precision=precision, preferred_element_type=F32)


def tn(a, b, precision=None):
    return lax.dot_general(a, b, (((0,), (0,)), ((), ())), precision=precision, preferred_element_type=F32)


def head_mask(width):
    shape = (HEADS, 1, width)
    head = width // HEADS
    return lax.broadcasted_iota(jnp.int32, shape, 2) // head == lax.broadcasted_iota(jnp.int32, shape, 0)


def spread(x, mask):
    rows, width = x.shape
    return jnp.where(mask, x[None], 0.0).reshape(HEADS * rows, width)


def gather_heads(x, mask):
    total, width = x.shape
    return jnp.sum(jnp.where(mask, x.reshape(HEADS, total // HEADS, width), 0.0), 0)


def spread_low(x, mask):
    return spread(x, mask).astype(LOW)


def head_onehot(width, lanes, transposed=False):
    head = width // HEADS
    if transposed:
        shape, a, b = (width, lanes), 0, 1
    else:
        shape, a, b = (lanes, width), 1, 0
    hit = lax.broadcasted_iota(jnp.int32, shape, a) // head == lax.broadcasted_iota(jnp.int32, shape, b)
    return hit.astype(F32)


def slabs_in(scr, value):
    for t in range(scr.shape[0]):
        scr[t] = value[:, t * 128:(t + 1) * 128]


def take_image(scr, image, count, images):
    rows = pl.ds(image, count, images)
    return jnp.concatenate([scr[t, rows, :] for t in range(scr.shape[0])], 1)


def put_image(scr, image, count, images, value):
    for t in range(scr.shape[0]):
        scr[t, pl.ds(image, count, images), :] = value[:, t * 128:(t + 1) * 128]


def slabs(rows, columns):
    return pltpu.VMEM((columns // 128, rows, 128), F32)


def cost(flops, nbytes, trans=0):
    return pl.CostEstimate(flops=int(flops), bytes_accessed=int(nbytes), transcendentals=int(trans))


def whole(x):
    shape = x.shape
    return pl.BlockSpec(shape, lambda *_: (0,) * len(shape))


def params(mib):
    return pltpu.CompilerParams(vmem_limit_bytes=mib * MIB, dimension_semantics=("arbitrary",))


def pair_rows(x, pair):
    width = x.shape[1]
    head = width // HEADS
    at = 2 * pair * head // 128 * 128
    col = lax.broadcasted_iota(jnp.int32, (1, 128), 1) + at
    part = x[:, at:at + 128]
    return jnp.concatenate([jnp.where(col // head == 2 * pair + k, part, 0.0) for k in range(2)], 0)


def pair_turned(both, pair, head):
    at = 2 * pair * head % 128
    return jnp.transpose(both)[at:at + 2 * head].astype(LOW)


def heads_back(parts, rows, head):
    per = 128 // (2 * head)
    out = []
    for at in range(0, len(parts), per):
        turned = jnp.transpose(jnp.concatenate(parts[at:at + per], 0))
        first = lax.broadcasted_iota(jnp.int32, (rows, 128), 1) % (2 * head) < head
        out.append(jnp.where(first, turned[0:rows], turned[rows:2 * rows]))
    return jnp.concatenate(out, 1)


def attend_kernel(key, me_ref, q_ref, f_ref, bits_ref, flag_ref, mc_ref, mf_ref, wq_ref, bq_ref, wkv_ref, vb_ref, elo_ref,
                  ehi_ref, e_ref, kv_ref, pay_ref, cq_ref, q_scr, w_scr, all_scr, wq_scr, vb_scr):
    i = pl.program_id(0)
    images = flag_ref.shape[0]
    matched = mc_ref.shape[1]
    image = (me_ref[0] ^ key) * f_ref.shape[0] * pl.num_programs(0) + i
    width = q_ref.shape[1]
    count = q_ref.shape[0] // images
    rows = q_scr.shape[0]
    pixels = f_ref.shape[1]
    tall = rows + HEADS
    head = width // HEADS

    @pl.when(i == 0)
    def _():
        q_scr[...] = jnp.zeros_like(q_scr)
        w_scr[...] = jnp.zeros_like(w_scr)
        slabs_in(all_scr, q_ref[...])
        wq_scr[...] = wq_ref[...].astype(LOW)
        vb_scr[...] = jnp.transpose(jnp.broadcast_to(vb_ref[...], (128, width)))

    pay_ref[0, tall:] = jnp.zeros((pay_ref.shape[1] - tall, width), F32)
    pay_ref[0, tall:tall + matched] = nn(mc_ref[0], mf_ref[0])

    q_scr[0:count] = take_image(all_scr, image, count, images)
    w_scr[:, 0:count] = jnp.where(flag_ref[pl.ds(image, 1), :] > 0, 65535, bits_ref[0])

    scale = 1.0 / math.sqrt(head)
    cq = ((nn(q_scr[...].astype(LOW), wq_scr[...]) + bq_ref[...]) * scale).astype(LOW).astype(F32)
    cq_ref[0] = cq

    bits = w_scr[...]
    low = (bits & 255).astype(F32).astype(LOW)
    high = (bits >> 8).astype(F32).astype(LOW)
    byte = (tn(low, elo_ref[...]) + tn(high, ehi_ref[...])).astype(jnp.int32)
    shift = lax.broadcasted_iota(jnp.int32, (rows, pixels), 1) & 7
    pen = jnp.where(((byte >> shift) & 1) == 1, 0.0, -PENALTY)

    keyval = nt(wkv_ref[...], f_ref[0])
    ck = keyval[:width].astype(LOW)
    cv = (keyval[width:] + jnp.concatenate([vb_scr[...]] * (pixels // 128), 1)).astype(LOW)
    kv_ref[0, :width] = ck
    kv_ref[0, width:] = cv

    def scores(p):
        at = 2 * p * head // 128 * 128
        s = nn(pair_rows(cq, p).astype(LOW), ck[at:at + 128])
        return (s.reshape(2, rows, pixels) + pen[None]).reshape(2 * rows, pixels)

    lane = lax.broadcasted_iota(jnp.int32, (rows, 128), 1)
    stats = jnp.zeros((rows, 128), F32)
    parts = []
    following = scores(0)
    for p in range(HEADS // 2):
        s = following
        if p + 1 < HEADS // 2:
            following = scores(p + 1)
        m = jnp.max(s, -1, keepdims=True)
        e = jnp.exp(s - m)
        total = jnp.sum(e, -1, keepdims=True)
        e_low = e.astype(LOW)
        e_ref[0, p] = e_low
        parts.append(nt(cv[2 * p * head:2 * (p + 1) * head], e_low))
        for k in range(2):
            stats = jnp.where(lane == 2 * p + k, m[k * rows:(k + 1) * rows], stats)
            stats = jnp.where(lane == HEADS + 2 * p + k, total[k * rows:(k + 1) * rows], stats)
    pay_ref[0, 0:rows] = heads_back(parts, rows, head)
    full = jnp.concatenate([stats, jnp.ones((128 - rows, 128), F32)], 0)
    turned = jnp.transpose(full)
    pay_ref[0, rows:tall, 0:128] = turned[0:HEADS]
    pay_ref[0, rows:tall, 128:256] = turned[HEADS:2 * HEADS]


def attend(key, me, queries, features, bits, reopen_flags, mask_cotan, mask_features, query_weight, query_bias,
           keyval_turned, value_bias, parts):
    images, pixels, width = features.shape
    words, count = bits.shape[1:]
    rows = up(count, 8)
    matched, wide = mask_cotan.shape[1:]
    tall = rows + HEADS + up(matched, 8)
    pixel = jnp.arange(pixels)
    word = jnp.arange(words)
    here = pixel[None, :] // 16 == word[:, None]
    e_lo = (here & (pixel[None, :] % 16 < 8)).astype(LOW)
    e_hi = (here & (pixel[None, :] % 16 >= 8)).astype(LOW)
    n = images // parts
    theirs = lambda *shape: pl.BlockSpec((1,) + shape, lambda i, me: ((me[0] ^ key) * n + i,) + (0,) * len(shape))
    per = lambda *shape: pl.BlockSpec((1,) + shape, lambda i, me: (i,) + (0,) * len(shape))
    args = (queries, features, bits, reopen_flags, mask_cotan, mask_features, query_weight, query_bias[None],
            keyval_turned, value_bias[None], e_lo, e_hi)
    in_specs = [whole(a) for a in args]
    in_specs[1] = theirs(pixels, width)
    in_specs[2] = theirs(words, count)
    in_specs[4] = theirs(matched, wide)
    in_specs[5] = theirs(wide, width)
    flops = 2 * n * (pixels * width * 2 * width + 2 * HEADS * rows * pixels * width + 64 * wide * width)
    nbytes = n * (pixels * width * 6 + HEADS * rows * pixels * 2 + wide * (width + matched) * 2)
    return pl.pallas_call(
        functools.partial(attend_kernel, key),
        grid_spec=pltpu.PrefetchScalarGridSpec(
            num_scalar_prefetch=1,
            grid=(n,),
            in_specs=in_specs,
            out_specs=(per(HEADS // 2, 2 * rows, pixels), per(2 * width, pixels), per(tall, width), per(rows, width)),
            scratch_shapes=[
                pltpu.VMEM((rows, width), F32),
                pltpu.VMEM((words, rows), jnp.int32),
                slabs(count * images, width),
                pltpu.VMEM((width, width), LOW),
                pltpu.VMEM((width, 128), F32),
            ],
        ),
        out_shape=(
            jax.ShapeDtypeStruct((n, HEADS // 2, 2 * rows, pixels), LOW),
            jax.ShapeDtypeStruct((n, 2 * width, pixels), LOW),
            jax.ShapeDtypeStruct((n, tall, width), F32),
            jax.ShapeDtypeStruct((n, rows, width), F32),
        ),
        compiler_params=params(60),
        cost_estimate=cost(flops, nbytes, n * HEADS * rows * pixels),
        name="attend",
    )(me, *args)


def combine_kernel(rows, *refs):
    parts, out_ref = refs[:-1], refs[-1]
    images, full, width = out_ref.shape
    tall = rows + HEADS
    onehot = head_onehot(width, HEADS)
    for i in range(images):
        ms = [p[i, rows:tall, 0:128] for p in parts]
        ls = [p[i, rows:tall, 128:256] for p in parts]
        top = functools.reduce(jnp.maximum, ms)
        rs = [jnp.exp(m - top) for m in ms]
        total = sum(r * l for r, l in zip(rs, ls))
        acc = jnp.zeros((rows, width), F32)
        es = jnp.zeros((full - tall, width), F32)
        for p, r in zip(parts, rs):
            acc = acc + p[i, 0:rows] * tn(r / total, onehot, HIGH)[0:rows]
            es = es + p[i, tall:]
        out_ref[i, 0:rows] = acc
        out_ref[i, rows:tall, 0:128] = top
        out_ref[i, rows:tall, 128:256] = total
        out_ref[i, tall:] = es


def combine(parts, rows):
    shape = parts[0].shape
    return pl.pallas_call(
        functools.partial(combine_kernel, rows),
        out_shape=jax.ShapeDtypeStruct(shape, F32),
        compiler_params=pltpu.CompilerParams(vmem_limit_bytes=32 * MIB),
        cost_estimate=cost(1e6, 5 * 4 * math.prod(shape)),
        name="combine",
    )(*parts)


def lower_kernel(*refs):
    n = len(refs) // 2
    for raw, out in zip(refs[:n], refs[n:]):
        out[...] = raw[...].astype(LOW)


def lower(weights):
    out_shape = tuple(jax.ShapeDtypeStruct(w.shape, LOW) for w in weights)
    size = sum(math.prod(w.shape) for w in weights)
    return pl.pallas_call(
        lower_kernel,
        out_shape=out_shape,
        compiler_params=pltpu.CompilerParams(vmem_limit_bytes=60 * MIB),
        cost_estimate=cost(size, 6 * size),
        name="lower",
    )(*weights)


def norm_forward(x, gain, bias):
    centre = x - jnp.mean(x, -1, keepdims=True)
    inverse = lax.rsqrt(jnp.mean(centre * centre, -1, keepdims=True) + EPS)
    normed = centre * inverse
    return normed * gain + bias, normed, inverse


def norm_backward(normed, inverse, gain, grad):
    dnormed = grad * gain
    return inverse * (
        dnormed - jnp.mean(dnormed, -1, keepdims=True) - normed * jnp.mean(dnormed * normed, -1, keepdims=True)
    )


def gelu_pair(x):
    square = x * x
    t = jnp.tanh(x * (CURVE + (CURVE * CUBE) * square))
    half = 0.5 + 0.5 * t
    slope = half + (0.5 * x) * (1.0 - t * t) * (CURVE + (3.0 * CURVE * CUBE) * square)
    return x * half, slope


def column_sum(x):
    return jnp.sum(x, 0, keepdims=True)


def chain_kernel(
    pieces, me_ref, *refs
):
    att_parts, refs = refs[:pieces], refs[pieces:]
    locals_, refs = refs[:PARTS], refs[PARTS:]
    chain_body(me_ref, att_parts, locals_, *refs)


def chain_body(
    me_ref, att_parts, locals_, q_ref, match_ref, cot_ref, wc_ref, bc_ref, gain_ref, nbias_ref, ws_ref, bs_ref, wso_ref,
    bso_ref, wh_ref, bh_ref, who_ref, bho_ref, we_ref, be_ref,
    x3_ref, emb_ref, dn_ref, dt_ref, dp1_ref, mine_ref, away_ref,
    g_ref, all_scr, cot_scr, out_scr, att_scr, emb_scr, loc_scr,
    q_scr, sq_scr, sk_scr, sv_scr, so_scr, pr_scr, h_scr, gp_scr, dso_scr, dm_scr
):
    step = pl.program_id(0)
    batch, rows, width = dn_ref.shape
    matched = match_ref.shape[1]
    count, images = cot_ref.shape[:2]
    tall = rows + HEADS
    flat = batch * rows
    hidden = wh_ref.shape[1]
    scale = 1.0 / math.sqrt(width // HEADS)
    hm = head_mask(width)

    @pl.when(step == 0)
    def _():
        q_scr[...] = jnp.zeros_like(q_scr)
        g_ref[...] = jnp.zeros_like(g_ref)
        n = att_parts[0].shape[0]
        for k, part in enumerate(att_parts):
            att_scr[pl.ds((me_ref[0] ^ k) * n, n)] = part[...]
        n = locals_[0].shape[0]
        for k, part in enumerate(locals_):
            loc_scr[pl.ds((me_ref[0] ^ k) * n, n)] = part[:, rows:tall]
        slabs_in(all_scr, q_ref[...])
        slabs_in(cot_scr, cot_ref[...].astype(F32).reshape(count * images, width))

    def put(tile, value):
        g_ref[tile * width:(tile + 1) * width] += value

    bias_at = (T_HIDDEN + 2 * (hidden // width)) * width

    def put_bias(index, value):
        g_ref[bias_at + index:bias_at + index + 1] += value

    first = step * batch
    for b in range(batch):
        q_scr[b, 0:count] = take_image(all_scr, first + b, count, images)
    att = att_scr[pl.ds(first, batch), 0:rows].reshape(flat, width)
    att_low = att.astype(LOW)
    queries = q_scr[...].reshape(flat, width)
    x1, n1, i1 = norm_forward(queries + nn(att_low, wc_ref[...]) + bc_ref[...], gain_ref[0:1], nbias_ref[0:1])
    x1_low = x1.astype(LOW)
    mixed = nn(x1_low, ws_ref[...])
    three = (batch, rows, width)
    sq_scr[...] = ((mixed[:, :width] + bs_ref[0:1]) * scale).reshape(three)
    sk_scr[...] = mixed[:, width:2 * width].reshape(three)
    sv_scr[...] = (mixed[:, 2 * width:] + bs_ref[1:2]).reshape(three)

    head = width // HEADS
    lanes = lambda h: slice(h * 128, (h + 1) * 128)
    fill = jnp.zeros((128 - rows, width), F32)

    def tall_heads(x):
        return spread_low(jnp.concatenate([x, fill], 0), hm)

    def turn(x):
        return jnp.transpose(jnp.concatenate([x, fill], 0))[:, 0:rows].astype(LOW)

    def by_head(turned, x):
        return jnp.transpose(jnp.concatenate(
            [nn(turned[h * head:(h + 1) * head], x[:, lanes(h)]) for h in range(HEADS)], 0))[0:rows]

    for b in range(batch):
        ss = nt(sk_scr[b].astype(LOW), tall_heads(sq_scr[b]))
        keys = lax.broadcasted_iota(jnp.int32, ss.shape, 0)
        ss = jnp.where(keys < count, ss, -1e30)
        p = jnp.exp(ss - jnp.max(ss, 0, keepdims=True))
        p = p * (1.0 / jnp.sum(p, 0, keepdims=True))
        pr_scr[b] = p
        so_scr[b] = by_head(turn(sv_scr[b]), p.astype(LOW))
    so_low = so_scr[...].reshape(flat, width).astype(LOW)
    x2, n2, i2 = norm_forward(x1 + nn(so_low, wso_ref[...]) + bso_ref[...], gain_ref[1:2], nbias_ref[1:2])
    x2_low = x2.astype(LOW)
    block = 2 * width

    def ff_forward(j, acc):
        cols = pl.ds(pl.multiple_of(j * block, block), block)
        h, slope = gelu_pair(nn(x2_low, wh_ref[:, cols]) + bh_ref[:, cols])
        h = h.astype(LOW)
        h_scr[:, cols] = h
        gp_scr[:, cols] = slope.astype(gp_scr.dtype)
        return acc + nn(h, who_ref[cols, :])

    ff = lax.fori_loop(0, hidden // block, ff_forward, jnp.zeros((flat, width), F32))
    x3, n3, i3 = norm_forward(x2 + ff + bho_ref[...], gain_ref[2:3], nbias_ref[2:3])
    for b in range(batch):
        put_image(out_scr, first + b, count, images, x3[b * rows:b * rows + count])

    x3_low = x3.astype(LOW)
    h1, slope1 = gelu_pair(nn(x3_low, we_ref[0]) + be_ref[0:1])
    h1 = h1.astype(LOW)
    h2, slope2 = gelu_pair(nn(h1, we_ref[1]) + be_ref[1:2])
    h2 = h2.astype(LOW)
    emb = nn(h2, we_ref[2]) + be_ref[2:3]
    for b in range(batch):
        put_image(emb_scr, first + b, count, images, emb[b * rows:b * rows + count])

    grads = []
    for b in range(batch):
        spots = match_ref[pl.ds(first + b, 1), :]
        pick = (lax.broadcasted_iota(jnp.int32, (rows, matched), 0) == spots).astype(F32).astype(LOW)
        grads.append(nn(pick, att_scr[first + b, tall:tall + matched].astype(LOW)))
    dz3 = jnp.concatenate(grads, 0)
    dz3_low = dz3.astype(LOW)
    put(T_EMBED + 2, tn(h2, dz3_low))
    put_bias(19, column_sum(dz3_low.astype(F32)))
    dz2 = (nt(dz3_low, we_ref[2]) * slope2).astype(LOW)
    put(T_EMBED + 1, tn(h1, dz2))
    put_bias(18, column_sum(dz2.astype(F32)))
    dz1 = (nt(dz2, we_ref[1]) * slope1).astype(LOW)
    put(T_EMBED, tn(x3_low, dz1))
    put_bias(17, column_sum(dz1.astype(F32)))
    for b in range(batch):
        q_scr[b, 0:count] = take_image(cot_scr, first + b, count, images)
    dx3 = q_scr[...].reshape(flat, width) + nt(dz1, we_ref[0])
    put_bias(3, column_sum(dx3 * n3))
    put_bias(6, column_sum(dx3))
    dp3 = norm_backward(n3, i3, gain_ref[2:3], dx3)
    dff = dp3.astype(LOW)
    put_bias(16, column_sum(dff.astype(F32)))

    def ff_backward(j, acc):
        cols = pl.ds(pl.multiple_of(j * block, block), block)
        base = (T_HIDDEN + hidden // width) * width
        spot = pl.ds(pl.multiple_of(base + j * block, block), block)
        g_ref[spot] += tn(h_scr[:, cols], dff)
        dz = (nt(dff, who_ref[cols, :]) * gp_scr[:, cols].astype(F32)).astype(LOW)
        gh = tn(x2_low, dz)
        sums = column_sum(dz.astype(F32))
        for t in range(block // width):
            tile = pl.ds(pl.multiple_of(T_HIDDEN * width + j * block + t * width, width), width)
            g_ref[tile] += gh[:, t * width:(t + 1) * width]
            g_ref[pl.ds(bias_at + 8 + j * (block // width) + t, 1)] += sums[:, t * width:(t + 1) * width]
        return acc + nt(dz, wh_ref[:, cols])

    dx2 = dp3 + lax.fori_loop(0, hidden // block, ff_backward, jnp.zeros((flat, width), F32))
    put_bias(2, column_sum(dx2 * n2))
    put_bias(5, column_sum(dx2))
    dp2 = norm_backward(n2, i2, gain_ref[1:2], dx2)
    dsa = dp2.astype(LOW)
    put(T_SELFOUT, tn(so_low, dsa))
    put_bias(7, column_sum(dsa.astype(F32)))
    dso_scr[...] = nt(dsa, wso_ref[...]).reshape(three)

    for b in range(batch):
        dsox = tall_heads(dso_scr[b])
        p = pr_scr[b]
        dp = nt(sv_scr[b].astype(LOW), dsox)
        dss = (p * (dp - jnp.sum(p * dp, 0, keepdims=True))).astype(LOW)
        dm_scr[b, :, 0:width] = by_head(turn(sk_scr[b]), dss) * scale
        dm_scr[b, :, width:2 * width] = nn(dss, tall_heads(sq_scr[b]))
        dm_scr[b, :, 2 * width:] = nn(p.astype(LOW), dsox)

    dm = dm_scr[...].reshape(flat, 3 * width).astype(LOW)
    gs = tn(x1_low, dm)
    for t in range(3):
        put(T_SELF + t, gs[:, t * width:(t + 1) * width])
    put_bias(20, column_sum(dm[:, :width].astype(F32)))
    put_bias(21, column_sum(dm[:, 2 * width:].astype(F32)))
    dx1 = dp2 + nt(dm, ws_ref[...])
    put_bias(1, column_sum(dx1 * n1))
    put_bias(4, column_sum(dx1))
    dp1 = norm_backward(n1, i1, gain_ref[0:1], dx1)
    dp1_ref[...] = dp1.reshape(three)
    dca = dp1.astype(LOW)
    put(T_CROSS, tn(att_low, dca))
    put_bias(0, column_sum(dca.astype(F32)))
    d_att = nt(dca, wc_ref[...]).reshape(three)
    onehot = head_onehot(width, HEADS)
    back = head_onehot(width, 128, True)
    for b in range(batch):
        top = att_scr[first + b, rows:tall, 0:128]
        total = att_scr[first + b, rows:tall, 128:256]
        ratio = jnp.exp(loc_scr[first + b, :, 0:128] - top) / total
        dn = d_att[b] * tn(ratio, onehot, HIGH)[0:rows]
        dn_ref[b] = dn
        dt_ref[b] = -nn(dn * att_scr[first + b, 0:rows], back, HIGH)

    @pl.when(step == 1)
    def _():
        x3_ref[...] = jnp.concatenate([out_scr[t] for t in range(out_scr.shape[0])], 1)
        emb_ref[...] = jnp.concatenate([emb_scr[t] for t in range(emb_scr.shape[0])], 1)
        share = mine_ref.shape[0]
        at = me_ref[1] * 2 + me_ref[2]
        mine_ref[...] = g_ref[pl.ds(pl.multiple_of(at * share, 8), share)]
        away_ref[...] = g_ref[pl.ds(pl.multiple_of((at + 1 - 2 * me_ref[2]) * share, 8), share)]


def chain(me, parts, pays, queries, matched, query_cotan, weights, n_pix):
    full, width = pays[0].shape[1:]
    images = pays[0].shape[0] * len(pays)
    count = query_cotan.shape[0]
    rows = up(count, 8)
    batch = images // 2
    hidden = weights[8].shape[1]
    tiles = T_HIDDEN + 2 * (hidden // width)
    grads = up(tiles * width + 22, 256)
    half = lambda *shape: pl.BlockSpec((batch,) + shape, lambda i, *_: (i,) + (0,) * len(shape))
    pieces = len(parts)
    args = tuple(parts) + tuple(pays) + (queries, matched, query_cotan) + weights
    in_specs = [whole(a) for a in args]
    out_shape = (
        jax.ShapeDtypeStruct((count * images, width), F32),
        jax.ShapeDtypeStruct((count * images, width), F32),
        jax.ShapeDtypeStruct((images, rows, width), F32),
        jax.ShapeDtypeStruct((images, rows, 128), F32),
        jax.ShapeDtypeStruct((images, rows, width), F32),
        jax.ShapeDtypeStruct((grads // n_pix // 2, width), F32),
        jax.ShapeDtypeStruct((grads // n_pix // 2, width), F32),
    )
    flat = batch * rows
    three = (batch, rows, width)
    many = slabs(count * images, width)
    return pl.pallas_call(
        functools.partial(chain_kernel, pieces),
        grid_spec=pltpu.PrefetchScalarGridSpec(
            num_scalar_prefetch=1,
            grid=(2,),
            in_specs=in_specs,
            out_specs=(whole(out_shape[0]), whole(out_shape[1]), half(rows, width), half(rows, 128), half(rows, width),
                       whole(out_shape[5]), whole(out_shape[6])),
            scratch_shapes=[
                pltpu.VMEM((grads, width), F32),
                many,
                many,
                many,
                pltpu.VMEM((images, full, width), F32),
                many,
                pltpu.VMEM((images, HEADS, width), F32),
                pltpu.VMEM(three, F32),
                pltpu.VMEM(three, F32),
                pltpu.VMEM(three, F32),
                pltpu.VMEM(three, F32),
                pltpu.VMEM(three, F32),
                pltpu.VMEM((batch, rows, HEADS * 128), F32),
                pltpu.VMEM((flat, hidden), LOW),
                pltpu.VMEM((flat, hidden), LOW),
                pltpu.VMEM(three, F32),
                pltpu.VMEM((batch, rows, 3 * width), F32),
            ],
        ),
        out_shape=out_shape,
        compiler_params=params(62),
        cost_estimate=cost(2 * 8e9, 20e6, 4e6),
        name="chain",
    )(me, *args)


def mask_out_kernel(emb_ref, match_ref, mc_ref, mf_ref, logit_old, grad_old, logit_ref, grad_ref, chosen_scr,
                    emb_scr, low_scr, logit_scr):
    images, matched, width = chosen_scr.shape
    count = logit_ref.shape[0] // images
    part = mc_ref.shape[2]

    @pl.when(pl.program_id(0) == 0)
    def _():
        slabs_in(emb_scr, emb_ref[...])
        low_scr[...] = jnp.zeros_like(low_scr)
        for b in range(images):
            pick = (lax.broadcasted_iota(jnp.int32, (count, matched), 0) == match_ref[b:b + 1, :]).astype(F32).astype(LOW)
            emb = take_image(emb_scr, b, count, images).astype(LOW)
            low_scr[b, 0:count] = emb.astype(F32)
            chosen_scr[b] = tn(pick, emb)

    for b in range(images):
        put_image(logit_scr, b, count, images, nt(low_scr[b].astype(LOW), mf_ref[b])[0:count])
        grad_ref[b] = tn(mc_ref[b], chosen_scr[b].astype(LOW))
    for t in range(part // 128):
        logit_ref[:, t * 128:(t + 1) * 128] = logit_scr[t]


def mask_out(emb, matched_queries, mask_cotan, mask_features, count, pieces, steps, old=None):
    images, matched, pixels = mask_cotan.shape
    width = emb.shape[1]
    part = pixels // pieces
    first, last = steps
    out_shape = (
        jax.ShapeDtypeStruct((count * images, pixels), F32),
        jax.ShapeDtypeStruct((images, pixels, width), F32),
    )
    args = (emb, matched_queries, mask_cotan, mask_features)
    here = pl.BlockSpec(memory_space=pl.ANY)
    kernel = mask_out_kernel
    aliases = {}
    specs = []
    if old is None:
        def kernel(a, b, c, d, *rest):
            mask_out_kernel(a, b, c, d, None, None, *rest)
    else:
        args += old
        aliases = {4: 0, 5: 1}
        specs = [here, here]
    return pl.pallas_call(
        kernel,
        grid=(last - first,),
        in_specs=[
            whole(emb),
            whole(matched_queries),
            pl.BlockSpec((images, matched, part), lambda j: (0, 0, j + first)),
            pl.BlockSpec((images, part, width), lambda j: (0, j + first, 0)),
        ] + specs,
        out_specs=(
            pl.BlockSpec((count * images, part), lambda j: (0, j + first)),
            pl.BlockSpec((images, part, width), lambda j: (0, j + first, 0)),
        ),
        out_shape=out_shape,
        input_output_aliases=aliases,
        scratch_shapes=[pltpu.VMEM((images, matched, width), F32),
                        slabs(count * images, width), pltpu.VMEM((images, up(count, 8), width), F32),
                        slabs(count * images, part)],
        compiler_params=params(60),
        cost_estimate=cost(
            2 * images * pixels * width * 160 * (last - first) / pieces,
            images * pixels * (width * 6 + count * 4 + matched * 2) * (last - first) / pieces),
        name="mask_out",
    )(*args)


def attend_back_kernel(last, me_ref, e_ref, kv_ref, f_ref, cq_ref, dn_ref, dt_ref, wkv_ref, fg_old, acc_old, vb_old,
                       fg_ref, qp_ref, acc_ref, vb_ref):
    i = pl.program_id(0)
    rows, width = cq_ref.shape[1:]
    pixels = f_ref.shape[1]
    head = width // HEADS
    acc, vb = acc_ref, vb_ref
    if last:
        acc, vb = vb_ref, fg_old

    @pl.when(i == 0)
    def _():
        acc[...] = jnp.zeros_like(acc) if acc_old is None else acc_old[...]
        vb[...] = jnp.zeros_like(vb) if vb_old is None else vb_old[...]

    dn = dn_ref[0]
    cq = cq_ref[0]

    def weigh(p):
        at = 2 * p * head // 128 * 128
        both = pair_rows(dn, p)
        dt = jnp.concatenate([dt_ref[0, :, 2 * p + k:2 * p + k + 1] for k in range(2)], 0)
        return both, nn(both.astype(LOW), kv_ref[0, width + at:width + at + 128]) + dt

    parts, keys, values = [], [], []
    following = weigh(0)
    for p in range(HEADS // 2):
        at = slice(2 * p * head, 2 * (p + 1) * head)
        both, dw = following
        if p + 1 < HEADS // 2:
            following = weigh(p + 1)
        e_low = e_ref[0, p]
        ds = (e_low.astype(F32) * dw).astype(LOW)
        values.append(nn(pair_turned(both, p, head), e_low).astype(LOW))
        keys.append(nn(pair_turned(pair_rows(cq, p), p, head), ds).astype(LOW))
        parts.append(nt(kv_ref[0, at], ds))
    qp_ref[0] = heads_back(parts, rows, head)
    turned = jnp.concatenate(keys + values, 0)
    acc[...] += nn(turned, f_ref[0])
    summed = turned[width:].astype(F32)
    lanes_sum = summed[:, 0:128]
    for t in range(1, pixels // 128):
        lanes_sum = lanes_sum + summed[:, t * 128:(t + 1) * 128]
    vb[...] += lanes_sum
    fg_ref[0] = tn(turned, wkv_ref[...])

    if last:
        @pl.when(i == pl.num_programs(0) - 1)
        def _():
            sums = jnp.sum(jnp.transpose(vb[...]), 0, keepdims=True)
            fill = jnp.zeros((acc_ref.shape[0] - 2 * width - 1, width), F32)
            acc_ref[...] = jnp.concatenate([jnp.transpose(acc[0:width]), jnp.transpose(acc[width:]), sums, fill], 0)


def attend_back(key, me, kept, features, dn, dt, keyval_turned, old, last):
    e, kv, cq = kept
    images, pixels, width = features.shape
    n, rows = cq.shape[:2]
    theirs = lambda *shape: pl.BlockSpec((1,) + shape, lambda i, me: ((me[0] ^ key) * n + i,) + (0,) * len(shape))
    per = lambda *shape: pl.BlockSpec((1,) + shape, lambda i, me: (i,) + (0,) * len(shape))
    tall = HEADS * rows
    flops = 2 * n * (4 * tall * pixels * width + 4 * pixels * width * width)
    nbytes = n * (tall * pixels * 2 + pixels * width * 10)
    sums = (jax.ShapeDtypeStruct((2 * width, width), F32), jax.ShapeDtypeStruct((width, 128), F32))
    out_shape = (
        jax.ShapeDtypeStruct((images, pixels, width), F32),
        jax.ShapeDtypeStruct((n, rows, width), F32),
    )
    scratch = []
    if last:
        out_shape += (jax.ShapeDtypeStruct((2 * width + 32, width), F32),)
        scratch = [pltpu.VMEM(x.shape, F32) for x in sums]
    else:
        out_shape += sums
    args = (e, kv, features, cq, dn, dt, keyval_turned)
    in_specs = [per(HEADS // 2, 2 * rows, pixels), per(2 * width, pixels), theirs(pixels, width), per(rows, width),
                theirs(rows, width), theirs(rows, 128), whole(keyval_turned)]
    aliases = {}

    def kernel(*refs):
        ins, outs = refs[:8], refs[8:]
        olds = (None, None, None)
        if old is not None:
            olds, outs = (None,) + outs[1:3], outs[3:]
        if last:
            fg, qp, g, acc, vb = outs
            attend_back_kernel(True, *ins, vb, *olds[1:], fg, qp, g, acc)
        else:
            attend_back_kernel(False, *ins, *olds, *outs)

    if old is not None:
        args += old
        in_specs += [pl.BlockSpec(memory_space=pl.ANY)] + [whole(x) for x in sums]
        aliases = {8: 0}
    return pl.pallas_call(
        kernel,
        grid_spec=pltpu.PrefetchScalarGridSpec(
            num_scalar_prefetch=1,
            grid=(n,),
            in_specs=in_specs,
            out_specs=(theirs(pixels, width), per(rows, width)) + tuple(whole(x) for x in out_shape[2:]),
            scratch_shapes=scratch,
        ),
        out_shape=out_shape,
        input_output_aliases=aliases,
        compiler_params=params(60),
        cost_estimate=cost(flops, nbytes),
        name="attend_back",
    )(me, *args)


def query_sum_kernel(me_ref, *refs):
    parts, kv_ref, outs = refs[:PARTS], refs[PARTS], refs[PARTS + 1:]
    n, rows, width = parts[0].shape
    total = parts[0][...]
    for p in parts[1:]:
        total = total + p[...]
    total = total.reshape(n * rows, width)
    share = kv_ref.shape[0] // PARTS
    for k, out in enumerate(outs):
        out[0:n * rows] = total
        out[n * rows:] = kv_ref[pl.ds(pl.multiple_of((me_ref[0] ^ k) * share, 8), share)]


def query_sum(me, parts, g_kv):
    n, rows, width = parts[0].shape
    args = tuple(parts) + (g_kv,)
    out = jax.ShapeDtypeStruct((n * rows + g_kv.shape[0] // PARTS, width), F32)
    return pl.pallas_call(
        query_sum_kernel,
        grid_spec=pltpu.PrefetchScalarGridSpec(
            num_scalar_prefetch=1, grid=(1,), in_specs=[whole(a) for a in args], out_specs=(whole(out),) * PARTS),
        out_shape=(out,) * PARTS,
        compiler_params=params(60),
        cost_estimate=cost(1e6, 3e6),
        name="query_sum",
    )(me, *args)


def query_back_kernel(pieces, me_ref, *refs):
    parts = refs[:pieces]
    (q_ref, dp_ref, wq_ref, qg_ref, mine_ref, away_ref, scr, sum_scr, all_scr, out_scr, g_scr, tail_scr) = refs[pieces:]
    images, rows, width = dp_ref.shape
    count = q_ref.shape[0] // images
    scale = 1.0 / math.sqrt(width // HEADS)
    n = images // pieces
    kv = jnp.zeros((parts[0].shape[0] - n * rows, width), F32)
    for k, part in enumerate(parts):
        sum_scr[pl.ds((me_ref[0] ^ k) * n, n)] = part[0:n * rows].reshape(n, rows, width)
        kv = kv + part[n * rows:]
    scr[...] = jnp.zeros_like(scr)
    slabs_in(all_scr, q_ref[...])
    for b in range(images):
        scr[b, 0:count] = take_image(all_scr, b, count, images)
    d_cq = (sum_scr[...].reshape(images * rows, width) * scale).astype(LOW)
    out = dp_ref[...] + nt(d_cq, wq_ref[...].astype(LOW)).reshape(images, rows, width)
    for b in range(images):
        put_image(out_scr, b, count, images, out[b, 0:count])
    qg_ref[...] = jnp.concatenate([out_scr[t] for t in range(out_scr.shape[0])], 1)
    g_scr[0:width] = tn(scr[...].reshape(images * rows, width).astype(LOW), d_cq)
    g_scr[width:] = jnp.zeros((g_scr.shape[0] - width, width), F32)
    g_scr[width:width + 1] = column_sum(d_cq.astype(F32))
    share = g_scr.shape[0] // pieces
    small = mine_ref.shape[0]
    tail_scr[0:kv.shape[0]] = kv
    tail_scr[kv.shape[0]:] = g_scr[pl.ds(pl.multiple_of(me_ref[0] * share, 8), share)]
    mine_ref[...] = tail_scr[pl.ds(pl.multiple_of(me_ref[2] * small, 8), small)]
    away_ref[...] = tail_scr[pl.ds(pl.multiple_of((1 - me_ref[2]) * small, 8), small)]


def query_back(me, parts, queries, dp1, query_weight):
    images, rows, width = dp1.shape
    pieces = len(parts)
    args = tuple(parts) + (queries, dp1, query_weight)
    share = parts[0].shape[0] - images // pieces * rows
    full = (width + 32) // pieces + share
    half = jax.ShapeDtypeStruct((full // 2, width), F32)
    out_shape = (jax.ShapeDtypeStruct(queries.shape, F32), half, half)
    return pl.pallas_call(
        functools.partial(query_back_kernel, pieces),
        grid_spec=pltpu.PrefetchScalarGridSpec(
            num_scalar_prefetch=1,
            grid=(1,),
            in_specs=[whole(a) for a in args],
            out_specs=tuple(whole(o) for o in out_shape),
            scratch_shapes=[pltpu.VMEM((images, rows, width), F32), pltpu.VMEM((images, rows, width), F32),
                            slabs(*queries.shape), slabs(*queries.shape), pltpu.VMEM((width + 32, width), F32),
                            pltpu.VMEM((full, width), F32)],
        ),
        out_shape=out_shape,
        compiler_params=params(60),
        cost_estimate=cost(5e8, 8e6),
        name="query_back",
    )(me, *args)


def unpack_kernel(split, me_ref, *refs):
    (sa, sb, ra, rb, sa2, sb2, ra2, rb2, tail, tail2,
     query_ref, query_bias_ref, keyval_ref, value_bias_ref, cross_ref, cross_bias_ref, gain_ref, nbias_ref,
     self_ref, self_bias_ref, selfout_ref, selfout_bias_ref, hidden_ref, hidden_bias_ref, hidout_ref, hidout_bias_ref,
     embed_ref, embed_bias_ref, g, t) = refs
    pix, core = me_ref[1], me_ref[2]
    width = query_ref.shape[0]
    short = sa.shape[0] // 2

    def place(ref, row, block, half, second):
        at = ((pix ^ block) * 2 + half) * 2 + second
        g[pl.ds(pl.multiple_of(at * short, 8), short)] = ref[row * short:(row + 1) * short]

    for half, four in ((core, (sa, sb, ra, rb)), (1 - core, (sa2, sb2, ra2, rb2))):
        for row in range(2):
            place(four[0], row, (0, 1)[row], half, 0)
            place(four[1], row, (0, 2)[row], half, 1)
            place(four[2], row, (2, 3)[row], half, 0)
            place(four[3], row, (1, 3)[row], half, 1)
    small = tail.shape[0] // 4
    for half, ref in ((core, tail), (1 - core, tail2)):
        for k in range(4):
            at = (pix ^ k) * 2 + half
            t[pl.ds(pl.multiple_of(at * small, 8), small)] = ref[k * small:(k + 1) * small]

    def tile(n, k=1):
        return g[n * width:(n + k) * width]

    many = hidden_ref.shape[1] // width
    bias = (T_HIDDEN + 2 * many) * width
    cross_ref[...] = tile(T_CROSS)
    selfout_ref[...] = tile(T_SELFOUT)
    embed_ref[...] = tile(T_EMBED, 3)
    hidout_ref[...] = tile(T_HIDDEN + many, many)
    for n in range(3):
        self_ref[:, n * width:(n + 1) * width] = tile(T_SELF + n)
    for n in range(many):
        hidden_ref[:, n * width:(n + 1) * width] = tile(T_HIDDEN + n)
        hidden_bias_ref[:, n * width:(n + 1) * width] = g[bias + 8 + n:bias + 9 + n]
    cross_bias_ref[...] = g[bias:bias + 1]
    gain_ref[...] = g[bias + 1:bias + 4]
    nbias_ref[...] = g[bias + 4:bias + 7]
    selfout_bias_ref[...] = g[bias + 7:bias + 8]
    hidout_bias_ref[...] = g[bias + 16:bias + 17]
    embed_bias_ref[...] = g[bias + 17:bias + 20]
    self_bias_ref[...] = g[bias + 20:bias + 22]
    block = 2 * small
    low, high = [], []
    for k in range(4):
        low.append(t[k * block:k * block + split])
        high.append(t[k * block + split:(k + 1) * block])
    low, high = jnp.concatenate(low, 0), jnp.concatenate(high, 0)
    keyval_ref[:, 0:width] = low[0:width]
    keyval_ref[:, width:] = low[width:2 * width]
    value_bias_ref[...] = low[2 * width:2 * width + 1]
    query_ref[...] = high[0:width]
    query_bias_ref[...] = high[width:width + 1]


def unpack(me, pieces, tails, split, width, hidden):
    args = tuple(pieces) + tuple(tails)
    shapes = ((width, width), (1, width), (width, 2 * width), (1, width), (width, width), (1, width), (3, width), (3, width),
              (width, 3 * width), (2, width), (width, width), (1, width), (width, hidden), (1, hidden), (hidden, width),
              (1, width), (3 * width, width), (3, width))
    out_shape = tuple(jax.ShapeDtypeStruct(shape, F32) for shape in shapes)
    rows = sum(p.shape[0] for p in pieces)
    return pl.pallas_call(
        functools.partial(unpack_kernel, split),
        grid_spec=pltpu.PrefetchScalarGridSpec(
            num_scalar_prefetch=1,
            grid=(1,),
            in_specs=[whole(a) for a in args],
            out_specs=tuple(whole(o) for o in out_shape),
            scratch_shapes=[pltpu.VMEM((rows, width), F32), pltpu.VMEM((2 * tails[0].shape[0], width), F32)],
        ),
        out_shape=out_shape,
        compiler_params=params(60),
        cost_estimate=cost(1e6, 16e6),
        name="unpack",
    )(me, *args)


def beside(*values):
    return lax.optimization_barrier(values)


def swap(x, axis, n, key):
    return lax.ppermute(x, axis, [(d, d ^ key) for d in range(n)])


def scatter_out(x, axis, n):
    me = lax.axis_index(axis)
    chunks = [lax.dynamic_index_in_dim(x, me ^ k, 0, keepdims=False) for k in range(n)]
    return tuple(c if k == 0 else swap(c, axis, n, k) for k, c in enumerate(chunks))


def gather_in(x, axis, n):
    return tuple(x if k == 0 else swap(x, axis, n, k) for k in range(n))


def side(axis, key):
    return (lax.axis_index(axis) // key) % 2


def halve(x, axis, n, key):
    halves = x.reshape((2, -1) + x.shape[1:])
    mine = lax.dynamic_index_in_dim(halves, side(axis, key), 0, keepdims=False)
    away = lax.dynamic_index_in_dim(halves, 1 - side(axis, key), 0, keepdims=False)
    return mine, swap(away, axis, n, key)


def join(mine, other, axis, key):
    first = side(axis, key) == 0
    return jnp.concatenate([jnp.where(first, mine, other), jnp.where(first, other, mine)], 0)


def local(
    queries, features, mask_features, attend_bits, reopen_flags, matched_queries, query_cotan, mask_cotan,
    query_weight, query_bias, keyval_weight, value_bias, cross_out, cross_out_bias, norm_gain, norm_bias,
    self_weight, self_bias, self_out, self_out_bias, hidden_weight, hidden_bias, hidden_out, hidden_out_bias,
    embed_weight, embed_bias, *, n_pix, n_batch,
):
    images, count, width = queries.shape
    hidden = hidden_weight.shape[1]
    rows = up(count, 8)
    tall = rows + HEADS
    pix = lax.axis_index("pix")
    direct = n_pix == 4 and n_batch == 8

    queries = jnp.transpose(queries, (1, 0, 2)).reshape(count * images, width)
    query_cotan = jnp.transpose(query_cotan, (1, 0, 2))
    bits = jnp.transpose(attend_bits, (0, 2, 1))
    keyval_turned = jnp.transpose(keyval_weight).astype(LOW)
    core = lax.axis_index("batch") % 2
    me = jnp.stack([pix if direct else 0 * pix, pix, core]).astype(jnp.int32)

    def forward(key, flags):
        return attend(key, me, queries, features, bits, flags, mask_cotan, mask_features, query_weight, query_bias,
                      keyval_turned, value_bias, PARTS)

    order = (3, 1, 2, 0)
    kept, pays, got = {}, {}, {}
    before = None
    for key in order:
        e, kv, pay, cq = forward(key, reopen_flags)
        if before is not None and direct:
            got[before], pay, reopen_flags = beside(got[before], pay, reopen_flags)
        else:
            pay, reopen_flags = beside(pay, reopen_flags)
        kept[key], pays[key] = (e, kv, cq), pay
        if direct:
            got[key] = pay if key == 0 else swap(pay, "pix", n_pix, key)
        before = key
    pays = [pays[k] for k in range(PARTS)]
    weights = (
        cross_out, cross_out_bias[None], norm_gain, norm_bias, self_weight, self_bias, self_out, self_out_bias[None],
        hidden_weight, hidden_bias[None], hidden_out, hidden_out_bias[None], embed_weight, embed_bias,
    )
    large = (0, 4, 6, 8, 10, 12)
    if direct:
        share = combine([got[k] for k in range(PARTS)], rows)
        share, *raw = beside(share, *[weights[k] for k in large])
        att = gather_in(share, "pix", n_pix)
    else:
        raw = [weights[k] for k in large]
        pay = jnp.concatenate(pays, 0)
        top = lax.pmax(pay[:, rows:tall, :128], "pix")
        ratio = jnp.exp(pay[:, rows:tall, :128] - top)

        def widen(x):
            return jnp.repeat(jnp.transpose(x, (0, 2, 1))[:, :rows], width // HEADS, axis=2)

        numer, total, es = lax.psum(
            (pay[:, :rows] * widen(ratio), pay[:, rows:tall, 128:] * ratio, pay[:, tall:]), "pix")
        att = (jnp.concatenate([numer / widen(total), jnp.concatenate([top, total], 2), es], 1),)
    lowered = dict(zip(large, lower(raw)))
    weights = tuple(lowered.get(k, w) for k, w in enumerate(weights))
    x3, emb, dn, dt, dp1, mine, away = chain(
        me, att, pays, queries, matched_queries, query_cotan, weights, n_pix)

    def unflat(x):
        return jnp.transpose(x.reshape(count, images, -1), (1, 0, 2))

    blocks = mask_features.shape[1] // 512
    mask = functools.partial(mask_out, emb, matched_queries, mask_cotan, mask_features, count, blocks)

    def backward(key, dn, old, last=False):
        return attend_back(key, me, kept[key], features, dn, dt, keyval_turned, old, last)

    other = swap(away, "batch", n_batch, 1)
    if direct:
        grads = {}

        def pass_on(key, back, other):
            fg, qp, acc, vb = back
            other, fg, qp, acc, vb = beside(other, fg, qp, acc, vb)
            grads[key] = swap(qp, "pix", n_pix, key)
            return other, (fg, acc, vb)

        other, old = pass_on(3, backward(3, dn, None), other)
        own, other = halve(mine + other, "batch", n_batch, 2)
        other, old = pass_on(1, backward(1, dn, old), other)
        own, other = halve(own + other, "batch", n_batch, 4)
        other, old = pass_on(2, backward(2, dn, old), other)
        own = own + other
        other = swap(own, "batch", n_batch, 4)
        feat_grad, qp, g_kv = backward(0, dn, old, True)
        grads[0] = qp
        other, feat_grad, g_kv, *parts = beside(other, feat_grad, g_kv, *[grads[k] for k in range(n_pix)])
        own = join(own, other, "batch", 4)
        other = swap(own, "batch", n_batch, 2)
        split = g_kv.shape[0] // n_pix
        parts = query_sum(me, parts, g_kv)
        parts = tuple(p if k == 0 else swap(p, "pix", n_pix, k) for k, p in enumerate(parts))
        outs = mask((0, 2))
        other, parts, outs = beside(other, parts, outs)
        own = join(own, other, "batch", 2)
        low, high = own[:own.shape[0] // 2], own[own.shape[0] // 2:]
        low2, high2 = swap(low, "pix", n_pix, 1), swap(high, "pix", n_pix, 2)
        queries_grad, tail, tail2 = query_back(me, parts, queries, dp1, query_weight)
        tail2 = swap(tail2, "batch", n_batch, 1)
        outs = mask((2, 4), outs)
        low2, high2, tail2, outs = beside(low2, high2, tail2, outs)
        low, high = jnp.concatenate([low, low2], 0), jnp.concatenate([high, high2], 0)
        far = [swap(low, "pix", n_pix, 2), swap(high, "pix", n_pix, 1)]
        others = [swap(p, "batch", n_batch, 1) for p in (low, high)]
        tail = tail + tail2
        tail2 = swap(tail, "batch", n_batch, 2)
        outs = mask((4, 6), outs)
        tail2, outs = beside(tail2, outs)
        tail = tail + tail2
        tail2 = swap(tail, "batch", n_batch, 4)
        outs = mask((6, 8), outs)
        tail2, outs, *moved = beside(tail2, outs, *far, *others)
        tail = tail + tail2
        tail = jnp.concatenate([tail] + [swap(tail, "pix", n_pix, k) for k in (1, 2, 3)], 0)
        pieces = [low, high] + moved + [swap(p, "batch", n_batch, 1) for p in moved[:2]]
        tails = (tail, swap(tail, "batch", n_batch, 1))
        grads = unpack(me, pieces, tails, split, width, hidden)
        (d_query, d_query_bias, d_keyval, d_value_bias, d_cross, d_cross_bias, d_gain, d_nbias, d_self, d_self_bias,
         d_selfout, d_selfout_bias, d_hidden, d_hidden_bias, d_hidout, d_hidout_bias, d_embed, d_embed_bias) = grads
    else:
        old, parts = None, []
        for key in range(PARTS):
            back = backward(key, dn, old, key == PARTS - 1)
            old = back[:1] + back[2:]
            parts.append(back[1])
        feat_grad, g_kv = old
        qp = jnp.concatenate(parts, 0)
        outs = mask((0, blocks))
        sums = jnp.concatenate([lax.psum(qp, "pix").reshape(images * rows, width), g_kv], 0)
        queries_grad, tail, tail2 = query_back(me, (sums,), queries, dp1, query_weight)
        first = core == 0
        tail = jnp.concatenate([jnp.where(first, tail, tail2), jnp.where(first, tail2, tail)], 0)
        g_q = lax.psum(tail[g_kv.shape[0]:], "batch")
        g_kv = lax.psum(g_kv, ("batch", "pix"))
        every = [(2 * z, 2 * z + 1) for z in range(n_batch // 2)]
        groups = [[z[c] for z in every] for c in range(2)]
        part = lax.psum(mine + other, "batch", axis_index_groups=groups)
        both = lax.all_gather(part, "batch", axis_index_groups=[list(z) for z in every])
        packed = lax.all_gather(both, "pix").reshape(-1, width)

        def tile(t, k=1):
            return packed[t * width:(t + k) * width]

        def wide(t, k):
            return jnp.concatenate([tile(t + j) for j in range(k)], 1)

        many = hidden // width
        bias = packed[(T_HIDDEN + 2 * many) * width:]
        d_query, d_query_bias = g_q[:width], g_q[width]
        d_keyval, d_value_bias = jnp.concatenate([g_kv[:width], g_kv[width:2 * width]], 1), g_kv[2 * width]
        d_cross, d_cross_bias, d_gain, d_nbias = tile(T_CROSS), bias[0], bias[1:4], bias[4:7]
        d_self, d_self_bias, d_selfout, d_selfout_bias = wide(T_SELF, 3), bias[20:22], tile(T_SELFOUT), bias[7]
        d_hidden, d_hidden_bias = wide(T_HIDDEN, many), bias[8:8 + many]
        d_hidout, d_hidout_bias = tile(T_HIDDEN + many, many), bias[16]
        d_embed, d_embed_bias = tile(T_EMBED, 3), bias[17:20]
    logits, mask_grad = outs
    return (
        unflat(x3),
        unflat(logits),
        unflat(queries_grad),
        feat_grad,
        mask_grad,
        d_query,
        d_query_bias.reshape(-1),
        d_keyval,
        d_value_bias.reshape(-1),
        d_cross,
        d_cross_bias.reshape(-1),
        d_gain,
        d_nbias,
        d_self,
        d_self_bias,
        d_selfout,
        d_selfout_bias.reshape(-1),
        d_hidden,
        d_hidden_bias.reshape(-1),
        d_hidout,
        d_hidout_bias.reshape(-1),
        d_embed.reshape(3, width, width),
        d_embed_bias,
    )


def solution(mesh):
    n_pix, n_batch = mesh.shape["pix"], mesh.shape["batch"]
    rep = P()
    row, pixel, column = P("batch", None, None), P("batch", "pix", None), P("batch", None, "pix")
    in_specs = (row, pixel, pixel, column, P("batch", None), P("batch", None), row, column) + (rep,) * 18
    out_specs = (row, column, row, pixel, pixel) + (rep,) * 18
    body = functools.partial(local, n_pix=n_pix, n_batch=n_batch)
    return jax.shard_map(body, mesh=mesh, in_specs=in_specs, out_specs=out_specs, check_vma=False)
```

```python
import functools
import math

import jax
import jax.numpy as jnp
import numpy as np
from jax import lax
from jax.experimental import pallas as pl
from jax.experimental.pallas import tpu as pltpu
from jax.sharding import PartitionSpec as P

HEADS = 8
EPS = 1e-05
PENALTY = 10000.0
F32 = jnp.float32
LOW = jnp.bfloat16
HIGH = lax.Precision.HIGHEST
CURVE = math.sqrt(2.0 / math.pi)
CUBE = 0.044715
MIB = 1 << 20
PARTS = 4

T_CROSS, T_SELF, T_SELFOUT, T_EMBED, T_HIDDEN = 0, 1, 4, 5, 8


def up(n, m):
    return (n + m - 1) // m * m


def nn(a, b, precision=None):
    return lax.dot_general(a, b, (((1,), (0,)), ((), ())), precision=precision, preferred_element_type=F32)


def nt(a, b, precision=None):
    return lax.dot_general(a, b, (((1,), (1,)), ((), ())), precision=precision, preferred_element_type=F32)


def tn(a, b, precision=None):
    return lax.dot_general(a, b, (((0,), (0,)), ((), ())), precision=precision, preferred_element_type=F32)


def head_mask(width):
    shape = (HEADS, 1, width)
    head = width // HEADS
    return lax.broadcasted_iota(jnp.int32, shape, 2) // head == lax.broadcasted_iota(jnp.int32, shape, 0)


def spread(x, mask):
    rows, width = x.shape
    return jnp.where(mask, x[None], 0.0).reshape(HEADS * rows, width)


def gather_heads(x, mask):
    total, width = x.shape
    return jnp.sum(jnp.where(mask, x.reshape(HEADS, total // HEADS, width), 0.0), 0)


def spread_low(x, mask):
    return spread(x, mask).astype(LOW)


def head_onehot(width, lanes, transposed=False):
    head = width // HEADS
    if transposed:
        shape, a, b = (width, lanes), 0, 1
    else:
        shape, a, b = (lanes, width), 1, 0
    hit = lax.broadcasted_iota(jnp.int32, shape, a) // head == lax.broadcasted_iota(jnp.int32, shape, b)
    return hit.astype(F32)


def slabs_in(scr, value):
    for t in range(scr.shape[0]):
        scr[t] = value[:, t * 128:(t + 1) * 128]


def take_image(scr, image, count, images):
    rows = pl.ds(image, count, images)
    return jnp.concatenate([scr[t, rows, :] for t in range(scr.shape[0])], 1)


def put_image(scr, image, count, images, value):
    for t in range(scr.shape[0]):
        scr[t, pl.ds(image, count, images), :] = value[:, t * 128:(t + 1) * 128]


def slabs(rows, columns):
    return pltpu.VMEM((columns // 128, rows, 128), F32)


def cost(flops, nbytes, trans=0):
    return pl.CostEstimate(flops=int(flops), bytes_accessed=int(nbytes), transcendentals=int(trans))


def whole(x):
    shape = x.shape
    return pl.BlockSpec(shape, lambda *_: (0,) * len(shape))


def params(mib, fuse=False):
    return pltpu.CompilerParams(
        vmem_limit_bytes=mib * MIB, dimension_semantics=("arbitrary",), fuse_transposed_lhs_in_matmul=fuse)


def of_step(keys, n, i):
    key = keys[-1]
    for j in range(len(keys) - 2, -1, -1):
        key = jnp.where(i < (j + 1) * n, keys[j], key)
    return key


def pair_rows(x, pair):
    width = x.shape[1]
    head = width // HEADS
    at = 2 * pair * head // 128 * 128
    col = lax.broadcasted_iota(jnp.int32, (1, 128), 1) + at
    part = x[:, at:at + 128]
    return jnp.concatenate([jnp.where(col // head == 2 * pair + k, part, 0.0) for k in range(2)], 0)


def attend_kernel(keys, n, me_ref, q_ref, f_ref, bits_ref, flag_ref, mc_ref, mf_ref, wq_ref, bq_ref, wk_ref, vb_ref,
                  elo_ref, ehi_ref, e_ref, ck_ref, cv_ref, cq_ref, *refs):
    pays = refs[:len(keys)]
    q_scr, w_scr, all_scr, mc_scr, wq_scr, wk_scr, turned_scr, vb_scr, pay_ref = refs[len(keys):]
    i = pl.program_id(0)
    matched, images, wide = mc_ref.shape
    image = (me_ref[0] ^ of_step(keys, n, i)) * n + i % n
    width = q_ref.shape[1]
    count = q_ref.shape[0] // images
    rows = q_scr.shape[0]
    pixels = f_ref.shape[1]
    tall = rows + HEADS
    head = width // HEADS

    @pl.when(i == 0)
    def _():
        q_scr[...] = jnp.zeros_like(q_scr)
        w_scr[...] = jnp.zeros_like(w_scr)
        slabs_in(all_scr, q_ref[...])
        slabs_in(mc_scr, mc_ref[...].astype(F32).reshape(matched * images, wide))
        wq_scr[...] = wq_ref[...].astype(LOW)
        wk_scr[...] = wk_ref[...].astype(LOW)
        turned_scr[0:width] = jnp.transpose(wk_ref[:, :width]).astype(LOW)
        turned_scr[width:] = jnp.transpose(wk_ref[:, width:]).astype(LOW)
        vb_scr[...] = jnp.transpose(jnp.broadcast_to(vb_ref[...], (128, width)))
        pay_ref[...] = jnp.zeros_like(pay_ref)

    pay_ref[tall:tall + matched] = nn(take_image(mc_scr, image, matched, images).astype(LOW), mf_ref[0])

    q_scr[0:count] = take_image(all_scr, image, count, images)
    w_scr[:, 0:count] = jnp.where(flag_ref[pl.ds(image, 1), :] > 0, 65535, bits_ref[0])

    scale = 1.0 / math.sqrt(head)
    cq = ((nn(q_scr[...].astype(LOW), wq_scr[...]) + bq_ref[...]) * scale).astype(LOW).astype(F32)
    cq_ref[0] = cq

    bits = w_scr[...]
    low = (bits & 255).astype(F32).astype(LOW)
    high = (bits >> 8).astype(F32).astype(LOW)
    byte = (tn(low, elo_ref[...]) + tn(high, ehi_ref[...])).astype(jnp.int32)
    shift = lax.broadcasted_iota(jnp.int32, (rows, pixels), 1) & 7
    pen = jnp.where(((byte >> shift) & 1) == 1, 0.0, -PENALTY)

    f = f_ref[0]
    turned = nt(turned_scr[...], f)
    ck = turned[:width].astype(LOW)
    cv_ref[0] = (turned[width:] + jnp.concatenate([vb_scr[...]] * (pixels // 128), 1)).astype(LOW)
    keyval = nn(f, wk_scr[...])
    ck_ref[0] = keyval[:, :width].astype(LOW)
    cv = (keyval[:, width:] + vb_ref[...]).astype(LOW)
    hm = head_mask(width)

    def scores(p):
        at = 2 * p * head // 128 * 128
        s = nn(pair_rows(cq, p).astype(LOW), ck[at:at + 128])
        return (s.reshape(2, rows, pixels) + pen[None]).reshape(2 * rows, pixels)

    lane = lax.broadcasted_iota(jnp.int32, (rows, 128), 1)
    stats = jnp.zeros((rows, 128), F32)
    numer = jnp.zeros((rows, width), F32)
    following = scores(0)
    for p in range(HEADS // 2):
        s = following
        if p + 1 < HEADS // 2:
            following = scores(p + 1)
        m = jnp.max(s, -1, keepdims=True)
        e = jnp.exp(s - m)
        total = jnp.sum(e, -1, keepdims=True)
        e_low = e.astype(LOW)
        e_ref[0, p] = e_low
        part = nn(e_low, cv).reshape(2, rows, width)
        numer = numer + jnp.sum(jnp.where(hm[2 * p:2 * p + 2], part, 0.0), 0)
        for k in range(2):
            stats = jnp.where(lane == 2 * p + k, m[k * rows:(k + 1) * rows], stats)
            stats = jnp.where(lane == HEADS + 2 * p + k, total[k * rows:(k + 1) * rows], stats)
    pay_ref[0:rows] = numer
    full = jnp.concatenate([stats, jnp.ones((128 - rows, 128), F32)], 0)
    turned = jnp.transpose(full)
    pay_ref[rows:tall, 0:128] = turned[0:HEADS]
    pay_ref[rows:tall, 128:256] = turned[HEADS:2 * HEADS]
    for j, out in enumerate(pays):
        @pl.when(i // n == j)
        def _(out=out):
            out[0] = pay_ref[...]


def attend(keys, me, queries, features, bits, reopen_flags, mask_cotan, mask_features, query_weight, query_bias,
           keyval_weight, value_bias, parts):
    images, pixels, width = features.shape
    words, count = bits.shape[1:]
    rows = up(count, 8)
    matched, _, wide = mask_cotan.shape
    tall = rows + HEADS + up(matched, 8)
    pixel = np.arange(pixels)
    word = np.arange(words)
    here = pixel[None, :] // 16 == word[:, None]
    e_lo = (here & (pixel[None, :] % 16 < 8)).astype(LOW)
    e_hi = (here & (pixel[None, :] % 16 >= 8)).astype(LOW)
    n = images // parts
    steps = n * len(keys)

    def theirs(*shape):
        return pl.BlockSpec(
            (1,) + shape, lambda i, me: ((me[0] ^ of_step(keys, n, i)) * n + i % n,) + (0,) * len(shape))

    def of_key(j, *shape):
        return pl.BlockSpec((1,) + shape, lambda i, me: (jnp.clip(i - j * n, 0, n - 1),) + (0,) * len(shape))

    per = lambda *shape: pl.BlockSpec((1,) + shape, lambda i, me: (i,) + (0,) * len(shape))
    args = (queries, features, bits, reopen_flags, mask_cotan, mask_features, query_weight, query_bias[None],
            keyval_weight, value_bias[None], e_lo, e_hi)
    in_specs = [whole(a) for a in args]
    in_specs[1] = theirs(pixels, width)
    in_specs[2] = theirs(words, count)
    in_specs[5] = theirs(wide, width)
    flops = 2 * steps * (pixels * width * 2 * width + 2 * HEADS * rows * pixels * width + 64 * wide * width)
    nbytes = steps * (pixels * width * 6 + HEADS * rows * pixels * 2 + wide * (width + matched) * 2)
    return pl.pallas_call(
        functools.partial(attend_kernel, keys, n),
        grid_spec=pltpu.PrefetchScalarGridSpec(
            num_scalar_prefetch=1,
            grid=(steps,),
            in_specs=in_specs,
            out_specs=(per(HEADS // 2, 2 * rows, pixels), per(pixels, width), per(width, pixels), per(rows, width)) + tuple(
                of_key(j, tall, width) for j in range(len(keys))),
            scratch_shapes=[
                pltpu.VMEM((rows, width), F32),
                pltpu.VMEM((words, rows), jnp.int32),
                slabs(count * images, width),
                slabs(matched * images, wide),
                pltpu.VMEM((width, width), LOW),
                pltpu.VMEM((width, 2 * width), LOW),
                pltpu.VMEM((2 * width, width), LOW),
                pltpu.VMEM((width, 128), F32),
                pltpu.VMEM((tall, width), F32),
            ],
        ),
        out_shape=(
            jax.ShapeDtypeStruct((steps, HEADS // 2, 2 * rows, pixels), LOW),
            jax.ShapeDtypeStruct((steps, pixels, width), LOW),
            jax.ShapeDtypeStruct((steps, width, pixels), LOW),
            jax.ShapeDtypeStruct((steps, rows, width), F32),
        ) + (jax.ShapeDtypeStruct((n, tall, width), F32),) * len(keys),
        compiler_params=params(60),
        cost_estimate=cost(flops, nbytes, steps * HEADS * rows * pixels),
        name="attend",
    )(me, *args)


def combine_kernel(rows, *refs):
    parts, out_ref = refs[:-1], refs[-1]
    images, full, width = out_ref.shape
    tall = rows + HEADS
    onehot = head_onehot(width, HEADS)
    for i in range(images):
        ms = [p[i, rows:tall, 0:128] for p in parts]
        ls = [p[i, rows:tall, 128:256] for p in parts]
        top = functools.reduce(jnp.maximum, ms)
        rs = [jnp.exp(m - top) for m in ms]
        total = sum(r * l for r, l in zip(rs, ls))
        acc = jnp.zeros((rows, width), F32)
        es = jnp.zeros((full - tall, width), F32)
        for p, r in zip(parts, rs):
            acc = acc + p[i, 0:rows] * tn(r / total, onehot, HIGH)[0:rows]
            es = es + p[i, tall:]
        out_ref[i, 0:rows] = acc
        out_ref[i, rows:tall, 0:128] = top
        out_ref[i, rows:tall, 128:256] = total
        out_ref[i, tall:] = es


def combine(parts, rows):
    shape = parts[0].shape
    return pl.pallas_call(
        functools.partial(combine_kernel, rows),
        out_shape=jax.ShapeDtypeStruct(shape, F32),
        compiler_params=pltpu.CompilerParams(vmem_limit_bytes=32 * MIB),
        cost_estimate=cost(1e6, 5 * 4 * math.prod(shape)),
        name="combine",
    )(*parts)


def lower_kernel(*refs):
    n = len(refs) // 2
    for raw, out in zip(refs[:n], refs[n:]):
        out[...] = raw[...].astype(LOW)


def lower(weights):
    out_shape = tuple(jax.ShapeDtypeStruct(w.shape, LOW) for w in weights)
    size = sum(math.prod(w.shape) for w in weights)
    return pl.pallas_call(
        lower_kernel,
        out_shape=out_shape,
        compiler_params=pltpu.CompilerParams(vmem_limit_bytes=60 * MIB),
        cost_estimate=cost(size, 6 * size),
        name="lower",
    )(*weights)


def norm_forward(x, gain, bias):
    centre = x - jnp.mean(x, -1, keepdims=True)
    inverse = lax.rsqrt(jnp.mean(centre * centre, -1, keepdims=True) + EPS)
    normed = centre * inverse
    return normed * gain + bias, normed, inverse


def norm_backward(normed, inverse, gain, grad):
    dnormed = grad * gain
    return inverse * (
        dnormed - jnp.mean(dnormed, -1, keepdims=True) - normed * jnp.mean(dnormed * normed, -1, keepdims=True)
    )


def gelu_pair(x):
    square = x * x
    t = jnp.tanh(x * (CURVE + (CURVE * CUBE) * square))
    half = 0.5 + 0.5 * t
    slope = half + (0.5 * x) * (1.0 - t * t) * (CURVE + (3.0 * CURVE * CUBE) * square)
    return x * half, slope


def column_sum(x):
    return jnp.sum(x, 0, keepdims=True)


def chain_kernel(
    pieces, me_ref, *refs
):
    att_parts, refs = refs[:pieces], refs[pieces:]
    locals_, refs = refs[:PARTS], refs[PARTS:]
    chain_body(me_ref, att_parts, locals_, *refs)


def chain_body(
    me_ref, att_parts, locals_, q_ref, match_ref, cot_ref, wc_ref, bc_ref, gain_ref, nbias_ref, ws_ref, bs_ref, wso_ref,
    bso_ref, wh_ref, bh_ref, who_ref, bho_ref, we_ref, be_ref,
    x3_ref, emb_ref, dn_ref, dt_ref, dp1_ref, mine_ref, away_ref,
    g_ref, all_scr, cot_scr, out_scr, att_scr, emb_scr, loc_scr,
    q_scr, sq_scr, sk_scr, sv_scr, so_scr, pr_scr, h_scr, gp_scr, dso_scr, dm_scr
):
    step = pl.program_id(0)
    batch, rows, width = dn_ref.shape
    matched = match_ref.shape[1]
    count, images = cot_ref.shape[:2]
    tall = rows + HEADS
    flat = batch * rows
    hidden = wh_ref.shape[1]
    scale = 1.0 / math.sqrt(width // HEADS)
    hm = head_mask(width)

    @pl.when(step == 0)
    def _():
        q_scr[...] = jnp.zeros_like(q_scr)
        g_ref[...] = jnp.zeros_like(g_ref)
        n = att_parts[0].shape[0]
        for k, part in enumerate(att_parts):
            att_scr[pl.ds((me_ref[0] ^ k) * n, n)] = part[...]
        n = locals_[0].shape[0]
        for k, part in enumerate(locals_):
            loc_scr[pl.ds((me_ref[0] ^ k) * n, n)] = part[:, rows:tall]
        slabs_in(all_scr, q_ref[...])
        slabs_in(cot_scr, cot_ref[...].astype(F32).reshape(count * images, width))

    def put(tile, value):
        g_ref[tile * width:(tile + 1) * width] += value

    bias_at = (T_HIDDEN + 2 * (hidden // width)) * width

    def put_bias(index, value):
        g_ref[bias_at + index:bias_at + index + 1] += value

    first = step * batch
    for b in range(batch):
        q_scr[b, 0:count] = take_image(all_scr, first + b, count, images)
    att = att_scr[pl.ds(first, batch), 0:rows].reshape(flat, width)
    att_low = att.astype(LOW)
    queries = q_scr[...].reshape(flat, width)
    x1, n1, i1 = norm_forward(queries + nn(att_low, wc_ref[...]) + bc_ref[...], gain_ref[0:1], nbias_ref[0:1])
    x1_low = x1.astype(LOW)
    mixed = nn(x1_low, ws_ref[...])
    three = (batch, rows, width)
    sq_scr[...] = ((mixed[:, :width] + bs_ref[0:1]) * scale).reshape(three)
    sk_scr[...] = mixed[:, width:2 * width].reshape(three)
    sv_scr[...] = (mixed[:, 2 * width:] + bs_ref[1:2]).reshape(three)

    head = width // HEADS
    lanes = lambda h: slice(h * 128, (h + 1) * 128)
    fill = jnp.zeros((128 - rows, width), F32)

    def tall_heads(x):
        return spread_low(jnp.concatenate([x, fill], 0), hm)

    def turn(x):
        return jnp.transpose(jnp.concatenate([x, fill], 0))[:, 0:rows].astype(LOW)

    def by_head(turned, x):
        return jnp.transpose(jnp.concatenate(
            [nn(turned[h * head:(h + 1) * head], x[:, lanes(h)]) for h in range(HEADS)], 0))[0:rows]

    for b in range(batch):
        ss = nt(sk_scr[b].astype(LOW), tall_heads(sq_scr[b]))
        keys = lax.broadcasted_iota(jnp.int32, ss.shape, 0)
        ss = jnp.where(keys < count, ss, -1e30)
        p = jnp.exp(ss - jnp.max(ss, 0, keepdims=True))
        p = p * (1.0 / jnp.sum(p, 0, keepdims=True))
        pr_scr[b] = p
        so_scr[b] = by_head(turn(sv_scr[b]), p.astype(LOW))
    so_low = so_scr[...].reshape(flat, width).astype(LOW)
    x2, n2, i2 = norm_forward(x1 + nn(so_low, wso_ref[...]) + bso_ref[...], gain_ref[1:2], nbias_ref[1:2])
    x2_low = x2.astype(LOW)
    block = 2 * width

    def ff_forward(j, acc):
        cols = pl.ds(pl.multiple_of(j * block, block), block)
        h, slope = gelu_pair(nn(x2_low, wh_ref[:, cols]) + bh_ref[:, cols])
        h = h.astype(LOW)
        h_scr[:, cols] = h
        gp_scr[:, cols] = slope.astype(gp_scr.dtype)
        return acc + nn(h, who_ref[cols, :])

    ff = lax.fori_loop(0, hidden // block, ff_forward, jnp.zeros((flat, width), F32))
    x3, n3, i3 = norm_forward(x2 + ff + bho_ref[...], gain_ref[2:3], nbias_ref[2:3])
    for b in range(batch):
        put_image(out_scr, first + b, count, images, x3[b * rows:b * rows + count])

    x3_low = x3.astype(LOW)
    h1, slope1 = gelu_pair(nn(x3_low, we_ref[0]) + be_ref[0:1])
    h1 = h1.astype(LOW)
    h2, slope2 = gelu_pair(nn(h1, we_ref[1]) + be_ref[1:2])
    h2 = h2.astype(LOW)
    emb = nn(h2, we_ref[2]) + be_ref[2:3]
    for b in range(batch):
        put_image(emb_scr, first + b, count, images, emb[b * rows:b * rows + count])

    grads = []
    for b in range(batch):
        spots = match_ref[pl.ds(first + b, 1), :]
        pick = (lax.broadcasted_iota(jnp.int32, (rows, matched), 0) == spots).astype(F32).astype(LOW)
        grads.append(nn(pick, att_scr[first + b, tall:tall + matched].astype(LOW)))
    dz3 = jnp.concatenate(grads, 0)
    dz3_low = dz3.astype(LOW)
    put(T_EMBED + 2, tn(h2, dz3_low))
    put_bias(19, column_sum(dz3_low.astype(F32)))
    dz2 = (nt(dz3_low, we_ref[2]) * slope2).astype(LOW)
    put(T_EMBED + 1, tn(h1, dz2))
    put_bias(18, column_sum(dz2.astype(F32)))
    dz1 = (nt(dz2, we_ref[1]) * slope1).astype(LOW)
    put(T_EMBED, tn(x3_low, dz1))
    put_bias(17, column_sum(dz1.astype(F32)))
    for b in range(batch):
        q_scr[b, 0:count] = take_image(cot_scr, first + b, count, images)
    dx3 = q_scr[...].reshape(flat, width) + nt(dz1, we_ref[0])
    put_bias(3, column_sum(dx3 * n3))
    put_bias(6, column_sum(dx3))
    dp3 = norm_backward(n3, i3, gain_ref[2:3], dx3)
    dff = dp3.astype(LOW)
    put_bias(16, column_sum(dff.astype(F32)))

    def ff_backward(j, acc):
        cols = pl.ds(pl.multiple_of(j * block, block), block)
        base = (T_HIDDEN + hidden // width) * width
        spot = pl.ds(pl.multiple_of(base + j * block, block), block)
        g_ref[spot] += tn(h_scr[:, cols], dff)
        dz = (nt(dff, who_ref[cols, :]) * gp_scr[:, cols].astype(F32)).astype(LOW)
        gh = tn(x2_low, dz)
        sums = column_sum(dz.astype(F32))
        for t in range(block // width):
            tile = pl.ds(pl.multiple_of(T_HIDDEN * width + j * block + t * width, width), width)
            g_ref[tile] += gh[:, t * width:(t + 1) * width]
            g_ref[pl.ds(bias_at + 8 + j * (block // width) + t, 1)] += sums[:, t * width:(t + 1) * width]
        return acc + nt(dz, wh_ref[:, cols])

    dx2 = dp3 + lax.fori_loop(0, hidden // block, ff_backward, jnp.zeros((flat, width), F32))
    put_bias(2, column_sum(dx2 * n2))
    put_bias(5, column_sum(dx2))
    dp2 = norm_backward(n2, i2, gain_ref[1:2], dx2)
    dsa = dp2.astype(LOW)
    put(T_SELFOUT, tn(so_low, dsa))
    put_bias(7, column_sum(dsa.astype(F32)))
    dso_scr[...] = nt(dsa, wso_ref[...]).reshape(three)

    for b in range(batch):
        dsox = tall_heads(dso_scr[b])
        p = pr_scr[b]
        dp = nt(sv_scr[b].astype(LOW), dsox)
        dss = (p * (dp - jnp.sum(p * dp, 0, keepdims=True))).astype(LOW)
        dm_scr[b, :, 0:width] = by_head(turn(sk_scr[b]), dss) * scale
        dm_scr[b, :, width:2 * width] = nn(dss, tall_heads(sq_scr[b]))
        dm_scr[b, :, 2 * width:] = nn(p.astype(LOW), dsox)

    dm = dm_scr[...].reshape(flat, 3 * width).astype(LOW)
    gs = tn(x1_low, dm)
    for t in range(3):
        put(T_SELF + t, gs[:, t * width:(t + 1) * width])
    put_bias(20, column_sum(dm[:, :width].astype(F32)))
    put_bias(21, column_sum(dm[:, 2 * width:].astype(F32)))
    dx1 = dp2 + nt(dm, ws_ref[...])
    put_bias(1, column_sum(dx1 * n1))
    put_bias(4, column_sum(dx1))
    dp1 = norm_backward(n1, i1, gain_ref[0:1], dx1)
    dp1_ref[...] = dp1.reshape(three)
    dca = dp1.astype(LOW)
    put(T_CROSS, tn(att_low, dca))
    put_bias(0, column_sum(dca.astype(F32)))
    d_att = nt(dca, wc_ref[...]).reshape(three)
    onehot = head_onehot(width, HEADS)
    back = head_onehot(width, 128, True)
    for b in range(batch):
        top = att_scr[first + b, rows:tall, 0:128]
        total = att_scr[first + b, rows:tall, 128:256]
        ratio = jnp.exp(loc_scr[first + b, :, 0:128] - top) / total
        dn = d_att[b] * tn(ratio, onehot, HIGH)[0:rows]
        dn_ref[b] = dn
        dt_ref[b] = -nn(dn * att_scr[first + b, 0:rows], back, HIGH)

    @pl.when(step == 1)
    def _():
        x3_ref[...] = jnp.concatenate([out_scr[t] for t in range(out_scr.shape[0])], 1)
        emb_ref[...] = jnp.concatenate([emb_scr[t] for t in range(emb_scr.shape[0])], 1)
        share = mine_ref.shape[0]
        at = me_ref[1] * 2 + me_ref[2]
        mine_ref[...] = g_ref[pl.ds(pl.multiple_of(at * share, 8), share)]
        away_ref[...] = g_ref[pl.ds(pl.multiple_of((at + 1 - 2 * me_ref[2]) * share, 8), share)]


def chain(me, parts, pays, queries, matched, query_cotan, weights, n_pix):
    full, width = pays[0].shape[1:]
    images = pays[0].shape[0] * len(pays)
    count = query_cotan.shape[0]
    rows = up(count, 8)
    batch = images // 2
    hidden = weights[8].shape[1]
    tiles = T_HIDDEN + 2 * (hidden // width)
    grads = up(tiles * width + 22, 256)
    half = lambda *shape: pl.BlockSpec((batch,) + shape, lambda i, *_: (i,) + (0,) * len(shape))
    pieces = len(parts)
    args = tuple(parts) + tuple(pays) + (queries, matched, query_cotan) + weights
    in_specs = [whole(a) for a in args]
    out_shape = (
        jax.ShapeDtypeStruct((count * images, width), F32),
        jax.ShapeDtypeStruct((count * images, width), F32),
        jax.ShapeDtypeStruct((images, rows, width), F32),
        jax.ShapeDtypeStruct((images, rows, 128), F32),
        jax.ShapeDtypeStruct((images, rows, width), F32),
        jax.ShapeDtypeStruct((grads // n_pix // 2, width), F32),
        jax.ShapeDtypeStruct((grads // n_pix // 2, width), F32),
    )
    flat = batch * rows
    three = (batch, rows, width)
    many = slabs(count * images, width)
    return pl.pallas_call(
        functools.partial(chain_kernel, pieces),
        grid_spec=pltpu.PrefetchScalarGridSpec(
            num_scalar_prefetch=1,
            grid=(2,),
            in_specs=in_specs,
            out_specs=(whole(out_shape[0]), whole(out_shape[1]), half(rows, width), half(rows, 128), half(rows, width),
                       whole(out_shape[5]), whole(out_shape[6])),
            scratch_shapes=[
                pltpu.VMEM((grads, width), F32),
                many,
                many,
                many,
                pltpu.VMEM((images, full, width), F32),
                many,
                pltpu.VMEM((images, HEADS, width), F32),
                pltpu.VMEM(three, F32),
                pltpu.VMEM(three, F32),
                pltpu.VMEM(three, F32),
                pltpu.VMEM(three, F32),
                pltpu.VMEM(three, F32),
                pltpu.VMEM((batch, rows, HEADS * 128), F32),
                pltpu.VMEM((flat, hidden), LOW),
                pltpu.VMEM((flat, hidden), LOW),
                pltpu.VMEM(three, F32),
                pltpu.VMEM((batch, rows, 3 * width), F32),
            ],
        ),
        out_shape=out_shape,
        compiler_params=params(62, True),
        cost_estimate=cost(2 * 8e9, 20e6, 4e6),
        name="chain",
    )(me, *args)


def mask_out_kernel(emb_ref, match_ref, mc_ref, mf_ref, logit_old, grad_old, logit_ref, grad_ref, chosen_scr,
                    emb_scr, low_scr, logit_scr, mc_scr):
    images, matched, width = chosen_scr.shape
    count = logit_ref.shape[0] // images
    part = mc_ref.shape[2]

    @pl.when(pl.program_id(0) == 0)
    def _():
        slabs_in(emb_scr, emb_ref[...])
        low_scr[...] = jnp.zeros_like(low_scr)
        for b in range(images):
            pick = (lax.broadcasted_iota(jnp.int32, (count, matched), 0) == match_ref[b:b + 1, :]).astype(F32).astype(LOW)
            emb = take_image(emb_scr, b, count, images).astype(LOW)
            low_scr[b, 0:count] = emb.astype(F32)
            chosen_scr[b] = tn(pick, emb)

    slabs_in(mc_scr, mc_ref[...].astype(F32).reshape(matched * images, part))
    for b in range(images):
        put_image(logit_scr, b, count, images, nt(low_scr[b].astype(LOW), mf_ref[b])[0:count])
        grad_ref[b] = tn(take_image(mc_scr, b, matched, images).astype(LOW), chosen_scr[b].astype(LOW))
    for t in range(part // 128):
        logit_ref[:, t * 128:(t + 1) * 128] = logit_scr[t]


def mask_out(emb, matched_queries, mask_cotan, mask_features, count, pieces, steps, old=None):
    matched, images, pixels = mask_cotan.shape
    width = emb.shape[1]
    part = pixels // pieces
    first, last = steps
    out_shape = (
        jax.ShapeDtypeStruct((count * images, pixels), F32),
        jax.ShapeDtypeStruct((images, pixels, width), F32),
    )
    args = (emb, matched_queries, mask_cotan, mask_features)
    here = pl.BlockSpec(memory_space=pl.ANY)
    kernel = mask_out_kernel
    aliases = {}
    specs = []
    if old is None:
        def kernel(a, b, c, d, *rest):
            mask_out_kernel(a, b, c, d, None, None, *rest)
    else:
        args += old
        aliases = {4: 0, 5: 1}
        specs = [here, here]
    return pl.pallas_call(
        kernel,
        grid=(last - first,),
        in_specs=[
            whole(emb),
            whole(matched_queries),
            pl.BlockSpec((matched, images, part), lambda j: (0, 0, j + first)),
            pl.BlockSpec((images, part, width), lambda j: (0, j + first, 0)),
        ] + specs,
        out_specs=(
            pl.BlockSpec((count * images, part), lambda j: (0, j + first)),
            pl.BlockSpec((images, part, width), lambda j: (0, j + first, 0)),
        ),
        out_shape=out_shape,
        input_output_aliases=aliases,
        scratch_shapes=[pltpu.VMEM((images, matched, width), F32),
                        slabs(count * images, width), pltpu.VMEM((images, up(count, 8), width), F32),
                        slabs(count * images, part), slabs(matched * images, part)],
        compiler_params=params(60, True),
        cost_estimate=cost(
            2 * images * pixels * width * 160 * (last - first) / pieces,
            images * pixels * (width * 6 + count * 4 + matched * 2) * (last - first) / pieces),
        name="mask_out",
    )(*args)


def attend_back_kernel(keys, n, last, me_ref, e_ref, ck_ref, cv_ref, f_ref, cq_ref, dn_ref, dt_ref, wkv_ref, acc_old,
                       vb_old, fg_ref, qps, acc_ref, vb_ref, g_ref):
    i = pl.program_id(0)
    rows, width = cq_ref.shape[1:]
    pixels = f_ref.shape[1]
    head = width // HEADS
    hm = head_mask(width)

    @pl.when(i == 0)
    def _():
        acc_ref[...] = jnp.zeros_like(acc_ref) if acc_old is None else acc_old[...]
        vb_ref[...] = jnp.zeros_like(vb_ref) if vb_old is None else vb_old[...]

    dn = dn_ref[0]
    cq = cq_ref[0]
    wide = 128

    def weigh(p):
        at = 2 * p * head // wide * wide
        both = pair_rows(dn, p).astype(LOW)
        dt = jnp.concatenate([dt_ref[0, :, 2 * p + k:2 * p + k + 1] for k in range(2)], 0)
        return both, nn(both, cv_ref[0, at:at + wide]) + dt

    def plus(old, new):
        return new if old is None else old + new

    part = jnp.zeros((rows, width), F32)
    keys_sum = [None] * (width // wide)
    values_sum = [None] * (width // wide)
    following = weigh(0)
    for p in range(HEADS // 2):
        slot = 2 * p * head // wide
        both, dw = following
        if p + 1 < HEADS // 2:
            following = weigh(p + 1)
        e_low = e_ref[0, p]
        ds = (e_low.astype(F32) * dw).astype(LOW)
        values_sum[slot] = plus(values_sum[slot], tn(both, e_low))
        back = nn(ds, ck_ref[0]).reshape(2, rows, width)
        part = part + jnp.sum(jnp.where(hm[2 * p:2 * p + 2], back, 0.0), 0)
        keys_sum[slot] = plus(keys_sum[slot], tn(pair_rows(cq, p).astype(LOW), ds))
    for j, out in enumerate(qps):
        @pl.when(i // n == j)
        def _(out=out):
            out[0] = part
    turned = jnp.concatenate(keys_sum + values_sum, 0).astype(LOW)
    acc_ref[...] += nn(turned, f_ref[0])
    summed = turned[width:].astype(F32)
    lanes_sum = summed[:, 0:128]
    for t in range(1, pixels // 128):
        lanes_sum = lanes_sum + summed[:, t * 128:(t + 1) * 128]
    vb_ref[...] += lanes_sum
    fg_ref[0] = tn(turned, wkv_ref[...])

    if last:
        @pl.when(i == pl.num_programs(0) - 1)
        def _():
            sums = jnp.sum(jnp.transpose(vb_ref[...]), 0, keepdims=True)
            fill = jnp.zeros((g_ref.shape[0] - 2 * width - 1, width), F32)
            g_ref[...] = jnp.concatenate(
                [jnp.transpose(acc_ref[0:width]), jnp.transpose(acc_ref[width:]), sums, fill], 0)


def attend_back(keys, me, kept, offset, features, dn, dt, keyval_turned, old, last):
    e, ck, cv, cq = kept
    images, pixels, width = features.shape
    rows = cq.shape[1]
    n = images // PARTS
    steps = n * len(keys)

    def theirs(*shape):
        return pl.BlockSpec(
            (1,) + shape, lambda i, me: ((me[0] ^ of_step(keys, n, i)) * n + i % n,) + (0,) * len(shape))

    def of_key(j, *shape):
        return pl.BlockSpec((1,) + shape, lambda i, me: (jnp.clip(i - j * n, 0, n - 1),) + (0,) * len(shape))

    per = lambda *shape: pl.BlockSpec((1,) + shape, lambda i, me: (i + offset,) + (0,) * len(shape))
    tall = HEADS * rows
    flops = 2 * steps * (4 * tall * pixels * width + 4 * pixels * width * width)
    nbytes = steps * (tall * pixels * 2 + pixels * width * 10)
    sums = (jax.ShapeDtypeStruct((2 * width, width), F32), jax.ShapeDtypeStruct((width, 128), F32))
    fg = jax.ShapeDtypeStruct((images, pixels, width), F32)
    qps = (jax.ShapeDtypeStruct((n, rows, width), F32),) * len(keys)
    scratch = []
    middle = sums
    if last:
        middle = (jax.ShapeDtypeStruct((2 * width + 32, width), F32),)
        scratch = [pltpu.VMEM(x.shape, F32) for x in sums]
    args = (e, ck, cv, features, cq, dn, dt, keyval_turned)
    in_specs = [per(HEADS // 2, 2 * rows, pixels), per(pixels, width), per(width, pixels), theirs(pixels, width),
                per(rows, width), theirs(rows, width), theirs(rows, 128), whole(keyval_turned)]
    aliases = {}

    def kernel(*refs):
        ins, refs = refs[:9], refs[9:]
        acc_old = vb_old = g = None
        if old is not None:
            acc_old, vb_old, refs = refs[1], refs[2], refs[3:]
        fg, refs = refs[0], refs[1:]
        if last:
            g, refs = refs[0], refs[1:]
            qp, (acc, vb) = refs[:len(keys)], refs[len(keys):]
        else:
            (acc, vb), qp = refs[:2], refs[2:]
        attend_back_kernel(keys, n, last, *ins, acc_old, vb_old, fg, qp, acc, vb, g)

    if old is not None:
        args += old
        in_specs += [pl.BlockSpec(memory_space=pl.ANY)] + [whole(x) for x in sums]
        aliases = {9: 0}
    return pl.pallas_call(
        kernel,
        grid_spec=pltpu.PrefetchScalarGridSpec(
            num_scalar_prefetch=1,
            grid=(steps,),
            in_specs=in_specs,
            out_specs=(theirs(pixels, width),) + tuple(whole(x) for x in middle) + tuple(
                of_key(j, rows, width) for j in range(len(keys))),
            scratch_shapes=scratch,
        ),
        out_shape=(fg,) + middle + qps,
        input_output_aliases=aliases,
        compiler_params=params(60, True),
        cost_estimate=cost(flops, nbytes),
        name="attend_back",
    )(me, *args)


def query_sum_kernel(me_ref, *refs):
    parts, kv_ref, outs = refs[:PARTS], refs[PARTS], refs[PARTS + 1:]
    n, rows, width = parts[0].shape
    total = parts[0][...]
    for p in parts[1:]:
        total = total + p[...]
    total = total.reshape(n * rows, width)
    share = kv_ref.shape[0] // PARTS
    for k, out in enumerate(outs):
        out[0:n * rows] = total
        out[n * rows:] = kv_ref[pl.ds(pl.multiple_of((me_ref[0] ^ k) * share, 8), share)]


def query_sum(me, parts, g_kv):
    n, rows, width = parts[0].shape
    args = tuple(parts) + (g_kv,)
    out = jax.ShapeDtypeStruct((n * rows + g_kv.shape[0] // PARTS, width), F32)
    return pl.pallas_call(
        query_sum_kernel,
        grid_spec=pltpu.PrefetchScalarGridSpec(
            num_scalar_prefetch=1, grid=(1,), in_specs=[whole(a) for a in args], out_specs=(whole(out),) * PARTS),
        out_shape=(out,) * PARTS,
        compiler_params=params(60),
        cost_estimate=cost(1e6, 3e6),
        name="query_sum",
    )(me, *args)


def query_back_kernel(pieces, me_ref, *refs):
    parts = refs[:pieces]
    (q_ref, dp_ref, wq_ref, qg_ref, mine_ref, away_ref, scr, sum_scr, all_scr, out_scr, g_scr, tail_scr) = refs[pieces:]
    images, rows, width = dp_ref.shape
    count = q_ref.shape[0] // images
    scale = 1.0 / math.sqrt(width // HEADS)
    n = images // pieces
    kv = jnp.zeros((parts[0].shape[0] - n * rows, width), F32)
    for k, part in enumerate(parts):
        sum_scr[pl.ds((me_ref[0] ^ k) * n, n)] = part[0:n * rows].reshape(n, rows, width)
        kv = kv + part[n * rows:]
    scr[...] = jnp.zeros_like(scr)
    slabs_in(all_scr, q_ref[...])
    for b in range(images):
        scr[b, 0:count] = take_image(all_scr, b, count, images)
    d_cq = (sum_scr[...].reshape(images * rows, width) * scale).astype(LOW)
    out = dp_ref[...] + nt(d_cq, wq_ref[...].astype(LOW)).reshape(images, rows, width)
    for b in range(images):
        put_image(out_scr, b, count, images, out[b, 0:count])
    qg_ref[...] = jnp.concatenate([out_scr[t] for t in range(out_scr.shape[0])], 1)
    g_scr[0:width] = tn(scr[...].reshape(images * rows, width).astype(LOW), d_cq)
    g_scr[width:] = jnp.zeros((g_scr.shape[0] - width, width), F32)
    g_scr[width:width + 1] = column_sum(d_cq.astype(F32))
    share = g_scr.shape[0] // pieces
    small = mine_ref.shape[0]
    tail_scr[0:kv.shape[0]] = kv
    tail_scr[kv.shape[0]:] = g_scr[pl.ds(pl.multiple_of(me_ref[0] * share, 8), share)]
    mine_ref[...] = tail_scr[pl.ds(pl.multiple_of(me_ref[2] * small, 8), small)]
    away_ref[...] = tail_scr[pl.ds(pl.multiple_of((1 - me_ref[2]) * small, 8), small)]


def query_back(me, parts, queries, dp1, query_weight):
    images, rows, width = dp1.shape
    pieces = len(parts)
    args = tuple(parts) + (queries, dp1, query_weight)
    share = parts[0].shape[0] - images // pieces * rows
    full = (width + 32) // pieces + share
    half = jax.ShapeDtypeStruct((full // 2, width), F32)
    out_shape = (jax.ShapeDtypeStruct(queries.shape, F32), half, half)
    return pl.pallas_call(
        functools.partial(query_back_kernel, pieces),
        grid_spec=pltpu.PrefetchScalarGridSpec(
            num_scalar_prefetch=1,
            grid=(1,),
            in_specs=[whole(a) for a in args],
            out_specs=tuple(whole(o) for o in out_shape),
            scratch_shapes=[pltpu.VMEM((images, rows, width), F32), pltpu.VMEM((images, rows, width), F32),
                            slabs(*queries.shape), slabs(*queries.shape), pltpu.VMEM((width + 32, width), F32),
                            pltpu.VMEM((full, width), F32)],
        ),
        out_shape=out_shape,
        compiler_params=params(60),
        cost_estimate=cost(5e8, 8e6),
        name="query_back",
    )(me, *args)


def unpack_kernel(split, me_ref, *refs):
    own, other = refs[:7], refs[7:14]
    (tail, tail2,
     query_ref, query_bias_ref, keyval_ref, value_bias_ref, cross_ref, cross_bias_ref, gain_ref, nbias_ref,
     self_ref, self_bias_ref, selfout_ref, selfout_bias_ref, hidden_ref, hidden_bias_ref, hidout_ref, hidout_bias_ref,
     embed_ref, embed_bias_ref, g, t) = refs[14:]
    pix, core = me_ref[1], me_ref[2]
    width = query_ref.shape[0]
    short = own[1].shape[0]

    def rows_of(block, half, second, size):
        at = ((pix ^ block) * 2 + half) * 2 + second
        return pl.ds(pl.multiple_of(at * short, 8), size)

    for half, seven in ((core, own), (1 - core, other)):
        g[rows_of(0, half, 0, 2 * short)] = seven[0][...]
        for k in range(1, 4):
            g[rows_of(k, half, 0, short)] = seven[2 * k - 1][...]
            g[rows_of(k, half, 1, short)] = seven[2 * k][...]
    small = tail.shape[0] // 4
    for half, ref in ((core, tail), (1 - core, tail2)):
        for k in range(4):
            at = (pix ^ k) * 2 + half
            t[pl.ds(pl.multiple_of(at * small, 8), small)] = ref[k * small:(k + 1) * small]

    def tile(n, k=1):
        return g[n * width:(n + k) * width]

    many = hidden_ref.shape[1] // width
    bias = (T_HIDDEN + 2 * many) * width
    cross_ref[...] = tile(T_CROSS)
    selfout_ref[...] = tile(T_SELFOUT)
    embed_ref[...] = tile(T_EMBED, 3)
    hidout_ref[...] = tile(T_HIDDEN + many, many)
    for n in range(3):
        self_ref[:, n * width:(n + 1) * width] = tile(T_SELF + n)
    for n in range(many):
        hidden_ref[:, n * width:(n + 1) * width] = tile(T_HIDDEN + n)
        hidden_bias_ref[:, n * width:(n + 1) * width] = g[bias + 8 + n:bias + 9 + n]
    cross_bias_ref[...] = g[bias:bias + 1]
    gain_ref[...] = g[bias + 1:bias + 4]
    nbias_ref[...] = g[bias + 4:bias + 7]
    selfout_bias_ref[...] = g[bias + 7:bias + 8]
    hidout_bias_ref[...] = g[bias + 16:bias + 17]
    embed_bias_ref[...] = g[bias + 17:bias + 20]
    self_bias_ref[...] = g[bias + 20:bias + 22]
    block = 2 * small
    low, high = [], []
    for k in range(4):
        low.append(t[k * block:k * block + split])
        high.append(t[k * block + split:(k + 1) * block])
    low, high = jnp.concatenate(low, 0), jnp.concatenate(high, 0)
    keyval_ref[:, 0:width] = low[0:width]
    keyval_ref[:, width:] = low[width:2 * width]
    value_bias_ref[...] = low[2 * width:2 * width + 1]
    query_ref[...] = high[0:width]
    query_bias_ref[...] = high[width:width + 1]


def unpack(me, pieces, tails, split, width, hidden):
    args = tuple(pieces) + tuple(tails)
    shapes = ((width, width), (1, width), (width, 2 * width), (1, width), (width, width), (1, width), (3, width), (3, width),
              (width, 3 * width), (2, width), (width, width), (1, width), (width, hidden), (1, hidden), (hidden, width),
              (1, width), (3 * width, width), (3, width))
    out_shape = tuple(jax.ShapeDtypeStruct(shape, F32) for shape in shapes)
    rows = sum(p.shape[0] for p in pieces)
    return pl.pallas_call(
        functools.partial(unpack_kernel, split),
        grid_spec=pltpu.PrefetchScalarGridSpec(
            num_scalar_prefetch=1,
            grid=(1,),
            in_specs=[whole(a) for a in args],
            out_specs=tuple(whole(o) for o in out_shape),
            scratch_shapes=[pltpu.VMEM((rows, width), F32), pltpu.VMEM((2 * tails[0].shape[0], width), F32)],
        ),
        out_shape=out_shape,
        compiler_params=params(60),
        cost_estimate=cost(1e6, 16e6),
        name="unpack",
    )(me, *args)


def beside(*values):
    return lax.optimization_barrier(values)


def swap(x, axis, n, key):
    return lax.ppermute(x, axis, [(d, d ^ key) for d in range(n)])


def scatter_out(x, axis, n):
    me = lax.axis_index(axis)
    chunks = [lax.dynamic_index_in_dim(x, me ^ k, 0, keepdims=False) for k in range(n)]
    return tuple(c if k == 0 else swap(c, axis, n, k) for k, c in enumerate(chunks))


def gather_in(x, axis, n):
    return tuple(x if k == 0 else swap(x, axis, n, k) for k in range(n))


def side(axis, key):
    return (lax.axis_index(axis) // key) % 2


def halve(x, axis, n, key):
    halves = x.reshape((2, -1) + x.shape[1:])
    mine = lax.dynamic_index_in_dim(halves, side(axis, key), 0, keepdims=False)
    away = lax.dynamic_index_in_dim(halves, 1 - side(axis, key), 0, keepdims=False)
    return mine, swap(away, axis, n, key)


def join(mine, other, axis, key):
    first = side(axis, key) == 0
    return jnp.concatenate([jnp.where(first, mine, other), jnp.where(first, other, mine)], 0)


def local(
    queries, features, mask_features, attend_bits, reopen_flags, matched_queries, query_cotan, mask_cotan,
    query_weight, query_bias, keyval_weight, value_bias, cross_out, cross_out_bias, norm_gain, norm_bias,
    self_weight, self_bias, self_out, self_out_bias, hidden_weight, hidden_bias, hidden_out, hidden_out_bias,
    embed_weight, embed_bias, *, n_pix, n_batch,
):
    images, count, width = queries.shape
    hidden = hidden_weight.shape[1]
    rows = up(count, 8)
    tall = rows + HEADS
    pix = lax.axis_index("pix")
    direct = n_pix == 4 and n_batch == 8

    queries = jnp.transpose(queries, (1, 0, 2)).reshape(count * images, width)
    query_cotan = jnp.transpose(query_cotan, (1, 0, 2))
    mask_cotan = jnp.transpose(mask_cotan, (1, 0, 2))
    bits = jnp.transpose(attend_bits, (0, 2, 1))
    core = lax.axis_index("batch") % 2
    me = jnp.stack([pix if direct else 0 * pix, pix, core]).astype(jnp.int32)

    def forward(keys, flags):
        return attend(keys, me, queries, features, bits, flags, mask_cotan, mask_features, query_weight, query_bias,
                      keyval_weight, value_bias, PARTS)

    far, near = (3, 1, 2), (0,)
    *kept, pay3, pay1, pay2 = forward(far, reopen_flags)
    pay3, pay1, pay2, reopen_flags = beside(pay3, pay1, pay2, reopen_flags)
    pays = {3: pay3, 1: pay1, 2: pay2}
    got = {k: swap(pays[k], "pix", n_pix, k) for k in far} if direct else {}
    *kept_near, pays[0] = forward(near, reopen_flags)
    if direct:
        pays[0], *arrived = beside(pays[0], *[got[k] for k in far])
        got.update(zip(far, arrived))
        got[0] = pays[0]
    keyval_turned = jnp.transpose(keyval_weight).astype(LOW)
    pays = [pays[k] for k in range(PARTS)]
    weights = (
        cross_out, cross_out_bias[None], norm_gain, norm_bias, self_weight, self_bias, self_out, self_out_bias[None],
        hidden_weight, hidden_bias[None], hidden_out, hidden_out_bias[None], embed_weight, embed_bias,
    )
    large = (0, 4, 6, 8, 10, 12)
    if direct:
        share = combine([got[k] for k in range(PARTS)], rows)
        share, keyval_turned, *raw = beside(share, keyval_turned, *[weights[k] for k in large])
        att = gather_in(share, "pix", n_pix)
    else:
        raw = [weights[k] for k in large]
        pay = jnp.concatenate(pays, 0)
        top = lax.pmax(pay[:, rows:tall, :128], "pix")
        ratio = jnp.exp(pay[:, rows:tall, :128] - top)

        def widen(x):
            return jnp.repeat(jnp.transpose(x, (0, 2, 1))[:, :rows], width // HEADS, axis=2)

        numer, total, es = lax.psum(
            (pay[:, :rows] * widen(ratio), pay[:, rows:tall, 128:] * ratio, pay[:, tall:]), "pix")
        att = (jnp.concatenate([numer / widen(total), jnp.concatenate([top, total], 2), es], 1),)
    lowered = dict(zip(large, lower(raw)))
    weights = tuple(lowered.get(k, w) for k, w in enumerate(weights))
    x3, emb, dn, dt, dp1, mine, away = chain(
        me, att, pays, queries, matched_queries, query_cotan, weights, n_pix)

    def unflat(x):
        return jnp.transpose(x.reshape(count, images, -1), (1, 0, 2))

    blocks = mask_features.shape[1] // 512
    mask = functools.partial(mask_out, emb, matched_queries, mask_cotan, mask_features, count, blocks)

    def backward(keys, old, last=False):
        offset = 0 if keys[0] in near else far.index(keys[0]) * images // PARTS
        return attend_back(keys, me, kept_near if keys[0] in near else kept, offset, features, dn, dt, keyval_turned, old, last)

    other = swap(away, "batch", n_batch, 1)
    if direct:
        fg, acc, vb, qp3 = backward((3,), None)
        other, fg, acc, vb, qp3 = beside(other, fg, acc, vb, qp3)
        own, other = halve(mine + other, "batch", n_batch, 2)
        qp3 = swap(qp3, "pix", n_pix, 3)
        fg, acc, vb, qp1, qp2 = backward((1, 2), (fg, acc, vb))
        other, qp3, fg, acc, vb, qp1, qp2 = beside(other, qp3, fg, acc, vb, qp1, qp2)
        own, other = halve(own + other, "batch", n_batch, 4)
        qp1, qp2 = swap(qp1, "pix", n_pix, 1), swap(qp2, "pix", n_pix, 2)
        feat_grad, g_kv, qp0 = backward((0,), (fg, acc, vb), True)
        other, qp1, qp2, feat_grad, g_kv, qp0 = beside(other, qp1, qp2, feat_grad, g_kv, qp0)
        own = own + other
        other = swap(own, "batch", n_batch, 4)
        split = g_kv.shape[0] // n_pix
        parts = query_sum(me, (qp0, qp1, qp2, qp3), g_kv)
        parts = tuple(p if k == 0 else swap(p, "pix", n_pix, k) for k, p in enumerate(parts))
        cuts = [blocks * k // 8 for k in (0, 3, 6, 8)]
        outs = mask((cuts[0], cuts[1]))
        other, parts, outs = beside(other, parts, outs)
        own = join(own, other, "batch", 4)
        other = swap(own, "batch", n_batch, 2)
        queries_grad, tail, tail2 = query_back(me, parts, queries, dp1, query_weight)
        tail2 = swap(tail2, "batch", n_batch, 1)
        outs = mask((cuts[1], cuts[2]), outs)
        other, tail2, outs = beside(other, tail2, outs)
        own = join(own, other, "batch", 2)
        low, high = own[:own.shape[0] // 2], own[own.shape[0] // 2:]
        low1, high2 = swap(low, "pix", n_pix, 1), swap(high, "pix", n_pix, 2)
        own2 = swap(own, "batch", n_batch, 1)
        tail = tail + tail2
        tail2 = swap(tail, "batch", n_batch, 2)
        outs = mask((cuts[2], cuts[3]), outs)
        low1, high2, own2, tail2, outs = beside(low1, high2, own2, tail2, outs)
        low2, high1 = swap(low, "pix", n_pix, 2), swap(high, "pix", n_pix, 1)
        low3, high3 = swap(low1, "pix", n_pix, 2), swap(high2, "pix", n_pix, 1)
        tail = tail + tail2
        tail = tail + swap(tail, "batch", n_batch, 4)
        tail = jnp.concatenate([tail] + [swap(tail, "pix", n_pix, k) for k in (1, 2, 3)], 0)
        pieces = [own, low1, high1, low2, high2, low3, high3]
        pieces += [own2] + [swap(p, "batch", n_batch, 1) for p in pieces[1:]]
        tails = (tail, swap(tail, "batch", n_batch, 1))
        grads = unpack(me, pieces, tails, split, width, hidden)
        (d_query, d_query_bias, d_keyval, d_value_bias, d_cross, d_cross_bias, d_gain, d_nbias, d_self, d_self_bias,
         d_selfout, d_selfout_bias, d_hidden, d_hidden_bias, d_hidout, d_hidout_bias, d_embed, d_embed_bias) = grads
    else:
        old, parts = None, {}
        for keys, last in ((far, False), (near, True)):
            back = backward(keys, old, last)
            count_sums = 1 if last else 2
            old = back[:1 + count_sums]
            parts.update(zip(keys, back[1 + count_sums:]))
        feat_grad, g_kv = old
        parts = [parts[k] for k in range(PARTS)]
        qp = jnp.concatenate(parts, 0)
        outs = mask((0, blocks))
        sums = jnp.concatenate([lax.psum(qp, "pix").reshape(images * rows, width), g_kv], 0)
        queries_grad, tail, tail2 = query_back(me, (sums,), queries, dp1, query_weight)
        first = core == 0
        tail = jnp.concatenate([jnp.where(first, tail, tail2), jnp.where(first, tail2, tail)], 0)
        g_q = lax.psum(tail[g_kv.shape[0]:], "batch")
        g_kv = lax.psum(g_kv, ("batch", "pix"))
        every = [(2 * z, 2 * z + 1) for z in range(n_batch // 2)]
        groups = [[z[c] for z in every] for c in range(2)]
        part = lax.psum(mine + other, "batch", axis_index_groups=groups)
        both = lax.all_gather(part, "batch", axis_index_groups=[list(z) for z in every])
        packed = lax.all_gather(both, "pix").reshape(-1, width)

        def tile(t, k=1):
            return packed[t * width:(t + k) * width]

        def wide(t, k):
            return jnp.concatenate([tile(t + j) for j in range(k)], 1)

        many = hidden // width
        bias = packed[(T_HIDDEN + 2 * many) * width:]
        d_query, d_query_bias = g_q[:width], g_q[width]
        d_keyval, d_value_bias = jnp.concatenate([g_kv[:width], g_kv[width:2 * width]], 1), g_kv[2 * width]
        d_cross, d_cross_bias, d_gain, d_nbias = tile(T_CROSS), bias[0], bias[1:4], bias[4:7]
        d_self, d_self_bias, d_selfout, d_selfout_bias = wide(T_SELF, 3), bias[20:22], tile(T_SELFOUT), bias[7]
        d_hidden, d_hidden_bias = wide(T_HIDDEN, many), bias[8:8 + many]
        d_hidout, d_hidout_bias = tile(T_HIDDEN + many, many), bias[16]
        d_embed, d_embed_bias = tile(T_EMBED, 3), bias[17:20]
    logits, mask_grad = outs
    return (
        unflat(x3),
        unflat(logits),
        unflat(queries_grad),
        feat_grad,
        mask_grad,
        d_query,
        d_query_bias.reshape(-1),
        d_keyval,
        d_value_bias.reshape(-1),
        d_cross,
        d_cross_bias.reshape(-1),
        d_gain,
        d_nbias,
        d_self,
        d_self_bias,
        d_selfout,
        d_selfout_bias.reshape(-1),
        d_hidden,
        d_hidden_bias.reshape(-1),
        d_hidout,
        d_hidout_bias.reshape(-1),
        d_embed.reshape(3, width, width),
        d_embed_bias,
    )


def solution(mesh):
    n_pix, n_batch = mesh.shape["pix"], mesh.shape["batch"]
    rep = P()
    row, pixel, column = P("batch", None, None), P("batch", "pix", None), P("batch", None, "pix")
    in_specs = (row, pixel, pixel, column, P("batch", None), P("batch", None), row, column) + (rep,) * 18
    out_specs = (row, column, row, pixel, pixel) + (rep,) * 18
    body = functools.partial(local, n_pix=n_pix, n_batch=n_batch)
    return jax.shard_map(body, mesh=mesh, in_specs=in_specs, out_specs=out_specs, check_vma=False)
```

```python
import functools
import math

import jax
import jax.numpy as jnp
import numpy as np
from jax import lax
from jax.experimental import pallas as pl
from jax.experimental.pallas import tpu as pltpu
from jax.sharding import PartitionSpec as P

HEADS = 8
EPS = 1e-05
PENALTY = 10000.0
F32 = jnp.float32
LOW = jnp.bfloat16
HIGH = lax.Precision.HIGHEST
CURVE = math.sqrt(2.0 / math.pi)
CUBE = 0.044715
MIB = 1 << 20
PARTS = 4

T_CROSS, T_SELF, T_SELFOUT, T_EMBED, T_HIDDEN = 0, 1, 4, 5, 8


def up(n, m):
    return (n + m - 1) // m * m


def nn(a, b, precision=None):
    return lax.dot_general(a, b, (((1,), (0,)), ((), ())), precision=precision, preferred_element_type=F32)


def nt(a, b, precision=None):
    return lax.dot_general(a, b, (((1,), (1,)), ((), ())), precision=precision, preferred_element_type=F32)


def tn(a, b, precision=None):
    return lax.dot_general(a, b, (((0,), (0,)), ((), ())), precision=precision, preferred_element_type=F32)


def head_mask(width):
    shape = (HEADS, 1, width)
    head = width // HEADS
    return lax.broadcasted_iota(jnp.int32, shape, 2) // head == lax.broadcasted_iota(jnp.int32, shape, 0)


def spread(x, mask):
    rows, width = x.shape
    return jnp.where(mask, x[None], 0.0).reshape(HEADS * rows, width)


def gather_heads(x, mask):
    total, width = x.shape
    return jnp.sum(jnp.where(mask, x.reshape(HEADS, total // HEADS, width), 0.0), 0)


def spread_low(x, mask):
    return spread(x, mask).astype(LOW)


def head_onehot(width, lanes, transposed=False):
    head = width // HEADS
    if transposed:
        shape, a, b = (width, lanes), 0, 1
    else:
        shape, a, b = (lanes, width), 1, 0
    hit = lax.broadcasted_iota(jnp.int32, shape, a) // head == lax.broadcasted_iota(jnp.int32, shape, b)
    return hit.astype(F32)


def slabs_in(scr, value):
    for t in range(scr.shape[0]):
        scr[t] = value[:, t * 128:(t + 1) * 128]


def take_image(scr, image, count, images):
    rows = pl.ds(image, count, images)
    return jnp.concatenate([scr[t, rows, :] for t in range(scr.shape[0])], 1)


def put_image(scr, image, count, images, value):
    for t in range(scr.shape[0]):
        scr[t, pl.ds(image, count, images), :] = value[:, t * 128:(t + 1) * 128]


def slabs(rows, columns):
    return pltpu.VMEM((columns // 128, rows, 128), F32)


def cost(flops, nbytes, trans=0):
    return pl.CostEstimate(flops=int(flops), bytes_accessed=int(nbytes), transcendentals=int(trans))


def whole(x):
    shape = x.shape
    return pl.BlockSpec(shape, lambda *_: (0,) * len(shape))


def params(mib):
    return pltpu.CompilerParams(vmem_limit_bytes=mib * MIB, dimension_semantics=("arbitrary",))


def of_step(keys, n, i):
    key = keys[-1]
    for j in range(len(keys) - 2, -1, -1):
        key = jnp.where(i < (j + 1) * n, keys[j], key)
    return key


def turned_heads(x, fill):
    return jnp.transpose(jnp.concatenate([x, fill], 0))[:, 0:x.shape[0]].astype(LOW)


def attend_kernel(keys, n, with_mask, me_ref, *refs):
    q_ref, f_ref, bits_ref, flag_ref, wq_ref, bq_ref, wkv_ref, vb_ref, elo_ref, ehi_ref = refs[:10]
    refs = refs[10:]
    if with_mask:
        mc_ref, mf_ref, mf_own_ref = refs[:3]
        refs = refs[3:]
    e_ref, kv_ref, cq_ref = refs[:3]
    pays, refs = refs[3:3 + len(keys)], refs[3 + len(keys):]
    if with_mask:
        es_ref, refs = refs[0], refs[1:]
        mc_scr, refs = refs[0], refs[1:]
    q_scr, w_scr, all_scr, wq_scr, wkv_scr, vb_scr, pay_ref = refs
    i = pl.program_id(0)
    images = flag_ref.shape[0]
    image = (me_ref[0] ^ of_step(keys, n, i)) * n + i % n
    width = q_ref.shape[1]
    count = q_ref.shape[0] // images
    rows = q_scr.shape[0]
    pixels = f_ref.shape[1]
    tall = rows + HEADS
    head = width // HEADS

    @pl.when(i == 0)
    def _():
        q_scr[...] = jnp.zeros_like(q_scr)
        w_scr[...] = jnp.zeros_like(w_scr)
        slabs_in(all_scr, q_ref[...])
        wq_scr[...] = wq_ref[...].astype(LOW)
        wkv_scr[0:width] = jnp.transpose(wkv_ref[:, :width]).astype(LOW)
        wkv_scr[width:] = jnp.transpose(wkv_ref[:, width:]).astype(LOW)
        vb_scr[...] = jnp.transpose(jnp.broadcast_to(vb_ref[...], (128, width)))
        pay_ref[...] = jnp.zeros_like(pay_ref)
        if with_mask:
            es_ref[...] = jnp.zeros_like(es_ref)
            slabs_in(mc_scr, mc_ref[...].astype(F32).reshape(mc_ref.shape[0] * images, mc_ref.shape[2]))

    if with_mask:
        matched = mc_ref.shape[0]
        pay_ref[tall:tall + matched] = nn(take_image(mc_scr, image, matched, images).astype(LOW), mf_ref[0])

        @pl.when(i < n)
        def _():
            own = take_image(mc_scr, me_ref[0] * n + i % n, matched, images).astype(LOW)
            es_ref[i % n, 0:matched] = nn(own, mf_own_ref[0])

    q_scr[0:count] = take_image(all_scr, image, count, images)
    w_scr[:, 0:count] = jnp.where(flag_ref[pl.ds(image, 1), :] > 0, 65535, bits_ref[0])

    scale = 1.0 / math.sqrt(head)
    cq = ((nn(q_scr[...].astype(LOW), wq_scr[...]) + bq_ref[...]) * scale).astype(LOW).astype(F32)
    cq_ref[0] = cq

    bits = w_scr[...]
    low = (bits & 255).astype(F32).astype(LOW)
    high = (bits >> 8).astype(F32).astype(LOW)
    byte = (tn(low, elo_ref[...]) + tn(high, ehi_ref[...])).astype(jnp.int32)
    shift = lax.broadcasted_iota(jnp.int32, (rows, pixels), 1) & 7
    pen = jnp.where(((byte >> shift) & 1) == 1, 0.0, -PENALTY)

    keyval = nt(wkv_scr[...], f_ref[0])
    ck = keyval[:width].astype(LOW)
    cv = (keyval[width:] + jnp.concatenate([vb_scr[...]] * (pixels // 128), 1)).astype(LOW)
    kv_ref[0, :width] = ck
    kv_ref[0, width:] = cv

    def scores(h):
        at = slice(h * head, (h + 1) * head)
        return nn(cq[:, at].astype(LOW), ck[at]) + pen

    lane = lax.broadcasted_iota(jnp.int32, (rows, 128), 1)
    stats = jnp.zeros((rows, 128), F32)
    parts = []
    following = scores(0)
    for h in range(HEADS):
        s = following
        if h + 1 < HEADS:
            following = scores(h + 1)
        m = jnp.max(s, -1, keepdims=True)
        e = jnp.exp(s - m)
        total = jnp.sum(e, -1, keepdims=True)
        e_low = e.astype(LOW)
        e_ref[0, h] = e_low
        parts.append(nt(cv[h * head:(h + 1) * head], e_low))
        stats = jnp.where(lane == h, m, stats)
        stats = jnp.where(lane == HEADS + h, total, stats)
    pay_ref[0:rows] = jnp.transpose(jnp.concatenate(parts, 0))
    full = jnp.concatenate([stats, jnp.ones((128 - rows, 128), F32)], 0)
    turned = jnp.transpose(full)
    pay_ref[rows:tall, 0:128] = turned[0:HEADS]
    pay_ref[rows:tall, 128:256] = turned[HEADS:2 * HEADS]
    for j, out in enumerate(pays):
        @pl.when(i // n == j)
        def _(out=out):
            out[0] = pay_ref[0:out.shape[1]]


def attend(keys, me, queries, features, bits, reopen_flags, query_weight, query_bias, keyval_weight, value_bias, parts,
           masks=None):
    images, pixels, width = features.shape
    words, count = bits.shape[1:]
    rows = up(count, 8)
    pixel = np.arange(pixels)
    word = np.arange(words)
    here = pixel[None, :] // 16 == word[:, None]
    e_lo = (here & (pixel[None, :] % 16 < 8)).astype(LOW)
    e_hi = (here & (pixel[None, :] % 16 >= 8)).astype(LOW)
    n = images // parts
    steps = n * len(keys)

    def theirs(*shape):
        return pl.BlockSpec(
            (1,) + shape, lambda i, me: ((me[0] ^ of_step(keys, n, i)) * n + i % n,) + (0,) * len(shape))

    def of_key(j, *shape):
        return pl.BlockSpec((1,) + shape, lambda i, me: (jnp.clip(i - j * n, 0, n - 1),) + (0,) * len(shape))

    per = lambda *shape: pl.BlockSpec((1,) + shape, lambda i, me: (i,) + (0,) * len(shape))
    args = (queries, features, bits, reopen_flags, query_weight, query_bias[None], keyval_weight, value_bias[None], e_lo, e_hi)
    in_specs = [whole(a) for a in args]
    in_specs[1] = theirs(pixels, width)
    in_specs[2] = theirs(words, count)
    flops = 2 * steps * (pixels * width * 2 * width + 2 * HEADS * rows * pixels * width)
    nbytes = steps * (pixels * width * 6 + HEADS * rows * pixels * 2)
    tall = rows + HEADS
    out_shape = [
        jax.ShapeDtypeStruct((steps, HEADS, rows, pixels), LOW),
        jax.ShapeDtypeStruct((steps, 2 * width, pixels), LOW),
        jax.ShapeDtypeStruct((steps, rows, width), F32),
    ]
    scratch = []
    if masks is not None:
        matched, _, wide = masks[0].shape
        args += masks + masks[1:]
        in_specs += [whole(masks[0]), theirs(wide, width),
                     pl.BlockSpec((1, wide, width), lambda i, me: (me[0] * n + jnp.minimum(i, n - 1), 0, 0))]
        nbytes += steps * wide * (width + matched) * 2
        scratch = [slabs(matched * images, wide)]
        tall += up(matched, 8)
    out_shape += [jax.ShapeDtypeStruct((n, tall, width), F32)] * len(keys)
    out_specs = [per(HEADS, rows, pixels), per(2 * width, pixels), per(rows, width)]
    out_specs += [of_key(j, tall, width) for j in range(len(keys))]
    if masks is not None:
        out_shape.append(jax.ShapeDtypeStruct((n, up(matched, 8), width), F32))
        out_specs.append(whole(out_shape[-1]))
    return pl.pallas_call(
        functools.partial(attend_kernel, keys, n, masks is not None),
        grid_spec=pltpu.PrefetchScalarGridSpec(
            num_scalar_prefetch=1,
            grid=(steps,),
            in_specs=in_specs,
            out_specs=tuple(out_specs),
            scratch_shapes=scratch + [
                pltpu.VMEM((rows, width), F32),
                pltpu.VMEM((words, rows), jnp.int32),
                slabs(count * images, width),
                pltpu.VMEM((width, width), LOW),
                pltpu.VMEM((2 * width, width), LOW),
                pltpu.VMEM((width, 128), F32),
                pltpu.VMEM((tall, width), F32),
            ],
        ),
        out_shape=tuple(out_shape),
        compiler_params=params(60),
        cost_estimate=cost(flops, nbytes, steps * HEADS * rows * pixels),
        name="attend",
    )(me, *args)


def combine_kernel(rows, *refs):
    parts, es_ref, out_ref = refs[:-2], refs[-2], refs[-1]
    images, full, width = out_ref.shape
    tall = rows + HEADS
    onehot = head_onehot(width, HEADS)
    for i in range(images):
        ms = [p[i, rows:tall, 0:128] for p in parts]
        ls = [p[i, rows:tall, 128:256] for p in parts]
        top = functools.reduce(jnp.maximum, ms)
        rs = [jnp.exp(m - top) for m in ms]
        total = sum(r * l for r, l in zip(rs, ls))
        acc = jnp.zeros((rows, width), F32)
        for p, r in zip(parts, rs):
            acc = acc + p[i, 0:rows] * tn(r / total, onehot, HIGH)[0:rows]
        es = es_ref[i]
        for p in parts[1:]:
            es = es + p[i, tall:]
        out_ref[i, 0:rows] = acc
        out_ref[i, rows:tall, 0:128] = top
        out_ref[i, rows:tall, 128:256] = total
        out_ref[i, tall:] = es


def combine(parts, es, rows):
    shape = parts[1].shape
    return pl.pallas_call(
        functools.partial(combine_kernel, rows),
        out_shape=jax.ShapeDtypeStruct(shape, F32),
        compiler_params=pltpu.CompilerParams(vmem_limit_bytes=16 * MIB),
        cost_estimate=cost(1e6, 5 * 4 * math.prod(shape)),
        name="combine",
    )(*parts, es)


def lower_kernel(*refs):
    n = len(refs) // 2
    for raw, out in zip(refs[:n], refs[n:]):
        out[...] = raw[...].astype(LOW)


def lower(weights):
    out_shape = tuple(jax.ShapeDtypeStruct(w.shape, LOW) for w in weights)
    size = sum(math.prod(w.shape) for w in weights)
    return pl.pallas_call(
        lower_kernel,
        out_shape=out_shape,
        compiler_params=pltpu.CompilerParams(vmem_limit_bytes=24 * MIB),
        cost_estimate=cost(size, 6 * size),
        name="lower",
    )(*weights)


def norm_forward(x, gain, bias):
    centre = x - jnp.mean(x, -1, keepdims=True)
    inverse = lax.rsqrt(jnp.mean(centre * centre, -1, keepdims=True) + EPS)
    normed = centre * inverse
    return normed * gain + bias, normed, inverse


def norm_backward(normed, inverse, gain, grad):
    dnormed = grad * gain
    return inverse * (
        dnormed - jnp.mean(dnormed, -1, keepdims=True) - normed * jnp.mean(dnormed * normed, -1, keepdims=True)
    )


def gelu_pair(x):
    square = x * x
    t = jnp.tanh(x * (CURVE + (CURVE * CUBE) * square))
    half = 0.5 + 0.5 * t
    slope = half + (0.5 * x) * (1.0 - t * t) * (CURVE + (3.0 * CURVE * CUBE) * square)
    return x * half, slope


def column_sum(x):
    return jnp.sum(x, 0, keepdims=True)


def chain_kernel(
    pieces, me_ref, *refs
):
    att_parts, refs = refs[:pieces], refs[pieces:]
    locals_, refs = refs[:PARTS], refs[PARTS:]
    chain_body(me_ref, att_parts, locals_, *refs)


def chain_body(
    me_ref, att_parts, locals_, q_ref, match_ref, cot_ref, wc_ref, bc_ref, gain_ref, nbias_ref, ws_ref, bs_ref, wso_ref,
    bso_ref, wh_ref, bh_ref, who_ref, bho_ref, we_ref, be_ref,
    x3_ref, emb_ref, dn_ref, dt_ref, dp1_ref, mine_ref, away_ref,
    g_ref, all_scr, cot_scr, out_scr, att_scr, emb_scr, loc_scr,
    q_scr, sq_scr, sk_scr, sv_scr, so_scr, pr_scr, h_scr, gp_scr, dso_scr, dm_scr
):
    step = pl.program_id(0)
    batch, rows, width = dn_ref.shape
    matched = match_ref.shape[1]
    count, images = cot_ref.shape[:2]
    tall = rows + HEADS
    flat = batch * rows
    hidden = wh_ref.shape[1]
    scale = 1.0 / math.sqrt(width // HEADS)
    hm = head_mask(width)

    @pl.when(step == 0)
    def _():
        q_scr[...] = jnp.zeros_like(q_scr)
        g_ref[...] = jnp.zeros_like(g_ref)
        n = att_parts[0].shape[0]
        for k, part in enumerate(att_parts):
            att_scr[pl.ds((me_ref[0] ^ k) * n, n)] = part[...]
        n = locals_[0].shape[0]
        for k, part in enumerate(locals_):
            loc_scr[pl.ds((me_ref[0] ^ k) * n, n)] = part[:, rows:tall]
        slabs_in(all_scr, q_ref[...])
        slabs_in(cot_scr, cot_ref[...].astype(F32).reshape(count * images, width))

    def put(tile, value):
        g_ref[tile * width:(tile + 1) * width] += value

    bias_at = (T_HIDDEN + 2 * (hidden // width)) * width

    def put_bias(index, value):
        g_ref[bias_at + index:bias_at + index + 1] += value

    first = step * batch
    for b in range(batch):
        q_scr[b, 0:count] = take_image(all_scr, first + b, count, images)
    att = att_scr[pl.ds(first, batch), 0:rows].reshape(flat, width)
    att_low = att.astype(LOW)
    queries = q_scr[...].reshape(flat, width)
    x1, n1, i1 = norm_forward(queries + nn(att_low, wc_ref[...]) + bc_ref[...], gain_ref[0:1], nbias_ref[0:1])
    x1_low = x1.astype(LOW)
    mixed = nn(x1_low, ws_ref[...])
    three = (batch, rows, width)
    sq_scr[...] = ((mixed[:, :width] + bs_ref[0:1]) * scale).reshape(three)
    sk_scr[...] = mixed[:, width:2 * width].reshape(three)
    sv_scr[...] = (mixed[:, 2 * width:] + bs_ref[1:2]).reshape(three)

    head = width // HEADS
    lanes = lambda h: slice(h * 128, (h + 1) * 128)
    fill = jnp.zeros((128 - rows, width), F32)

    def tall_heads(x):
        return spread_low(jnp.concatenate([x, fill], 0), hm)

    def turn(x):
        return jnp.transpose(jnp.concatenate([x, fill], 0))[:, 0:rows].astype(LOW)

    def by_head(turned, x):
        return jnp.transpose(jnp.concatenate(
            [nn(turned[h * head:(h + 1) * head], x[:, lanes(h)]) for h in range(HEADS)], 0))[0:rows]

    for b in range(batch):
        ss = nt(sk_scr[b].astype(LOW), tall_heads(sq_scr[b]))
        keys = lax.broadcasted_iota(jnp.int32, ss.shape, 0)
        ss = jnp.where(keys < count, ss, -1e30)
        p = jnp.exp(ss - jnp.max(ss, 0, keepdims=True))
        p = p * (1.0 / jnp.sum(p, 0, keepdims=True))
        pr_scr[b] = p
        so_scr[b] = by_head(turn(sv_scr[b]), p.astype(LOW))
    so_low = so_scr[...].reshape(flat, width).astype(LOW)
    x2, n2, i2 = norm_forward(x1 + nn(so_low, wso_ref[...]) + bso_ref[...], gain_ref[1:2], nbias_ref[1:2])
    x2_low = x2.astype(LOW)
    block = 2 * width

    def ff_forward(j, acc):
        cols = pl.ds(pl.multiple_of(j * block, block), block)
        h, slope = gelu_pair(nn(x2_low, wh_ref[:, cols]) + bh_ref[:, cols])
        h = h.astype(LOW)
        h_scr[:, cols] = h
        gp_scr[:, cols] = slope.astype(gp_scr.dtype)
        return acc + nn(h, who_ref[cols, :])

    ff = lax.fori_loop(0, hidden // block, ff_forward, jnp.zeros((flat, width), F32))
    x3, n3, i3 = norm_forward(x2 + ff + bho_ref[...], gain_ref[2:3], nbias_ref[2:3])
    for b in range(batch):
        put_image(out_scr, first + b, count, images, x3[b * rows:b * rows + count])

    x3_low = x3.astype(LOW)
    h1, slope1 = gelu_pair(nn(x3_low, we_ref[0]) + be_ref[0:1])
    h1 = h1.astype(LOW)
    h2, slope2 = gelu_pair(nn(h1, we_ref[1]) + be_ref[1:2])
    h2 = h2.astype(LOW)
    emb = nn(h2, we_ref[2]) + be_ref[2:3]
    for b in range(batch):
        put_image(emb_scr, first + b, count, images, emb[b * rows:b * rows + count])

    grads = []
    for b in range(batch):
        spots = match_ref[pl.ds(first + b, 1), :]
        pick = (lax.broadcasted_iota(jnp.int32, (rows, matched), 0) == spots).astype(F32).astype(LOW)
        grads.append(nn(pick, att_scr[first + b, tall:tall + matched].astype(LOW)))
    dz3 = jnp.concatenate(grads, 0)
    dz3_low = dz3.astype(LOW)
    put(T_EMBED + 2, tn(h2, dz3_low))
    put_bias(19, column_sum(dz3_low.astype(F32)))
    dz2 = (nt(dz3_low, we_ref[2]) * slope2).astype(LOW)
    put(T_EMBED + 1, tn(h1, dz2))
    put_bias(18, column_sum(dz2.astype(F32)))
    dz1 = (nt(dz2, we_ref[1]) * slope1).astype(LOW)
    put(T_EMBED, tn(x3_low, dz1))
    put_bias(17, column_sum(dz1.astype(F32)))
    for b in range(batch):
        q_scr[b, 0:count] = take_image(cot_scr, first + b, count, images)
    dx3 = q_scr[...].reshape(flat, width) + nt(dz1, we_ref[0])
    put_bias(3, column_sum(dx3 * n3))
    put_bias(6, column_sum(dx3))
    dp3 = norm_backward(n3, i3, gain_ref[2:3], dx3)
    dff = dp3.astype(LOW)
    put_bias(16, column_sum(dff.astype(F32)))

    def ff_backward(j, acc):
        cols = pl.ds(pl.multiple_of(j * block, block), block)
        base = (T_HIDDEN + hidden // width) * width
        spot = pl.ds(pl.multiple_of(base + j * block, block), block)
        g_ref[spot] += tn(h_scr[:, cols], dff)
        dz = (nt(dff, who_ref[cols, :]) * gp_scr[:, cols].astype(F32)).astype(LOW)
        gh = tn(x2_low, dz)
        sums = column_sum(dz.astype(F32))
        for t in range(block // width):
            tile = pl.ds(pl.multiple_of(T_HIDDEN * width + j * block + t * width, width), width)
            g_ref[tile] += gh[:, t * width:(t + 1) * width]
            g_ref[pl.ds(bias_at + 8 + j * (block // width) + t, 1)] += sums[:, t * width:(t + 1) * width]
        return acc + nt(dz, wh_ref[:, cols])

    dx2 = dp3 + lax.fori_loop(0, hidden // block, ff_backward, jnp.zeros((flat, width), F32))
    put_bias(2, column_sum(dx2 * n2))
    put_bias(5, column_sum(dx2))
    dp2 = norm_backward(n2, i2, gain_ref[1:2], dx2)
    dsa = dp2.astype(LOW)
    put(T_SELFOUT, tn(so_low, dsa))
    put_bias(7, column_sum(dsa.astype(F32)))
    dso_scr[...] = nt(dsa, wso_ref[...]).reshape(three)

    for b in range(batch):
        dsox = tall_heads(dso_scr[b])
        p = pr_scr[b]
        dp = nt(sv_scr[b].astype(LOW), dsox)
        dss = (p * (dp - jnp.sum(p * dp, 0, keepdims=True))).astype(LOW)
        dm_scr[b, :, 0:width] = by_head(turn(sk_scr[b]), dss) * scale
        dm_scr[b, :, width:2 * width] = nn(dss, tall_heads(sq_scr[b]))
        dm_scr[b, :, 2 * width:] = nn(p.astype(LOW), dsox)

    dm = dm_scr[...].reshape(flat, 3 * width).astype(LOW)
    gs = tn(x1_low, dm)
    for t in range(3):
        put(T_SELF + t, gs[:, t * width:(t + 1) * width])
    put_bias(20, column_sum(dm[:, :width].astype(F32)))
    put_bias(21, column_sum(dm[:, 2 * width:].astype(F32)))
    dx1 = dp2 + nt(dm, ws_ref[...])
    put_bias(1, column_sum(dx1 * n1))
    put_bias(4, column_sum(dx1))
    dp1 = norm_backward(n1, i1, gain_ref[0:1], dx1)
    dp1_ref[...] = dp1.reshape(three)
    dca = dp1.astype(LOW)
    put(T_CROSS, tn(att_low, dca))
    put_bias(0, column_sum(dca.astype(F32)))
    d_att = nt(dca, wc_ref[...]).reshape(three)
    onehot = head_onehot(width, HEADS)
    back = head_onehot(width, 128, True)
    for b in range(batch):
        top = att_scr[first + b, rows:tall, 0:128]
        total = att_scr[first + b, rows:tall, 128:256]
        ratio = jnp.exp(loc_scr[first + b, :, 0:128] - top) / total
        dn = d_att[b] * tn(ratio, onehot, HIGH)[0:rows]
        dn_ref[b] = dn
        dt_ref[b] = -nn(dn * att_scr[first + b, 0:rows], back, HIGH)

    @pl.when(step == 1)
    def _():
        x3_ref[...] = jnp.concatenate([out_scr[t] for t in range(out_scr.shape[0])], 1)
        emb_ref[...] = jnp.concatenate([emb_scr[t] for t in range(emb_scr.shape[0])], 1)
        share = mine_ref.shape[0]
        at = me_ref[1] * 2 + me_ref[2]
        mine_ref[...] = g_ref[pl.ds(pl.multiple_of(at * share, 8), share)]
        away_ref[...] = g_ref[pl.ds(pl.multiple_of((at + 1 - 2 * me_ref[2]) * share, 8), share)]


def chain(me, parts, pays, queries, matched, query_cotan, weights, n_pix):
    full, width = parts[0].shape[1:]
    images = pays[0].shape[0] * len(pays)
    count = query_cotan.shape[0]
    rows = up(count, 8)
    batch = images // 2
    hidden = weights[8].shape[1]
    tiles = T_HIDDEN + 2 * (hidden // width)
    grads = up(tiles * width + 22, 256)
    half = lambda *shape: pl.BlockSpec((batch,) + shape, lambda i, *_: (i,) + (0,) * len(shape))
    pieces = len(parts)
    args = tuple(parts) + tuple(pays) + (queries, matched, query_cotan) + weights
    in_specs = [whole(a) for a in args]
    out_shape = (
        jax.ShapeDtypeStruct((count * images, width), F32),
        jax.ShapeDtypeStruct((count * images, width), F32),
        jax.ShapeDtypeStruct((images, rows, width), F32),
        jax.ShapeDtypeStruct((images, rows, 128), F32),
        jax.ShapeDtypeStruct((images, rows, width), F32),
        jax.ShapeDtypeStruct((grads // n_pix // 2, width), F32),
        jax.ShapeDtypeStruct((grads // n_pix // 2, width), F32),
    )
    flat = batch * rows
    three = (batch, rows, width)
    many = slabs(count * images, width)
    return pl.pallas_call(
        functools.partial(chain_kernel, pieces),
        grid_spec=pltpu.PrefetchScalarGridSpec(
            num_scalar_prefetch=1,
            grid=(2,),
            in_specs=in_specs,
            out_specs=(whole(out_shape[0]), whole(out_shape[1]), half(rows, width), half(rows, 128), half(rows, width),
                       whole(out_shape[5]), whole(out_shape[6])),
            scratch_shapes=[
                pltpu.VMEM((grads, width), F32),
                many,
                many,
                many,
                pltpu.VMEM((images, full, width), F32),
                many,
                pltpu.VMEM((images, HEADS, width), F32),
                pltpu.VMEM(three, F32),
                pltpu.VMEM(three, F32),
                pltpu.VMEM(three, F32),
                pltpu.VMEM(three, F32),
                pltpu.VMEM(three, F32),
                pltpu.VMEM((batch, rows, HEADS * 128), F32),
                pltpu.VMEM((flat, hidden), LOW),
                pltpu.VMEM((flat, hidden), LOW),
                pltpu.VMEM(three, F32),
                pltpu.VMEM((batch, rows, 3 * width), F32),
            ],
        ),
        out_shape=out_shape,
        compiler_params=params(62),
        cost_estimate=cost(2 * 8e9, 20e6, 4e6),
        name="chain",
    )(me, *args)


def mask_out_kernel(emb_ref, match_ref, mc_ref, mf_ref, logit_old, grad_old, logit_ref, grad_ref, chosen_scr,
                    emb_scr, low_scr, logit_scr, mc_scr):
    images, matched, width = chosen_scr.shape
    count = logit_ref.shape[0] // images
    part = mc_ref.shape[2]

    @pl.when(pl.program_id(0) == 0)
    def _():
        slabs_in(emb_scr, emb_ref[...])
        low_scr[...] = jnp.zeros_like(low_scr)
        for b in range(images):
            pick = (lax.broadcasted_iota(jnp.int32, (count, matched), 0) == match_ref[b:b + 1, :]).astype(F32).astype(LOW)
            emb = take_image(emb_scr, b, count, images).astype(LOW)
            low_scr[b, 0:count] = emb.astype(F32)
            chosen_scr[b] = tn(pick, emb)

    slabs_in(mc_scr, mc_ref[...].astype(F32).reshape(matched * images, part))
    for b in range(images):
        put_image(logit_scr, b, count, images, nt(low_scr[b].astype(LOW), mf_ref[b])[0:count])
        grad_ref[b] = tn(take_image(mc_scr, b, matched, images).astype(LOW), chosen_scr[b].astype(LOW))
    for t in range(part // 128):
        logit_ref[:, t * 128:(t + 1) * 128] = logit_scr[t]


def mask_out(emb, matched_queries, mask_cotan, mask_features, count, pieces, steps, old=None):
    matched, images, pixels = mask_cotan.shape
    width = emb.shape[1]
    part = pixels // pieces
    first, last = steps
    out_shape = (
        jax.ShapeDtypeStruct((count * images, pixels), F32),
        jax.ShapeDtypeStruct((images, pixels, width), F32),
    )
    args = (emb, matched_queries, mask_cotan, mask_features)
    here = pl.BlockSpec(memory_space=pl.ANY)
    kernel = mask_out_kernel
    aliases = {}
    specs = []
    if old is None:
        def kernel(a, b, c, d, *rest):
            mask_out_kernel(a, b, c, d, None, None, *rest)
    else:
        args += old
        aliases = {4: 0, 5: 1}
        specs = [here, here]
    return pl.pallas_call(
        kernel,
        grid=(last - first,),
        in_specs=[
            whole(emb),
            whole(matched_queries),
            pl.BlockSpec((matched, images, part), lambda j: (0, 0, j + first)),
            pl.BlockSpec((images, part, width), lambda j: (0, j + first, 0)),
        ] + specs,
        out_specs=(
            pl.BlockSpec((count * images, part), lambda j: (0, j + first)),
            pl.BlockSpec((images, part, width), lambda j: (0, j + first, 0)),
        ),
        out_shape=out_shape,
        input_output_aliases=aliases,
        scratch_shapes=[pltpu.VMEM((images, matched, width), F32),
                        slabs(count * images, width), pltpu.VMEM((images, up(count, 8), width), F32),
                        slabs(count * images, part), slabs(matched * images, part)],
        compiler_params=params(60),
        cost_estimate=cost(
            2 * images * pixels * width * 160 * (last - first) / pieces,
            images * pixels * (width * 6 + count * 4 + matched * 2) * (last - first) / pieces),
        name="mask_out",
    )(*args)


def attend_back_kernel(keys, n, last, me_ref, e_ref, kv_ref, f_ref, cq_ref, dn_ref, dt_ref, wkv_ref, acc_old, vb_old,
                       fg_ref, qps, acc_ref, vb_ref, g_ref, w_scr):
    i = pl.program_id(0)
    rows, width = cq_ref.shape[1:]
    pixels = f_ref.shape[1]
    head = width // HEADS

    @pl.when(i == 0)
    def _():
        acc_ref[...] = jnp.zeros_like(acc_ref) if acc_old is None else acc_old[...]
        vb_ref[...] = jnp.zeros_like(vb_ref) if vb_old is None else vb_old[...]
        w_scr[0:width] = jnp.transpose(wkv_ref[:, :width]).astype(LOW)
        w_scr[width:] = jnp.transpose(wkv_ref[:, width:]).astype(LOW)

    dn = dn_ref[0]
    fill = jnp.zeros((128 - rows, width), F32)
    cq_turned = turned_heads(cq_ref[0], fill)
    dn_turned = turned_heads(dn, fill)

    def weigh(h):
        at = slice(h * head, (h + 1) * head)
        return nn(dn[:, at].astype(LOW), kv_ref[0, width + h * head:width + (h + 1) * head]) + dt_ref[0, :, h:h + 1]

    parts, keys_sum, values_sum = [], [], []
    following = weigh(0)
    for h in range(HEADS):
        at = slice(h * head, (h + 1) * head)
        dw = following
        if h + 1 < HEADS:
            following = weigh(h + 1)
        e_low = e_ref[0, h]
        ds = (e_low.astype(F32) * dw).astype(LOW)
        values_sum.append(nn(dn_turned[at], e_low).astype(LOW))
        keys_sum.append(nn(cq_turned[at], ds).astype(LOW))
        parts.append(nt(kv_ref[0, at], ds))
    part = jnp.transpose(jnp.concatenate(parts, 0))
    for j, out in enumerate(qps):
        @pl.when(i // n == j)
        def _(out=out):
            out[0] = part
    turned = jnp.concatenate(keys_sum + values_sum, 0)
    acc_ref[...] += nn(turned, f_ref[0])
    summed = turned[width:].astype(F32)
    lanes_sum = summed[:, 0:128]
    for t in range(1, pixels // 128):
        lanes_sum = lanes_sum + summed[:, t * 128:(t + 1) * 128]
    vb_ref[...] += lanes_sum
    fg_ref[0] = tn(turned, w_scr[...])

    if last:
        @pl.when(i == pl.num_programs(0) - 1)
        def _():
            sums = jnp.sum(jnp.transpose(vb_ref[...]), 0, keepdims=True)
            fill = jnp.zeros((g_ref.shape[0] - 2 * width - 1, width), F32)
            g_ref[...] = jnp.concatenate(
                [jnp.transpose(acc_ref[0:width]), jnp.transpose(acc_ref[width:]), sums, fill], 0)


def attend_back(keys, me, kept, offset, features, dn, dt, keyval_weight, old, last):
    e, kv, cq = kept
    images, pixels, width = features.shape
    rows = cq.shape[1]
    n = images // PARTS
    steps = n * len(keys)

    def theirs(*shape):
        return pl.BlockSpec(
            (1,) + shape, lambda i, me: ((me[0] ^ of_step(keys, n, i)) * n + i % n,) + (0,) * len(shape))

    def of_key(j, *shape):
        return pl.BlockSpec((1,) + shape, lambda i, me: (jnp.clip(i - j * n, 0, n - 1),) + (0,) * len(shape))

    per = lambda *shape: pl.BlockSpec((1,) + shape, lambda i, me: (i + offset,) + (0,) * len(shape))
    tall = HEADS * rows
    flops = 2 * steps * (4 * tall * pixels * width + 4 * pixels * width * width)
    nbytes = steps * (tall * pixels * 2 + pixels * width * 10)
    sums = (jax.ShapeDtypeStruct((2 * width, width), F32), jax.ShapeDtypeStruct((width, 128), F32))
    fg = jax.ShapeDtypeStruct((images, pixels, width), F32)
    qps = (jax.ShapeDtypeStruct((n, rows, width), F32),) * len(keys)
    scratch = [pltpu.VMEM((2 * width, width), LOW)]
    middle = sums
    if last:
        middle = (jax.ShapeDtypeStruct((2 * width + 32, width), F32),)
        scratch = [pltpu.VMEM(x.shape, F32) for x in sums] + scratch
    args = (e, kv, features, cq, dn, dt, keyval_weight)
    in_specs = [per(HEADS, rows, pixels), per(2 * width, pixels), theirs(pixels, width),
                per(rows, width), theirs(rows, width), theirs(rows, 128), whole(keyval_weight)]
    aliases = {}

    def kernel(*refs):
        ins, refs = refs[:8], refs[8:]
        w_scr, refs = refs[-1], refs[:-1]
        acc_old = vb_old = g = None
        if old is not None:
            acc_old, vb_old, refs = refs[1], refs[2], refs[3:]
        fg, refs = refs[0], refs[1:]
        if last:
            g, refs = refs[0], refs[1:]
            qp, (acc, vb) = refs[:len(keys)], refs[len(keys):]
        else:
            (acc, vb), qp = refs[:2], refs[2:]
        attend_back_kernel(keys, n, last, *ins, acc_old, vb_old, fg, qp, acc, vb, g, w_scr)

    if old is not None:
        args += old
        in_specs += [pl.BlockSpec(memory_space=pl.ANY)] + [whole(x) for x in sums]
        aliases = {8: 0}
    return pl.pallas_call(
        kernel,
        grid_spec=pltpu.PrefetchScalarGridSpec(
            num_scalar_prefetch=1,
            grid=(steps,),
            in_specs=in_specs,
            out_specs=(theirs(pixels, width),) + tuple(whole(x) for x in middle) + tuple(
                of_key(j, rows, width) for j in range(len(keys))),
            scratch_shapes=scratch,
        ),
        out_shape=(fg,) + middle + qps,
        input_output_aliases=aliases,
        compiler_params=params(60),
        cost_estimate=cost(flops, nbytes),
        name="attend_back",
    )(me, *args)


def query_sum_kernel(me_ref, *refs):
    parts, kv_ref, outs = refs[:PARTS], refs[PARTS], refs[PARTS + 1:]
    n, rows, width = parts[0].shape
    total = parts[0][...]
    for p in parts[1:]:
        total = total + p[...]
    total = total.reshape(n * rows, width)
    share = kv_ref.shape[0] // PARTS
    for k, out in enumerate(outs):
        out[0:n * rows] = total
        out[n * rows:] = kv_ref[pl.ds(pl.multiple_of((me_ref[0] ^ k) * share, 8), share)]


def query_sum(me, parts, g_kv):
    n, rows, width = parts[0].shape
    args = tuple(parts) + (g_kv,)
    out = jax.ShapeDtypeStruct((n * rows + g_kv.shape[0] // PARTS, width), F32)
    return pl.pallas_call(
        query_sum_kernel,
        grid_spec=pltpu.PrefetchScalarGridSpec(
            num_scalar_prefetch=1, grid=(1,), in_specs=[whole(a) for a in args], out_specs=(whole(out),) * PARTS),
        out_shape=(out,) * PARTS,
        compiler_params=params(16),
        cost_estimate=cost(1e6, 3e6),
        name="query_sum",
    )(me, *args)


def query_back_kernel(pieces, me_ref, *refs):
    parts = refs[:pieces]
    (q_ref, dp_ref, wq_ref, qg_ref, mine_ref, away_ref, scr, sum_scr, all_scr, out_scr, g_scr, tail_scr) = refs[pieces:]
    images, rows, width = dp_ref.shape
    count = q_ref.shape[0] // images
    scale = 1.0 / math.sqrt(width // HEADS)
    n = images // pieces
    kv = jnp.zeros((parts[0].shape[0] - n * rows, width), F32)
    for k, part in enumerate(parts):
        sum_scr[pl.ds((me_ref[0] ^ k) * n, n)] = part[0:n * rows].reshape(n, rows, width)
        kv = kv + part[n * rows:]
    scr[...] = jnp.zeros_like(scr)
    slabs_in(all_scr, q_ref[...])
    for b in range(images):
        scr[b, 0:count] = take_image(all_scr, b, count, images)
    d_cq = (sum_scr[...].reshape(images * rows, width) * scale).astype(LOW)
    out = dp_ref[...] + nt(d_cq, wq_ref[...].astype(LOW)).reshape(images, rows, width)
    for b in range(images):
        put_image(out_scr, b, count, images, out[b, 0:count])
    qg_ref[...] = jnp.concatenate([out_scr[t] for t in range(out_scr.shape[0])], 1)
    g_scr[0:width] = tn(scr[...].reshape(images * rows, width).astype(LOW), d_cq)
    g_scr[width:] = jnp.zeros((g_scr.shape[0] - width, width), F32)
    g_scr[width:width + 1] = column_sum(d_cq.astype(F32))
    share = g_scr.shape[0] // pieces
    small = mine_ref.shape[0]
    tail_scr[0:kv.shape[0]] = kv
    tail_scr[kv.shape[0]:] = g_scr[pl.ds(pl.multiple_of(me_ref[0] * share, 8), share)]
    mine_ref[...] = tail_scr[pl.ds(pl.multiple_of(me_ref[2] * small, 8), small)]
    away_ref[...] = tail_scr[pl.ds(pl.multiple_of((1 - me_ref[2]) * small, 8), small)]


def query_back(me, parts, queries, dp1, query_weight):
    images, rows, width = dp1.shape
    pieces = len(parts)
    args = tuple(parts) + (queries, dp1, query_weight)
    share = parts[0].shape[0] - images // pieces * rows
    full = (width + 32) // pieces + share
    half = jax.ShapeDtypeStruct((full // 2, width), F32)
    out_shape = (jax.ShapeDtypeStruct(queries.shape, F32), half, half)
    return pl.pallas_call(
        functools.partial(query_back_kernel, pieces),
        grid_spec=pltpu.PrefetchScalarGridSpec(
            num_scalar_prefetch=1,
            grid=(1,),
            in_specs=[whole(a) for a in args],
            out_specs=tuple(whole(o) for o in out_shape),
            scratch_shapes=[pltpu.VMEM((images, rows, width), F32), pltpu.VMEM((images, rows, width), F32),
                            slabs(*queries.shape), slabs(*queries.shape), pltpu.VMEM((width + 32, width), F32),
                            pltpu.VMEM((full, width), F32)],
        ),
        out_shape=out_shape,
        compiler_params=params(24),
        cost_estimate=cost(5e8, 8e6),
        name="query_back",
    )(me, *args)


def unpack_kernel(split, me_ref, *refs):
    own, other = refs[:8], refs[8:16]
    (tail, tail2,
     query_ref, query_bias_ref, keyval_ref, value_bias_ref, cross_ref, cross_bias_ref, gain_ref, nbias_ref,
     self_ref, self_bias_ref, selfout_ref, selfout_bias_ref, hidden_ref, hidden_bias_ref, hidout_ref, hidout_bias_ref,
     embed_ref, embed_bias_ref, g, t) = refs[16:]
    pix, core, z = me_ref[1], me_ref[2], me_ref[3]
    width = query_ref.shape[0]
    short = own[0].shape[0] // 2
    for half, eight in ((core, own), (1 - core, other)):
        for k in range(4):
            for j in range(4):
                at = ((pix ^ k) * 2 + half) * 4 + (z ^ j)
                piece = eight[2 * k + j // 2]
                g[pl.ds(pl.multiple_of(at * short, 8), short)] = piece[j % 2 * short:(j % 2 + 1) * short]
    small = tail.shape[0] // 4
    for half, ref in ((core, tail), (1 - core, tail2)):
        for k in range(4):
            at = (pix ^ k) * 2 + half
            t[pl.ds(pl.multiple_of(at * small, 8), small)] = ref[k * small:(k + 1) * small]

    def tile(n, k=1):
        return g[n * width:(n + k) * width]

    many = hidden_ref.shape[1] // width
    bias = (T_HIDDEN + 2 * many) * width
    cross_ref[...] = tile(T_CROSS)
    selfout_ref[...] = tile(T_SELFOUT)
    embed_ref[...] = tile(T_EMBED, 3)
    hidout_ref[...] = tile(T_HIDDEN + many, many)
    for n in range(3):
        self_ref[:, n * width:(n + 1) * width] = tile(T_SELF + n)
    for n in range(many):
        hidden_ref[:, n * width:(n + 1) * width] = tile(T_HIDDEN + n)
        hidden_bias_ref[:, n * width:(n + 1) * width] = g[bias + 8 + n:bias + 9 + n]
    cross_bias_ref[...] = g[bias:bias + 1]
    gain_ref[...] = g[bias + 1:bias + 4]
    nbias_ref[...] = g[bias + 4:bias + 7]
    selfout_bias_ref[...] = g[bias + 7:bias + 8]
    hidout_bias_ref[...] = g[bias + 16:bias + 17]
    embed_bias_ref[...] = g[bias + 17:bias + 20]
    self_bias_ref[...] = g[bias + 20:bias + 22]
    block = 2 * small
    low, high = [], []
    for k in range(4):
        low.append(t[k * block:k * block + split])
        high.append(t[k * block + split:(k + 1) * block])
    low, high = jnp.concatenate(low, 0), jnp.concatenate(high, 0)
    keyval_ref[:, 0:width] = low[0:width]
    keyval_ref[:, width:] = low[width:2 * width]
    value_bias_ref[...] = low[2 * width:2 * width + 1]
    query_ref[...] = high[0:width]
    query_bias_ref[...] = high[width:width + 1]


def unpack(me, pieces, tails, split, width, hidden):
    args = tuple(pieces) + tuple(tails)
    shapes = ((width, width), (1, width), (width, 2 * width), (1, width), (width, width), (1, width), (3, width), (3, width),
              (width, 3 * width), (2, width), (width, width), (1, width), (width, hidden), (1, hidden), (hidden, width),
              (1, width), (3 * width, width), (3, width))
    out_shape = tuple(jax.ShapeDtypeStruct(shape, F32) for shape in shapes)
    rows = sum(p.shape[0] for p in pieces)
    return pl.pallas_call(
        functools.partial(unpack_kernel, split),
        grid_spec=pltpu.PrefetchScalarGridSpec(
            num_scalar_prefetch=1,
            grid=(1,),
            in_specs=[whole(a) for a in args],
            out_specs=tuple(whole(o) for o in out_shape),
            scratch_shapes=[pltpu.VMEM((rows, width), F32), pltpu.VMEM((2 * tails[0].shape[0], width), F32)],
        ),
        out_shape=out_shape,
        compiler_params=params(32),
        cost_estimate=cost(1e6, 16e6),
        name="unpack",
    )(me, *args)


def beside(*values):
    return lax.optimization_barrier(values)


def swap(x, axis, n, key):
    return lax.ppermute(x, axis, [(d, d ^ key) for d in range(n)])


def scatter_out(x, axis, n):
    me = lax.axis_index(axis)
    chunks = [lax.dynamic_index_in_dim(x, me ^ k, 0, keepdims=False) for k in range(n)]
    return tuple(c if k == 0 else swap(c, axis, n, k) for k, c in enumerate(chunks))


def gather_in(x, axis, n):
    return tuple(x if k == 0 else swap(x, axis, n, k) for k in range(n))


def side(axis, key):
    return (lax.axis_index(axis) // key) % 2


def halve(x, axis, n, key):
    halves = x.reshape((2, -1) + x.shape[1:])
    mine = lax.dynamic_index_in_dim(halves, side(axis, key), 0, keepdims=False)
    away = lax.dynamic_index_in_dim(halves, 1 - side(axis, key), 0, keepdims=False)
    return mine, swap(away, axis, n, key)


def join(mine, other, axis, key):
    first = side(axis, key) == 0
    return jnp.concatenate([jnp.where(first, mine, other), jnp.where(first, other, mine)], 0)


def local(
    queries, features, mask_features, attend_bits, reopen_flags, matched_queries, query_cotan, mask_cotan,
    query_weight, query_bias, keyval_weight, value_bias, cross_out, cross_out_bias, norm_gain, norm_bias,
    self_weight, self_bias, self_out, self_out_bias, hidden_weight, hidden_bias, hidden_out, hidden_out_bias,
    embed_weight, embed_bias, *, n_pix, n_batch,
):
    images, count, width = queries.shape
    hidden = hidden_weight.shape[1]
    rows = up(count, 8)
    tall = rows + HEADS
    pix = lax.axis_index("pix")
    direct = n_pix == 4 and n_batch == 8

    queries = jnp.transpose(queries, (1, 0, 2)).reshape(count * images, width)
    query_cotan = jnp.transpose(query_cotan, (1, 0, 2))
    mask_cotan = jnp.transpose(mask_cotan, (1, 0, 2))
    bits = jnp.transpose(attend_bits, (0, 2, 1))
    core = lax.axis_index("batch") % 2
    chip = lax.axis_index("batch") // 2
    me = jnp.stack([pix if direct else 0 * pix, pix, core, chip]).astype(jnp.int32)

    def forward(keys, flags, masks=None):
        return attend(keys, me, queries, features, bits, flags, query_weight, query_bias, keyval_weight, value_bias,
                      PARTS, masks)

    far, near = (3, 1, 2), (0,)
    *kept, pay3, pay1, pay2, es = forward(far, reopen_flags, (mask_cotan, mask_features))
    pay3, pay1, pay2, reopen_flags = beside(pay3, pay1, pay2, reopen_flags)
    pays = {3: pay3, 1: pay1, 2: pay2}
    got = {k: swap(pays[k], "pix", n_pix, k) for k in far} if direct else {}
    *kept_near, pays[0] = forward(near, reopen_flags)
    if direct:
        pays[0], *arrived = beside(pays[0], *[got[k] for k in far])
        got.update(zip(far, arrived))
        got[0] = pays[0]
    pays = [pays[k] for k in range(PARTS)]
    weights = (
        cross_out, cross_out_bias[None], norm_gain, norm_bias, self_weight, self_bias, self_out, self_out_bias[None],
        hidden_weight, hidden_bias[None], hidden_out, hidden_out_bias[None], embed_weight, embed_bias,
    )
    large = (0, 4, 6, 8, 10, 12)
    if direct:
        share = combine([got[k] for k in range(PARTS)], es, rows)
        share, *raw = beside(share, *[weights[k] for k in large])
        att = gather_in(share, "pix", n_pix)
    else:
        raw = [weights[k] for k in large]
        pay = jnp.concatenate([jnp.concatenate([pays[0], es], 1)] + pays[1:], 0)
        top = lax.pmax(pay[:, rows:tall, :128], "pix")
        ratio = jnp.exp(pay[:, rows:tall, :128] - top)

        def widen(x):
            return jnp.repeat(jnp.transpose(x, (0, 2, 1))[:, :rows], width // HEADS, axis=2)

        numer, total, es = lax.psum(
            (pay[:, :rows] * widen(ratio), pay[:, rows:tall, 128:] * ratio, pay[:, tall:]), "pix")
        att = (jnp.concatenate([numer / widen(total), jnp.concatenate([top, total], 2), es], 1),)
    lowered = dict(zip(large, lower(raw)))
    weights = tuple(lowered.get(k, w) for k, w in enumerate(weights))
    x3, emb, dn, dt, dp1, mine, away = chain(
        me, att, pays, queries, matched_queries, query_cotan, weights, n_pix)

    def unflat(x):
        return jnp.transpose(x.reshape(count, images, -1), (1, 0, 2))

    blocks = mask_features.shape[1] // 512
    mask = functools.partial(mask_out, emb, matched_queries, mask_cotan, mask_features, count, blocks)

    def backward(keys, old, last=False):
        offset = 0 if keys[0] in near else far.index(keys[0]) * images // PARTS
        return attend_back(keys, me, kept_near if keys[0] in near else kept, offset, features, dn, dt, keyval_weight, old, last)

    def z_scatter(chunks):
        got = [lax.dynamic_index_in_dim(chunks, chip ^ k, 0, keepdims=False) for k in range(4)]
        return [got[0]] + [swap(got[k], "batch", n_batch, 2 * k) for k in (1, 2, 3)]

    other = swap(away, "batch", n_batch, 1)
    if direct:
        fg, acc, vb, qp0 = backward(near, None)
        other, fg, acc, vb, qp0 = beside(other, fg, acc, vb, qp0)
        sums = z_scatter((mine + other).reshape(n_batch // 2, -1, width))
        feat_grad, g_kv, qp3, qp1, qp2 = backward(far, (fg, acc, vb), True)
        *sums, feat_grad, g_kv, qp1, qp2, qp3 = beside(*sums, feat_grad, g_kv, qp1, qp2, qp3)
        qp1, qp2, qp3 = [swap(q, "pix", n_pix, k) for k, q in zip((1, 2, 3), (qp1, qp2, qp3))]
        own = functools.reduce(jnp.add, sums)
        same = [own] + [swap(own, "batch", n_batch, k) for k in (2, 4, 6)]
        cuts = [blocks * k // 8 for k in (0, 2, 5, 8)]
        outs = mask((cuts[0], cuts[1]))
        qp1, qp2, qp3, outs = beside(qp1, qp2, qp3, outs)
        split = g_kv.shape[0] // n_pix
        parts = query_sum(me, (qp0, qp1, qp2, qp3), g_kv)
        parts = tuple(p if k == 0 else swap(p, "pix", n_pix, k) for k, p in enumerate(parts))
        outs = mask((cuts[1], cuts[2]), outs)
        parts, outs, *same = beside(parts, outs, *same)
        low, high = jnp.concatenate(same[:2], 0), jnp.concatenate(same[2:], 0)
        low1, high2 = swap(low, "pix", n_pix, 1), swap(high, "pix", n_pix, 2)
        low0, high0 = swap(low, "batch", n_batch, 1), swap(high, "batch", n_batch, 1)
        queries_grad, tail, tail2 = query_back(me, parts, queries, dp1, query_weight)
        tail2 = swap(tail2, "batch", n_batch, 1)
        outs = mask((cuts[2], cuts[3]), outs)
        low1, high2, low0, high0, tail2, outs = beside(low1, high2, low0, high0, tail2, outs)
        tail = tail + tail2
        tail2 = swap(tail, "batch", n_batch, 2)
        low2, high1 = swap(low, "pix", n_pix, 2), swap(high, "pix", n_pix, 1)
        low3, high3 = swap(low1, "pix", n_pix, 2), swap(high2, "pix", n_pix, 1)
        tail = tail + tail2
        tail = tail + swap(tail, "batch", n_batch, 4)
        tail = jnp.concatenate([tail] + [swap(tail, "pix", n_pix, k) for k in (1, 2, 3)], 0)
        pieces = [low, high, low1, high1, low2, high2, low3, high3]
        pieces += [low0, high0] + [swap(p, "batch", n_batch, 1) for p in pieces[2:]]
        tails = (tail, swap(tail, "batch", n_batch, 1))
        grads = unpack(me, pieces, tails, split, width, hidden)
        (d_query, d_query_bias, d_keyval, d_value_bias, d_cross, d_cross_bias, d_gain, d_nbias, d_self, d_self_bias,
         d_selfout, d_selfout_bias, d_hidden, d_hidden_bias, d_hidout, d_hidout_bias, d_embed, d_embed_bias) = grads
    else:
        old, parts = None, {}
        for keys, last in ((near, False), (far, True)):
            back = backward(keys, old, last)
            count_sums = 1 if last else 2
            old = back[:1 + count_sums]
            parts.update(zip(keys, back[1 + count_sums:]))
        feat_grad, g_kv = old
        parts = [parts[k] for k in range(PARTS)]
        qp = jnp.concatenate(parts, 0)
        outs = mask((0, blocks))
        sums = jnp.concatenate([lax.psum(qp, "pix").reshape(images * rows, width), g_kv], 0)
        queries_grad, tail, tail2 = query_back(me, (sums,), queries, dp1, query_weight)
        first = core == 0
        tail = jnp.concatenate([jnp.where(first, tail, tail2), jnp.where(first, tail2, tail)], 0)
        g_q = lax.psum(tail[g_kv.shape[0]:], "batch")
        g_kv = lax.psum(g_kv, ("batch", "pix"))
        every = [(2 * z, 2 * z + 1) for z in range(n_batch // 2)]
        groups = [[z[c] for z in every] for c in range(2)]
        part = lax.psum(mine + other, "batch", axis_index_groups=groups)
        both = lax.all_gather(part, "batch", axis_index_groups=[list(z) for z in every])
        packed = lax.all_gather(both, "pix").reshape(-1, width)

        def tile(t, k=1):
            return packed[t * width:(t + k) * width]

        def wide(t, k):
            return jnp.concatenate([tile(t + j) for j in range(k)], 1)

        many = hidden // width
        bias = packed[(T_HIDDEN + 2 * many) * width:]
        d_query, d_query_bias = g_q[:width], g_q[width]
        d_keyval, d_value_bias = jnp.concatenate([g_kv[:width], g_kv[width:2 * width]], 1), g_kv[2 * width]
        d_cross, d_cross_bias, d_gain, d_nbias = tile(T_CROSS), bias[0], bias[1:4], bias[4:7]
        d_self, d_self_bias, d_selfout, d_selfout_bias = wide(T_SELF, 3), bias[20:22], tile(T_SELFOUT), bias[7]
        d_hidden, d_hidden_bias = wide(T_HIDDEN, many), bias[8:8 + many]
        d_hidout, d_hidout_bias = tile(T_HIDDEN + many, many), bias[16]
        d_embed, d_embed_bias = tile(T_EMBED, 3), bias[17:20]
    logits, mask_grad = outs
    return (
        unflat(x3),
        unflat(logits),
        unflat(queries_grad),
        feat_grad,
        mask_grad,
        d_query,
        d_query_bias.reshape(-1),
        d_keyval,
        d_value_bias.reshape(-1),
        d_cross,
        d_cross_bias.reshape(-1),
        d_gain,
        d_nbias,
        d_self,
        d_self_bias,
        d_selfout,
        d_selfout_bias.reshape(-1),
        d_hidden,
        d_hidden_bias.reshape(-1),
        d_hidout,
        d_hidout_bias.reshape(-1),
        d_embed.reshape(3, width, width),
        d_embed_bias,
    )


def solution(mesh):
    n_pix, n_batch = mesh.shape["pix"], mesh.shape["batch"]
    rep = P()
    row, pixel, column = P("batch", None, None), P("batch", "pix", None), P("batch", None, "pix")
    in_specs = (row, pixel, pixel, column, P("batch", None), P("batch", None), row, column) + (rep,) * 18
    out_specs = (row, column, row, pixel, pixel) + (rep,) * 18
    body = functools.partial(local, n_pix=n_pix, n_batch=n_batch)
    return jax.shard_map(body, mesh=mesh, in_specs=in_specs, out_specs=out_specs, check_vma=False)
```

```python
import functools
import math

import jax
import jax.numpy as jnp
import numpy as np
from jax import lax
from jax.experimental import pallas as pl
from jax.experimental.pallas import tpu as pltpu
from jax.sharding import PartitionSpec as P

HEADS = 8
EPS = 1e-05
PENALTY = 10000.0
F32 = jnp.float32
LOW = jnp.bfloat16
HIGH = lax.Precision.HIGHEST
CURVE = math.sqrt(2.0 / math.pi)
CUBE = 0.044715
MIB = 1 << 20
PARTS = 4

T_CROSS, T_SELF, T_SELFOUT, T_EMBED, T_HIDDEN = 0, 1, 4, 5, 8


def up(n, m):
    return (n + m - 1) // m * m


def nn(a, b, precision=None):
    return lax.dot_general(a, b, (((1,), (0,)), ((), ())), precision=precision, preferred_element_type=F32)


def nt(a, b, precision=None):
    return lax.dot_general(a, b, (((1,), (1,)), ((), ())), precision=precision, preferred_element_type=F32)


def tn(a, b, precision=None):
    return lax.dot_general(a, b, (((0,), (0,)), ((), ())), precision=precision, preferred_element_type=F32)


def head_mask(width):
    shape = (HEADS, 1, width)
    head = width // HEADS
    return lax.broadcasted_iota(jnp.int32, shape, 2) // head == lax.broadcasted_iota(jnp.int32, shape, 0)


def spread(x, mask):
    rows, width = x.shape
    return jnp.where(mask, x[None], 0.0).reshape(HEADS * rows, width)


def gather_heads(x, mask):
    total, width = x.shape
    return jnp.sum(jnp.where(mask, x.reshape(HEADS, total // HEADS, width), 0.0), 0)


def spread_low(x, mask):
    return spread(x, mask).astype(LOW)


def head_onehot(width, lanes, transposed=False):
    head = width // HEADS
    if transposed:
        shape, a, b = (width, lanes), 0, 1
    else:
        shape, a, b = (lanes, width), 1, 0
    hit = lax.broadcasted_iota(jnp.int32, shape, a) // head == lax.broadcasted_iota(jnp.int32, shape, b)
    return hit.astype(F32)


def slabs_in(scr, value):
    for t in range(scr.shape[0]):
        scr[t] = value[:, t * 128:(t + 1) * 128]


def take_image(scr, image, count, images):
    rows = pl.ds(image, count, images)
    return jnp.concatenate([scr[t, rows, :] for t in range(scr.shape[0])], 1)


def put_image(scr, image, count, images, value):
    for t in range(scr.shape[0]):
        scr[t, pl.ds(image, count, images), :] = value[:, t * 128:(t + 1) * 128]


def slabs(rows, columns):
    return pltpu.VMEM((columns // 128, rows, 128), F32)


def cost(flops, nbytes, trans=0):
    return pl.CostEstimate(flops=int(flops), bytes_accessed=int(nbytes), transcendentals=int(trans))


def whole(x):
    shape = x.shape
    return pl.BlockSpec(shape, lambda *_: (0,) * len(shape))


def params(mib):
    return pltpu.CompilerParams(vmem_limit_bytes=mib * MIB, dimension_semantics=("arbitrary",))


def of_step(keys, n, i):
    key = keys[-1]
    for j in range(len(keys) - 2, -1, -1):
        key = jnp.where(i < (j + 1) * n, keys[j], key)
    return key


def turned_heads(x, fill):
    return jnp.transpose(jnp.concatenate([x, fill], 0))[:, 0:x.shape[0]].astype(LOW)


def attend_kernel(keys, n, me_ref, q_ref, f_ref, bits_ref, flag_ref, wq_ref, bq_ref, wkv_ref, vb_ref, elo_ref, ehi_ref,
                  mc_ref, mf_ref, e_ref, kv_ref, cq_ref, *refs):
    pays = refs[:len(keys)]
    mc_scr, q_scr, w_scr, all_scr, wq_scr, wkv_scr, vb_scr, pay_ref = refs[len(keys):]
    i = pl.program_id(0)
    images = flag_ref.shape[0]
    image = (me_ref[0] ^ of_step(keys, n, i)) * n + i % n
    width = q_ref.shape[1]
    count = q_ref.shape[0] // images
    rows = q_scr.shape[0]
    pixels = f_ref.shape[1]
    tall = rows + HEADS
    head = width // HEADS

    @pl.when(i == 0)
    def _():
        q_scr[...] = jnp.zeros_like(q_scr)
        w_scr[...] = jnp.zeros_like(w_scr)
        slabs_in(all_scr, q_ref[...])
        wq_scr[...] = wq_ref[...].astype(LOW)
        wkv_scr[0:width] = jnp.transpose(wkv_ref[:, :width]).astype(LOW)
        wkv_scr[width:] = jnp.transpose(wkv_ref[:, width:]).astype(LOW)
        vb_scr[...] = jnp.transpose(jnp.broadcast_to(vb_ref[...], (128, width)))
        pay_ref[...] = jnp.zeros_like(pay_ref)
        slabs_in(mc_scr, mc_ref[...].astype(F32).reshape(mc_ref.shape[0] * images, mc_ref.shape[2]))

    matched = mc_ref.shape[0]
    pay_ref[tall:tall + matched] = nn(take_image(mc_scr, image, matched, images).astype(LOW), mf_ref[0])
    q_scr[0:count] = take_image(all_scr, image, count, images)
    w_scr[:, 0:count] = jnp.where(flag_ref[pl.ds(image, 1), :] > 0, 65535, bits_ref[0])

    scale = 1.0 / math.sqrt(head)
    cq = ((nn(q_scr[...].astype(LOW), wq_scr[...]) + bq_ref[...]) * scale).astype(LOW).astype(F32)
    cq_ref[0] = cq

    bits = w_scr[...]
    low = (bits & 255).astype(F32).astype(LOW)
    high = (bits >> 8).astype(F32).astype(LOW)
    byte = (tn(low, elo_ref[...]) + tn(high, ehi_ref[...])).astype(jnp.int32)
    shift = lax.broadcasted_iota(jnp.int32, (rows, pixels), 1) & 7
    pen = jnp.where(((byte >> shift) & 1) == 1, 0.0, -PENALTY)

    keyval = nt(wkv_scr[...], f_ref[0])
    ck = keyval[:width].astype(LOW)
    cv = (keyval[width:] + jnp.concatenate([vb_scr[...]] * (pixels // 128), 1)).astype(LOW)
    kv_ref[0, :width] = ck
    kv_ref[0, width:] = cv

    def scores(h):
        at = slice(h * head, (h + 1) * head)
        return nn(cq[:, at].astype(LOW), ck[at]) + pen

    lane = lax.broadcasted_iota(jnp.int32, (rows, 128), 1)
    stats = jnp.zeros((rows, 128), F32)
    parts = []
    following = scores(0)
    for h in range(HEADS):
        s = following
        if h + 1 < HEADS:
            following = scores(h + 1)
        m = jnp.max(s, -1, keepdims=True)
        e = jnp.exp(s - m)
        total = jnp.sum(e, -1, keepdims=True)
        e_low = e.astype(LOW)
        e_ref[0, h] = e_low
        parts.append(nt(cv[h * head:(h + 1) * head], e_low))
        stats = jnp.where(lane == h, m, stats)
        stats = jnp.where(lane == HEADS + h, total, stats)
    pay_ref[0:rows] = jnp.transpose(jnp.concatenate(parts, 0))
    full = jnp.concatenate([stats, jnp.ones((128 - rows, 128), F32)], 0)
    turned = jnp.transpose(full)
    pay_ref[rows:tall, 0:128] = turned[0:HEADS]
    pay_ref[rows:tall, 128:256] = turned[HEADS:2 * HEADS]
    for j, out in enumerate(pays):
        @pl.when(i // n == j)
        def _(out=out):
            out[0] = pay_ref[...]


def attend(keys, me, queries, features, bits, reopen_flags, query_weight, query_bias, keyval_weight, value_bias,
           mask_cotan, mask_features, parts):
    images, pixels, width = features.shape
    words, count = bits.shape[1:]
    rows = up(count, 8)
    pixel = np.arange(pixels)
    word = np.arange(words)
    here = pixel[None, :] // 16 == word[:, None]
    e_lo = (here & (pixel[None, :] % 16 < 8)).astype(LOW)
    e_hi = (here & (pixel[None, :] % 16 >= 8)).astype(LOW)
    n = images // parts
    steps = n * len(keys)

    def theirs(*shape):
        return pl.BlockSpec(
            (1,) + shape, lambda i, me: ((me[0] ^ of_step(keys, n, i)) * n + i % n,) + (0,) * len(shape))

    def of_key(j, *shape):
        return pl.BlockSpec((1,) + shape, lambda i, me: (jnp.clip(i - j * n, 0, n - 1),) + (0,) * len(shape))

    per = lambda *shape: pl.BlockSpec((1,) + shape, lambda i, me: (i,) + (0,) * len(shape))
    args = (queries, features, bits, reopen_flags, query_weight, query_bias[None], keyval_weight, value_bias[None], e_lo, e_hi,
            mask_cotan, mask_features)
    matched, _, wide = mask_cotan.shape
    in_specs = [whole(a) for a in args]
    in_specs[1] = theirs(pixels, width)
    in_specs[2] = theirs(words, count)
    in_specs[11] = theirs(wide, width)
    flops = 2 * steps * (pixels * width * 2 * width + 2 * HEADS * rows * pixels * width)
    nbytes = steps * (pixels * width * 6 + HEADS * rows * pixels * 2)
    tall = rows + HEADS + up(matched, 8)
    nbytes += steps * wide * (width + matched) * 2
    out_shape = [
        jax.ShapeDtypeStruct((steps, HEADS, rows, pixels), LOW),
        jax.ShapeDtypeStruct((steps, 2 * width, pixels), LOW),
        jax.ShapeDtypeStruct((steps, rows, width), F32),
    ]
    out_shape += [jax.ShapeDtypeStruct((n, tall, width), F32)] * len(keys)
    out_specs = [per(HEADS, rows, pixels), per(2 * width, pixels), per(rows, width)]
    out_specs += [of_key(j, tall, width) for j in range(len(keys))]
    return pl.pallas_call(
        functools.partial(attend_kernel, keys, n),
        grid_spec=pltpu.PrefetchScalarGridSpec(
            num_scalar_prefetch=1,
            grid=(steps,),
            in_specs=in_specs,
            out_specs=tuple(out_specs),
            scratch_shapes=[
                slabs(matched * images, wide),
                pltpu.VMEM((rows, width), F32),
                pltpu.VMEM((words, rows), jnp.int32),
                slabs(count * images, width),
                pltpu.VMEM((width, width), LOW),
                pltpu.VMEM((2 * width, width), LOW),
                pltpu.VMEM((width, 128), F32),
                pltpu.VMEM((tall, width), F32),
            ],
        ),
        out_shape=tuple(out_shape),
        compiler_params=params(60),
        cost_estimate=cost(flops, nbytes, steps * HEADS * rows * pixels),
        name="attend",
    )(me, *args)


def combine_kernel(rows, *refs):
    parts, out_ref = refs[:-1], refs[-1]
    images, full, width = out_ref.shape
    tall = rows + HEADS
    onehot = head_onehot(width, HEADS)
    for i in range(images):
        ms = [p[i, rows:tall, 0:128] for p in parts]
        ls = [p[i, rows:tall, 128:256] for p in parts]
        top = functools.reduce(jnp.maximum, ms)
        rs = [jnp.exp(m - top) for m in ms]
        total = sum(r * l for r, l in zip(rs, ls))
        acc = jnp.zeros((rows, width), F32)
        for p, r in zip(parts, rs):
            acc = acc + p[i, 0:rows] * tn(r / total, onehot, HIGH)[0:rows]
        es = functools.reduce(jnp.add, [p[i, tall:] for p in parts])
        out_ref[i, 0:rows] = acc
        out_ref[i, rows:tall, 0:128] = top
        out_ref[i, rows:tall, 128:256] = total
        out_ref[i, tall:] = es


def combine(parts, rows):
    shape = parts[0].shape
    return pl.pallas_call(
        functools.partial(combine_kernel, rows),
        out_shape=jax.ShapeDtypeStruct(shape, F32),
        compiler_params=pltpu.CompilerParams(vmem_limit_bytes=32 * MIB),
        cost_estimate=cost(1e6, 5 * 4 * math.prod(shape)),
        name="combine",
    )(*parts)


def lower_kernel(*refs):
    n = len(refs) // 2
    for raw, out in zip(refs[:n], refs[n:]):
        out[...] = raw[...].astype(LOW)


def lower(weights):
    out_shape = tuple(jax.ShapeDtypeStruct(w.shape, LOW) for w in weights)
    size = sum(math.prod(w.shape) for w in weights)
    return pl.pallas_call(
        lower_kernel,
        out_shape=out_shape,
        compiler_params=pltpu.CompilerParams(vmem_limit_bytes=60 * MIB),
        cost_estimate=cost(size, 6 * size),
        name="lower",
    )(*weights)


def norm_forward(x, gain, bias):
    centre = x - jnp.mean(x, -1, keepdims=True)
    inverse = lax.rsqrt(jnp.mean(centre * centre, -1, keepdims=True) + EPS)
    normed = centre * inverse
    return normed * gain + bias, normed, inverse


def norm_backward(normed, inverse, gain, grad):
    dnormed = grad * gain
    return inverse * (
        dnormed - jnp.mean(dnormed, -1, keepdims=True) - normed * jnp.mean(dnormed * normed, -1, keepdims=True)
    )


def gelu_pair(x):
    square = x * x
    t = jnp.tanh(x * (CURVE + (CURVE * CUBE) * square))
    half = 0.5 + 0.5 * t
    slope = half + (0.5 * x) * (1.0 - t * t) * (CURVE + (3.0 * CURVE * CUBE) * square)
    return x * half, slope


def column_sum(x):
    return jnp.sum(x, 0, keepdims=True)


def chain_kernel(
    pieces, me_ref, *refs
):
    att_parts, refs = refs[:pieces], refs[pieces:]
    locals_, refs = refs[:PARTS], refs[PARTS:]
    chain_body(me_ref, att_parts, locals_, *refs)


def chain_body(
    me_ref, att_parts, locals_, q_ref, match_ref, cot_ref, wc_ref, bc_ref, gain_ref, nbias_ref, ws_ref, bs_ref, wso_ref,
    bso_ref, wh_ref, bh_ref, who_ref, bho_ref, we_ref, be_ref,
    x3_ref, emb_ref, dn_ref, dt_ref, dp1_ref, mine_ref, away_ref,
    g_ref, all_scr, cot_scr, out_scr, att_scr, emb_scr, loc_scr,
    q_scr, sq_scr, sk_scr, sv_scr, so_scr, pr_scr, h_scr, gp_scr, dso_scr, dm_scr
):
    step = pl.program_id(0)
    batch, rows, width = dn_ref.shape
    matched = match_ref.shape[1]
    count, images = cot_ref.shape[:2]
    tall = rows + HEADS
    flat = batch * rows
    hidden = wh_ref.shape[1]
    scale = 1.0 / math.sqrt(width // HEADS)
    hm = head_mask(width)

    @pl.when(step == 0)
    def _():
        q_scr[...] = jnp.zeros_like(q_scr)
        g_ref[...] = jnp.zeros_like(g_ref)
        n = att_parts[0].shape[0]
        for k, part in enumerate(att_parts):
            att_scr[pl.ds((me_ref[0] ^ k) * n, n)] = part[...]
        n = locals_[0].shape[0]
        for k, part in enumerate(locals_):
            loc_scr[pl.ds((me_ref[0] ^ k) * n, n)] = part[:, rows:tall]
        slabs_in(all_scr, q_ref[...])
        slabs_in(cot_scr, cot_ref[...].astype(F32).reshape(count * images, width))

    def put(tile, value):
        g_ref[tile * width:(tile + 1) * width] += value

    bias_at = (T_HIDDEN + 2 * (hidden // width)) * width

    def put_bias(index, value):
        g_ref[bias_at + index:bias_at + index + 1] += value

    first = step * batch
    for b in range(batch):
        q_scr[b, 0:count] = take_image(all_scr, first + b, count, images)
    att = att_scr[pl.ds(first, batch), 0:rows].reshape(flat, width)
    att_low = att.astype(LOW)
    queries = q_scr[...].reshape(flat, width)
    x1, n1, i1 = norm_forward(queries + nn(att_low, wc_ref[...]) + bc_ref[...], gain_ref[0:1], nbias_ref[0:1])
    x1_low = x1.astype(LOW)
    mixed = nn(x1_low, ws_ref[...])
    three = (batch, rows, width)
    sq_scr[...] = ((mixed[:, :width] + bs_ref[0:1]) * scale).reshape(three)
    sk_scr[...] = mixed[:, width:2 * width].reshape(three)
    sv_scr[...] = (mixed[:, 2 * width:] + bs_ref[1:2]).reshape(three)

    head = width // HEADS
    lanes = lambda h: slice(h * 128, (h + 1) * 128)
    fill = jnp.zeros((128 - rows, width), F32)

    def tall_heads(x):
        return spread_low(jnp.concatenate([x, fill], 0), hm)

    def turn(x):
        return jnp.transpose(jnp.concatenate([x, fill], 0))[:, 0:rows].astype(LOW)

    def by_head(turned, x):
        return jnp.transpose(jnp.concatenate(
            [nn(turned[h * head:(h + 1) * head], x[:, lanes(h)]) for h in range(HEADS)], 0))[0:rows]

    for b in range(batch):
        ss = nt(sk_scr[b].astype(LOW), tall_heads(sq_scr[b]))
        keys = lax.broadcasted_iota(jnp.int32, ss.shape, 0)
        ss = jnp.where(keys < count, ss, -1e30)
        p = jnp.exp(ss - jnp.max(ss, 0, keepdims=True))
        p = p * (1.0 / jnp.sum(p, 0, keepdims=True))
        pr_scr[b] = p
        so_scr[b] = by_head(turn(sv_scr[b]), p.astype(LOW))
    so_low = so_scr[...].reshape(flat, width).astype(LOW)
    x2, n2, i2 = norm_forward(x1 + nn(so_low, wso_ref[...]) + bso_ref[...], gain_ref[1:2], nbias_ref[1:2])
    x2_low = x2.astype(LOW)
    block = 2 * width

    def ff_forward(j, acc):
        cols = pl.ds(pl.multiple_of(j * block, block), block)
        h, slope = gelu_pair(nn(x2_low, wh_ref[:, cols]) + bh_ref[:, cols])
        h = h.astype(LOW)
        h_scr[:, cols] = h
        gp_scr[:, cols] = slope.astype(gp_scr.dtype)
        return acc + nn(h, who_ref[cols, :])

    ff = lax.fori_loop(0, hidden // block, ff_forward, jnp.zeros((flat, width), F32))
    x3, n3, i3 = norm_forward(x2 + ff + bho_ref[...], gain_ref[2:3], nbias_ref[2:3])
    for b in range(batch):
        put_image(out_scr, first + b, count, images, x3[b * rows:b * rows + count])

    x3_low = x3.astype(LOW)
    h1, slope1 = gelu_pair(nn(x3_low, we_ref[0]) + be_ref[0:1])
    h1 = h1.astype(LOW)
    h2, slope2 = gelu_pair(nn(h1, we_ref[1]) + be_ref[1:2])
    h2 = h2.astype(LOW)
    emb = nn(h2, we_ref[2]) + be_ref[2:3]
    for b in range(batch):
        put_image(emb_scr, first + b, count, images, emb[b * rows:b * rows + count])

    grads = []
    for b in range(batch):
        spots = match_ref[pl.ds(first + b, 1), :]
        pick = (lax.broadcasted_iota(jnp.int32, (rows, matched), 0) == spots).astype(F32).astype(LOW)
        grads.append(nn(pick, att_scr[first + b, tall:tall + matched].astype(LOW)))
    dz3 = jnp.concatenate(grads, 0)
    dz3_low = dz3.astype(LOW)
    put(T_EMBED + 2, tn(h2, dz3_low))
    put_bias(19, column_sum(dz3_low.astype(F32)))
    dz2 = (nt(dz3_low, we_ref[2]) * slope2).astype(LOW)
    put(T_EMBED + 1, tn(h1, dz2))
    put_bias(18, column_sum(dz2.astype(F32)))
    dz1 = (nt(dz2, we_ref[1]) * slope1).astype(LOW)
    put(T_EMBED, tn(x3_low, dz1))
    put_bias(17, column_sum(dz1.astype(F32)))
    for b in range(batch):
        q_scr[b, 0:count] = take_image(cot_scr, first + b, count, images)
    dx3 = q_scr[...].reshape(flat, width) + nt(dz1, we_ref[0])
    put_bias(3, column_sum(dx3 * n3))
    put_bias(6, column_sum(dx3))
    dp3 = norm_backward(n3, i3, gain_ref[2:3], dx3)
    dff = dp3.astype(LOW)
    put_bias(16, column_sum(dff.astype(F32)))

    def ff_backward(j, acc):
        cols = pl.ds(pl.multiple_of(j * block, block), block)
        base = (T_HIDDEN + hidden // width) * width
        spot = pl.ds(pl.multiple_of(base + j * block, block), block)
        g_ref[spot] += tn(h_scr[:, cols], dff)
        dz = (nt(dff, who_ref[cols, :]) * gp_scr[:, cols].astype(F32)).astype(LOW)
        gh = tn(x2_low, dz)
        sums = column_sum(dz.astype(F32))
        for t in range(block // width):
            tile = pl.ds(pl.multiple_of(T_HIDDEN * width + j * block + t * width, width), width)
            g_ref[tile] += gh[:, t * width:(t + 1) * width]
            g_ref[pl.ds(bias_at + 8 + j * (block // width) + t, 1)] += sums[:, t * width:(t + 1) * width]
        return acc + nt(dz, wh_ref[:, cols])

    dx2 = dp3 + lax.fori_loop(0, hidden // block, ff_backward, jnp.zeros((flat, width), F32))
    put_bias(2, column_sum(dx2 * n2))
    put_bias(5, column_sum(dx2))
    dp2 = norm_backward(n2, i2, gain_ref[1:2], dx2)
    dsa = dp2.astype(LOW)
    put(T_SELFOUT, tn(so_low, dsa))
    put_bias(7, column_sum(dsa.astype(F32)))
    dso_scr[...] = nt(dsa, wso_ref[...]).reshape(three)

    for b in range(batch):
        dsox = tall_heads(dso_scr[b])
        p = pr_scr[b]
        dp = nt(sv_scr[b].astype(LOW), dsox)
        dss = (p * (dp - jnp.sum(p * dp, 0, keepdims=True))).astype(LOW)
        dm_scr[b, :, 0:width] = by_head(turn(sk_scr[b]), dss) * scale
        dm_scr[b, :, width:2 * width] = nn(dss, tall_heads(sq_scr[b]))
        dm_scr[b, :, 2 * width:] = nn(p.astype(LOW), dsox)

    dm = dm_scr[...].reshape(flat, 3 * width).astype(LOW)
    gs = tn(x1_low, dm)
    for t in range(3):
        put(T_SELF + t, gs[:, t * width:(t + 1) * width])
    put_bias(20, column_sum(dm[:, :width].astype(F32)))
    put_bias(21, column_sum(dm[:, 2 * width:].astype(F32)))
    dx1 = dp2 + nt(dm, ws_ref[...])
    put_bias(1, column_sum(dx1 * n1))
    put_bias(4, column_sum(dx1))
    dp1 = norm_backward(n1, i1, gain_ref[0:1], dx1)
    dp1_ref[...] = dp1.reshape(three)
    dca = dp1.astype(LOW)
    put(T_CROSS, tn(att_low, dca))
    put_bias(0, column_sum(dca.astype(F32)))
    d_att = nt(dca, wc_ref[...]).reshape(three)
    onehot = head_onehot(width, HEADS)
    back = head_onehot(width, 128, True)
    for b in range(batch):
        top = att_scr[first + b, rows:tall, 0:128]
        total = att_scr[first + b, rows:tall, 128:256]
        ratio = jnp.exp(loc_scr[first + b, :, 0:128] - top) / total
        dn = d_att[b] * tn(ratio, onehot, HIGH)[0:rows]
        dn_ref[b] = dn
        dt_ref[b] = -nn(dn * att_scr[first + b, 0:rows], back, HIGH)

    @pl.when(step == 1)
    def _():
        x3_ref[...] = jnp.concatenate([out_scr[t] for t in range(out_scr.shape[0])], 1)
        emb_ref[...] = jnp.concatenate([emb_scr[t] for t in range(emb_scr.shape[0])], 1)
        share = mine_ref.shape[0]
        at = me_ref[1] * 2 + me_ref[2]
        mine_ref[...] = g_ref[pl.ds(pl.multiple_of(at * share, 8), share)]
        away_ref[...] = g_ref[pl.ds(pl.multiple_of((at + 1 - 2 * me_ref[2]) * share, 8), share)]


def chain(me, parts, pays, queries, matched, query_cotan, weights, n_pix):
    full, width = parts[0].shape[1:]
    images = pays[0].shape[0] * len(pays)
    count = query_cotan.shape[0]
    rows = up(count, 8)
    batch = images // 2
    hidden = weights[8].shape[1]
    tiles = T_HIDDEN + 2 * (hidden // width)
    grads = up(tiles * width + 22, 256)
    half = lambda *shape: pl.BlockSpec((batch,) + shape, lambda i, *_: (i,) + (0,) * len(shape))
    pieces = len(parts)
    args = tuple(parts) + tuple(pays) + (queries, matched, query_cotan) + weights
    in_specs = [whole(a) for a in args]
    out_shape = (
        jax.ShapeDtypeStruct((count * images, width), F32),
        jax.ShapeDtypeStruct((count * images, width), F32),
        jax.ShapeDtypeStruct((images, rows, width), F32),
        jax.ShapeDtypeStruct((images, rows, 128), F32),
        jax.ShapeDtypeStruct((images, rows, width), F32),
        jax.ShapeDtypeStruct((grads // n_pix // 2, width), F32),
        jax.ShapeDtypeStruct((grads // n_pix // 2, width), F32),
    )
    flat = batch * rows
    three = (batch, rows, width)
    many = slabs(count * images, width)
    return pl.pallas_call(
        functools.partial(chain_kernel, pieces),
        grid_spec=pltpu.PrefetchScalarGridSpec(
            num_scalar_prefetch=1,
            grid=(2,),
            in_specs=in_specs,
            out_specs=(whole(out_shape[0]), whole(out_shape[1]), half(rows, width), half(rows, 128), half(rows, width),
                       whole(out_shape[5]), whole(out_shape[6])),
            scratch_shapes=[
                pltpu.VMEM((grads, width), F32),
                many,
                many,
                many,
                pltpu.VMEM((images, full, width), F32),
                many,
                pltpu.VMEM((images, HEADS, width), F32),
                pltpu.VMEM(three, F32),
                pltpu.VMEM(three, F32),
                pltpu.VMEM(three, F32),
                pltpu.VMEM(three, F32),
                pltpu.VMEM(three, F32),
                pltpu.VMEM((batch, rows, HEADS * 128), F32),
                pltpu.VMEM((flat, hidden), LOW),
                pltpu.VMEM((flat, hidden), LOW),
                pltpu.VMEM(three, F32),
                pltpu.VMEM((batch, rows, 3 * width), F32),
            ],
        ),
        out_shape=out_shape,
        compiler_params=params(62),
        cost_estimate=cost(2 * 8e9, 20e6, 4e6),
        name="chain",
    )(me, *args)


def mask_out_kernel(emb_ref, match_ref, mc_ref, mf_ref, logit_old, grad_old, logit_ref, grad_ref, chosen_scr,
                    emb_scr, low_scr, logit_scr, mc_scr):
    images, matched, width = chosen_scr.shape
    count = logit_ref.shape[0] // images
    part = mc_ref.shape[2]

    @pl.when(pl.program_id(0) == 0)
    def _():
        slabs_in(emb_scr, emb_ref[...])
        low_scr[...] = jnp.zeros_like(low_scr)
        for b in range(images):
            pick = (lax.broadcasted_iota(jnp.int32, (count, matched), 0) == match_ref[b:b + 1, :]).astype(F32).astype(LOW)
            emb = take_image(emb_scr, b, count, images).astype(LOW)
            low_scr[b, 0:count] = emb.astype(F32)
            chosen_scr[b] = tn(pick, emb)

    slabs_in(mc_scr, mc_ref[...].astype(F32).reshape(matched * images, part))
    for b in range(images):
        put_image(logit_scr, b, count, images, nt(low_scr[b].astype(LOW), mf_ref[b])[0:count])
        grad_ref[b] = tn(take_image(mc_scr, b, matched, images).astype(LOW), chosen_scr[b].astype(LOW))
    for t in range(part // 128):
        logit_ref[:, t * 128:(t + 1) * 128] = logit_scr[t]


def mask_out(emb, matched_queries, mask_cotan, mask_features, count, pieces, steps, old=None):
    matched, images, pixels = mask_cotan.shape
    width = emb.shape[1]
    part = pixels // pieces
    first, last = steps
    out_shape = (
        jax.ShapeDtypeStruct((count * images, pixels), F32),
        jax.ShapeDtypeStruct((images, pixels, width), F32),
    )
    args = (emb, matched_queries, mask_cotan, mask_features)
    here = pl.BlockSpec(memory_space=pl.ANY)
    kernel = mask_out_kernel
    aliases = {}
    specs = []
    if old is None:
        def kernel(a, b, c, d, *rest):
            mask_out_kernel(a, b, c, d, None, None, *rest)
    else:
        args += old
        aliases = {4: 0, 5: 1}
        specs = [here, here]
    return pl.pallas_call(
        kernel,
        grid=(last - first,),
        in_specs=[
            whole(emb),
            whole(matched_queries),
            pl.BlockSpec((matched, images, part), lambda j: (0, 0, j + first)),
            pl.BlockSpec((images, part, width), lambda j: (0, j + first, 0)),
        ] + specs,
        out_specs=(
            pl.BlockSpec((count * images, part), lambda j: (0, j + first)),
            pl.BlockSpec((images, part, width), lambda j: (0, j + first, 0)),
        ),
        out_shape=out_shape,
        input_output_aliases=aliases,
        scratch_shapes=[pltpu.VMEM((images, matched, width), F32),
                        slabs(count * images, width), pltpu.VMEM((images, up(count, 8), width), F32),
                        slabs(count * images, part), slabs(matched * images, part)],
        compiler_params=params(60),
        cost_estimate=cost(
            2 * images * pixels * width * 160 * (last - first) / pieces,
            images * pixels * (width * 6 + count * 4 + matched * 2) * (last - first) / pieces),
        name="mask_out",
    )(*args)


def attend_back_kernel(keys, n, last, me_ref, e_ref, kv_ref, f_ref, cq_ref, dn_ref, dt_ref, wkv_ref, acc_old, vb_old,
                       fg_ref, qps, acc_ref, vb_ref, g_ref, w_scr):
    i = pl.program_id(0)
    rows, width = cq_ref.shape[1:]
    pixels = f_ref.shape[1]
    head = width // HEADS

    @pl.when(i == 0)
    def _():
        acc_ref[...] = jnp.zeros_like(acc_ref) if acc_old is None else acc_old[...]
        vb_ref[...] = jnp.zeros_like(vb_ref) if vb_old is None else vb_old[...]
        w_scr[0:width] = jnp.transpose(wkv_ref[:, :width]).astype(LOW)
        w_scr[width:] = jnp.transpose(wkv_ref[:, width:]).astype(LOW)

    dn = dn_ref[0]
    fill = jnp.zeros((128 - rows, width), F32)
    cq_turned = turned_heads(cq_ref[0], fill)
    dn_turned = turned_heads(dn, fill)

    def weigh(h):
        at = slice(h * head, (h + 1) * head)
        return nn(dn[:, at].astype(LOW), kv_ref[0, width + h * head:width + (h + 1) * head]) + dt_ref[0, :, h:h + 1]

    parts, keys_sum, values_sum = [], [], []
    following = weigh(0)
    for h in range(HEADS):
        at = slice(h * head, (h + 1) * head)
        dw = following
        if h + 1 < HEADS:
            following = weigh(h + 1)
        e_low = e_ref[0, h]
        ds = (e_low.astype(F32) * dw).astype(LOW)
        values_sum.append(nn(dn_turned[at], e_low).astype(LOW))
        keys_sum.append(nn(cq_turned[at], ds).astype(LOW))
        parts.append(nt(kv_ref[0, at], ds))
    part = jnp.transpose(jnp.concatenate(parts, 0))
    for j, out in enumerate(qps):
        @pl.when(i // n == j)
        def _(out=out):
            out[0] = part
    turned = jnp.concatenate(keys_sum + values_sum, 0)
    acc_ref[...] += nn(turned, f_ref[0])
    summed = turned[width:].astype(F32)
    lanes_sum = summed[:, 0:128]
    for t in range(1, pixels // 128):
        lanes_sum = lanes_sum + summed[:, t * 128:(t + 1) * 128]
    vb_ref[...] += lanes_sum
    fg_ref[0] = tn(turned, w_scr[...])

    if last:
        @pl.when(i == pl.num_programs(0) - 1)
        def _():
            sums = jnp.sum(jnp.transpose(vb_ref[...]), 0, keepdims=True)
            fill = jnp.zeros((g_ref.shape[0] - 2 * width - 1, width), F32)
            g_ref[...] = jnp.concatenate(
                [jnp.transpose(acc_ref[0:width]), jnp.transpose(acc_ref[width:]), sums, fill], 0)


def attend_back(keys, me, kept, offset, features, dn, dt, keyval_weight, old, last):
    e, kv, cq = kept
    images, pixels, width = features.shape
    rows = cq.shape[1]
    n = images // PARTS
    steps = n * len(keys)

    def theirs(*shape):
        return pl.BlockSpec(
            (1,) + shape, lambda i, me: ((me[0] ^ of_step(keys, n, i)) * n + i % n,) + (0,) * len(shape))

    def of_key(j, *shape):
        return pl.BlockSpec((1,) + shape, lambda i, me: (jnp.clip(i - j * n, 0, n - 1),) + (0,) * len(shape))

    per = lambda *shape: pl.BlockSpec((1,) + shape, lambda i, me: (i + offset,) + (0,) * len(shape))
    tall = HEADS * rows
    flops = 2 * steps * (4 * tall * pixels * width + 4 * pixels * width * width)
    nbytes = steps * (tall * pixels * 2 + pixels * width * 10)
    sums = (jax.ShapeDtypeStruct((2 * width, width), F32), jax.ShapeDtypeStruct((width, 128), F32))
    fg = jax.ShapeDtypeStruct((images, pixels, width), F32)
    qps = (jax.ShapeDtypeStruct((n, rows, width), F32),) * len(keys)
    scratch = [pltpu.VMEM((2 * width, width), LOW)]
    middle = sums
    if last:
        middle = (jax.ShapeDtypeStruct((2 * width + 32, width), F32),)
        scratch = [pltpu.VMEM(x.shape, F32) for x in sums] + scratch
    args = (e, kv, features, cq, dn, dt, keyval_weight)
    in_specs = [per(HEADS, rows, pixels), per(2 * width, pixels), theirs(pixels, width),
                per(rows, width), theirs(rows, width), theirs(rows, 128), whole(keyval_weight)]
    aliases = {}

    def kernel(*refs):
        ins, refs = refs[:8], refs[8:]
        w_scr, refs = refs[-1], refs[:-1]
        acc_old = vb_old = g = None
        if old is not None:
            acc_old, vb_old, refs = refs[1], refs[2], refs[3:]
        fg, refs = refs[0], refs[1:]
        if last:
            g, refs = refs[0], refs[1:]
            qp, (acc, vb) = refs[:len(keys)], refs[len(keys):]
        else:
            (acc, vb), qp = refs[:2], refs[2:]
        attend_back_kernel(keys, n, last, *ins, acc_old, vb_old, fg, qp, acc, vb, g, w_scr)

    if old is not None:
        args += old
        in_specs += [pl.BlockSpec(memory_space=pl.ANY)] + [whole(x) for x in sums]
        aliases = {8: 0}
    return pl.pallas_call(
        kernel,
        grid_spec=pltpu.PrefetchScalarGridSpec(
            num_scalar_prefetch=1,
            grid=(steps,),
            in_specs=in_specs,
            out_specs=(theirs(pixels, width),) + tuple(whole(x) for x in middle) + tuple(
                of_key(j, rows, width) for j in range(len(keys))),
            scratch_shapes=scratch,
        ),
        out_shape=(fg,) + middle + qps,
        input_output_aliases=aliases,
        compiler_params=params(60),
        cost_estimate=cost(flops, nbytes),
        name="attend_back",
    )(me, *args)


def query_sum_kernel(me_ref, *refs):
    parts, kv_ref, outs = refs[:PARTS], refs[PARTS], refs[PARTS + 1:]
    n, rows, width = parts[0].shape
    total = parts[0][...]
    for p in parts[1:]:
        total = total + p[...]
    total = total.reshape(n * rows, width)
    share = kv_ref.shape[0] // PARTS
    for k, out in enumerate(outs):
        out[0:n * rows] = total
        out[n * rows:] = kv_ref[pl.ds(pl.multiple_of((me_ref[0] ^ k) * share, 8), share)]


def query_sum(me, parts, g_kv):
    n, rows, width = parts[0].shape
    args = tuple(parts) + (g_kv,)
    out = jax.ShapeDtypeStruct((n * rows + g_kv.shape[0] // PARTS, width), F32)
    return pl.pallas_call(
        query_sum_kernel,
        grid_spec=pltpu.PrefetchScalarGridSpec(
            num_scalar_prefetch=1, grid=(1,), in_specs=[whole(a) for a in args], out_specs=(whole(out),) * PARTS),
        out_shape=(out,) * PARTS,
        compiler_params=params(16),
        cost_estimate=cost(1e6, 3e6),
        name="query_sum",
    )(me, *args)


def query_back_kernel(pieces, me_ref, *refs):
    parts = refs[:pieces]
    (q_ref, dp_ref, wq_ref, qg_ref, mine_ref, away_ref, scr, sum_scr, all_scr, out_scr, g_scr, tail_scr) = refs[pieces:]
    images, rows, width = dp_ref.shape
    count = q_ref.shape[0] // images
    scale = 1.0 / math.sqrt(width // HEADS)
    n = images // pieces
    kv = jnp.zeros((parts[0].shape[0] - n * rows, width), F32)
    for k, part in enumerate(parts):
        sum_scr[pl.ds((me_ref[0] ^ k) * n, n)] = part[0:n * rows].reshape(n, rows, width)
        kv = kv + part[n * rows:]
    scr[...] = jnp.zeros_like(scr)
    slabs_in(all_scr, q_ref[...])
    for b in range(images):
        scr[b, 0:count] = take_image(all_scr, b, count, images)
    d_cq = (sum_scr[...].reshape(images * rows, width) * scale).astype(LOW)
    out = dp_ref[...] + nt(d_cq, wq_ref[...].astype(LOW)).reshape(images, rows, width)
    for b in range(images):
        put_image(out_scr, b, count, images, out[b, 0:count])
    qg_ref[...] = jnp.concatenate([out_scr[t] for t in range(out_scr.shape[0])], 1)
    g_scr[0:width] = tn(scr[...].reshape(images * rows, width).astype(LOW), d_cq)
    g_scr[width:] = jnp.zeros((g_scr.shape[0] - width, width), F32)
    g_scr[width:width + 1] = column_sum(d_cq.astype(F32))
    share = g_scr.shape[0] // pieces
    small = mine_ref.shape[0]
    tail_scr[0:kv.shape[0]] = kv
    tail_scr[kv.shape[0]:] = g_scr[pl.ds(pl.multiple_of(me_ref[0] * share, 8), share)]
    mine_ref[...] = tail_scr[pl.ds(pl.multiple_of(me_ref[2] * small, 8), small)]
    away_ref[...] = tail_scr[pl.ds(pl.multiple_of((1 - me_ref[2]) * small, 8), small)]


def query_back(me, parts, queries, dp1, query_weight):
    images, rows, width = dp1.shape
    pieces = len(parts)
    args = tuple(parts) + (queries, dp1, query_weight)
    share = parts[0].shape[0] - images // pieces * rows
    full = (width + 32) // pieces + share
    half = jax.ShapeDtypeStruct((full // 2, width), F32)
    out_shape = (jax.ShapeDtypeStruct(queries.shape, F32), half, half)
    return pl.pallas_call(
        functools.partial(query_back_kernel, pieces),
        grid_spec=pltpu.PrefetchScalarGridSpec(
            num_scalar_prefetch=1,
            grid=(1,),
            in_specs=[whole(a) for a in args],
            out_specs=tuple(whole(o) for o in out_shape),
            scratch_shapes=[pltpu.VMEM((images, rows, width), F32), pltpu.VMEM((images, rows, width), F32),
                            slabs(*queries.shape), slabs(*queries.shape), pltpu.VMEM((width + 32, width), F32),
                            pltpu.VMEM((full, width), F32)],
        ),
        out_shape=out_shape,
        compiler_params=params(60),
        cost_estimate=cost(5e8, 8e6),
        name="query_back",
    )(me, *args)


def unpack_kernel(split, me_ref, *refs):
    own, other = refs[:5], refs[5:10]
    (tail, tail2,
     query_ref, query_bias_ref, keyval_ref, value_bias_ref, cross_ref, cross_bias_ref, gain_ref, nbias_ref,
     self_ref, self_bias_ref, selfout_ref, selfout_bias_ref, hidden_ref, hidden_bias_ref, hidout_ref, hidout_bias_ref,
     embed_ref, embed_bias_ref, g, t) = refs[10:]
    pix, core = me_ref[1], me_ref[2]
    width = query_ref.shape[0]
    short = own[1].shape[0]
    places = (((0, 0), (0, 1)), ((1, 0),), ((2, 1),), ((2, 0), (3, 0)), ((1, 1), (3, 1)))
    for half, five in ((core, own), (1 - core, other)):
        for piece, spots in zip(five, places):
            for row, (k, second) in enumerate(spots):
                at = ((pix ^ k) * 2 + half) * 2 + second
                g[pl.ds(pl.multiple_of(at * short, 8), short)] = piece[row * short:(row + 1) * short]
    small = tail.shape[0] // 4
    for half, ref in ((core, tail), (1 - core, tail2)):
        for k in range(4):
            at = (pix ^ k) * 2 + half
            t[pl.ds(pl.multiple_of(at * small, 8), small)] = ref[k * small:(k + 1) * small]

    def tile(n, k=1):
        return g[n * width:(n + k) * width]

    many = hidden_ref.shape[1] // width
    bias = (T_HIDDEN + 2 * many) * width
    cross_ref[...] = tile(T_CROSS)
    selfout_ref[...] = tile(T_SELFOUT)
    embed_ref[...] = tile(T_EMBED, 3)
    hidout_ref[...] = tile(T_HIDDEN + many, many)
    for n in range(3):
        self_ref[:, n * width:(n + 1) * width] = tile(T_SELF + n)
    for n in range(many):
        hidden_ref[:, n * width:(n + 1) * width] = tile(T_HIDDEN + n)
        hidden_bias_ref[:, n * width:(n + 1) * width] = g[bias + 8 + n:bias + 9 + n]
    cross_bias_ref[...] = g[bias:bias + 1]
    gain_ref[...] = g[bias + 1:bias + 4]
    nbias_ref[...] = g[bias + 4:bias + 7]
    selfout_bias_ref[...] = g[bias + 7:bias + 8]
    hidout_bias_ref[...] = g[bias + 16:bias + 17]
    embed_bias_ref[...] = g[bias + 17:bias + 20]
    self_bias_ref[...] = g[bias + 20:bias + 22]
    block = 2 * small
    low, high = [], []
    for k in range(4):
        low.append(t[k * block:k * block + split])
        high.append(t[k * block + split:(k + 1) * block])
    low, high = jnp.concatenate(low, 0), jnp.concatenate(high, 0)
    keyval_ref[:, 0:width] = low[0:width]
    keyval_ref[:, width:] = low[width:2 * width]
    value_bias_ref[...] = low[2 * width:2 * width + 1]
    query_ref[...] = high[0:width]
    query_bias_ref[...] = high[width:width + 1]


def unpack(me, pieces, tails, split, width, hidden):
    args = tuple(pieces) + tuple(tails)
    shapes = ((width, width), (1, width), (width, 2 * width), (1, width), (width, width), (1, width), (3, width), (3, width),
              (width, 3 * width), (2, width), (width, width), (1, width), (width, hidden), (1, hidden), (hidden, width),
              (1, width), (3 * width, width), (3, width))
    out_shape = tuple(jax.ShapeDtypeStruct(shape, F32) for shape in shapes)
    rows = sum(p.shape[0] for p in pieces)
    return pl.pallas_call(
        functools.partial(unpack_kernel, split),
        grid_spec=pltpu.PrefetchScalarGridSpec(
            num_scalar_prefetch=1,
            grid=(1,),
            in_specs=[whole(a) for a in args],
            out_specs=tuple(whole(o) for o in out_shape),
            scratch_shapes=[pltpu.VMEM((rows, width), F32), pltpu.VMEM((2 * tails[0].shape[0], width), F32)],
        ),
        out_shape=out_shape,
        compiler_params=params(32),
        cost_estimate=cost(1e6, 16e6),
        name="unpack",
    )(me, *args)


def beside(*values):
    return lax.optimization_barrier(values)


def swap(x, axis, n, key):
    return lax.ppermute(x, axis, [(d, d ^ key) for d in range(n)])


def scatter_out(x, axis, n):
    me = lax.axis_index(axis)
    chunks = [lax.dynamic_index_in_dim(x, me ^ k, 0, keepdims=False) for k in range(n)]
    return tuple(c if k == 0 else swap(c, axis, n, k) for k, c in enumerate(chunks))


def gather_in(x, axis, n):
    return tuple(x if k == 0 else swap(x, axis, n, k) for k in range(n))


def side(axis, key):
    return (lax.axis_index(axis) // key) % 2


def halve(x, axis, n, key):
    halves = x.reshape((2, -1) + x.shape[1:])
    mine = lax.dynamic_index_in_dim(halves, side(axis, key), 0, keepdims=False)
    away = lax.dynamic_index_in_dim(halves, 1 - side(axis, key), 0, keepdims=False)
    return mine, swap(away, axis, n, key)


def join(mine, other, axis, key):
    first = side(axis, key) == 0
    return jnp.concatenate([jnp.where(first, mine, other), jnp.where(first, other, mine)], 0)


def local(
    queries, features, mask_features, attend_bits, reopen_flags, matched_queries, query_cotan, mask_cotan,
    query_weight, query_bias, keyval_weight, value_bias, cross_out, cross_out_bias, norm_gain, norm_bias,
    self_weight, self_bias, self_out, self_out_bias, hidden_weight, hidden_bias, hidden_out, hidden_out_bias,
    embed_weight, embed_bias, *, n_pix, n_batch,
):
    images, count, width = queries.shape
    hidden = hidden_weight.shape[1]
    rows = up(count, 8)
    tall = rows + HEADS
    pix = lax.axis_index("pix")
    direct = n_pix == 4 and n_batch == 8

    queries = jnp.transpose(queries, (1, 0, 2)).reshape(count * images, width)
    query_cotan = jnp.transpose(query_cotan, (1, 0, 2))
    mask_cotan = jnp.transpose(mask_cotan, (1, 0, 2))
    bits = jnp.transpose(attend_bits, (0, 2, 1))
    core = lax.axis_index("batch") % 2
    chip = lax.axis_index("batch") // 2
    me = jnp.stack([pix if direct else 0 * pix, pix, core, chip]).astype(jnp.int32)

    order = (3, 1, 2, 0)
    e, kv, cq, *pays = attend(order, me, queries, features, bits, reopen_flags, query_weight, query_bias, keyval_weight,
                              value_bias, mask_cotan, mask_features, PARTS)
    kept = (e, kv, cq)
    pays = dict(zip(order, pays))
    got = {k: swap(pays[k], "pix", n_pix, k) if k else pays[k] for k in order} if direct else {}
    pays = [pays[k] for k in range(PARTS)]
    weights = (
        cross_out, cross_out_bias[None], norm_gain, norm_bias, self_weight, self_bias, self_out, self_out_bias[None],
        hidden_weight, hidden_bias[None], hidden_out, hidden_out_bias[None], embed_weight, embed_bias,
    )
    large = (0, 4, 6, 8, 10, 12)
    if direct:
        share = combine([got[k] for k in range(PARTS)], rows)
        share, *raw = beside(share, *[weights[k] for k in large])
        att = gather_in(share, "pix", n_pix)
    else:
        raw = [weights[k] for k in large]
        pay = jnp.concatenate(pays, 0)
        top = lax.pmax(pay[:, rows:tall, :128], "pix")
        ratio = jnp.exp(pay[:, rows:tall, :128] - top)

        def widen(x):
            return jnp.repeat(jnp.transpose(x, (0, 2, 1))[:, :rows], width // HEADS, axis=2)

        numer, total, es = lax.psum(
            (pay[:, :rows] * widen(ratio), pay[:, rows:tall, 128:] * ratio, pay[:, tall:]), "pix")
        att = (jnp.concatenate([numer / widen(total), jnp.concatenate([top, total], 2), es], 1),)
    lowered = dict(zip(large, lower(raw)))
    weights = tuple(lowered.get(k, w) for k, w in enumerate(weights))
    x3, emb, dn, dt, dp1, mine, away = chain(
        me, att, pays, queries, matched_queries, query_cotan, weights, n_pix)

    def unflat(x):
        return jnp.transpose(x.reshape(count, images, -1), (1, 0, 2))

    blocks = mask_features.shape[1] // 512
    mask = functools.partial(mask_out, emb, matched_queries, mask_cotan, mask_features, count, blocks)

    def backward(keys, old, last=False):
        offset = order.index(keys[0]) * images // PARTS
        return attend_back(keys, me, kept, offset, features, dn, dt, keyval_weight, old, last)

    def z_scatter(chunks):
        got = [lax.dynamic_index_in_dim(chunks, (chip ^ k) % 2 * 2 + (chip ^ k) // 2, 0, keepdims=False) for k in range(4)]
        return [got[0]] + [swap(got[k], "batch", n_batch, 2 * k) for k in (1, 2, 3)]

    other = swap(away, "batch", n_batch, 1)
    if direct:
        fg, acc, vb, qp3 = backward((3,), None)
        other, fg, acc, vb, qp3 = beside(other, fg, acc, vb, qp3)
        sums = z_scatter((mine + other).reshape(n_batch // 2, -1, width))
        qp3 = swap(qp3, "pix", n_pix, 3)
        feat_grad, g_kv, qp1, qp2, qp0 = backward((1, 2, 0), (fg, acc, vb), True)
        *sums, feat_grad, g_kv, qp0, qp1, qp2, qp3 = beside(*sums, feat_grad, g_kv, qp0, qp1, qp2, qp3)
        qp1, qp2 = swap(qp1, "pix", n_pix, 1), swap(qp2, "pix", n_pix, 2)
        own = functools.reduce(jnp.add, sums)
        other = swap(own, "batch", n_batch, 4)
        cuts = [blocks * k // 8 for k in (0, 2, 5, 8)]
        outs = mask((cuts[0], cuts[1]))
        qp1, qp2, other, outs = beside(qp1, qp2, other, outs)
        own = join(own, other, "batch", 4)
        other = swap(own, "batch", n_batch, 2)
        split = g_kv.shape[0] // n_pix
        *parts, outs = beside(*query_sum(me, (qp0, qp1, qp2, qp3), g_kv), outs)
        parts = tuple(p if k == 0 else swap(p, "pix", n_pix, k) for k, p in enumerate(parts))
        outs = mask((cuts[1], cuts[2]), outs)
        *parts, other, outs = beside(*parts, other, outs)
        own = join(own, other, "batch", 2)
        low, high = own[:own.shape[0] // 2], own[own.shape[0] // 2:]
        low1, high2 = swap(low, "pix", n_pix, 1), swap(high, "pix", n_pix, 2)
        own2 = swap(own, "batch", n_batch, 1)
        queries_grad, tail, tail2 = query_back(me, parts, queries, dp1, query_weight)
        tail = tail + swap(tail2, "batch", n_batch, 1)
        tail2 = swap(tail, "batch", n_batch, 2)
        low1, high2, own2, tail2, outs = beside(low1, high2, own2, tail2, outs)
        low3, high3 = jnp.concatenate([low, low1], 0), jnp.concatenate([high, high2], 0)
        low3, high3 = swap(low3, "pix", n_pix, 2), swap(high3, "pix", n_pix, 1)
        low12, high22 = swap(low1, "batch", n_batch, 1), swap(high2, "batch", n_batch, 1)
        tail = tail + tail2
        tail2 = swap(tail, "batch", n_batch, 4)
        outs = mask((cuts[2], cuts[3]), outs)
        low12, high22, tail2, outs = beside(low12, high22, tail2, outs)
        low3, high3, outs = beside(low3, high3, outs)
        tail = tail + tail2
        tail = jnp.concatenate([tail] + [swap(tail, "pix", n_pix, k) for k in (1, 2, 3)], 0)
        pieces = [own, low1, high2, low3, high3]
        pieces += [own2, low12, high22, swap(low3, "batch", n_batch, 1), swap(high3, "batch", n_batch, 1)]
        tails = (tail, swap(tail, "batch", n_batch, 1))
        grads = unpack(me, pieces, tails, split, width, hidden)
        (d_query, d_query_bias, d_keyval, d_value_bias, d_cross, d_cross_bias, d_gain, d_nbias, d_self, d_self_bias,
         d_selfout, d_selfout_bias, d_hidden, d_hidden_bias, d_hidout, d_hidout_bias, d_embed, d_embed_bias) = grads
    else:
        old, parts = None, {}
        for keys, last in (((3,), False), ((1, 2, 0), True)):
            back = backward(keys, old, last)
            count_sums = 1 if last else 2
            old = back[:1 + count_sums]
            parts.update(zip(keys, back[1 + count_sums:]))
        feat_grad, g_kv = old
        parts = [parts[k] for k in range(PARTS)]
        qp = jnp.concatenate(parts, 0)
        outs = mask((0, blocks))
        sums = jnp.concatenate([lax.psum(qp, "pix").reshape(images * rows, width), g_kv], 0)
        queries_grad, tail, tail2 = query_back(me, (sums,), queries, dp1, query_weight)
        first = core == 0
        tail = jnp.concatenate([jnp.where(first, tail, tail2), jnp.where(first, tail2, tail)], 0)
        g_q = lax.psum(tail[g_kv.shape[0]:], "batch")
        g_kv = lax.psum(g_kv, ("batch", "pix"))
        every = [(2 * z, 2 * z + 1) for z in range(n_batch // 2)]
        groups = [[z[c] for z in every] for c in range(2)]
        part = lax.psum(mine + other, "batch", axis_index_groups=groups)
        both = lax.all_gather(part, "batch", axis_index_groups=[list(z) for z in every])
        packed = lax.all_gather(both, "pix").reshape(-1, width)

        def tile(t, k=1):
            return packed[t * width:(t + k) * width]

        def wide(t, k):
            return jnp.concatenate([tile(t + j) for j in range(k)], 1)

        many = hidden // width
        bias = packed[(T_HIDDEN + 2 * many) * width:]
        d_query, d_query_bias = g_q[:width], g_q[width]
        d_keyval, d_value_bias = jnp.concatenate([g_kv[:width], g_kv[width:2 * width]], 1), g_kv[2 * width]
        d_cross, d_cross_bias, d_gain, d_nbias = tile(T_CROSS), bias[0], bias[1:4], bias[4:7]
        d_self, d_self_bias, d_selfout, d_selfout_bias = wide(T_SELF, 3), bias[20:22], tile(T_SELFOUT), bias[7]
        d_hidden, d_hidden_bias = wide(T_HIDDEN, many), bias[8:8 + many]
        d_hidout, d_hidout_bias = tile(T_HIDDEN + many, many), bias[16]
        d_embed, d_embed_bias = tile(T_EMBED, 3), bias[17:20]
    logits, mask_grad = outs
    return (
        unflat(x3),
        unflat(logits),
        unflat(queries_grad),
        feat_grad,
        mask_grad,
        d_query,
        d_query_bias.reshape(-1),
        d_keyval,
        d_value_bias.reshape(-1),
        d_cross,
        d_cross_bias.reshape(-1),
        d_gain,
        d_nbias,
        d_self,
        d_self_bias,
        d_selfout,
        d_selfout_bias.reshape(-1),
        d_hidden,
        d_hidden_bias.reshape(-1),
        d_hidout,
        d_hidout_bias.reshape(-1),
        d_embed.reshape(3, width, width),
        d_embed_bias,
    )


def solution(mesh):
    n_pix, n_batch = mesh.shape["pix"], mesh.shape["batch"]
    rep = P()
    row, pixel, column = P("batch", None, None), P("batch", "pix", None), P("batch", None, "pix")
    in_specs = (row, pixel, pixel, column, P("batch", None), P("batch", None), row, column) + (rep,) * 18
    out_specs = (row, column, row, pixel, pixel) + (rep,) * 18
    body = functools.partial(local, n_pix=n_pix, n_batch=n_batch)
    return jax.shard_map(body, mesh=mesh, in_specs=in_specs, out_specs=out_specs, check_vma=False)
```

```python
import functools
import math

import jax
import jax.numpy as jnp
import numpy as np
from jax import lax
from jax.experimental import pallas as pl
from jax.experimental.pallas import tpu as pltpu
from jax.sharding import PartitionSpec as P

HEADS = 8
EPS = 1e-05
PENALTY = 10000.0
F32 = jnp.float32
LOW = jnp.bfloat16
HIGH = lax.Precision.HIGHEST
CURVE = math.sqrt(2.0 / math.pi)
CUBE = 0.044715
MIB = 1 << 20
PARTS = 4

T_CROSS, T_SELF, T_SELFOUT, T_EMBED, T_HIDDEN = 0, 1, 4, 5, 8


def up(n, m):
    return (n + m - 1) // m * m


def nn(a, b, precision=None):
    return lax.dot_general(a, b, (((1,), (0,)), ((), ())), precision=precision, preferred_element_type=F32)


def nt(a, b, precision=None):
    return lax.dot_general(a, b, (((1,), (1,)), ((), ())), precision=precision, preferred_element_type=F32)


def tn(a, b, precision=None):
    return lax.dot_general(a, b, (((0,), (0,)), ((), ())), precision=precision, preferred_element_type=F32)


def head_mask(width):
    shape = (HEADS, 1, width)
    head = width // HEADS
    return lax.broadcasted_iota(jnp.int32, shape, 2) // head == lax.broadcasted_iota(jnp.int32, shape, 0)


def spread(x, mask):
    rows, width = x.shape
    return jnp.where(mask, x[None], 0.0).reshape(HEADS * rows, width)


def gather_heads(x, mask):
    total, width = x.shape
    return jnp.sum(jnp.where(mask, x.reshape(HEADS, total // HEADS, width), 0.0), 0)


def spread_low(x, mask):
    return spread(x, mask).astype(LOW)


def head_onehot(width, lanes, transposed=False):
    head = width // HEADS
    if transposed:
        shape, a, b = (width, lanes), 0, 1
    else:
        shape, a, b = (lanes, width), 1, 0
    hit = lax.broadcasted_iota(jnp.int32, shape, a) // head == lax.broadcasted_iota(jnp.int32, shape, b)
    return hit.astype(F32)


def slabs_in(scr, value):
    for t in range(scr.shape[0]):
        scr[t] = value[:, t * 128:(t + 1) * 128]


def take_image(scr, image, count, images):
    rows = pl.ds(image, count, images)
    return jnp.concatenate([scr[t, rows, :] for t in range(scr.shape[0])], 1)


def put_image(scr, image, count, images, value):
    for t in range(scr.shape[0]):
        scr[t, pl.ds(image, count, images), :] = value[:, t * 128:(t + 1) * 128]


def slabs(rows, columns):
    return pltpu.VMEM((columns // 128, rows, 128), F32)


def cost(flops, nbytes, trans=0):
    return pl.CostEstimate(flops=int(flops), bytes_accessed=int(nbytes), transcendentals=int(trans))


def whole(x):
    shape = x.shape
    return pl.BlockSpec(shape, lambda *_: (0,) * len(shape))


def params(mib):
    return pltpu.CompilerParams(vmem_limit_bytes=mib * MIB, dimension_semantics=("arbitrary",))


def of_step(keys, n, i):
    key = keys[-1]
    for j in range(len(keys) - 2, -1, -1):
        key = jnp.where(i < (j + 1) * n, keys[j], key)
    return key


def turned_heads(x, fill):
    return jnp.transpose(jnp.concatenate([x, fill], 0))[:, 0:x.shape[0]].astype(LOW)


def attend_kernel(keys, n, me_ref, q_ref, f_ref, bits_ref, flag_ref, wq_ref, bq_ref, wkv_ref, vb_ref, elo_ref, ehi_ref,
                  mc_ref, mf_ref, e_ref, kv_ref, cq_ref, *refs):
    pays = refs[:len(keys)]
    mc_scr, q_scr, w_scr, all_scr, wq_scr, wkv_scr, vb_scr, pay_ref = refs[len(keys):]
    i = pl.program_id(0)
    images = flag_ref.shape[0]
    image = (me_ref[0] ^ of_step(keys, n, i)) * n + i % n
    width = q_ref.shape[1]
    count = q_ref.shape[0] // images
    rows = q_scr.shape[0]
    pixels = f_ref.shape[1]
    tall = rows + HEADS
    head = width // HEADS

    @pl.when(i == 0)
    def _():
        q_scr[...] = jnp.zeros_like(q_scr)
        w_scr[...] = jnp.zeros_like(w_scr)
        slabs_in(all_scr, q_ref[...])
        wq_scr[...] = wq_ref[...].astype(LOW)
        wkv_scr[0:width] = jnp.transpose(wkv_ref[:, :width]).astype(LOW)
        wkv_scr[width:] = jnp.transpose(wkv_ref[:, width:]).astype(LOW)
        vb_scr[...] = jnp.transpose(jnp.broadcast_to(vb_ref[...], (128, width)))
        pay_ref[...] = jnp.zeros_like(pay_ref)
        slabs_in(mc_scr, mc_ref[...].astype(F32).reshape(mc_ref.shape[0] * images, mc_ref.shape[2]))

    matched = mc_ref.shape[0]
    pay_ref[tall:tall + matched] = nn(take_image(mc_scr, image, matched, images).astype(LOW), mf_ref[0])
    q_scr[0:count] = take_image(all_scr, image, count, images)
    w_scr[:, 0:count] = jnp.where(flag_ref[pl.ds(image, 1), :] > 0, 65535, bits_ref[0])

    scale = 1.0 / math.sqrt(head)
    cq = ((nn(q_scr[...].astype(LOW), wq_scr[...]) + bq_ref[...]) * scale).astype(LOW).astype(F32)
    cq_ref[0] = cq

    bits = w_scr[...]
    low = (bits & 255).astype(F32).astype(LOW)
    high = (bits >> 8).astype(F32).astype(LOW)
    byte = (tn(low, elo_ref[...]) + tn(high, ehi_ref[...])).astype(jnp.int32)
    shift = lax.broadcasted_iota(jnp.int32, (rows, pixels), 1) & 7
    pen = jnp.where(((byte >> shift) & 1) == 1, 0.0, -PENALTY)

    keyval = nt(wkv_scr[...], f_ref[0])
    ck = keyval[:width].astype(LOW)
    cv = (keyval[width:] + jnp.concatenate([vb_scr[...]] * (pixels // 128), 1)).astype(LOW)
    kv_ref[0, :width] = ck
    kv_ref[0, width:] = cv

    def scores(h):
        at = slice(h * head, (h + 1) * head)
        return nn(cq[:, at].astype(LOW), ck[at]) + pen

    lane = lax.broadcasted_iota(jnp.int32, (rows, 128), 1)
    stats = jnp.zeros((rows, 128), F32)
    parts = []
    following = scores(0)
    for h in range(HEADS):
        s = following
        if h + 1 < HEADS:
            following = scores(h + 1)
        m = jnp.max(s, -1, keepdims=True)
        e = jnp.exp(s - m)
        total = jnp.sum(e, -1, keepdims=True)
        e_low = e.astype(LOW)
        e_ref[0, h] = e_low
        parts.append(nt(cv[h * head:(h + 1) * head], e_low))
        stats = jnp.where(lane == h, m, stats)
        stats = jnp.where(lane == HEADS + h, total, stats)
    pay_ref[0:rows] = jnp.transpose(jnp.concatenate(parts, 0))
    full = jnp.concatenate([stats, jnp.ones((128 - rows, 128), F32)], 0)
    turned = jnp.transpose(full)
    pay_ref[rows:tall, 0:128] = turned[0:HEADS]
    pay_ref[rows:tall, 128:256] = turned[HEADS:2 * HEADS]
    for j, out in enumerate(pays):
        @pl.when(i // n == j)
        def _(out=out):
            out[0] = pay_ref[...]


def attend(keys, me, queries, features, bits, reopen_flags, query_weight, query_bias, keyval_weight, value_bias,
           mask_cotan, mask_features, parts):
    images, pixels, width = features.shape
    words, count = bits.shape[1:]
    rows = up(count, 8)
    pixel = np.arange(pixels)
    word = np.arange(words)
    here = pixel[None, :] // 16 == word[:, None]
    e_lo = (here & (pixel[None, :] % 16 < 8)).astype(LOW)
    e_hi = (here & (pixel[None, :] % 16 >= 8)).astype(LOW)
    n = images // parts
    steps = n * len(keys)

    def theirs(*shape):
        return pl.BlockSpec(
            (1,) + shape, lambda i, me: ((me[0] ^ of_step(keys, n, i)) * n + i % n,) + (0,) * len(shape))

    def of_key(j, *shape):
        return pl.BlockSpec((1,) + shape, lambda i, me: (jnp.clip(i - j * n, 0, n - 1),) + (0,) * len(shape))

    per = lambda *shape: pl.BlockSpec((1,) + shape, lambda i, me: (i,) + (0,) * len(shape))
    args = (queries, features, bits, reopen_flags, query_weight, query_bias[None], keyval_weight, value_bias[None], e_lo, e_hi,
            mask_cotan, mask_features)
    matched, _, wide = mask_cotan.shape
    in_specs = [whole(a) for a in args]
    in_specs[1] = theirs(pixels, width)
    in_specs[2] = theirs(words, count)
    in_specs[11] = theirs(wide, width)
    flops = 2 * steps * (pixels * width * 2 * width + 2 * HEADS * rows * pixels * width)
    nbytes = steps * (pixels * width * 6 + HEADS * rows * pixels * 2)
    tall = rows + HEADS + up(matched, 8)
    nbytes += steps * wide * (width + matched) * 2
    out_shape = [
        jax.ShapeDtypeStruct((steps, HEADS, rows, pixels), LOW),
        jax.ShapeDtypeStruct((steps, 2 * width, pixels), LOW),
        jax.ShapeDtypeStruct((steps, rows, width), F32),
    ]
    out_shape += [jax.ShapeDtypeStruct((n, tall, width), F32)] * len(keys)
    out_specs = [per(HEADS, rows, pixels), per(2 * width, pixels), per(rows, width)]
    out_specs += [of_key(j, tall, width) for j in range(len(keys))]
    return pl.pallas_call(
        functools.partial(attend_kernel, keys, n),
        grid_spec=pltpu.PrefetchScalarGridSpec(
            num_scalar_prefetch=1,
            grid=(steps,),
            in_specs=in_specs,
            out_specs=tuple(out_specs),
            scratch_shapes=[
                slabs(matched * images, wide),
                pltpu.VMEM((rows, width), F32),
                pltpu.VMEM((words, rows), jnp.int32),
                slabs(count * images, width),
                pltpu.VMEM((width, width), LOW),
                pltpu.VMEM((2 * width, width), LOW),
                pltpu.VMEM((width, 128), F32),
                pltpu.VMEM((tall, width), F32),
            ],
        ),
        out_shape=tuple(out_shape),
        compiler_params=params(60),
        cost_estimate=cost(flops, nbytes, steps * HEADS * rows * pixels),
        name="attend",
    )(me, *args)


def combine_kernel(rows, *refs):
    parts, out_ref = refs[:-1], refs[-1]
    images, full, width = out_ref.shape
    tall = rows + HEADS
    onehot = head_onehot(width, HEADS)
    for i in range(images):
        ms = [p[i, rows:tall, 0:128] for p in parts]
        ls = [p[i, rows:tall, 128:256] for p in parts]
        top = functools.reduce(jnp.maximum, ms)
        rs = [jnp.exp(m - top) for m in ms]
        total = sum(r * l for r, l in zip(rs, ls))
        acc = jnp.zeros((rows, width), F32)
        for p, r in zip(parts, rs):
            acc = acc + p[i, 0:rows] * tn(r / total, onehot, HIGH)[0:rows]
        es = functools.reduce(jnp.add, [p[i, tall:] for p in parts])
        out_ref[i, 0:rows] = acc
        out_ref[i, rows:tall, 0:128] = top
        out_ref[i, rows:tall, 128:256] = total
        out_ref[i, tall:] = es


def combine(parts, rows):
    shape = parts[0].shape
    return pl.pallas_call(
        functools.partial(combine_kernel, rows),
        out_shape=jax.ShapeDtypeStruct(shape, F32),
        compiler_params=pltpu.CompilerParams(vmem_limit_bytes=32 * MIB),
        cost_estimate=cost(1e6, 5 * 4 * math.prod(shape)),
        name="combine",
    )(*parts)


def lower_kernel(*refs):
    n = len(refs) // 2
    for raw, out in zip(refs[:n], refs[n:]):
        out[...] = raw[...].astype(LOW)


def lower(weights):
    out_shape = tuple(jax.ShapeDtypeStruct(w.shape, LOW) for w in weights)
    size = sum(math.prod(w.shape) for w in weights)
    return pl.pallas_call(
        lower_kernel,
        out_shape=out_shape,
        compiler_params=pltpu.CompilerParams(vmem_limit_bytes=60 * MIB),
        cost_estimate=cost(size, 6 * size),
        name="lower",
    )(*weights)


def norm_forward(x, gain, bias):
    centre = x - jnp.mean(x, -1, keepdims=True)
    inverse = lax.rsqrt(jnp.mean(centre * centre, -1, keepdims=True) + EPS)
    normed = centre * inverse
    return normed * gain + bias, normed, inverse


def norm_backward(normed, inverse, gain, grad):
    dnormed = grad * gain
    return inverse * (
        dnormed - jnp.mean(dnormed, -1, keepdims=True) - normed * jnp.mean(dnormed * normed, -1, keepdims=True)
    )


def gelu_pair(x):
    square = x * x
    t = jnp.tanh(x * (CURVE + (CURVE * CUBE) * square))
    half = 0.5 + 0.5 * t
    slope = half + (0.5 * x) * (1.0 - t * t) * (CURVE + (3.0 * CURVE * CUBE) * square)
    return x * half, slope


def column_sum(x):
    return jnp.sum(x, 0, keepdims=True)


def chain_kernel(
    pieces, me_ref, *refs
):
    att_parts, refs = refs[:pieces], refs[pieces:]
    locals_, refs = refs[:PARTS], refs[PARTS:]
    chain_body(me_ref, att_parts, locals_, *refs)


def chain_body(
    me_ref, att_parts, locals_, q_ref, match_ref, cot_ref, wc_ref, bc_ref, gain_ref, nbias_ref, ws_ref, bs_ref, wso_ref,
    bso_ref, wh_ref, bh_ref, who_ref, bho_ref, we_ref, be_ref,
    x3_ref, emb_ref, dn_ref, dt_ref, dp1_ref, mine_ref, away_ref,
    g_ref, all_scr, cot_scr, out_scr, att_scr, emb_scr, loc_scr,
    q_scr, sq_scr, sk_scr, sv_scr, so_scr, pr_scr, h_scr, gp_scr, dso_scr, dm_scr
):
    step = pl.program_id(0)
    batch, rows, width = dn_ref.shape
    matched = match_ref.shape[1]
    count, images = cot_ref.shape[:2]
    tall = rows + HEADS
    flat = batch * rows
    hidden = wh_ref.shape[1]
    scale = 1.0 / math.sqrt(width // HEADS)
    hm = head_mask(width)

    @pl.when(step == 0)
    def _():
        q_scr[...] = jnp.zeros_like(q_scr)
        g_ref[...] = jnp.zeros_like(g_ref)
        n = att_parts[0].shape[0]
        for k, part in enumerate(att_parts):
            att_scr[pl.ds((me_ref[0] ^ k) * n, n)] = part[...]
        n = locals_[0].shape[0]
        for k, part in enumerate(locals_):
            loc_scr[pl.ds((me_ref[0] ^ k) * n, n)] = part[:, rows:tall]
        slabs_in(all_scr, q_ref[...])
        slabs_in(cot_scr, cot_ref[...].astype(F32).reshape(count * images, width))

    def put(tile, value):
        g_ref[tile * width:(tile + 1) * width] += value

    bias_at = (T_HIDDEN + 2 * (hidden // width)) * width

    def put_bias(index, value):
        g_ref[bias_at + index:bias_at + index + 1] += value

    first = step * batch
    for b in range(batch):
        q_scr[b, 0:count] = take_image(all_scr, first + b, count, images)
    att = att_scr[pl.ds(first, batch), 0:rows].reshape(flat, width)
    att_low = att.astype(LOW)
    queries = q_scr[...].reshape(flat, width)
    x1, n1, i1 = norm_forward(queries + nn(att_low, wc_ref[...]) + bc_ref[...], gain_ref[0:1], nbias_ref[0:1])
    x1_low = x1.astype(LOW)
    mixed = nn(x1_low, ws_ref[...])
    three = (batch, rows, width)
    sq_scr[...] = ((mixed[:, :width] + bs_ref[0:1]) * scale).reshape(three)
    sk_scr[...] = mixed[:, width:2 * width].reshape(three)
    sv_scr[...] = (mixed[:, 2 * width:] + bs_ref[1:2]).reshape(three)

    head = width // HEADS
    lanes = lambda h: slice(h * 128, (h + 1) * 128)
    fill = jnp.zeros((128 - rows, width), F32)

    def tall_heads(x):
        return spread_low(jnp.concatenate([x, fill], 0), hm)

    def turn(x):
        return jnp.transpose(jnp.concatenate([x, fill], 0))[:, 0:rows].astype(LOW)

    def by_head(turned, x):
        return jnp.transpose(jnp.concatenate(
            [nn(turned[h * head:(h + 1) * head], x[:, lanes(h)]) for h in range(HEADS)], 0))[0:rows]

    for b in range(batch):
        ss = nt(sk_scr[b].astype(LOW), tall_heads(sq_scr[b]))
        keys = lax.broadcasted_iota(jnp.int32, ss.shape, 0)
        ss = jnp.where(keys < count, ss, -1e30)
        p = jnp.exp(ss - jnp.max(ss, 0, keepdims=True))
        p = p * (1.0 / jnp.sum(p, 0, keepdims=True))
        pr_scr[b] = p
        so_scr[b] = by_head(turn(sv_scr[b]), p.astype(LOW))
    so_low = so_scr[...].reshape(flat, width).astype(LOW)
    x2, n2, i2 = norm_forward(x1 + nn(so_low, wso_ref[...]) + bso_ref[...], gain_ref[1:2], nbias_ref[1:2])
    x2_low = x2.astype(LOW)
    block = 2 * width

    def ff_forward(j, acc):
        cols = pl.ds(pl.multiple_of(j * block, block), block)
        h, slope = gelu_pair(nn(x2_low, wh_ref[:, cols]) + bh_ref[:, cols])
        h = h.astype(LOW)
        h_scr[:, cols] = h
        gp_scr[:, cols] = slope.astype(gp_scr.dtype)
        return acc + nn(h, who_ref[cols, :])

    ff = lax.fori_loop(0, hidden // block, ff_forward, jnp.zeros((flat, width), F32))
    x3, n3, i3 = norm_forward(x2 + ff + bho_ref[...], gain_ref[2:3], nbias_ref[2:3])
    for b in range(batch):
        put_image(out_scr, first + b, count, images, x3[b * rows:b * rows + count])

    x3_low = x3.astype(LOW)
    h1, slope1 = gelu_pair(nn(x3_low, we_ref[0]) + be_ref[0:1])
    h1 = h1.astype(LOW)
    h2, slope2 = gelu_pair(nn(h1, we_ref[1]) + be_ref[1:2])
    h2 = h2.astype(LOW)
    emb = nn(h2, we_ref[2]) + be_ref[2:3]
    for b in range(batch):
        put_image(emb_scr, first + b, count, images, emb[b * rows:b * rows + count])

    grads = []
    for b in range(batch):
        spots = match_ref[pl.ds(first + b, 1), :]
        pick = (lax.broadcasted_iota(jnp.int32, (rows, matched), 0) == spots).astype(F32).astype(LOW)
        grads.append(nn(pick, att_scr[first + b, tall:tall + matched].astype(LOW)))
    dz3 = jnp.concatenate(grads, 0)
    dz3_low = dz3.astype(LOW)
    put(T_EMBED + 2, tn(h2, dz3_low))
    put_bias(19, column_sum(dz3_low.astype(F32)))
    dz2 = (nt(dz3_low, we_ref[2]) * slope2).astype(LOW)
    put(T_EMBED + 1, tn(h1, dz2))
    put_bias(18, column_sum(dz2.astype(F32)))
    dz1 = (nt(dz2, we_ref[1]) * slope1).astype(LOW)
    put(T_EMBED, tn(x3_low, dz1))
    put_bias(17, column_sum(dz1.astype(F32)))
    for b in range(batch):
        q_scr[b, 0:count] = take_image(cot_scr, first + b, count, images)
    dx3 = q_scr[...].reshape(flat, width) + nt(dz1, we_ref[0])
    put_bias(3, column_sum(dx3 * n3))
    put_bias(6, column_sum(dx3))
    dp3 = norm_backward(n3, i3, gain_ref[2:3], dx3)
    dff = dp3.astype(LOW)
    put_bias(16, column_sum(dff.astype(F32)))

    def ff_backward(j, acc):
        cols = pl.ds(pl.multiple_of(j * block, block), block)
        base = (T_HIDDEN + hidden // width) * width
        spot = pl.ds(pl.multiple_of(base + j * block, block), block)
        g_ref[spot] += tn(h_scr[:, cols], dff)
        dz = (nt(dff, who_ref[cols, :]) * gp_scr[:, cols].astype(F32)).astype(LOW)
        gh = tn(x2_low, dz)
        sums = column_sum(dz.astype(F32))
        for t in range(block // width):
            tile = pl.ds(pl.multiple_of(T_HIDDEN * width + j * block + t * width, width), width)
            g_ref[tile] += gh[:, t * width:(t + 1) * width]
            g_ref[pl.ds(bias_at + 8 + j * (block // width) + t, 1)] += sums[:, t * width:(t + 1) * width]
        return acc + nt(dz, wh_ref[:, cols])

    dx2 = dp3 + lax.fori_loop(0, hidden // block, ff_backward, jnp.zeros((flat, width), F32))
    put_bias(2, column_sum(dx2 * n2))
    put_bias(5, column_sum(dx2))
    dp2 = norm_backward(n2, i2, gain_ref[1:2], dx2)
    dsa = dp2.astype(LOW)
    put(T_SELFOUT, tn(so_low, dsa))
    put_bias(7, column_sum(dsa.astype(F32)))
    dso_scr[...] = nt(dsa, wso_ref[...]).reshape(three)

    for b in range(batch):
        dsox = tall_heads(dso_scr[b])
        p = pr_scr[b]
        dp = nt(sv_scr[b].astype(LOW), dsox)
        dss = (p * (dp - jnp.sum(p * dp, 0, keepdims=True))).astype(LOW)
        dm_scr[b, :, 0:width] = by_head(turn(sk_scr[b]), dss) * scale
        dm_scr[b, :, width:2 * width] = nn(dss, tall_heads(sq_scr[b]))
        dm_scr[b, :, 2 * width:] = nn(p.astype(LOW), dsox)

    dm = dm_scr[...].reshape(flat, 3 * width).astype(LOW)
    gs = tn(x1_low, dm)
    for t in range(3):
        put(T_SELF + t, gs[:, t * width:(t + 1) * width])
    put_bias(20, column_sum(dm[:, :width].astype(F32)))
    put_bias(21, column_sum(dm[:, 2 * width:].astype(F32)))
    dx1 = dp2 + nt(dm, ws_ref[...])
    put_bias(1, column_sum(dx1 * n1))
    put_bias(4, column_sum(dx1))
    dp1 = norm_backward(n1, i1, gain_ref[0:1], dx1)
    dp1_ref[...] = dp1.reshape(three)
    dca = dp1.astype(LOW)
    put(T_CROSS, tn(att_low, dca))
    put_bias(0, column_sum(dca.astype(F32)))
    d_att = nt(dca, wc_ref[...]).reshape(three)
    onehot = head_onehot(width, HEADS)
    back = head_onehot(width, 128, True)
    for b in range(batch):
        top = att_scr[first + b, rows:tall, 0:128]
        total = att_scr[first + b, rows:tall, 128:256]
        ratio = jnp.exp(loc_scr[first + b, :, 0:128] - top) / total
        dn = d_att[b] * tn(ratio, onehot, HIGH)[0:rows]
        dn_ref[b] = dn
        dt_ref[b] = -nn(dn * att_scr[first + b, 0:rows], back, HIGH)

    @pl.when(step == 1)
    def _():
        x3_ref[...] = jnp.concatenate([out_scr[t] for t in range(out_scr.shape[0])], 1)
        emb_ref[...] = jnp.concatenate([emb_scr[t] for t in range(emb_scr.shape[0])], 1)
        share = mine_ref.shape[0]
        at = me_ref[1] * 2 + me_ref[2]
        mine_ref[...] = g_ref[pl.ds(pl.multiple_of(at * share, 8), share)]
        away_ref[...] = g_ref[pl.ds(pl.multiple_of((at + 1 - 2 * me_ref[2]) * share, 8), share)]


def chain(me, parts, pays, queries, matched, query_cotan, weights, n_pix):
    full, width = parts[0].shape[1:]
    images = pays[0].shape[0] * len(pays)
    count = query_cotan.shape[0]
    rows = up(count, 8)
    batch = images // 2
    hidden = weights[8].shape[1]
    tiles = T_HIDDEN + 2 * (hidden // width)
    grads = up(tiles * width + 22, 256)
    half = lambda *shape: pl.BlockSpec((batch,) + shape, lambda i, *_: (i,) + (0,) * len(shape))
    pieces = len(parts)
    args = tuple(parts) + tuple(pays) + (queries, matched, query_cotan) + weights
    in_specs = [whole(a) for a in args]
    out_shape = (
        jax.ShapeDtypeStruct((count * images, width), F32),
        jax.ShapeDtypeStruct((count * images, width), F32),
        jax.ShapeDtypeStruct((images, rows, width), F32),
        jax.ShapeDtypeStruct((images, rows, 128), F32),
        jax.ShapeDtypeStruct((images, rows, width), F32),
        jax.ShapeDtypeStruct((grads // n_pix // 2, width), F32),
        jax.ShapeDtypeStruct((grads // n_pix // 2, width), F32),
    )
    flat = batch * rows
    three = (batch, rows, width)
    many = slabs(count * images, width)
    return pl.pallas_call(
        functools.partial(chain_kernel, pieces),
        grid_spec=pltpu.PrefetchScalarGridSpec(
            num_scalar_prefetch=1,
            grid=(2,),
            in_specs=in_specs,
            out_specs=(whole(out_shape[0]), whole(out_shape[1]), half(rows, width), half(rows, 128), half(rows, width),
                       whole(out_shape[5]), whole(out_shape[6])),
            scratch_shapes=[
                pltpu.VMEM((grads, width), F32),
                many,
                many,
                many,
                pltpu.VMEM((images, full, width), F32),
                many,
                pltpu.VMEM((images, HEADS, width), F32),
                pltpu.VMEM(three, F32),
                pltpu.VMEM(three, F32),
                pltpu.VMEM(three, F32),
                pltpu.VMEM(three, F32),
                pltpu.VMEM(three, F32),
                pltpu.VMEM((batch, rows, HEADS * 128), F32),
                pltpu.VMEM((flat, hidden), LOW),
                pltpu.VMEM((flat, hidden), LOW),
                pltpu.VMEM(three, F32),
                pltpu.VMEM((batch, rows, 3 * width), F32),
            ],
        ),
        out_shape=out_shape,
        compiler_params=params(62),
        cost_estimate=cost(2 * 8e9, 20e6, 4e6),
        name="chain",
    )(me, *args)


def mask_out_kernel(emb_ref, match_ref, mc_ref, mf_ref, logit_old, grad_old, logit_ref, grad_ref, chosen_scr,
                    emb_scr, low_scr, logit_scr, mc_scr):
    images, matched, width = chosen_scr.shape
    count = logit_ref.shape[0] // images
    part = mc_ref.shape[2]

    @pl.when(pl.program_id(0) == 0)
    def _():
        slabs_in(emb_scr, emb_ref[...])
        low_scr[...] = jnp.zeros_like(low_scr)
        for b in range(images):
            pick = (lax.broadcasted_iota(jnp.int32, (count, matched), 0) == match_ref[b:b + 1, :]).astype(F32).astype(LOW)
            emb = take_image(emb_scr, b, count, images).astype(LOW)
            low_scr[b, 0:count] = emb.astype(F32)
            chosen_scr[b] = tn(pick, emb)

    slabs_in(mc_scr, mc_ref[...].astype(F32).reshape(matched * images, part))
    for b in range(images):
        put_image(logit_scr, b, count, images, nt(low_scr[b].astype(LOW), mf_ref[b])[0:count])
        grad_ref[b] = tn(take_image(mc_scr, b, matched, images).astype(LOW), chosen_scr[b].astype(LOW))
    for t in range(part // 128):
        logit_ref[:, t * 128:(t + 1) * 128] = logit_scr[t]


def mask_out(emb, matched_queries, mask_cotan, mask_features, count, pieces, steps, old=None):
    matched, images, pixels = mask_cotan.shape
    width = emb.shape[1]
    part = pixels // pieces
    first, last = steps
    out_shape = (
        jax.ShapeDtypeStruct((count * images, pixels), F32),
        jax.ShapeDtypeStruct((images, pixels, width), F32),
    )
    args = (emb, matched_queries, mask_cotan, mask_features)
    here = pl.BlockSpec(memory_space=pl.ANY)
    kernel = mask_out_kernel
    aliases = {}
    specs = []
    if old is None:
        def kernel(a, b, c, d, *rest):
            mask_out_kernel(a, b, c, d, None, None, *rest)
    else:
        args += old
        aliases = {4: 0, 5: 1}
        specs = [here, here]
    return pl.pallas_call(
        kernel,
        grid=(last - first,),
        in_specs=[
            whole(emb),
            whole(matched_queries),
            pl.BlockSpec((matched, images, part), lambda j: (0, 0, j + first)),
            pl.BlockSpec((images, part, width), lambda j: (0, j + first, 0)),
        ] + specs,
        out_specs=(
            pl.BlockSpec((count * images, part), lambda j: (0, j + first)),
            pl.BlockSpec((images, part, width), lambda j: (0, j + first, 0)),
        ),
        out_shape=out_shape,
        input_output_aliases=aliases,
        scratch_shapes=[pltpu.VMEM((images, matched, width), F32),
                        slabs(count * images, width), pltpu.VMEM((images, up(count, 8), width), F32),
                        slabs(count * images, part), slabs(matched * images, part)],
        compiler_params=params(60),
        cost_estimate=cost(
            2 * images * pixels * width * 160 * (last - first) / pieces,
            images * pixels * (width * 6 + count * 4 + matched * 2) * (last - first) / pieces),
        name="mask_out",
    )(*args)


def attend_back_kernel(keys, n, last, me_ref, e_ref, kv_ref, f_ref, cq_ref, dn_ref, dt_ref, wkv_ref, acc_old, vb_old,
                       fg_ref, qps, acc_ref, vb_ref, g_ref, w_scr):
    i = pl.program_id(0)
    rows, width = cq_ref.shape[1:]
    pixels = f_ref.shape[1]
    head = width // HEADS

    @pl.when(i == 0)
    def _():
        acc_ref[...] = jnp.zeros_like(acc_ref) if acc_old is None else acc_old[...]
        vb_ref[...] = jnp.zeros_like(vb_ref) if vb_old is None else vb_old[...]
        w_scr[0:width] = jnp.transpose(wkv_ref[:, :width]).astype(LOW)
        w_scr[width:] = jnp.transpose(wkv_ref[:, width:]).astype(LOW)

    dn = dn_ref[0]
    fill = jnp.zeros((128 - rows, width), F32)
    cq_turned = turned_heads(cq_ref[0], fill)
    dn_turned = turned_heads(dn, fill)

    def weigh(h):
        at = slice(h * head, (h + 1) * head)
        return nn(dn[:, at].astype(LOW), kv_ref[0, width + h * head:width + (h + 1) * head]) + dt_ref[0, :, h:h + 1]

    parts, keys_sum, values_sum = [], [], []
    following = weigh(0)
    for h in range(HEADS):
        at = slice(h * head, (h + 1) * head)
        dw = following
        if h + 1 < HEADS:
            following = weigh(h + 1)
        e_low = e_ref[0, h]
        ds = (e_low.astype(F32) * dw).astype(LOW)
        values_sum.append(nn(dn_turned[at], e_low).astype(LOW))
        keys_sum.append(nn(cq_turned[at], ds).astype(LOW))
        parts.append(nt(kv_ref[0, at], ds))
    part = jnp.transpose(jnp.concatenate(parts, 0))
    for j, out in enumerate(qps):
        @pl.when(i // n == j)
        def _(out=out):
            out[0] = part
    turned = jnp.concatenate(keys_sum + values_sum, 0)
    acc_ref[...] += nn(turned, f_ref[0])
    summed = turned[width:].astype(F32)
    lanes_sum = summed[:, 0:128]
    for t in range(1, pixels // 128):
        lanes_sum = lanes_sum + summed[:, t * 128:(t + 1) * 128]
    vb_ref[...] += lanes_sum
    fg_ref[0] = tn(turned, w_scr[...])

    if last:
        @pl.when(i == pl.num_programs(0) - 1)
        def _():
            sums = jnp.sum(jnp.transpose(vb_ref[...]), 0, keepdims=True)
            fill = jnp.zeros((g_ref.shape[0] - 2 * width - 1, width), F32)
            g_ref[...] = jnp.concatenate(
                [jnp.transpose(acc_ref[0:width]), jnp.transpose(acc_ref[width:]), sums, fill], 0)


def attend_back(keys, me, kept, offset, features, dn, dt, keyval_weight, old, last):
    e, kv, cq = kept
    images, pixels, width = features.shape
    rows = cq.shape[1]
    n = images // PARTS
    steps = n * len(keys)

    def theirs(*shape):
        return pl.BlockSpec(
            (1,) + shape, lambda i, me: ((me[0] ^ of_step(keys, n, i)) * n + i % n,) + (0,) * len(shape))

    def of_key(j, *shape):
        return pl.BlockSpec((1,) + shape, lambda i, me: (jnp.clip(i - j * n, 0, n - 1),) + (0,) * len(shape))

    per = lambda *shape: pl.BlockSpec((1,) + shape, lambda i, me: (i + offset,) + (0,) * len(shape))
    tall = HEADS * rows
    flops = 2 * steps * (4 * tall * pixels * width + 4 * pixels * width * width)
    nbytes = steps * (tall * pixels * 2 + pixels * width * 10)
    sums = (jax.ShapeDtypeStruct((2 * width, width), F32), jax.ShapeDtypeStruct((width, 128), F32))
    fg = jax.ShapeDtypeStruct((images, pixels, width), F32)
    qps = (jax.ShapeDtypeStruct((n, rows, width), F32),) * len(keys)
    scratch = [pltpu.VMEM((2 * width, width), LOW)]
    middle = sums
    if last:
        middle = (jax.ShapeDtypeStruct((2 * width + 32, width), F32),)
        scratch = [pltpu.VMEM(x.shape, F32) for x in sums] + scratch
    args = (e, kv, features, cq, dn, dt, keyval_weight)
    in_specs = [per(HEADS, rows, pixels), per(2 * width, pixels), theirs(pixels, width),
                per(rows, width), theirs(rows, width), theirs(rows, 128), whole(keyval_weight)]
    aliases = {}

    def kernel(*refs):
        ins, refs = refs[:8], refs[8:]
        w_scr, refs = refs[-1], refs[:-1]
        acc_old = vb_old = g = None
        if old is not None:
            acc_old, vb_old, refs = refs[1], refs[2], refs[3:]
        fg, refs = refs[0], refs[1:]
        if last:
            g, refs = refs[0], refs[1:]
            qp, (acc, vb) = refs[:len(keys)], refs[len(keys):]
        else:
            (acc, vb), qp = refs[:2], refs[2:]
        attend_back_kernel(keys, n, last, *ins, acc_old, vb_old, fg, qp, acc, vb, g, w_scr)

    if old is not None:
        args += old
        in_specs += [pl.BlockSpec(memory_space=pl.ANY)] + [whole(x) for x in sums]
        aliases = {8: 0}
    return pl.pallas_call(
        kernel,
        grid_spec=pltpu.PrefetchScalarGridSpec(
            num_scalar_prefetch=1,
            grid=(steps,),
            in_specs=in_specs,
            out_specs=(theirs(pixels, width),) + tuple(whole(x) for x in middle) + tuple(
                of_key(j, rows, width) for j in range(len(keys))),
            scratch_shapes=scratch,
        ),
        out_shape=(fg,) + middle + qps,
        input_output_aliases=aliases,
        compiler_params=params(60),
        cost_estimate=cost(flops, nbytes),
        name="attend_back",
    )(me, *args)


def query_sum_kernel(me_ref, *refs):
    parts, kv_ref, outs = refs[:PARTS], refs[PARTS], refs[PARTS + 1:]
    n, rows, width = parts[0].shape
    total = parts[0][...]
    for p in parts[1:]:
        total = total + p[...]
    total = total.reshape(n * rows, width)
    share = kv_ref.shape[0] // PARTS
    for k, out in enumerate(outs):
        out[0:n * rows] = total
        out[n * rows:] = kv_ref[pl.ds(pl.multiple_of((me_ref[0] ^ k) * share, 8), share)]


def query_sum(me, parts, g_kv):
    n, rows, width = parts[0].shape
    args = tuple(parts) + (g_kv,)
    out = jax.ShapeDtypeStruct((n * rows + g_kv.shape[0] // PARTS, width), F32)
    return pl.pallas_call(
        query_sum_kernel,
        grid_spec=pltpu.PrefetchScalarGridSpec(
            num_scalar_prefetch=1, grid=(1,), in_specs=[whole(a) for a in args], out_specs=(whole(out),) * PARTS),
        out_shape=(out,) * PARTS,
        compiler_params=params(16),
        cost_estimate=cost(1e6, 3e6),
        name="query_sum",
    )(me, *args)


def query_back_kernel(pieces, me_ref, *refs):
    parts = refs[:pieces]
    (q_ref, dp_ref, wq_ref, qg_ref, mine_ref, away_ref, scr, sum_scr, all_scr, out_scr, g_scr, tail_scr) = refs[pieces:]
    images, rows, width = dp_ref.shape
    count = q_ref.shape[0] // images
    scale = 1.0 / math.sqrt(width // HEADS)
    n = images // pieces
    kv = jnp.zeros((parts[0].shape[0] - n * rows, width), F32)
    for k, part in enumerate(parts):
        sum_scr[pl.ds((me_ref[0] ^ k) * n, n)] = part[0:n * rows].reshape(n, rows, width)
        kv = kv + part[n * rows:]
    scr[...] = jnp.zeros_like(scr)
    slabs_in(all_scr, q_ref[...])
    for b in range(images):
        scr[b, 0:count] = take_image(all_scr, b, count, images)
    d_cq = (sum_scr[...].reshape(images * rows, width) * scale).astype(LOW)
    out = dp_ref[...] + nt(d_cq, wq_ref[...].astype(LOW)).reshape(images, rows, width)
    for b in range(images):
        put_image(out_scr, b, count, images, out[b, 0:count])
    qg_ref[...] = jnp.concatenate([out_scr[t] for t in range(out_scr.shape[0])], 1)
    g_scr[0:width] = tn(scr[...].reshape(images * rows, width).astype(LOW), d_cq)
    g_scr[width:] = jnp.zeros((g_scr.shape[0] - width, width), F32)
    g_scr[width:width + 1] = column_sum(d_cq.astype(F32))
    share = g_scr.shape[0] // pieces
    small = mine_ref.shape[0]
    tail_scr[0:kv.shape[0]] = kv
    tail_scr[kv.shape[0]:] = g_scr[pl.ds(pl.multiple_of(me_ref[0] * share, 8), share)]
    mine_ref[...] = tail_scr[pl.ds(pl.multiple_of(me_ref[2] * small, 8), small)]
    away_ref[...] = tail_scr[pl.ds(pl.multiple_of((1 - me_ref[2]) * small, 8), small)]


def query_back(me, parts, queries, dp1, query_weight):
    images, rows, width = dp1.shape
    pieces = len(parts)
    args = tuple(parts) + (queries, dp1, query_weight)
    share = parts[0].shape[0] - images // pieces * rows
    full = (width + 32) // pieces + share
    half = jax.ShapeDtypeStruct((full // 2, width), F32)
    out_shape = (jax.ShapeDtypeStruct(queries.shape, F32), half, half)
    return pl.pallas_call(
        functools.partial(query_back_kernel, pieces),
        grid_spec=pltpu.PrefetchScalarGridSpec(
            num_scalar_prefetch=1,
            grid=(1,),
            in_specs=[whole(a) for a in args],
            out_specs=tuple(whole(o) for o in out_shape),
            scratch_shapes=[pltpu.VMEM((images, rows, width), F32), pltpu.VMEM((images, rows, width), F32),
                            slabs(*queries.shape), slabs(*queries.shape), pltpu.VMEM((width + 32, width), F32),
                            pltpu.VMEM((full, width), F32)],
        ),
        out_shape=out_shape,
        compiler_params=params(60),
        cost_estimate=cost(5e8, 8e6),
        name="query_back",
    )(me, *args)


def unpack_kernel(split, me_ref, *refs):
    own, other = refs[:5], refs[5:10]
    (tail, tail2,
     query_ref, query_bias_ref, keyval_ref, value_bias_ref, cross_ref, cross_bias_ref, gain_ref, nbias_ref,
     self_ref, self_bias_ref, selfout_ref, selfout_bias_ref, hidden_ref, hidden_bias_ref, hidout_ref, hidout_bias_ref,
     embed_ref, embed_bias_ref, g, t) = refs[10:]
    pix, core = me_ref[1], me_ref[2]
    width = query_ref.shape[0]
    short = own[1].shape[0]
    places = (((0, 0), (0, 1)), ((1, 0),), ((2, 1),), ((2, 0), (3, 0)), ((1, 1), (3, 1)))
    for half, five in ((core, own), (1 - core, other)):
        for piece, spots in zip(five, places):
            for row, (k, second) in enumerate(spots):
                at = ((pix ^ k) * 2 + half) * 2 + second
                g[pl.ds(pl.multiple_of(at * short, 8), short)] = piece[row * short:(row + 1) * short]
    small = tail.shape[0] // 4
    for half, ref in ((core, tail), (1 - core, tail2)):
        for k in range(4):
            at = (pix ^ k) * 2 + half
            t[pl.ds(pl.multiple_of(at * small, 8), small)] = ref[k * small:(k + 1) * small]

    def tile(n, k=1):
        return g[n * width:(n + k) * width]

    many = hidden_ref.shape[1] // width
    bias = (T_HIDDEN + 2 * many) * width
    cross_ref[...] = tile(T_CROSS)
    selfout_ref[...] = tile(T_SELFOUT)
    embed_ref[...] = tile(T_EMBED, 3)
    hidout_ref[...] = tile(T_HIDDEN + many, many)
    for n in range(3):
        self_ref[:, n * width:(n + 1) * width] = tile(T_SELF + n)
    for n in range(many):
        hidden_ref[:, n * width:(n + 1) * width] = tile(T_HIDDEN + n)
        hidden_bias_ref[:, n * width:(n + 1) * width] = g[bias + 8 + n:bias + 9 + n]
    cross_bias_ref[...] = g[bias:bias + 1]
    gain_ref[...] = g[bias + 1:bias + 4]
    nbias_ref[...] = g[bias + 4:bias + 7]
    selfout_bias_ref[...] = g[bias + 7:bias + 8]
    hidout_bias_ref[...] = g[bias + 16:bias + 17]
    embed_bias_ref[...] = g[bias + 17:bias + 20]
    self_bias_ref[...] = g[bias + 20:bias + 22]
    block = 2 * small
    low, high = [], []
    for k in range(4):
        low.append(t[k * block:k * block + split])
        high.append(t[k * block + split:(k + 1) * block])
    low, high = jnp.concatenate(low, 0), jnp.concatenate(high, 0)
    keyval_ref[:, 0:width] = low[0:width]
    keyval_ref[:, width:] = low[width:2 * width]
    value_bias_ref[...] = low[2 * width:2 * width + 1]
    query_ref[...] = high[0:width]
    query_bias_ref[...] = high[width:width + 1]


def unpack(me, pieces, tails, split, width, hidden):
    args = tuple(pieces) + tuple(tails)
    shapes = ((width, width), (1, width), (width, 2 * width), (1, width), (width, width), (1, width), (3, width), (3, width),
              (width, 3 * width), (2, width), (width, width), (1, width), (width, hidden), (1, hidden), (hidden, width),
              (1, width), (3 * width, width), (3, width))
    out_shape = tuple(jax.ShapeDtypeStruct(shape, F32) for shape in shapes)
    rows = sum(p.shape[0] for p in pieces)
    return pl.pallas_call(
        functools.partial(unpack_kernel, split),
        grid_spec=pltpu.PrefetchScalarGridSpec(
            num_scalar_prefetch=1,
            grid=(1,),
            in_specs=[whole(a) for a in args],
            out_specs=tuple(whole(o) for o in out_shape),
            scratch_shapes=[pltpu.VMEM((rows, width), F32), pltpu.VMEM((2 * tails[0].shape[0], width), F32)],
        ),
        out_shape=out_shape,
        compiler_params=params(32),
        cost_estimate=cost(1e6, 16e6),
        name="unpack",
    )(me, *args)


def beside(*values):
    return lax.optimization_barrier(values)


def swap(x, axis, n, key):
    return lax.ppermute(x, axis, [(d, d ^ key) for d in range(n)])


def scatter_out(x, axis, n):
    me = lax.axis_index(axis)
    chunks = [lax.dynamic_index_in_dim(x, me ^ k, 0, keepdims=False) for k in range(n)]
    return tuple(c if k == 0 else swap(c, axis, n, k) for k, c in enumerate(chunks))


def gather_in(x, axis, n):
    return tuple(x if k == 0 else swap(x, axis, n, k) for k in range(n))


def side(axis, key):
    return (lax.axis_index(axis) // key) % 2


def halve(x, axis, n, key):
    halves = x.reshape((2, -1) + x.shape[1:])
    mine = lax.dynamic_index_in_dim(halves, side(axis, key), 0, keepdims=False)
    away = lax.dynamic_index_in_dim(halves, 1 - side(axis, key), 0, keepdims=False)
    return mine, swap(away, axis, n, key)


def join(mine, other, axis, key):
    first = side(axis, key) == 0
    return jnp.concatenate([jnp.where(first, mine, other), jnp.where(first, other, mine)], 0)


def local(
    queries, features, mask_features, attend_bits, reopen_flags, matched_queries, query_cotan, mask_cotan,
    query_weight, query_bias, keyval_weight, value_bias, cross_out, cross_out_bias, norm_gain, norm_bias,
    self_weight, self_bias, self_out, self_out_bias, hidden_weight, hidden_bias, hidden_out, hidden_out_bias,
    embed_weight, embed_bias, *, n_pix, n_batch,
):
    images, count, width = queries.shape
    hidden = hidden_weight.shape[1]
    rows = up(count, 8)
    tall = rows + HEADS
    pix = lax.axis_index("pix")
    direct = n_pix == 4 and n_batch == 8

    queries = jnp.transpose(queries, (1, 0, 2)).reshape(count * images, width)
    query_cotan = jnp.transpose(query_cotan, (1, 0, 2))
    mask_cotan = jnp.transpose(mask_cotan, (1, 0, 2))
    bits = jnp.transpose(attend_bits, (0, 2, 1))
    core = lax.axis_index("batch") % 2
    chip = lax.axis_index("batch") // 2
    me = jnp.stack([pix if direct else 0 * pix, pix, core, chip]).astype(jnp.int32)

    order = (3, 1, 2, 0)
    e, kv, cq, *pays = attend(order, me, queries, features, bits, reopen_flags, query_weight, query_bias, keyval_weight,
                              value_bias, mask_cotan, mask_features, PARTS)
    kept = (e, kv, cq)
    pays = dict(zip(order, pays))
    got = {k: swap(pays[k], "pix", n_pix, k) if k else pays[k] for k in order} if direct else {}
    pays = [pays[k] for k in range(PARTS)]
    weights = (
        cross_out, cross_out_bias[None], norm_gain, norm_bias, self_weight, self_bias, self_out, self_out_bias[None],
        hidden_weight, hidden_bias[None], hidden_out, hidden_out_bias[None], embed_weight, embed_bias,
    )
    large = (0, 4, 6, 8, 10, 12)
    if direct:
        share = combine([got[k] for k in range(PARTS)], rows)
        share, *raw = beside(share, *[weights[k] for k in large])
        att = gather_in(share, "pix", n_pix)
    else:
        raw = [weights[k] for k in large]
        pay = jnp.concatenate(pays, 0)
        top = lax.pmax(pay[:, rows:tall, :128], "pix")
        ratio = jnp.exp(pay[:, rows:tall, :128] - top)

        def widen(x):
            return jnp.repeat(jnp.transpose(x, (0, 2, 1))[:, :rows], width // HEADS, axis=2)

        numer, total, es = lax.psum(
            (pay[:, :rows] * widen(ratio), pay[:, rows:tall, 128:] * ratio, pay[:, tall:]), "pix")
        att = (jnp.concatenate([numer / widen(total), jnp.concatenate([top, total], 2), es], 1),)
    lowered = dict(zip(large, lower(raw)))
    weights = tuple(lowered.get(k, w) for k, w in enumerate(weights))
    x3, emb, dn, dt, dp1, mine, away = chain(
        me, att, pays, queries, matched_queries, query_cotan, weights, n_pix)

    def unflat(x):
        return jnp.transpose(x.reshape(count, images, -1), (1, 0, 2))

    blocks = mask_features.shape[1] // 512
    mask = functools.partial(mask_out, emb, matched_queries, mask_cotan, mask_features, count, blocks)

    def backward(keys, old, last=False):
        offset = order.index(keys[0]) * images // PARTS
        return attend_back(keys, me, kept, offset, features, dn, dt, keyval_weight, old, last)

    def z_scatter(chunks):
        got = [lax.dynamic_index_in_dim(chunks, (chip ^ k) % 2 * 2 + (chip ^ k) // 2, 0, keepdims=False) for k in range(4)]
        return [got[0]] + [swap(got[k], "batch", n_batch, 2 * k) for k in (1, 2, 3)]

    other = swap(away, "batch", n_batch, 1)
    if direct:
        fg, acc, vb, qp3 = backward((3,), None)
        other, fg, acc, vb, qp3 = beside(other, fg, acc, vb, qp3)
        sums = z_scatter((mine + other).reshape(n_batch // 2, -1, width))
        qp3 = swap(qp3, "pix", n_pix, 3)
        feat_grad, g_kv, qp1, qp2, qp0 = backward((1, 2, 0), (fg, acc, vb), True)
        *sums, feat_grad, g_kv, qp0, qp1, qp2, qp3 = beside(*sums, feat_grad, g_kv, qp0, qp1, qp2, qp3)
        qp1, qp2 = swap(qp1, "pix", n_pix, 1), swap(qp2, "pix", n_pix, 2)
        own = functools.reduce(jnp.add, sums)
        other = swap(own, "batch", n_batch, 4)
        cuts = [blocks * k // 8 for k in (0, 2, 5, 6, 8)]
        outs = mask((cuts[0], cuts[1]))
        qp1, qp2, other, outs = beside(qp1, qp2, other, outs)
        own = join(own, other, "batch", 4)
        other = swap(own, "batch", n_batch, 2)
        split = g_kv.shape[0] // n_pix
        *parts, outs = beside(*query_sum(me, (qp0, qp1, qp2, qp3), g_kv), outs)
        parts = tuple(p if k == 0 else swap(p, "pix", n_pix, k) for k, p in enumerate(parts))
        outs = mask((cuts[1], cuts[2]), outs)
        *parts, other, outs = beside(*parts, other, outs)
        own = join(own, other, "batch", 2)
        low, high = own[:own.shape[0] // 2], own[own.shape[0] // 2:]
        low1, high2 = swap(low, "pix", n_pix, 1), swap(high, "pix", n_pix, 2)
        own2 = swap(own, "batch", n_batch, 1)
        queries_grad, tail, tail2 = query_back(me, parts, queries, dp1, query_weight)
        tail = tail + swap(tail2, "batch", n_batch, 1)
        low1, high2, own2, tail, outs = beside(low1, high2, own2, tail, outs)
        low3, high3 = jnp.concatenate([low, low1], 0), jnp.concatenate([high, high2], 0)
        low3, high3 = swap(low3, "pix", n_pix, 2), swap(high3, "pix", n_pix, 1)
        low12, high22 = swap(low1, "batch", n_batch, 1), swap(high2, "batch", n_batch, 1)
        tail2 = swap(tail, "batch", n_batch, 2)
        outs = mask((cuts[2], cuts[3]), outs)
        tail2, outs = beside(tail2, outs)
        tail = tail + tail2
        tail2 = swap(tail, "batch", n_batch, 4)
        outs = mask((cuts[3], cuts[4]), outs)
        low12, high22, tail2, outs = beside(low12, high22, tail2, outs)
        low3, high3, outs = beside(low3, high3, outs)
        tail = tail + tail2
        tail = jnp.concatenate([tail] + [swap(tail, "pix", n_pix, k) for k in (1, 2, 3)], 0)
        pieces = [own, low1, high2, low3, high3]
        pieces += [own2, low12, high22, swap(low3, "batch", n_batch, 1), swap(high3, "batch", n_batch, 1)]
        tails = (tail, swap(tail, "batch", n_batch, 1))
        grads = unpack(me, pieces, tails, split, width, hidden)
        (d_query, d_query_bias, d_keyval, d_value_bias, d_cross, d_cross_bias, d_gain, d_nbias, d_self, d_self_bias,
         d_selfout, d_selfout_bias, d_hidden, d_hidden_bias, d_hidout, d_hidout_bias, d_embed, d_embed_bias) = grads
    else:
        old, parts = None, {}
        for keys, last in (((3,), False), ((1, 2, 0), True)):
            back = backward(keys, old, last)
            count_sums = 1 if last else 2
            old = back[:1 + count_sums]
            parts.update(zip(keys, back[1 + count_sums:]))
        feat_grad, g_kv = old
        parts = [parts[k] for k in range(PARTS)]
        qp = jnp.concatenate(parts, 0)
        outs = mask((0, blocks))
        sums = jnp.concatenate([lax.psum(qp, "pix").reshape(images * rows, width), g_kv], 0)
        queries_grad, tail, tail2 = query_back(me, (sums,), queries, dp1, query_weight)
        first = core == 0
        tail = jnp.concatenate([jnp.where(first, tail, tail2), jnp.where(first, tail2, tail)], 0)
        g_q = lax.psum(tail[g_kv.shape[0]:], "batch")
        g_kv = lax.psum(g_kv, ("batch", "pix"))
        every = [(2 * z, 2 * z + 1) for z in range(n_batch // 2)]
        groups = [[z[c] for z in every] for c in range(2)]
        part = lax.psum(mine + other, "batch", axis_index_groups=groups)
        both = lax.all_gather(part, "batch", axis_index_groups=[list(z) for z in every])
        packed = lax.all_gather(both, "pix").reshape(-1, width)

        def tile(t, k=1):
            return packed[t * width:(t + k) * width]

        def wide(t, k):
            return jnp.concatenate([tile(t + j) for j in range(k)], 1)

        many = hidden // width
        bias = packed[(T_HIDDEN + 2 * many) * width:]
        d_query, d_query_bias = g_q[:width], g_q[width]
        d_keyval, d_value_bias = jnp.concatenate([g_kv[:width], g_kv[width:2 * width]], 1), g_kv[2 * width]
        d_cross, d_cross_bias, d_gain, d_nbias = tile(T_CROSS), bias[0], bias[1:4], bias[4:7]
        d_self, d_self_bias, d_selfout, d_selfout_bias = wide(T_SELF, 3), bias[20:22], tile(T_SELFOUT), bias[7]
        d_hidden, d_hidden_bias = wide(T_HIDDEN, many), bias[8:8 + many]
        d_hidout, d_hidout_bias = tile(T_HIDDEN + many, many), bias[16]
        d_embed, d_embed_bias = tile(T_EMBED, 3), bias[17:20]
    logits, mask_grad = outs
    return (
        unflat(x3),
        unflat(logits),
        unflat(queries_grad),
        feat_grad,
        mask_grad,
        d_query,
        d_query_bias.reshape(-1),
        d_keyval,
        d_value_bias.reshape(-1),
        d_cross,
        d_cross_bias.reshape(-1),
        d_gain,
        d_nbias,
        d_self,
        d_self_bias,
        d_selfout,
        d_selfout_bias.reshape(-1),
        d_hidden,
        d_hidden_bias.reshape(-1),
        d_hidout,
        d_hidout_bias.reshape(-1),
        d_embed.reshape(3, width, width),
        d_embed_bias,
    )


def solution(mesh):
    n_pix, n_batch = mesh.shape["pix"], mesh.shape["batch"]
    rep = P()
    row, pixel, column = P("batch", None, None), P("batch", "pix", None), P("batch", None, "pix")
    in_specs = (row, pixel, pixel, column, P("batch", None), P("batch", None), row, column) + (rep,) * 18
    out_specs = (row, column, row, pixel, pixel) + (rep,) * 18
    body = functools.partial(local, n_pix=n_pix, n_batch=n_batch)
    return jax.shard_map(body, mesh=mesh, in_specs=in_specs, out_specs=out_specs, check_vma=False)
```

```python
import functools
import math

import jax
import jax.numpy as jnp
import numpy as np
from jax import lax
from jax.experimental import pallas as pl
from jax.experimental.pallas import tpu as pltpu
from jax.sharding import PartitionSpec as P

HEADS = 8
EPS = 1e-05
PENALTY = 10000.0
F32 = jnp.float32
LOW = jnp.bfloat16
HIGH = lax.Precision.HIGHEST
CURVE = math.sqrt(2.0 / math.pi)
CUBE = 0.044715
MIB = 1 << 20
PARTS = 4

T_CROSS, T_SELF, T_SELFOUT, T_EMBED, T_HIDDEN = 0, 1, 4, 5, 8


def up(n, m):
    return (n + m - 1) // m * m


def nn(a, b, precision=None):
    return lax.dot_general(a, b, (((1,), (0,)), ((), ())), precision=precision, preferred_element_type=F32)


def nt(a, b, precision=None):
    return lax.dot_general(a, b, (((1,), (1,)), ((), ())), precision=precision, preferred_element_type=F32)


def tn(a, b, precision=None):
    return lax.dot_general(a, b, (((0,), (0,)), ((), ())), precision=precision, preferred_element_type=F32)


def head_mask(width):
    shape = (HEADS, 1, width)
    head = width // HEADS
    return lax.broadcasted_iota(jnp.int32, shape, 2) // head == lax.broadcasted_iota(jnp.int32, shape, 0)


def spread(x, mask):
    rows, width = x.shape
    return jnp.where(mask, x[None], 0.0).reshape(HEADS * rows, width)


def gather_heads(x, mask):
    total, width = x.shape
    return jnp.sum(jnp.where(mask, x.reshape(HEADS, total // HEADS, width), 0.0), 0)


def spread_low(x, mask):
    return spread(x, mask).astype(LOW)


def head_onehot(width, lanes, transposed=False):
    head = width // HEADS
    if transposed:
        shape, a, b = (width, lanes), 0, 1
    else:
        shape, a, b = (lanes, width), 1, 0
    hit = lax.broadcasted_iota(jnp.int32, shape, a) // head == lax.broadcasted_iota(jnp.int32, shape, b)
    return hit.astype(F32)


def slabs_in(scr, value):
    for t in range(scr.shape[0]):
        scr[t] = value[:, t * 128:(t + 1) * 128]


def take_image(scr, image, count, images):
    rows = pl.ds(image, count, images)
    return jnp.concatenate([scr[t, rows, :] for t in range(scr.shape[0])], 1)


def put_image(scr, image, count, images, value):
    for t in range(scr.shape[0]):
        scr[t, pl.ds(image, count, images), :] = value[:, t * 128:(t + 1) * 128]


def slabs(rows, columns):
    return pltpu.VMEM((columns // 128, rows, 128), F32)


def cost(flops, nbytes, trans=0):
    return pl.CostEstimate(flops=int(flops), bytes_accessed=int(nbytes), transcendentals=int(trans))


def whole(x):
    shape = x.shape
    return pl.BlockSpec(shape, lambda *_: (0,) * len(shape))


def params(mib):
    return pltpu.CompilerParams(vmem_limit_bytes=mib * MIB, dimension_semantics=("arbitrary",))


def of_step(keys, n, i):
    key = keys[-1]
    for j in range(len(keys) - 2, -1, -1):
        key = jnp.where(i < (j + 1) * n, keys[j], key)
    return key


def turned_heads(x, fill):
    return jnp.transpose(jnp.concatenate([x, fill], 0))[:, 0:x.shape[0]].astype(LOW)


def attend_kernel(keys, n, me_ref, q_ref, f_ref, bits_ref, flag_ref, wq_ref, bq_ref, wkv_ref, vb_ref, elo_ref, ehi_ref,
                  mc_ref, mf_ref, e_ref, kv_ref, cq_ref, *refs):
    pays = refs[:len(keys)]
    mc_scr, q_scr, w_scr, all_scr, wq_scr, wkv_scr, vb_scr, pay_ref = refs[len(keys):]
    i = pl.program_id(0)
    images = flag_ref.shape[0]
    image = (me_ref[0] ^ of_step(keys, n, i)) * n + i % n
    width = q_ref.shape[1]
    count = q_ref.shape[0] // images
    rows = q_scr.shape[0]
    pixels = f_ref.shape[1]
    tall = rows + HEADS
    head = width // HEADS

    @pl.when(i == 0)
    def _():
        q_scr[...] = jnp.zeros_like(q_scr)
        w_scr[...] = jnp.zeros_like(w_scr)
        slabs_in(all_scr, q_ref[...])
        wq_scr[...] = wq_ref[...].astype(LOW)
        wkv_scr[0:width] = jnp.transpose(wkv_ref[:, :width]).astype(LOW)
        wkv_scr[width:] = jnp.transpose(wkv_ref[:, width:]).astype(LOW)
        vb_scr[...] = jnp.transpose(jnp.broadcast_to(vb_ref[...], (128, width)))
        pay_ref[...] = jnp.zeros_like(pay_ref)
        slabs_in(mc_scr, mc_ref[...].astype(F32).reshape(mc_ref.shape[0] * images, mc_ref.shape[2]))

    matched = mc_ref.shape[0]
    pay_ref[tall:tall + matched] = nn(take_image(mc_scr, image, matched, images).astype(LOW), mf_ref[0])
    q_scr[0:count] = take_image(all_scr, image, count, images)
    w_scr[:, 0:count] = jnp.where(flag_ref[pl.ds(image, 1), :] > 0, 65535, bits_ref[0])

    scale = 1.0 / math.sqrt(head)
    cq = ((nn(q_scr[...].astype(LOW), wq_scr[...]) + bq_ref[...]) * scale).astype(LOW).astype(F32)
    cq_ref[0] = cq

    bits = w_scr[...]
    low = (bits & 255).astype(F32).astype(LOW)
    high = (bits >> 8).astype(F32).astype(LOW)
    byte = (tn(low, elo_ref[...]) + tn(high, ehi_ref[...])).astype(jnp.int32)
    shift = lax.broadcasted_iota(jnp.int32, (rows, pixels), 1) & 7
    pen = jnp.where(((byte >> shift) & 1) == 1, 0.0, -PENALTY)

    keyval = nt(wkv_scr[...], f_ref[0])
    ck = keyval[:width].astype(LOW)
    cv = (keyval[width:] + jnp.concatenate([vb_scr[...]] * (pixels // 128), 1)).astype(LOW)
    kv_ref[0, :width] = ck
    kv_ref[0, width:] = cv

    def scores(h):
        at = slice(h * head, (h + 1) * head)
        return nn(cq[:, at].astype(LOW), ck[at]) + pen

    lane = lax.broadcasted_iota(jnp.int32, (rows, 128), 1)
    stats = jnp.zeros((rows, 128), F32)
    parts = []
    following = scores(0)
    for h in range(HEADS):
        s = following
        if h + 1 < HEADS:
            following = scores(h + 1)
        m = jnp.max(s, -1, keepdims=True)
        e = jnp.exp(s - m)
        total = jnp.sum(e, -1, keepdims=True)
        e_low = e.astype(LOW)
        e_ref[0, h] = e_low
        parts.append(nt(cv[h * head:(h + 1) * head], e_low))
        stats = jnp.where(lane == h, m, stats)
        stats = jnp.where(lane == HEADS + h, total, stats)
    pay_ref[0:rows] = jnp.transpose(jnp.concatenate(parts, 0))
    full = jnp.concatenate([stats, jnp.ones((128 - rows, 128), F32)], 0)
    turned = jnp.transpose(full)
    pay_ref[rows:tall, 0:128] = turned[0:HEADS]
    pay_ref[rows:tall, 128:256] = turned[HEADS:2 * HEADS]
    for j, out in enumerate(pays):
        @pl.when(i // n == j)
        def _(out=out):
            out[0] = pay_ref[...]


def attend(keys, me, queries, features, bits, reopen_flags, query_weight, query_bias, keyval_weight, value_bias,
           mask_cotan, mask_features, parts):
    images, pixels, width = features.shape
    words, count = bits.shape[1:]
    rows = up(count, 8)
    pixel = np.arange(pixels)
    word = np.arange(words)
    here = pixel[None, :] // 16 == word[:, None]
    e_lo = (here & (pixel[None, :] % 16 < 8)).astype(LOW)
    e_hi = (here & (pixel[None, :] % 16 >= 8)).astype(LOW)
    n = images // parts
    steps = n * len(keys)

    def theirs(*shape):
        return pl.BlockSpec(
            (1,) + shape, lambda i, me: ((me[0] ^ of_step(keys, n, i)) * n + i % n,) + (0,) * len(shape))

    def of_key(j, *shape):
        return pl.BlockSpec((1,) + shape, lambda i, me: (jnp.clip(i - j * n, 0, n - 1),) + (0,) * len(shape))

    per = lambda *shape: pl.BlockSpec((1,) + shape, lambda i, me: (i,) + (0,) * len(shape))
    args = (queries, features, bits, reopen_flags, query_weight, query_bias[None], keyval_weight, value_bias[None], e_lo, e_hi,
            mask_cotan, mask_features)
    matched, _, wide = mask_cotan.shape
    in_specs = [whole(a) for a in args]
    in_specs[1] = theirs(pixels, width)
    in_specs[2] = theirs(words, count)
    in_specs[11] = theirs(wide, width)
    flops = 2 * steps * (pixels * width * 2 * width + 2 * HEADS * rows * pixels * width)
    nbytes = steps * (pixels * width * 6 + HEADS * rows * pixels * 2)
    tall = rows + HEADS + up(matched, 8)
    nbytes += steps * wide * (width + matched) * 2
    out_shape = [
        jax.ShapeDtypeStruct((steps, HEADS, rows, pixels), LOW),
        jax.ShapeDtypeStruct((steps, 2 * width, pixels), LOW),
        jax.ShapeDtypeStruct((steps, rows, width), F32),
    ]
    out_shape += [jax.ShapeDtypeStruct((n, tall, width), F32)] * len(keys)
    out_specs = [per(HEADS, rows, pixels), per(2 * width, pixels), per(rows, width)]
    out_specs += [of_key(j, tall, width) for j in range(len(keys))]
    return pl.pallas_call(
        functools.partial(attend_kernel, keys, n),
        grid_spec=pltpu.PrefetchScalarGridSpec(
            num_scalar_prefetch=1,
            grid=(steps,),
            in_specs=in_specs,
            out_specs=tuple(out_specs),
            scratch_shapes=[
                slabs(matched * images, wide),
                pltpu.VMEM((rows, width), F32),
                pltpu.VMEM((words, rows), jnp.int32),
                slabs(count * images, width),
                pltpu.VMEM((width, width), LOW),
                pltpu.VMEM((2 * width, width), LOW),
                pltpu.VMEM((width, 128), F32),
                pltpu.VMEM((tall, width), F32),
            ],
        ),
        out_shape=tuple(out_shape),
        compiler_params=params(60),
        cost_estimate=cost(flops, nbytes, steps * HEADS * rows * pixels),
        name="attend",
    )(me, *args)


def combine_kernel(rows, *refs):
    parts, out_ref = refs[:-1], refs[-1]
    images, full, width = out_ref.shape
    tall = rows + HEADS
    onehot = head_onehot(width, HEADS)
    for i in range(images):
        ms = [p[i, rows:tall, 0:128] for p in parts]
        ls = [p[i, rows:tall, 128:256] for p in parts]
        top = functools.reduce(jnp.maximum, ms)
        rs = [jnp.exp(m - top) for m in ms]
        total = sum(r * l for r, l in zip(rs, ls))
        acc = jnp.zeros((rows, width), F32)
        for p, r in zip(parts, rs):
            acc = acc + p[i, 0:rows] * tn(r / total, onehot, HIGH)[0:rows]
        es = functools.reduce(jnp.add, [p[i, tall:] for p in parts])
        out_ref[i, 0:rows] = acc
        out_ref[i, rows:tall, 0:128] = top
        out_ref[i, rows:tall, 128:256] = total
        out_ref[i, tall:] = es


def combine(parts, rows):
    shape = parts[0].shape
    return pl.pallas_call(
        functools.partial(combine_kernel, rows),
        out_shape=jax.ShapeDtypeStruct(shape, F32),
        compiler_params=pltpu.CompilerParams(vmem_limit_bytes=32 * MIB),
        cost_estimate=cost(1e6, 5 * 4 * math.prod(shape)),
        name="combine",
    )(*parts)


def lower_kernel(*refs):
    n = len(refs) // 2
    for raw, out in zip(refs[:n], refs[n:]):
        out[...] = raw[...].astype(LOW)


def lower(weights):
    out_shape = tuple(jax.ShapeDtypeStruct(w.shape, LOW) for w in weights)
    size = sum(math.prod(w.shape) for w in weights)
    return pl.pallas_call(
        lower_kernel,
        out_shape=out_shape,
        compiler_params=pltpu.CompilerParams(vmem_limit_bytes=60 * MIB),
        cost_estimate=cost(size, 6 * size),
        name="lower",
    )(*weights)


def norm_forward(x, gain, bias):
    centre = x - jnp.mean(x, -1, keepdims=True)
    inverse = lax.rsqrt(jnp.mean(centre * centre, -1, keepdims=True) + EPS)
    normed = centre * inverse
    return normed * gain + bias, normed, inverse


def norm_backward(normed, inverse, gain, grad):
    dnormed = grad * gain
    return inverse * (
        dnormed - jnp.mean(dnormed, -1, keepdims=True) - normed * jnp.mean(dnormed * normed, -1, keepdims=True)
    )


def gelu_pair(x):
    square = x * x
    t = jnp.tanh(x * (CURVE + (CURVE * CUBE) * square))
    half = 0.5 + 0.5 * t
    slope = half + (0.5 * x) * (1.0 - t * t) * (CURVE + (3.0 * CURVE * CUBE) * square)
    return x * half, slope


def column_sum(x):
    return jnp.sum(x, 0, keepdims=True)


def chain_kernel(
    pieces, me_ref, *refs
):
    att_parts, refs = refs[:pieces], refs[pieces:]
    locals_, refs = refs[:PARTS], refs[PARTS:]
    chain_body(me_ref, att_parts, locals_, *refs)


def chain_body(
    me_ref, att_parts, locals_, q_ref, match_ref, cot_ref, wc_ref, bc_ref, gain_ref, nbias_ref, ws_ref, bs_ref, wso_ref,
    bso_ref, wh_ref, bh_ref, who_ref, bho_ref, we_ref, be_ref,
    x3_ref, emb_ref, dn_ref, dt_ref, dp1_ref, mine_ref, away_ref,
    g_ref, all_scr, cot_scr, out_scr, att_scr, emb_scr, loc_scr,
    q_scr, sq_scr, sk_scr, sv_scr, so_scr, pr_scr, h_scr, gp_scr, dso_scr, dm_scr
):
    step = pl.program_id(0)
    batch, rows, width = dn_ref.shape
    matched = match_ref.shape[1]
    count, images = cot_ref.shape[:2]
    tall = rows + HEADS
    flat = batch * rows
    hidden = wh_ref.shape[1]
    scale = 1.0 / math.sqrt(width // HEADS)
    hm = head_mask(width)

    @pl.when(step == 0)
    def _():
        q_scr[...] = jnp.zeros_like(q_scr)
        g_ref[...] = jnp.zeros_like(g_ref)
        n = att_parts[0].shape[0]
        for k, part in enumerate(att_parts):
            att_scr[pl.ds((me_ref[0] ^ k) * n, n)] = part[...]
        n = locals_[0].shape[0]
        for k, part in enumerate(locals_):
            loc_scr[pl.ds((me_ref[0] ^ k) * n, n)] = part[:, rows:tall]
        slabs_in(all_scr, q_ref[...])
        slabs_in(cot_scr, cot_ref[...].astype(F32).reshape(count * images, width))

    def put(tile, value):
        g_ref[tile * width:(tile + 1) * width] += value

    bias_at = (T_HIDDEN + 2 * (hidden // width)) * width

    def put_bias(index, value):
        g_ref[bias_at + index:bias_at + index + 1] += value

    first = step * batch
    for b in range(batch):
        q_scr[b, 0:count] = take_image(all_scr, first + b, count, images)
    att = att_scr[pl.ds(first, batch), 0:rows].reshape(flat, width)
    att_low = att.astype(LOW)
    queries = q_scr[...].reshape(flat, width)
    x1, n1, i1 = norm_forward(queries + nn(att_low, wc_ref[...]) + bc_ref[...], gain_ref[0:1], nbias_ref[0:1])
    x1_low = x1.astype(LOW)
    mixed = nn(x1_low, ws_ref[...])
    three = (batch, rows, width)
    sq_scr[...] = ((mixed[:, :width] + bs_ref[0:1]) * scale).reshape(three)
    sk_scr[...] = mixed[:, width:2 * width].reshape(three)
    sv_scr[...] = (mixed[:, 2 * width:] + bs_ref[1:2]).reshape(three)

    head = width // HEADS
    lanes = lambda h: slice(h * 128, (h + 1) * 128)
    fill = jnp.zeros((128 - rows, width), F32)

    def tall_heads(x):
        return spread_low(jnp.concatenate([x, fill], 0), hm)

    def turn(x):
        return jnp.transpose(jnp.concatenate([x, fill], 0))[:, 0:rows].astype(LOW)

    def by_head(turned, x):
        return jnp.transpose(jnp.concatenate(
            [nn(turned[h * head:(h + 1) * head], x[:, lanes(h)]) for h in range(HEADS)], 0))[0:rows]

    for b in range(batch):
        ss = nt(sk_scr[b].astype(LOW), tall_heads(sq_scr[b]))
        keys = lax.broadcasted_iota(jnp.int32, ss.shape, 0)
        ss = jnp.where(keys < count, ss, -1e30)
        p = jnp.exp(ss - jnp.max(ss, 0, keepdims=True))
        p = p * (1.0 / jnp.sum(p, 0, keepdims=True))
        pr_scr[b] = p
        so_scr[b] = by_head(turn(sv_scr[b]), p.astype(LOW))
    so_low = so_scr[...].reshape(flat, width).astype(LOW)
    x2, n2, i2 = norm_forward(x1 + nn(so_low, wso_ref[...]) + bso_ref[...], gain_ref[1:2], nbias_ref[1:2])
    x2_low = x2.astype(LOW)
    block = 2 * width

    def ff_forward(j, acc):
        cols = pl.ds(pl.multiple_of(j * block, block), block)
        h, slope = gelu_pair(nn(x2_low, wh_ref[:, cols]) + bh_ref[:, cols])
        h = h.astype(LOW)
        h_scr[:, cols] = h
        gp_scr[:, cols] = slope.astype(gp_scr.dtype)
        return acc + nn(h, who_ref[cols, :])

    ff = lax.fori_loop(0, hidden // block, ff_forward, jnp.zeros((flat, width), F32))
    x3, n3, i3 = norm_forward(x2 + ff + bho_ref[...], gain_ref[2:3], nbias_ref[2:3])
    for b in range(batch):
        put_image(out_scr, first + b, count, images, x3[b * rows:b * rows + count])

    x3_low = x3.astype(LOW)
    h1, slope1 = gelu_pair(nn(x3_low, we_ref[0]) + be_ref[0:1])
    h1 = h1.astype(LOW)
    h2, slope2 = gelu_pair(nn(h1, we_ref[1]) + be_ref[1:2])
    h2 = h2.astype(LOW)
    emb = nn(h2, we_ref[2]) + be_ref[2:3]
    for b in range(batch):
        put_image(emb_scr, first + b, count, images, emb[b * rows:b * rows + count])

    grads = []
    for b in range(batch):
        spots = match_ref[pl.ds(first + b, 1), :]
        pick = (lax.broadcasted_iota(jnp.int32, (rows, matched), 0) == spots).astype(F32).astype(LOW)
        grads.append(nn(pick, att_scr[first + b, tall:tall + matched].astype(LOW)))
    dz3 = jnp.concatenate(grads, 0)
    dz3_low = dz3.astype(LOW)
    put(T_EMBED + 2, tn(h2, dz3_low))
    put_bias(19, column_sum(dz3_low.astype(F32)))
    dz2 = (nt(dz3_low, we_ref[2]) * slope2).astype(LOW)
    put(T_EMBED + 1, tn(h1, dz2))
    put_bias(18, column_sum(dz2.astype(F32)))
    dz1 = (nt(dz2, we_ref[1]) * slope1).astype(LOW)
    put(T_EMBED, tn(x3_low, dz1))
    put_bias(17, column_sum(dz1.astype(F32)))
    for b in range(batch):
        q_scr[b, 0:count] = take_image(cot_scr, first + b, count, images)
    dx3 = q_scr[...].reshape(flat, width) + nt(dz1, we_ref[0])
    put_bias(3, column_sum(dx3 * n3))
    put_bias(6, column_sum(dx3))
    dp3 = norm_backward(n3, i3, gain_ref[2:3], dx3)
    dff = dp3.astype(LOW)
    put_bias(16, column_sum(dff.astype(F32)))

    def ff_backward(j, acc):
        cols = pl.ds(pl.multiple_of(j * block, block), block)
        base = (T_HIDDEN + hidden // width) * width
        spot = pl.ds(pl.multiple_of(base + j * block, block), block)
        g_ref[spot] += tn(h_scr[:, cols], dff)
        dz = (nt(dff, who_ref[cols, :]) * gp_scr[:, cols].astype(F32)).astype(LOW)
        gh = tn(x2_low, dz)
        sums = column_sum(dz.astype(F32))
        for t in range(block // width):
            tile = pl.ds(pl.multiple_of(T_HIDDEN * width + j * block + t * width, width), width)
            g_ref[tile] += gh[:, t * width:(t + 1) * width]
            g_ref[pl.ds(bias_at + 8 + j * (block // width) + t, 1)] += sums[:, t * width:(t + 1) * width]
        return acc + nt(dz, wh_ref[:, cols])

    dx2 = dp3 + lax.fori_loop(0, hidden // block, ff_backward, jnp.zeros((flat, width), F32))
    put_bias(2, column_sum(dx2 * n2))
    put_bias(5, column_sum(dx2))
    dp2 = norm_backward(n2, i2, gain_ref[1:2], dx2)
    dsa = dp2.astype(LOW)
    put(T_SELFOUT, tn(so_low, dsa))
    put_bias(7, column_sum(dsa.astype(F32)))
    dso_scr[...] = nt(dsa, wso_ref[...]).reshape(three)

    for b in range(batch):
        dsox = tall_heads(dso_scr[b])
        p = pr_scr[b]
        dp = nt(sv_scr[b].astype(LOW), dsox)
        dss = (p * (dp - jnp.sum(p * dp, 0, keepdims=True))).astype(LOW)
        dm_scr[b, :, 0:width] = by_head(turn(sk_scr[b]), dss) * scale
        dm_scr[b, :, width:2 * width] = nn(dss, tall_heads(sq_scr[b]))
        dm_scr[b, :, 2 * width:] = nn(p.astype(LOW), dsox)

    dm = dm_scr[...].reshape(flat, 3 * width).astype(LOW)
    gs = tn(x1_low, dm)
    for t in range(3):
        put(T_SELF + t, gs[:, t * width:(t + 1) * width])
    put_bias(20, column_sum(dm[:, :width].astype(F32)))
    put_bias(21, column_sum(dm[:, 2 * width:].astype(F32)))
    dx1 = dp2 + nt(dm, ws_ref[...])
    put_bias(1, column_sum(dx1 * n1))
    put_bias(4, column_sum(dx1))
    dp1 = norm_backward(n1, i1, gain_ref[0:1], dx1)
    dp1_ref[...] = dp1.reshape(three)
    dca = dp1.astype(LOW)
    put(T_CROSS, tn(att_low, dca))
    put_bias(0, column_sum(dca.astype(F32)))
    d_att = nt(dca, wc_ref[...]).reshape(three)
    onehot = head_onehot(width, HEADS)
    back = head_onehot(width, 128, True)
    for b in range(batch):
        top = att_scr[first + b, rows:tall, 0:128]
        total = att_scr[first + b, rows:tall, 128:256]
        ratio = jnp.exp(loc_scr[first + b, :, 0:128] - top) / total
        dn = d_att[b] * tn(ratio, onehot, HIGH)[0:rows]
        dn_ref[b] = dn
        dt_ref[b] = -nn(dn * att_scr[first + b, 0:rows], back, HIGH)

    @pl.when(step == 1)
    def _():
        x3_ref[...] = jnp.concatenate([out_scr[t] for t in range(out_scr.shape[0])], 1)
        emb_ref[...] = jnp.concatenate([emb_scr[t] for t in range(emb_scr.shape[0])], 1)
        share = mine_ref.shape[0]
        at = me_ref[1] * 2 + me_ref[2]
        mine_ref[...] = g_ref[pl.ds(pl.multiple_of(at * share, 8), share)]
        away_ref[...] = g_ref[pl.ds(pl.multiple_of((at + 1 - 2 * me_ref[2]) * share, 8), share)]


def chain(me, parts, pays, queries, matched, query_cotan, weights, n_pix):
    full, width = parts[0].shape[1:]
    images = pays[0].shape[0] * len(pays)
    count = query_cotan.shape[0]
    rows = up(count, 8)
    batch = images // 2
    hidden = weights[8].shape[1]
    tiles = T_HIDDEN + 2 * (hidden // width)
    grads = up(tiles * width + 22, 256)
    half = lambda *shape: pl.BlockSpec((batch,) + shape, lambda i, *_: (i,) + (0,) * len(shape))
    pieces = len(parts)
    args = tuple(parts) + tuple(pays) + (queries, matched, query_cotan) + weights
    in_specs = [whole(a) for a in args]
    out_shape = (
        jax.ShapeDtypeStruct((count * images, width), F32),
        jax.ShapeDtypeStruct((count * images, width), F32),
        jax.ShapeDtypeStruct((images, rows, width), F32),
        jax.ShapeDtypeStruct((images, rows, 128), F32),
        jax.ShapeDtypeStruct((images, rows, width), F32),
        jax.ShapeDtypeStruct((grads // n_pix // 2, width), F32),
        jax.ShapeDtypeStruct((grads // n_pix // 2, width), F32),
    )
    flat = batch * rows
    three = (batch, rows, width)
    many = slabs(count * images, width)
    return pl.pallas_call(
        functools.partial(chain_kernel, pieces),
        grid_spec=pltpu.PrefetchScalarGridSpec(
            num_scalar_prefetch=1,
            grid=(2,),
            in_specs=in_specs,
            out_specs=(whole(out_shape[0]), whole(out_shape[1]), half(rows, width), half(rows, 128), half(rows, width),
                       whole(out_shape[5]), whole(out_shape[6])),
            scratch_shapes=[
                pltpu.VMEM((grads, width), F32),
                many,
                many,
                many,
                pltpu.VMEM((images, full, width), F32),
                many,
                pltpu.VMEM((images, HEADS, width), F32),
                pltpu.VMEM(three, F32),
                pltpu.VMEM(three, F32),
                pltpu.VMEM(three, F32),
                pltpu.VMEM(three, F32),
                pltpu.VMEM(three, F32),
                pltpu.VMEM((batch, rows, HEADS * 128), F32),
                pltpu.VMEM((flat, hidden), LOW),
                pltpu.VMEM((flat, hidden), LOW),
                pltpu.VMEM(three, F32),
                pltpu.VMEM((batch, rows, 3 * width), F32),
            ],
        ),
        out_shape=out_shape,
        compiler_params=params(62),
        cost_estimate=cost(2 * 8e9, 20e6, 4e6),
        name="chain",
    )(me, *args)


def mask_out_kernel(emb_ref, match_ref, mc_ref, mf_ref, logit_old, grad_old, logit_ref, grad_ref, chosen_scr,
                    emb_scr, low_scr, logit_scr, mc_scr):
    images, matched, width = chosen_scr.shape
    count = logit_ref.shape[0] // images
    part = mc_ref.shape[2]

    @pl.when(pl.program_id(0) == 0)
    def _():
        slabs_in(emb_scr, emb_ref[...])
        low_scr[...] = jnp.zeros_like(low_scr)
        for b in range(images):
            pick = (lax.broadcasted_iota(jnp.int32, (count, matched), 0) == match_ref[b:b + 1, :]).astype(F32).astype(LOW)
            emb = take_image(emb_scr, b, count, images).astype(LOW)
            low_scr[b, 0:count] = emb.astype(F32)
            chosen_scr[b] = tn(pick, emb)

    slabs_in(mc_scr, mc_ref[...].astype(F32).reshape(matched * images, part))
    for b in range(images):
        put_image(logit_scr, b, count, images, nt(low_scr[b].astype(LOW), mf_ref[b])[0:count])
        grad_ref[b] = tn(take_image(mc_scr, b, matched, images).astype(LOW), chosen_scr[b].astype(LOW))
    for t in range(part // 128):
        logit_ref[:, t * 128:(t + 1) * 128] = logit_scr[t]


def mask_out(emb, matched_queries, mask_cotan, mask_features, count, pieces, steps, old=None):
    matched, images, pixels = mask_cotan.shape
    width = emb.shape[1]
    part = pixels // pieces
    first, last = steps
    out_shape = (
        jax.ShapeDtypeStruct((count * images, pixels), F32),
        jax.ShapeDtypeStruct((images, pixels, width), F32),
    )
    args = (emb, matched_queries, mask_cotan, mask_features)
    here = pl.BlockSpec(memory_space=pl.ANY)
    kernel = mask_out_kernel
    aliases = {}
    specs = []
    if old is None:
        def kernel(a, b, c, d, *rest):
            mask_out_kernel(a, b, c, d, None, None, *rest)
    else:
        args += old
        aliases = {4: 0, 5: 1}
        specs = [here, here]
    return pl.pallas_call(
        kernel,
        grid=(last - first,),
        in_specs=[
            whole(emb),
            whole(matched_queries),
            pl.BlockSpec((matched, images, part), lambda j: (0, 0, j + first)),
            pl.BlockSpec((images, part, width), lambda j: (0, j + first, 0)),
        ] + specs,
        out_specs=(
            pl.BlockSpec((count * images, part), lambda j: (0, j + first)),
            pl.BlockSpec((images, part, width), lambda j: (0, j + first, 0)),
        ),
        out_shape=out_shape,
        input_output_aliases=aliases,
        scratch_shapes=[pltpu.VMEM((images, matched, width), F32),
                        slabs(count * images, width), pltpu.VMEM((images, up(count, 8), width), F32),
                        slabs(count * images, part), slabs(matched * images, part)],
        compiler_params=params(60),
        cost_estimate=cost(
            2 * images * pixels * width * 160 * (last - first) / pieces,
            images * pixels * (width * 6 + count * 4 + matched * 2) * (last - first) / pieces),
        name="mask_out",
    )(*args)


def attend_back_kernel(keys, n, last, me_ref, e_ref, kv_ref, f_ref, cq_ref, dn_ref, dt_ref, wkv_ref, acc_old, vb_old,
                       fg_ref, qps, acc_ref, vb_ref, g_ref, w_scr):
    i = pl.program_id(0)
    rows, width = cq_ref.shape[1:]
    pixels = f_ref.shape[1]
    head = width // HEADS

    @pl.when(i == 0)
    def _():
        acc_ref[...] = jnp.zeros_like(acc_ref) if acc_old is None else acc_old[...]
        vb_ref[...] = jnp.zeros_like(vb_ref) if vb_old is None else vb_old[...]
        w_scr[0:width] = jnp.transpose(wkv_ref[:, :width]).astype(LOW)
        w_scr[width:] = jnp.transpose(wkv_ref[:, width:]).astype(LOW)

    dn = dn_ref[0]
    fill = jnp.zeros((128 - rows, width), F32)
    cq_turned = turned_heads(cq_ref[0], fill)
    dn_turned = turned_heads(dn, fill)

    def weigh(h):
        at = slice(h * head, (h + 1) * head)
        return nn(dn[:, at].astype(LOW), kv_ref[0, width + h * head:width + (h + 1) * head]) + dt_ref[0, :, h:h + 1]

    parts, keys_sum, values_sum = [], [], []
    following = weigh(0)
    for h in range(HEADS):
        at = slice(h * head, (h + 1) * head)
        dw = following
        if h + 1 < HEADS:
            following = weigh(h + 1)
        e_low = e_ref[0, h]
        ds = (e_low.astype(F32) * dw).astype(LOW)
        values_sum.append(nn(dn_turned[at], e_low).astype(LOW))
        keys_sum.append(nn(cq_turned[at], ds).astype(LOW))
        parts.append(nt(kv_ref[0, at], ds))
    part = jnp.transpose(jnp.concatenate(parts, 0))
    for j, out in enumerate(qps):
        @pl.when(i // n == j)
        def _(out=out):
            out[0] = part
    turned = jnp.concatenate(keys_sum + values_sum, 0)
    acc_ref[...] += nn(turned, f_ref[0])
    summed = turned[width:].astype(F32)
    lanes_sum = summed[:, 0:128]
    for t in range(1, pixels // 128):
        lanes_sum = lanes_sum + summed[:, t * 128:(t + 1) * 128]
    vb_ref[...] += lanes_sum
    fg_ref[0] = tn(turned, w_scr[...])

    if last:
        @pl.when(i == pl.num_programs(0) - 1)
        def _():
            sums = jnp.sum(jnp.transpose(vb_ref[...]), 0, keepdims=True)
            fill = jnp.zeros((g_ref.shape[0] - 2 * width - 1, width), F32)
            g_ref[...] = jnp.concatenate(
                [jnp.transpose(acc_ref[0:width]), jnp.transpose(acc_ref[width:]), sums, fill], 0)


def attend_back(keys, me, kept, offset, features, dn, dt, keyval_weight, old, last):
    e, kv, cq = kept
    images, pixels, width = features.shape
    rows = cq.shape[1]
    n = images // PARTS
    steps = n * len(keys)

    def theirs(*shape):
        return pl.BlockSpec(
            (1,) + shape, lambda i, me: ((me[0] ^ of_step(keys, n, i)) * n + i % n,) + (0,) * len(shape))

    def of_key(j, *shape):
        return pl.BlockSpec((1,) + shape, lambda i, me: (jnp.clip(i - j * n, 0, n - 1),) + (0,) * len(shape))

    per = lambda *shape: pl.BlockSpec((1,) + shape, lambda i, me: (i + offset,) + (0,) * len(shape))
    tall = HEADS * rows
    flops = 2 * steps * (4 * tall * pixels * width + 4 * pixels * width * width)
    nbytes = steps * (tall * pixels * 2 + pixels * width * 10)
    sums = (jax.ShapeDtypeStruct((2 * width, width), F32), jax.ShapeDtypeStruct((width, 128), F32))
    fg = jax.ShapeDtypeStruct((images, pixels, width), F32)
    qps = (jax.ShapeDtypeStruct((n, rows, width), F32),) * len(keys)
    scratch = [pltpu.VMEM((2 * width, width), LOW)]
    middle = sums
    if last:
        middle = (jax.ShapeDtypeStruct((2 * width + 32, width), F32),)
        scratch = [pltpu.VMEM(x.shape, F32) for x in sums] + scratch
    args = (e, kv, features, cq, dn, dt, keyval_weight)
    in_specs = [per(HEADS, rows, pixels), per(2 * width, pixels), theirs(pixels, width),
                per(rows, width), theirs(rows, width), theirs(rows, 128), whole(keyval_weight)]
    aliases = {}

    def kernel(*refs):
        ins, refs = refs[:8], refs[8:]
        w_scr, refs = refs[-1], refs[:-1]
        acc_old = vb_old = g = None
        if old is not None:
            acc_old, vb_old, refs = refs[1], refs[2], refs[3:]
        fg, refs = refs[0], refs[1:]
        if last:
            g, refs = refs[0], refs[1:]
            qp, (acc, vb) = refs[:len(keys)], refs[len(keys):]
        else:
            (acc, vb), qp = refs[:2], refs[2:]
        attend_back_kernel(keys, n, last, *ins, acc_old, vb_old, fg, qp, acc, vb, g, w_scr)

    if old is not None:
        args += old
        in_specs += [pl.BlockSpec(memory_space=pl.ANY)] + [whole(x) for x in sums]
        aliases = {8: 0}
    return pl.pallas_call(
        kernel,
        grid_spec=pltpu.PrefetchScalarGridSpec(
            num_scalar_prefetch=1,
            grid=(steps,),
            in_specs=in_specs,
            out_specs=(theirs(pixels, width),) + tuple(whole(x) for x in middle) + tuple(
                of_key(j, rows, width) for j in range(len(keys))),
            scratch_shapes=scratch,
        ),
        out_shape=(fg,) + middle + qps,
        input_output_aliases=aliases,
        compiler_params=params(60),
        cost_estimate=cost(flops, nbytes),
        name="attend_back",
    )(me, *args)


def query_sum_kernel(me_ref, *refs):
    parts, kv_ref, outs = refs[:PARTS], refs[PARTS], refs[PARTS + 1:]
    n, rows, width = parts[0].shape
    total = parts[0][...]
    for p in parts[1:]:
        total = total + p[...]
    total = total.reshape(n * rows, width)
    share = kv_ref.shape[0] // PARTS
    for k, out in enumerate(outs):
        out[0:n * rows] = total
        out[n * rows:] = kv_ref[pl.ds(pl.multiple_of((me_ref[0] ^ k) * share, 8), share)]


def query_sum(me, parts, g_kv):
    n, rows, width = parts[0].shape
    args = tuple(parts) + (g_kv,)
    out = jax.ShapeDtypeStruct((n * rows + g_kv.shape[0] // PARTS, width), F32)
    return pl.pallas_call(
        query_sum_kernel,
        grid_spec=pltpu.PrefetchScalarGridSpec(
            num_scalar_prefetch=1, grid=(1,), in_specs=[whole(a) for a in args], out_specs=(whole(out),) * PARTS),
        out_shape=(out,) * PARTS,
        compiler_params=params(16),
        cost_estimate=cost(1e6, 3e6),
        name="query_sum",
    )(me, *args)


def query_back_kernel(pieces, me_ref, *refs):
    parts = refs[:pieces]
    (q_ref, dp_ref, wq_ref, qg_ref, mine_ref, away_ref, scr, sum_scr, all_scr, out_scr, g_scr, tail_scr) = refs[pieces:]
    images, rows, width = dp_ref.shape
    count = q_ref.shape[0] // images
    scale = 1.0 / math.sqrt(width // HEADS)
    n = images // pieces
    kv = jnp.zeros((parts[0].shape[0] - n * rows, width), F32)
    for k, part in enumerate(parts):
        sum_scr[pl.ds((me_ref[0] ^ k) * n, n)] = part[0:n * rows].reshape(n, rows, width)
        kv = kv + part[n * rows:]
    scr[...] = jnp.zeros_like(scr)
    slabs_in(all_scr, q_ref[...])
    for b in range(images):
        scr[b, 0:count] = take_image(all_scr, b, count, images)
    d_cq = (sum_scr[...].reshape(images * rows, width) * scale).astype(LOW)
    out = dp_ref[...] + nt(d_cq, wq_ref[...].astype(LOW)).reshape(images, rows, width)
    for b in range(images):
        put_image(out_scr, b, count, images, out[b, 0:count])
    qg_ref[...] = jnp.concatenate([out_scr[t] for t in range(out_scr.shape[0])], 1)
    g_scr[0:width] = tn(scr[...].reshape(images * rows, width).astype(LOW), d_cq)
    g_scr[width:] = jnp.zeros((g_scr.shape[0] - width, width), F32)
    g_scr[width:width + 1] = column_sum(d_cq.astype(F32))
    share = g_scr.shape[0] // pieces
    small = mine_ref.shape[0]
    tail_scr[0:kv.shape[0]] = kv
    tail_scr[kv.shape[0]:] = g_scr[pl.ds(pl.multiple_of(me_ref[0] * share, 8), share)]
    mine_ref[...] = tail_scr[pl.ds(pl.multiple_of(me_ref[2] * small, 8), small)]
    away_ref[...] = tail_scr[pl.ds(pl.multiple_of((1 - me_ref[2]) * small, 8), small)]


def query_back(me, parts, queries, dp1, query_weight):
    images, rows, width = dp1.shape
    pieces = len(parts)
    args = tuple(parts) + (queries, dp1, query_weight)
    share = parts[0].shape[0] - images // pieces * rows
    full = (width + 32) // pieces + share
    half = jax.ShapeDtypeStruct((full // 2, width), F32)
    out_shape = (jax.ShapeDtypeStruct(queries.shape, F32), half, half)
    return pl.pallas_call(
        functools.partial(query_back_kernel, pieces),
        grid_spec=pltpu.PrefetchScalarGridSpec(
            num_scalar_prefetch=1,
            grid=(1,),
            in_specs=[whole(a) for a in args],
            out_specs=tuple(whole(o) for o in out_shape),
            scratch_shapes=[pltpu.VMEM((images, rows, width), F32), pltpu.VMEM((images, rows, width), F32),
                            slabs(*queries.shape), slabs(*queries.shape), pltpu.VMEM((width + 32, width), F32),
                            pltpu.VMEM((full, width), F32)],
        ),
        out_shape=out_shape,
        compiler_params=params(60),
        cost_estimate=cost(5e8, 8e6),
        name="query_back",
    )(me, *args)


def unpack_kernel(split, me_ref, *refs):
    own, other = refs[:5], refs[5:10]
    (tail, tail2,
     query_ref, query_bias_ref, keyval_ref, value_bias_ref, cross_ref, cross_bias_ref, gain_ref, nbias_ref,
     self_ref, self_bias_ref, selfout_ref, selfout_bias_ref, hidden_ref, hidden_bias_ref, hidout_ref, hidout_bias_ref,
     embed_ref, embed_bias_ref, g, t) = refs[10:]
    pix, core = me_ref[1], me_ref[2]
    width = query_ref.shape[0]
    short = own[1].shape[0]
    places = (((0, 0), (0, 1)), ((1, 0),), ((2, 1),), ((2, 0), (3, 0)), ((1, 1), (3, 1)))
    for half, five in ((core, own), (1 - core, other)):
        for piece, spots in zip(five, places):
            for row, (k, second) in enumerate(spots):
                at = ((pix ^ k) * 2 + half) * 2 + second
                g[pl.ds(pl.multiple_of(at * short, 8), short)] = piece[row * short:(row + 1) * short]
    small = tail.shape[0] // 4
    for half, ref in ((core, tail), (1 - core, tail2)):
        for k in range(4):
            at = (pix ^ k) * 2 + half
            t[pl.ds(pl.multiple_of(at * small, 8), small)] = ref[k * small:(k + 1) * small]

    def tile(n, k=1):
        return g[n * width:(n + k) * width]

    many = hidden_ref.shape[1] // width
    bias = (T_HIDDEN + 2 * many) * width
    cross_ref[...] = tile(T_CROSS)
    selfout_ref[...] = tile(T_SELFOUT)
    embed_ref[...] = tile(T_EMBED, 3)
    hidout_ref[...] = tile(T_HIDDEN + many, many)
    for n in range(3):
        self_ref[:, n * width:(n + 1) * width] = tile(T_SELF + n)
    for n in range(many):
        hidden_ref[:, n * width:(n + 1) * width] = tile(T_HIDDEN + n)
        hidden_bias_ref[:, n * width:(n + 1) * width] = g[bias + 8 + n:bias + 9 + n]
    cross_bias_ref[...] = g[bias:bias + 1]
    gain_ref[...] = g[bias + 1:bias + 4]
    nbias_ref[...] = g[bias + 4:bias + 7]
    selfout_bias_ref[...] = g[bias + 7:bias + 8]
    hidout_bias_ref[...] = g[bias + 16:bias + 17]
    embed_bias_ref[...] = g[bias + 17:bias + 20]
    self_bias_ref[...] = g[bias + 20:bias + 22]
    block = 2 * small
    low, high = [], []
    for k in range(4):
        low.append(t[k * block:k * block + split])
        high.append(t[k * block + split:(k + 1) * block])
    low, high = jnp.concatenate(low, 0), jnp.concatenate(high, 0)
    keyval_ref[:, 0:width] = low[0:width]
    keyval_ref[:, width:] = low[width:2 * width]
    value_bias_ref[...] = low[2 * width:2 * width + 1]
    query_ref[...] = high[0:width]
    query_bias_ref[...] = high[width:width + 1]


def unpack(me, pieces, tails, split, width, hidden):
    args = tuple(pieces) + tuple(tails)
    shapes = ((width, width), (1, width), (width, 2 * width), (1, width), (width, width), (1, width), (3, width), (3, width),
              (width, 3 * width), (2, width), (width, width), (1, width), (width, hidden), (1, hidden), (hidden, width),
              (1, width), (3 * width, width), (3, width))
    out_shape = tuple(jax.ShapeDtypeStruct(shape, F32) for shape in shapes)
    rows = sum(p.shape[0] for p in pieces)
    return pl.pallas_call(
        functools.partial(unpack_kernel, split),
        grid_spec=pltpu.PrefetchScalarGridSpec(
            num_scalar_prefetch=1,
            grid=(1,),
            in_specs=[whole(a) for a in args],
            out_specs=tuple(whole(o) for o in out_shape),
            scratch_shapes=[pltpu.VMEM((rows, width), F32), pltpu.VMEM((2 * tails[0].shape[0], width), F32)],
        ),
        out_shape=out_shape,
        compiler_params=params(32),
        cost_estimate=cost(1e6, 16e6),
        name="unpack",
    )(me, *args)


def beside(*values):
    return lax.optimization_barrier(values)


def swap(x, axis, n, key):
    return lax.ppermute(x, axis, [(d, d ^ key) for d in range(n)])


def scatter_out(x, axis, n):
    me = lax.axis_index(axis)
    chunks = [lax.dynamic_index_in_dim(x, me ^ k, 0, keepdims=False) for k in range(n)]
    return tuple(c if k == 0 else swap(c, axis, n, k) for k, c in enumerate(chunks))


def gather_in(x, axis, n):
    return tuple(x if k == 0 else swap(x, axis, n, k) for k in range(n))


def side(axis, key):
    return (lax.axis_index(axis) // key) % 2


def halve(x, axis, n, key):
    halves = x.reshape((2, -1) + x.shape[1:])
    mine = lax.dynamic_index_in_dim(halves, side(axis, key), 0, keepdims=False)
    away = lax.dynamic_index_in_dim(halves, 1 - side(axis, key), 0, keepdims=False)
    return mine, swap(away, axis, n, key)


def join(mine, other, axis, key):
    first = side(axis, key) == 0
    return jnp.concatenate([jnp.where(first, mine, other), jnp.where(first, other, mine)], 0)


def local(
    queries, features, mask_features, attend_bits, reopen_flags, matched_queries, query_cotan, mask_cotan,
    query_weight, query_bias, keyval_weight, value_bias, cross_out, cross_out_bias, norm_gain, norm_bias,
    self_weight, self_bias, self_out, self_out_bias, hidden_weight, hidden_bias, hidden_out, hidden_out_bias,
    embed_weight, embed_bias, *, n_pix, n_batch,
):
    images, count, width = queries.shape
    hidden = hidden_weight.shape[1]
    rows = up(count, 8)
    tall = rows + HEADS
    pix = lax.axis_index("pix")
    direct = n_pix == 4 and n_batch == 8

    queries = jnp.transpose(queries, (1, 0, 2)).reshape(count * images, width)
    query_cotan = jnp.transpose(query_cotan, (1, 0, 2))
    mask_cotan = jnp.transpose(mask_cotan, (1, 0, 2))
    bits = jnp.transpose(attend_bits, (0, 2, 1))
    core = lax.axis_index("batch") % 2
    chip = lax.axis_index("batch") // 2
    me = jnp.stack([pix if direct else 0 * pix, pix, core, chip]).astype(jnp.int32)

    order = (3, 1, 2, 0)
    e, kv, cq, *pays = attend(order, me, queries, features, bits, reopen_flags, query_weight, query_bias, keyval_weight,
                              value_bias, mask_cotan, mask_features, PARTS)
    kept = (e, kv, cq)
    pays = dict(zip(order, pays))
    got = {k: swap(pays[k], "pix", n_pix, k) if k else pays[k] for k in order} if direct else {}
    pays = [pays[k] for k in range(PARTS)]
    weights = (
        cross_out, cross_out_bias[None], norm_gain, norm_bias, self_weight, self_bias, self_out, self_out_bias[None],
        hidden_weight, hidden_bias[None], hidden_out, hidden_out_bias[None], embed_weight, embed_bias,
    )
    large = (0, 4, 6, 8, 10, 12)
    if direct:
        share = combine([got[k] for k in range(PARTS)], rows)
        share, *raw = beside(share, *[weights[k] for k in large])
        att = gather_in(share, "pix", n_pix)
    else:
        raw = [weights[k] for k in large]
        pay = jnp.concatenate(pays, 0)
        top = lax.pmax(pay[:, rows:tall, :128], "pix")
        ratio = jnp.exp(pay[:, rows:tall, :128] - top)

        def widen(x):
            return jnp.repeat(jnp.transpose(x, (0, 2, 1))[:, :rows], width // HEADS, axis=2)

        numer, total, es = lax.psum(
            (pay[:, :rows] * widen(ratio), pay[:, rows:tall, 128:] * ratio, pay[:, tall:]), "pix")
        att = (jnp.concatenate([numer / widen(total), jnp.concatenate([top, total], 2), es], 1),)
    lowered = dict(zip(large, lower(raw)))
    weights = tuple(lowered.get(k, w) for k, w in enumerate(weights))
    x3, emb, dn, dt, dp1, mine, away = chain(
        me, att, pays, queries, matched_queries, query_cotan, weights, n_pix)

    def unflat(x):
        return jnp.transpose(x.reshape(count, images, -1), (1, 0, 2))

    blocks = mask_features.shape[1] // 512
    mask = functools.partial(mask_out, emb, matched_queries, mask_cotan, mask_features, count, blocks)

    def backward(keys, old, last=False):
        offset = order.index(keys[0]) * images // PARTS
        return attend_back(keys, me, kept, offset, features, dn, dt, keyval_weight, old, last)

    def z_scatter(chunks):
        got = [lax.dynamic_index_in_dim(chunks, (chip ^ k) % 2 * 2 + (chip ^ k) // 2, 0, keepdims=False) for k in range(4)]
        return [got[0]] + [swap(got[k], "batch", n_batch, 2 * k) for k in (1, 2, 3)]

    other = swap(away, "batch", n_batch, 1)
    if direct:
        fg, acc, vb, qp3 = backward((3,), None)
        other, fg, acc, vb, qp3 = beside(other, fg, acc, vb, qp3)
        sums = z_scatter((mine + other).reshape(n_batch // 2, -1, width))
        qp3 = swap(qp3, "pix", n_pix, 3)
        feat_grad, g_kv, qp1, qp2, qp0 = backward((1, 2, 0), (fg, acc, vb), True)
        *sums, feat_grad, g_kv, qp0, qp1, qp2, qp3 = beside(*sums, feat_grad, g_kv, qp0, qp1, qp2, qp3)
        qp1, qp2 = swap(qp1, "pix", n_pix, 1), swap(qp2, "pix", n_pix, 2)
        own = functools.reduce(jnp.add, sums)
        other = swap(own, "batch", n_batch, 4)
        cuts = [blocks * k // 8 for k in (0, 2, 4, 8)]
        outs = mask((cuts[0], cuts[1]))
        qp1, qp2, other, outs = beside(qp1, qp2, other, outs)
        own = join(own, other, "batch", 4)
        other = swap(own, "batch", n_batch, 2)
        split = g_kv.shape[0] // n_pix
        *parts, outs = beside(*query_sum(me, (qp0, qp1, qp2, qp3), g_kv), outs)
        parts = tuple(p if k == 0 else swap(p, "pix", n_pix, k) for k, p in enumerate(parts))
        outs = mask((cuts[1], cuts[2]), outs)
        parts = list(parts)
        parts[1], other, outs = beside(parts[1], other, outs)
        own = join(own, other, "batch", 2)
        low, high = own[:own.shape[0] // 2], own[own.shape[0] // 2:]
        low1, high2 = swap(low, "pix", n_pix, 1), swap(high, "pix", n_pix, 2)
        own2 = swap(own, "batch", n_batch, 1)
        queries_grad, tail, tail2 = query_back(me, tuple(parts), queries, dp1, query_weight)
        tail = tail + swap(tail2, "batch", n_batch, 1)
        tail2 = swap(tail, "batch", n_batch, 2)
        low1, high2, own2, tail2, outs = beside(low1, high2, own2, tail2, outs)
        low3, high3 = jnp.concatenate([low, low1], 0), jnp.concatenate([high, high2], 0)
        low3, high3 = swap(low3, "pix", n_pix, 2), swap(high3, "pix", n_pix, 1)
        low12, high22 = swap(low1, "batch", n_batch, 1), swap(high2, "batch", n_batch, 1)
        tail = tail + tail2
        tail2 = swap(tail, "batch", n_batch, 4)
        outs = mask((cuts[2], cuts[3]), outs)
        low12, high22, tail2, outs = beside(low12, high22, tail2, outs)
        low3, high3, outs = beside(low3, high3, outs)
        tail = tail + tail2
        tail = jnp.concatenate([tail] + [swap(tail, "pix", n_pix, k) for k in (1, 2, 3)], 0)
        pieces = [own, low1, high2, low3, high3]
        pieces += [own2, low12, high22, swap(low3, "batch", n_batch, 1), swap(high3, "batch", n_batch, 1)]
        tails = (tail, swap(tail, "batch", n_batch, 1))
        grads = unpack(me, pieces, tails, split, width, hidden)
        (d_query, d_query_bias, d_keyval, d_value_bias, d_cross, d_cross_bias, d_gain, d_nbias, d_self, d_self_bias,
         d_selfout, d_selfout_bias, d_hidden, d_hidden_bias, d_hidout, d_hidout_bias, d_embed, d_embed_bias) = grads
    else:
        old, parts = None, {}
        for keys, last in (((3,), False), ((1, 2, 0), True)):
            back = backward(keys, old, last)
            count_sums = 1 if last else 2
            old = back[:1 + count_sums]
            parts.update(zip(keys, back[1 + count_sums:]))
        feat_grad, g_kv = old
        parts = [parts[k] for k in range(PARTS)]
        qp = jnp.concatenate(parts, 0)
        outs = mask((0, blocks))
        sums = jnp.concatenate([lax.psum(qp, "pix").reshape(images * rows, width), g_kv], 0)
        queries_grad, tail, tail2 = query_back(me, (sums,), queries, dp1, query_weight)
        first = core == 0
        tail = jnp.concatenate([jnp.where(first, tail, tail2), jnp.where(first, tail2, tail)], 0)
        g_q = lax.psum(tail[g_kv.shape[0]:], "batch")
        g_kv = lax.psum(g_kv, ("batch", "pix"))
        every = [(2 * z, 2 * z + 1) for z in range(n_batch // 2)]
        groups = [[z[c] for z in every] for c in range(2)]
        part = lax.psum(mine + other, "batch", axis_index_groups=groups)
        both = lax.all_gather(part, "batch", axis_index_groups=[list(z) for z in every])
        packed = lax.all_gather(both, "pix").reshape(-1, width)

        def tile(t, k=1):
            return packed[t * width:(t + k) * width]

        def wide(t, k):
            return jnp.concatenate([tile(t + j) for j in range(k)], 1)

        many = hidden // width
        bias = packed[(T_HIDDEN + 2 * many) * width:]
        d_query, d_query_bias = g_q[:width], g_q[width]
        d_keyval, d_value_bias = jnp.concatenate([g_kv[:width], g_kv[width:2 * width]], 1), g_kv[2 * width]
        d_cross, d_cross_bias, d_gain, d_nbias = tile(T_CROSS), bias[0], bias[1:4], bias[4:7]
        d_self, d_self_bias, d_selfout, d_selfout_bias = wide(T_SELF, 3), bias[20:22], tile(T_SELFOUT), bias[7]
        d_hidden, d_hidden_bias = wide(T_HIDDEN, many), bias[8:8 + many]
        d_hidout, d_hidout_bias = tile(T_HIDDEN + many, many), bias[16]
        d_embed, d_embed_bias = tile(T_EMBED, 3), bias[17:20]
    logits, mask_grad = outs
    return (
        unflat(x3),
        unflat(logits),
        unflat(queries_grad),
        feat_grad,
        mask_grad,
        d_query,
        d_query_bias.reshape(-1),
        d_keyval,
        d_value_bias.reshape(-1),
        d_cross,
        d_cross_bias.reshape(-1),
        d_gain,
        d_nbias,
        d_self,
        d_self_bias,
        d_selfout,
        d_selfout_bias.reshape(-1),
        d_hidden,
        d_hidden_bias.reshape(-1),
        d_hidout,
        d_hidout_bias.reshape(-1),
        d_embed.reshape(3, width, width),
        d_embed_bias,
    )


def solution(mesh):
    n_pix, n_batch = mesh.shape["pix"], mesh.shape["batch"]
    rep = P()
    row, pixel, column = P("batch", None, None), P("batch", "pix", None), P("batch", None, "pix")
    in_specs = (row, pixel, pixel, column, P("batch", None), P("batch", None), row, column) + (rep,) * 18
    out_specs = (row, column, row, pixel, pixel) + (rep,) * 18
    body = functools.partial(local, n_pix=n_pix, n_batch=n_batch)
    return jax.shard_map(body, mesh=mesh, in_specs=in_specs, out_specs=out_specs, check_vma=False)
```
